32 devices in a mesh: dp: 8 (over z, x), head: 4 (over y, core).
Axes of the slice: x: 2, y: 2, z: 4, core: 2. Of those that a mesh axis runs over, the one named last changes fastest.
Arguments:
- block_in: bfloat16 [65536, 512], P('dp', 'head'), may hold values from -6 to 6
- crop_ids: int32 [256, 16, 16], P('dp'), may hold values from 0 to 3, as said below
- cotangent: bfloat16 [65536, 512], P('dp', 'head'), may hold values from -6 to 6
- cpe_kernel: bfloat16 [9, 512], P(None, 'head'), may hold values from -2 to 2
- cpe_bias: bfloat16 [512], P('head'), may hold values from -1.75 to 1.75
- norm1_gain: bfloat16 [512], P('head'), may hold values from 0.5 to 1.5
- norm1_shift: bfloat16 [512], P('head'), may hold values from -1.75 to 1.75
- qkv_weight: bfloat16 [512, 3, 512], P(None, None, 'head'), may hold values from -0.25 to 0.25
- qv_bias: bfloat16 [2, 512], P(None, 'head'), may hold values from -3 to 3
- crpe_kernel: bfloat16 [49, 512], P(None, 'head'), may hold values from -1.25 to 1.25
- proj_weight: bfloat16 [512, 512], P('head'), may hold values from -0.25 to 0.25
- proj_bias: bfloat16 [512], P('head'), may hold values from -1.75 to 1.75
- norm2_gain: bfloat16 [512], P('head'), may hold values from 0.5 to 1.5
- norm2_shift: bfloat16 [512], P('head'), may hold values from -1.75 to 1.75
- fc1_weight: bfloat16 [512, 2048], P(None, 'head'), may hold values from -0.25 to 0.25
- fc1_bias: bfloat16 [2048], P('head'), may hold values from -3 to 3
- fc2_weight: bfloat16 [2048, 512], P('head'), may hold values from -0.125 to 0.125
- fc2_bias: bfloat16 [512], P('head'), may hold values from -1.75 to 1.75
Outputs:
- block_out: float32 [65536, 512], P('dp', 'head')
- input_grad: float32 [65536, 512], P('dp', 'head')
- cpe_kernel_grad: float32 [9, 512], P(None, 'head')
- cpe_bias_grad: float32 [512], P('head')
- norm1_gain_grad: float32 [512], P('head')
- norm1_shift_grad: float32 [512], P('head')
- qkv_weight_grad: float32 [512, 3, 512], P(None, None, 'head')
- qv_bias_grad: float32 [2, 512], P(None, 'head')
- crpe_kernel_grad: float32 [49, 512], P(None, 'head')
- proj_weight_grad: float32 [512, 512], P('head')
- proj_bias_grad: float32 [512], P('head')
- norm2_gain_grad: float32 [512], P('head')
- norm2_shift_grad: float32 [512], P('head')
- fc1_weight_grad: float32 [512, 2048], P(None, 'head')
- fc1_bias_grad: float32 [2048], P('head')
- fc2_weight_grad: float32 [2048, 512], P('head')
- fc2_bias_grad: float32 [512], P('head')
The draws below stay inside these ranges and needn't reach their ends.
Inputs may be any that keep to these rules, and one draw needn't show every extreme that they name: `crop_ids`: every canvas is cut by one row cut into an upper and a lower band, and each band by one column cut; ids are 0 upper left, 1 upper right, 2 lower left, 3 lower right; every rectangle is 3 or more tokens along each side, so all 4 ids occur in every canvas.
All inputs are finite; a program needn't handle non-finite values.
Results may differ from the reference program's by a relative error of at most 0.015.
Values may be sent and summed in bfloat16 or wider, within the bound.
A program may use at most 320 MiB of HBM per device.

```python
import math
import jax
import jax.numpy as jnp
from jax import lax

D = 512
HEADS = 8
HEAD_DIM = 64
HIDDEN_SIZE = 2048
SIDE = 16
CROPS = 4
CANVASES = 256
TOKENS = 65536


def draw_crop_ids(key, part):
    key = jax.random.fold_in(key, 11)
    keys_all = jax.random.split(key, 3)
    cut_row = jax.random.randint(keys_all[0], (CANVASES, 1, 1), 3, SIDE - 2)
    cut_upper = jax.random.randint(keys_all[1], (CANVASES, 1, 1), 3, SIDE - 2)
    cut_lower = jax.random.randint(keys_all[2], (CANVASES, 1, 1), 3, SIDE - 2)
    row_ids = jnp.arange(SIDE, dtype=jnp.int32)[None, :, None]
    col_ids = jnp.arange(SIDE, dtype=jnp.int32)[None, None, :]
    lower_band = (row_ids >= cut_row).astype(jnp.int32)
    col_cut = jnp.where(lower_band > 0, cut_lower, cut_upper)
    right_side = (col_ids >= col_cut).astype(jnp.int32)
    return (2 * lower_band + right_side).astype(jnp.int32)


def shard_levels(stream_key, extent, shards, least, top_value):
    def one(position, parts):
        heights = jax.random.uniform(jax.random.fold_in(jax.random.fold_in(stream_key, 6), position), (parts,), jnp.float32, least / len(shards), top_value / len(shards))
        return jnp.repeat(jnp.exp(heights), extent[position] // parts).reshape((-1,) + (1,) * (len(extent) - position - 1))

    gain = one(*shards[0])
    for cut in shards[1:]:
        gain = gain * one(*cut)
    return gain


def normal_values(rng, extent, deviation, reach, cuts=(), kind=jnp.bfloat16):
    array = deviation * jax.random.normal(rng, extent, jnp.float32)
    if cuts:
        array = array * shard_levels(rng, extent, cuts, -0.22, 0.18)
    return jnp.clip(array, -reach, reach).astype(kind)


def setup_inputs(seed: int = 0) -> dict:
    arg_keys = jax.random.split(jax.random.key(seed), 19)
    block_in = normal_values(arg_keys[0], (TOKENS, D), 1.0, 6.0, ((0, 8), (1, 4)))
    crop_ids = draw_crop_ids(jax.random.fold_in(arg_keys[18], 71), 0)
    cotangent = normal_values(arg_keys[2], (TOKENS, D), 1.0, 6.0, ((0, 8), (1, 4)))
    cpe_kernel = normal_values(arg_keys[3], (9, D), 9 ** -0.5, 2.0, ((1, 4),))
    cpe_bias = normal_values(arg_keys[4], (D,), 0.3, 1.75, ((0, 4),))
    norm1_gain = jnp.clip(1.0 + 0.1 * jax.random.normal(arg_keys[5], (D,), jnp.float32), 0.5, 1.5).astype(jnp.bfloat16)
    norm1_shift = normal_values(arg_keys[6], (D,), 0.3, 1.75, ((0, 4),))
    qkv_weight = normal_values(arg_keys[7], (D, 3, D), D ** -0.5, 0.25, ((2, 4),))
    qv_bias = normal_values(arg_keys[8], (2, D), 0.5, 3.0, ((1, 4),))
    crpe_kernel = normal_values(arg_keys[9], (49, D), 25 ** -0.5, 1.25, ((1, 4),))
    proj_weight = normal_values(arg_keys[10], (D, D), D ** -0.5, 0.25, ((0, 4),))
    proj_bias = normal_values(arg_keys[11], (D,), 0.3, 1.75, ((0, 4),))
    norm2_gain = jnp.clip(1.0 + 0.1 * jax.random.normal(arg_keys[12], (D,), jnp.float32), 0.5, 1.5).astype(jnp.bfloat16)
    norm2_shift = normal_values(arg_keys[13], (D,), 0.3, 1.75, ((0, 4),))
    fc1_weight = normal_values(arg_keys[14], (D, HIDDEN_SIZE), D ** -0.5, 0.25, ((1, 4),))
    fc1_bias = normal_values(arg_keys[15], (HIDDEN_SIZE,), 0.5, 3.0, ((0, 4),))
    fc2_weight = normal_values(arg_keys[16], (HIDDEN_SIZE, D), HIDDEN_SIZE ** -0.5, 0.125, ((0, 4),))
    fc2_bias = normal_values(arg_keys[17], (D,), 0.3, 1.75, ((0, 4),))
    return dict(block_in=block_in, crop_ids=crop_ids, cotangent=cotangent, cpe_kernel=cpe_kernel, cpe_bias=cpe_bias, norm1_gain=norm1_gain, norm1_shift=norm1_shift, qkv_weight=qkv_weight, qv_bias=qv_bias, crpe_kernel=crpe_kernel, proj_weight=proj_weight, proj_bias=proj_bias, norm2_gain=norm2_gain, norm2_shift=norm2_shift, fc1_weight=fc1_weight, fc1_bias=fc1_bias, fc2_weight=fc2_weight, fc2_bias=fc2_bias)


EPSILON = 1e-06
PRECISE = lax.Precision.HIGHEST

@jax.custom_vjp
def low(v):
    return lax.optimization_barrier(v.astype(jnp.bfloat16)).astype(jnp.float32)

@jax.custom_vjp
def low_back(v):
    return v

def low_keep(v):
    return (low(v), None)

def low_pass(kept, grad):
    return (grad,)

def back_keep(v):
    return (v, None)

def back_low(kept, grad):
    return (low(grad),)
low.defvjp(low_keep, low_pass)
low_back.defvjp(back_keep, back_low)

def matmul(left, right):
    return jnp.dot(left, right, precision=PRECISE, preferred_element_type=jnp.float32)

def shift_grid(values_grid, row_step, col_step):
    padded = jnp.pad(values_grid, ((0, 0), (3, 3), (3, 3), (0, 0)))
    return padded[:, 3 + row_step:3 + row_step + SIDE, 3 + col_step:3 + col_step + SIDE, :]

def same_crop(crop_map, row_step, col_step):
    padded = jnp.pad(crop_map, ((0, 0), (3, 3), (3, 3)), constant_values=-1)
    return (padded[:, 3 + row_step:3 + row_step + SIDE, 3 + col_step:3 + col_step + SIDE] == crop_map)[..., None]

def crop_conv(values_grid, crop_map, kernel, reach_size):
    tap_width = 2 * reach_size + 1
    accumulated = jnp.zeros_like(values_grid)
    for row_step in range(-reach_size, reach_size + 1):
        for col_step in range(-reach_size, reach_size + 1):
            tap_index = (row_step + reach_size) * tap_width + col_step + reach_size
            moved = jnp.where(same_crop(crop_map, row_step, col_step), shift_grid(values_grid, row_step, col_step), 0.0)
            accumulated = accumulated + kernel[tap_index] * moved
    return accumulated

def reach_mask(channel_start, channel_count):
    channel_ids = channel_start + jnp.arange(channel_count, dtype=jnp.int32)
    head_ids = channel_ids // HEAD_DIM
    reach_size = 1 + (head_ids >= HEADS // 4).astype(jnp.int32) + (head_ids >= 5 * HEADS // 8).astype(jnp.int32)
    tap_ids = jnp.arange(49, dtype=jnp.int32)
    cycle_size = jnp.maximum(jnp.abs(tap_ids // 7 - 3), jnp.abs(tap_ids % 7 - 3))
    return (cycle_size[:, None] <= reach_size[None, :]).astype(jnp.float32)

def norm_rows(full_rows, gain_vec, shift_vec):
    center = lax.optimization_barrier(jnp.mean(full_rows, axis=-1, keepdims=True))
    square = lax.optimization_barrier(jnp.mean(full_rows * full_rows, axis=-1, keepdims=True))
    inv_std = lax.rsqrt(square - center * center + EPSILON)
    return (full_rows - center) * inv_std * gain_vec + shift_vec

def attend(queries, key_rows, value_rows, crop_map, kernel_eff):
    canvas_count = crop_map.shape[0]
    places = SIDE * SIDE
    onehot = (crop_map.reshape(canvas_count, places)[:, :, None] == jnp.arange(CROPS, dtype=jnp.int32)[None, None, :]).astype(jnp.float32)
    keys_canvas = key_rows.reshape(canvas_count, places, D)
    highest = lax.optimization_barrier(jnp.max(jnp.where(onehot[..., None] > 0, keys_canvas[:, :, None, :], -1e+30), axis=1))
    lifted = jnp.einsum('btc,bcd->btd', onehot, highest, precision=PRECISE)
    exp_keys = jnp.exp(keys_canvas - lifted)
    totals = jnp.einsum('btc,btd->bcd', onehot, exp_keys, precision=PRECISE)
    key_soft = low(low_back(exp_keys / jnp.einsum('btc,bcd->btd', onehot, totals, precision=PRECISE)))
    head_shape = (canvas_count, places, HEADS, HEAD_DIM)
    spread_soft = onehot[:, :, :, None, None] * key_soft.reshape(head_shape)[:, :, None]
    context = jnp.einsum('btchd,bthe->bchde', spread_soft, value_rows.reshape(head_shape), precision=PRECISE)
    context = low(low_back(context))
    all_crops = jnp.einsum('bthd,bchde->btche', queries.reshape(head_shape), context, precision=PRECISE)
    factor = lax.optimization_barrier(jnp.sum(all_crops * onehot[:, :, :, None, None], axis=2)).reshape(canvas_count * places, D)
    conv_value = crop_conv(value_rows.reshape(canvas_count, SIDE, SIDE, D), crop_map, kernel_eff, 3)
    conv_value = conv_value.reshape(canvas_count * places, D)
    return factor * HEAD_DIM ** (-0.5) + queries * conv_value

def forward(param_set, inputs_now, crop_map):
    cpe_kernel, cpe_bias, gain_one, shift_one, qkv_weight, qv_bias, crpe_kernel, proj_weight, proj_bias, gain_two, shift_two, fc1_weight, fc1_bias, fc2_weight, fc2_bias = param_set
    canvas_count = crop_map.shape[0]
    first_sum = inputs_now + crop_conv(inputs_now.reshape(canvas_count, SIDE, SIDE, D), crop_map, cpe_kernel, 1).reshape(-1, D) + cpe_bias
    hidden_one = low(norm_rows(first_sum, gain_one, shift_one))
    projected = matmul(hidden_one, qkv_weight.reshape(D, 3 * D))
    queries = low(low_back(projected[:, :D] + qv_bias[0]))
    key_rows = low(low_back(projected[:, D:2 * D]))
    value_rows = low(low_back(projected[:, 2 * D:] + qv_bias[1]))
    kernel_eff = crpe_kernel * reach_mask(0, D)
    attended = low(low_back(attend(queries, key_rows, value_rows, crop_map, kernel_eff)))
    second = first_sum + low_back(matmul(attended, proj_weight) + proj_bias)
    hidden_two = low(norm_rows(second, gain_two, shift_two))
    pre_act = low_back(matmul(hidden_two, fc1_weight) + fc1_bias)
    active = low(jax.nn.gelu(pre_act, approximate=False))
    return second + low_back(matmul(active, fc2_weight) + fc2_bias)

def reference(block_in, crop_ids, cotangent, cpe_kernel, cpe_bias, norm1_gain, norm1_shift, qkv_weight, qv_bias, crpe_kernel, proj_weight, proj_bias, norm2_gain, norm2_shift, fc1_weight, fc1_bias, fc2_weight, fc2_bias):
    param_set = tuple((item.astype(jnp.float32) for item in (cpe_kernel, cpe_bias, norm1_gain, norm1_shift, qkv_weight, qv_bias, crpe_kernel, proj_weight, proj_bias, norm2_gain, norm2_shift, fc1_weight, fc1_bias, fc2_weight, fc2_bias)))
    group_size = math.gcd(CANVASES, 16)
    step_count = CANVASES // group_size
    inputs_all = block_in.astype(jnp.float32).reshape(step_count, group_size * SIDE * SIDE, D)
    crop_all = crop_ids.reshape(step_count, group_size, SIDE, SIDE)
    cot_all = cotangent.astype(jnp.float32).reshape(step_count, group_size * SIDE * SIDE, D)

    def one_group(carried, one_item):
        inputs_now, crop_map, cot_now = one_item
        outputs, pullback = jax.vjp(lambda params_now, rows_now: forward(params_now, rows_now, crop_map), param_set, inputs_now)
        gradients, rows_grad = pullback(cot_now)
        return (tuple((left + right for left, right in zip(carried, gradients))), (outputs, rows_grad))
    initial = tuple((jnp.zeros_like(item) for item in param_set))
    sums, (outputs_all, grads_all) = lax.scan(one_group, initial, (inputs_all, crop_all, cot_all))
    return (outputs_all.reshape(TOKENS, D), grads_all.reshape(TOKENS, D), sums[0], sums[1], sums[2], sums[3], sums[4], sums[5], sums[6], sums[7], sums[8], sums[9], sums[10], sums[11], sums[12], sums[13], sums[14])
```

```python
import jax
import jax.numpy as jnp
from jax import lax
from jax.experimental import pallas as pl
from jax.experimental.pallas import tpu as pltpu
from jax.sharding import PartitionSpec as P

D = 512
HEADS = 8
HEAD_DIM = 64
HIDDEN = 2048
SIDE = 16
PLACES = 256
LANES = 128
TILES = 4
REACH = (1, 2, 3, 3)
GAP = 3
GRID_ROWS = SIDE + 3 * GAP + 1
EPSILON = 1e-06
SCALE = HEAD_DIM ** (-0.5)
F32 = jnp.float32
BF16 = jnp.bfloat16


def dot(left, right, dims):
    return lax.dot_general(left, right, (dims, ((), ())), preferred_element_type=F32)


def nn(left, right):
    return dot(left, right, ((1,), (0,)))


def nt(left, right):
    return dot(left, right, ((1,), (1,)))


def tn(left, right):
    return dot(left, right, ((0,), (0,)))


def lane(tile):
    return pl.ds(LANES * tile, LANES)


def fill_masks(cut, col_cuts, mask_ref):
    col = lax.broadcasted_iota(jnp.int32, (SIDE, LANES), 0)
    for band in range(2):
        here = (col >= col_cuts[band]).astype(jnp.int32)
        for step in range(-3, 4):
            if step == 0:
                continue
            there = (col + step >= col_cuts[band]).astype(jnp.int32)
            good = (col + step >= 0) & (col + step < SIDE) & (here == there)
            mask_ref[band, step + 3] = jnp.where(good, 1.0, 0.0).astype(F32)


def place_ids(cut, col_cuts):
    place = lax.broadcasted_iota(jnp.int32, (PLACES, LANES), 0)
    row = lax.shift_right_logical(place, 4)
    col = lax.bitwise_and(place, 15)
    band = (row >= cut).astype(jnp.int32)
    col_cut = jnp.where(band > 0, col_cuts[1], col_cuts[0])
    side = (col >= col_cut).astype(jnp.int32)
    return band, side


def spread(read_row, reach, cut, mask_ref, grid_ref):
    zero = jnp.zeros((GAP * SIDE, LANES), F32)
    for step in range(-reach, reach + 1):
        start = pl.multiple_of(SIDE * (GAP + cut), SIDE)
        grid_ref[step + 3, pl.ds(start, GAP * SIDE), :] = zero
    for row in range(SIDE):
        lower = (row >= cut).astype(jnp.int32)
        start = pl.multiple_of(SIDE * (row + GAP + GAP * lower), SIDE)
        values = read_row(row)
        for step in range(-reach, reach + 1):
            moved = values
            if step != 0:
                moved = pltpu.roll(values, (-step) % SIDE, 0) * mask_ref[lower, step + 3]
            grid_ref[step + 3, pl.ds(start, SIDE), :] = moved


def pair_place(index, cut, upper_pairs, reach):
    lower = (index >= upper_pairs).astype(jnp.int32)
    row = 2 * index + lower * (cut - 2 * upper_pairs)
    base = row + GAP * lower + (GAP - reach)
    return lower, row, base


def conv_tile(reach, cut, grid_ref, taps_ref, tap_reach, tile, out_ref):
    upper_pairs = (cut + 1) // 2
    pairs = upper_pairs + (SIDE - cut + 1) // 2
    width = 2 * tap_reach + 1

    def body(index, carry):
        lower, row, base = pair_place(index, cut, upper_pairs, reach)
        total = [[None, None], [None, None]]
        for step in range(-reach, reach + 1):
            taps = [
                taps_ref[(dr + tap_reach) * width + step + tap_reach, :, lane(tile)]
                for dr in range(-reach, reach + 1)
            ]
            for place in range(2 * reach + 2):
                for half in range(2):
                    start = pl.multiple_of(SIDE * (base + place) + 8 * half, 8)
                    field = grid_ref[step + 3, pl.ds(start, 8), :]
                    for out in range(2):
                        tap = place - out
                        if 0 <= tap <= 2 * reach:
                            term = taps[tap] * field
                            old = total[out][half]
                            total[out][half] = term if old is None else old + term
        for out in range(2):
            for half in range(2):
                start = pl.multiple_of(SIDE * (row + out) + 8 * half, 8)
                out_ref[pl.ds(start, 8), :] = total[out][half]
        return carry

    lax.fori_loop(0, pairs, body, 0)


def conv_back_tile(reach, cut, grid_ref, taps_ref, tap_reach, tile, other_ref, out_ref, sum_ref):
    upper_pairs = (cut + 1) // 2
    pairs = upper_pairs + (SIDE - cut + 1) // 2
    width = 2 * tap_reach + 1

    def body(index, carry):
        lower, row, base = pair_place(index, cut, upper_pairs, reach)
        keep = jnp.where((lower == 0) & (row + 1 >= cut), 0.0, 1.0).astype(F32)
        other = []
        for out in range(2):
            halves = []
            for half in range(2):
                start = pl.multiple_of(SIDE * (row + out) + 8 * half, 8)
                value = other_ref[pl.ds(start, 8), :]
                halves.append(value * keep if out else value)
            other.append(halves)
        total = [[None, None], [None, None]]
        for step in range(-reach, reach + 1):
            sums = [None] * (2 * reach + 1)
            ids = [
                (tap_reach - dr) * width + tap_reach - step for dr in range(-reach, reach + 1)
            ]
            taps = [taps_ref[item, :, lane(tile)] for item in ids]
            for place in range(2 * reach + 2):
                for half in range(2):
                    start = pl.multiple_of(SIDE * (base + place) + 8 * half, 8)
                    field = grid_ref[step + 3, pl.ds(start, 8), :]
                    for out in range(2):
                        tap = place - out
                        if 0 <= tap <= 2 * reach:
                            term = taps[tap] * field
                            old = total[out][half]
                            total[out][half] = term if old is None else old + term
                            part = other[out][half] * field
                            old = sums[tap]
                            sums[tap] = part if old is None else old + part
            for tap in range(2 * reach + 1):
                sum_ref[ids[tap], :, lane(tile)] += sums[tap]
        for out in range(2):
            for half in range(2):
                start = pl.multiple_of(SIDE * (row + out) + 8 * half, 8)
                out_ref[pl.ds(start, 8), :] = total[out][half]
        return carry

    lax.fori_loop(0, pairs, body, 0)


def row_mean(values):
    return jnp.sum(values, axis=1, keepdims=True) * (1.0 / D)


def pick(ids, rows):
    out = rows[0]
    for crop in range(1, 4):
        out = jnp.where(ids >= crop, rows[crop], out)
    return out


def crop_reduce(ids, values, op, empty):
    return [op(jnp.where(ids == crop, values, empty), axis=0, keepdims=True) for crop in range(4)]


def head_block():
    row = lax.broadcasted_iota(jnp.int32, (2 * LANES, 2 * LANES), 0)
    col = lax.broadcasted_iota(jnp.int32, (2 * LANES, 2 * LANES), 1)
    same = lax.bitwise_and(row, HEAD_DIM) == lax.bitwise_and(col, HEAD_DIM)
    return jnp.where(same, 1.0, 0.0).astype(F32)


def both(values, masks):
    return jnp.concatenate([values * masks[0], values * masks[1]], axis=1)


def read_cuts(cuts_ref, base):
    step = pl.program_id(0) + base
    return cuts_ref[step, 0], (cuts_ref[step, 1], cuts_ref[step, 2])


def whole(shape):
    return pl.BlockSpec(shape, lambda *_: (0,) * len(shape))


def once(shape):
    return pl.BlockSpec(shape, lambda *_: (0,) * len(shape), pipeline_mode=pl.Buffered(1))


def rows_spec(width, base=0):
    return pl.BlockSpec((PLACES, width), lambda i, *_: (i + base, 0))


def context_spec(base):
    return pl.BlockSpec((1, TILES, 2 * LANES, 2 * LANES), lambda i, *_: (i + base, 0, 0, 0))


def like(shape, dtype):
    return jax.ShapeDtypeStruct(shape, dtype)


def params(**given):
    return pltpu.CompilerParams(vmem_limit_bytes=58 * 2**20, **given)


def front_kernel(base, kept, *refs):
    (cuts_ref, me_ref, x0_ref, x1_ref, x2_ref, x3_ref, cpe_ref, vec_ref, qkv_ref, crpe_ref) = refs[:10]
    (first_ref, hidden_ref, query_ref, value_ref, soft_ref, context_ref, conv_ref, attended_ref,
     mask_ref, grid_ref, out_ref, x_ref) = refs[10 + kept :]
    cut, col_cuts = read_cuts(cuts_ref, base)
    me = me_ref[0]

    @pl.when(pl.program_id(0) == 0)
    def _():
        grid_ref[...] = jnp.zeros_like(grid_ref)

    for move, piece_ref in enumerate((x0_ref, x1_ref, x2_ref, x3_ref)):
        start = pl.multiple_of(LANES * lax.bitwise_xor(me, move), LANES)
        x_ref[:, pl.ds(start, LANES)] = piece_ref[...].astype(F32)
    fill_masks(cut, col_cuts, mask_ref)
    for tile in range(TILES):
        spread(
            lambda row: x_ref[SIDE * row : SIDE * row + SIDE, lane(tile)],
            1, cut, mask_ref, grid_ref,
        )
        conv_tile(1, cut, grid_ref, cpe_ref, 1, tile, out_ref)
        first_ref[:, lane(tile)] = (
            x_ref[:, lane(tile)] + out_ref[:PLACES, :] + vec_ref[0:1, lane(tile)]
        )
    first = first_ref[...]
    center = row_mean(first)
    square = row_mean(first * first)
    inverse = lax.rsqrt(square - center * center + EPSILON)
    hidden = ((first - center) * inverse * vec_ref[1:2, :] + vec_ref[2:3, :]).astype(BF16)
    hidden_ref[...] = hidden
    band, side = place_ids(cut, col_cuts)
    ids = 2 * band + side
    sides = [(side == item).astype(F32).astype(BF16) for item in range(2)]
    bands = [(band == item).astype(F32).astype(BF16) for item in range(2)]
    blocks = head_block()
    for tile in range(TILES):
        reach = REACH[tile]
        three = nn(hidden, qkv_ref[lax.bitwise_xor(me, tile)])
        query = (three[:, :LANES] + vec_ref[3:4, lane(tile)]).astype(BF16)
        keys = three[:, LANES : 2 * LANES].astype(BF16).astype(F32)
        value = (three[:, 2 * LANES :] + vec_ref[4:5, lane(tile)]).astype(BF16)
        query_ref[:, lane(tile)] = query
        value_ref[:, lane(tile)] = value
        highest = crop_reduce(ids, keys, jnp.max, -1e30)
        powers = jnp.exp(keys - pick(ids, highest))
        totals = crop_reduce(ids, powers, jnp.sum, 0.0)
        soft = (powers * pick(ids, [1.0 / item for item in totals])).astype(BF16)
        soft_ref[:, lane(tile)] = soft
        context = (tn(both(soft, sides), both(value, bands)) * blocks).astype(BF16)
        context_ref[0, tile] = context
        factor = nn(both(query, sides), context)
        factor = jnp.where(band > 0, factor[:, LANES:], factor[:, :LANES])
        spread(
            lambda row: value_ref[SIDE * row : SIDE * row + SIDE, lane(tile)].astype(F32),
            reach, cut, mask_ref, grid_ref,
        )
        conv_tile(reach, cut, grid_ref, crpe_ref, 3, tile, out_ref)
        conv = out_ref[:PLACES, :]
        conv_ref[:, lane(tile)] = conv.astype(BF16)
        attended_ref[:, lane(tile)] = (factor * SCALE + query.astype(F32) * conv).astype(BF16)


def front(cuts, me, x_parts, base, kept, cpe, vec, qkv, crpe):
    count = x_parts[0].shape[0] // PLACES
    total = cuts.shape[0]
    rows = total * PLACES
    wide = rows_spec(D, base)
    flops = 2 * count * PLACES * D * D * 4
    return pl.pallas_call(
        lambda *refs: front_kernel(base, len(kept), *refs),
        grid_spec=pltpu.PrefetchScalarGridSpec(
            num_scalar_prefetch=2,
            grid=(count,),
            in_specs=[rows_spec(LANES)] * 4
            + [whole(cpe.shape), whole(vec.shape), whole(qkv.shape), whole(crpe.shape)]
            + [pl.BlockSpec(memory_space=pl.ANY)] * len(kept),
            out_specs=[wide, wide, wide, wide, wide, context_spec(base), wide, wide],
            scratch_shapes=[
                pltpu.VMEM((2, 7, SIDE, LANES), F32),
                pltpu.VMEM((7, GRID_ROWS * SIDE, LANES), F32),
                pltpu.VMEM((PLACES + SIDE, LANES), F32),
                pltpu.VMEM((PLACES, D), F32),
            ],
        ),
        out_shape=[
            like((rows, D), F32), like((rows, D), BF16), like((rows, D), BF16),
            like((rows, D), BF16), like((rows, D), BF16),
            like((total, TILES, 2 * LANES, 2 * LANES), BF16),
            like((rows, D), BF16), like((rows, D), BF16),
        ],
        input_output_aliases={10 + item: item for item in range(len(kept))},
        compiler_params=params(),
        cost_estimate=pl.CostEstimate(flops=flops * 6, bytes_accessed=count * 10**7, transcendentals=0),
        name="front",
    )(cuts, me, *x_parts, cpe, vec, qkv, crpe, *kept)


def gelu_both(pre):
    power = jnp.exp(pre * pre * -0.5)
    t = 1.0 / (1.0 + jnp.abs(pre) * (0.3275911 * 0.7071067811865476))
    poly = 0.5 * 1.061405429
    for item in (-1.453152027, 1.421413741, -0.284496736, 0.254829592):
        poly = poly * t + 0.5 * item
    tail = poly * t * power
    cdf = jnp.where(pre >= 0.0, 1.0 - tail, tail)
    return pre * cdf, cdf + pre * power * 0.3989422804014327


CHUNK = 256
BLOCK = 512


def middle_kernel(
    me_ref, attended_ref, first_ref, cot0_ref, cot1_ref, cot2_ref, cot3_ref, vec_ref, bias_ref,
    proj_ref, fc1_ref, fc2_ref,
    out0_ref, out1_ref, out2_ref, out3_ref, second_grad_ref, att_grad_ref, fc1_grad_ref,
    fc2_grad_ref, proj_grad_ref, sum_ref, bias_grad_ref,
    cot_ref, hat_ref, inverse_ref, hidden_ref, total_ref, back_ref, active_ref, pre_grad_ref,
):
    me = me_ref[0]
    step = pl.program_id(0)
    rows = attended_ref.shape[0]
    blocks = rows // BLOCK

    def part(index):
        return pl.ds(pl.multiple_of(BLOCK * index, BLOCK), BLOCK)

    @pl.when(step == 0)
    def _():
        sum_ref[...] = jnp.zeros_like(sum_ref)
        for move, piece_ref in enumerate((cot0_ref, cot1_ref, cot2_ref, cot3_ref)):
            start = pl.multiple_of(LANES * lax.bitwise_xor(me, move), LANES)
            cot_ref[:, pl.ds(start, LANES)] = piece_ref[...]

        def enter(index, carry):
            now = part(index)
            second = first_ref[now, :] + vec_ref[0:1, :]
            for tile in range(TILES):
                second += nn(attended_ref[now, lane(tile)], proj_ref[lax.bitwise_xor(me, tile)])
            center = row_mean(second)
            square = row_mean(second * second)
            inverse = lax.rsqrt(square - center * center + EPSILON)
            hat = (second - center) * inverse
            hidden_ref[now, :] = (hat * vec_ref[1:2, :] + vec_ref[2:3, :]).astype(BF16)
            hat_ref[now, :] = hat
            inverse_ref[now, :] = jnp.broadcast_to(inverse, (BLOCK, LANES))
            total_ref[now, :] = second + vec_ref[3:4, :]
            back_ref[now, :] = jnp.zeros((BLOCK, D), F32)
            sum_ref[0:1, :] += jnp.sum(cot_ref[now, :].astype(F32), axis=0, keepdims=True)
            return carry

        lax.fori_loop(0, blocks, enter, 0)

    bias_grad_ref[0] = jnp.zeros((1, CHUNK), F32)

    def chunk(index, carry):
        now = part(index)
        pre = nn(hidden_ref[now, :], fc1_ref[0]) + bias_ref[0]
        active, slope = gelu_both(pre)
        active = active.astype(BF16)
        active_ref[now, :] = active
        total_ref[now, :] += nn(active, fc2_ref[0])
        pre_grad_f = nt(cot_ref[now, :], fc2_ref[0]) * slope
        pre_grad = pre_grad_f.astype(BF16)
        pre_grad_ref[now, :] = pre_grad
        back_ref[now, :] += nt(pre_grad, fc1_ref[0])
        bias_grad_ref[0] += jnp.sum(pre_grad_f, axis=0, keepdims=True)
        return carry

    lax.fori_loop(0, blocks, chunk, 0)
    fc2_grad_ref[0] = tn(active_ref[...], cot_ref[...]).astype(fc2_grad_ref.dtype)
    fc1_grad_ref[0] = tn(hidden_ref[...], pre_grad_ref[...]).astype(fc1_grad_ref.dtype)

    @pl.when(step == pl.num_programs(0) - 1)
    def _():
        def leave(index, carry):
            now = part(index)
            for move, piece_ref in enumerate((out0_ref, out1_ref, out2_ref, out3_ref)):
                start = pl.multiple_of(LANES * lax.bitwise_xor(me, move), LANES)
                piece_ref[now, :] = total_ref[now, pl.ds(start, LANES)].astype(BF16)
            hat = hat_ref[now, :]
            norm_grad = back_ref[now, :]
            weighted = norm_grad * vec_ref[1:2, :]
            second_grad = cot_ref[now, :].astype(F32) + inverse_ref[now, 0:1] * (
                weighted - row_mean(weighted) - hat * row_mean(weighted * hat)
            )
            second_grad_ref[now, :] = second_grad
            low = second_grad.astype(BF16)
            hidden_ref[now, :] = low
            for tile in range(TILES):
                att_grad_ref[now, lane(tile)] = nt(low, proj_ref[lax.bitwise_xor(me, tile)]).astype(BF16)
            sum_ref[1:2, :] += jnp.sum(norm_grad * hat, axis=0, keepdims=True)
            sum_ref[2:3, :] += jnp.sum(norm_grad, axis=0, keepdims=True)
            sum_ref[3:4, :] += jnp.sum(low.astype(F32), axis=0, keepdims=True)
            return carry

        lax.fori_loop(0, blocks, leave, 0)
        for tile in range(TILES):
            proj_grad_ref[lax.bitwise_xor(me, tile)] = tn(
                attended_ref[:, lane(tile)], hidden_ref[...]
            ).astype(proj_grad_ref.dtype)


def middle(me, attended, first, cot_parts, vec, bias, proj, fc1, fc2):
    rows = attended.shape[0]
    split = fc1.shape[2] // CHUNK
    steps = 4 * split
    left = pl.BlockSpec((1, D, CHUNK), lambda i, *_: (i // split, 0, i % split))
    right = pl.BlockSpec((1, CHUNK, D), lambda i, *_: (i // split, i % split, 0))
    piece = once((rows, LANES))
    wide = once((rows, D))
    line = pl.BlockSpec((1, 1, CHUNK), lambda i, *_: (i // split, 0, i % split))
    return pl.pallas_call(
        middle_kernel,
        grid_spec=pltpu.PrefetchScalarGridSpec(
            num_scalar_prefetch=1,
            grid=(steps,),
            in_specs=[
                wide, wide, piece, piece, piece, piece, whole(vec.shape), line, once(proj.shape),
                left, right,
            ],
            out_specs=[
                piece, piece, piece, piece, wide, wide, left, right, once(proj.shape),
                whole((8, D)), line,
            ],
            scratch_shapes=[
                pltpu.VMEM((rows, D), BF16), pltpu.VMEM((rows, D), F32),
                pltpu.VMEM((rows, LANES), F32),
                pltpu.VMEM((rows, D), BF16), pltpu.VMEM((rows, D), F32),
                pltpu.VMEM((rows, D), F32), pltpu.VMEM((rows, CHUNK), BF16),
                pltpu.VMEM((rows, CHUNK), BF16),
            ],
        ),
        out_shape=[like((rows, LANES), BF16)] * 4 + [
            like((rows, D), F32), like((rows, D), BF16),
            like(fc1.shape, BF16), like(fc2.shape, BF16), like(proj.shape, BF16),
            like((8, D), F32), like(bias.shape, F32),
        ],
        compiler_params=params(),
        cost_estimate=pl.CostEstimate(flops=rows * D * D * 60, bytes_accessed=3 * 10**7, transcendentals=0),
        name="middle",
    )(me, attended, first, *cot_parts, vec, bias, proj, fc1, fc2)


def back_kernel(
    base,
    cuts_ref, me_ref, x0_ref, x1_ref, x2_ref, x3_ref,
    grad_ref, query_ref, value_ref, soft_ref, context_ref, conv_ref,
    first_ref, hidden_ref, second_grad_ref, vec_ref, qkv_ref, crpe_ref, cpe_ref,
    out0_ref, out1_ref, out2_ref, out3_ref, qkv_grad_ref, crpe_sum_ref, cpe_sum_ref, sum_ref,
    mask_ref, grid_ref, out_ref, other_ref, three_ref, first_grad_ref, norm_grad_ref,
):
    cut, col_cuts = read_cuts(cuts_ref, base)
    me = me_ref[0]

    @pl.when(pl.program_id(0) == 0)
    def _():
        grid_ref[...] = jnp.zeros_like(grid_ref)
        other_ref[...] = jnp.zeros_like(other_ref)
        qkv_grad_ref[...] = jnp.zeros_like(qkv_grad_ref)
        crpe_sum_ref[...] = jnp.zeros_like(crpe_sum_ref)
        cpe_sum_ref[...] = jnp.zeros_like(cpe_sum_ref)
        sum_ref[...] = jnp.zeros_like(sum_ref)

    fill_masks(cut, col_cuts, mask_ref)
    band, side = place_ids(cut, col_cuts)
    ids = 2 * band + side
    sides = [(side == item).astype(F32).astype(BF16) for item in range(2)]
    bands = [(band == item).astype(F32).astype(BF16) for item in range(2)]
    blocks = head_block() * SCALE
    hidden = hidden_ref[...]
    for tile in range(TILES):
        reach = REACH[tile]
        shard = lax.bitwise_xor(me, tile)
        grad = grad_ref[:, lane(tile)]
        query = query_ref[:, lane(tile)]
        value = value_ref[:, lane(tile)]
        soft = soft_ref[:, lane(tile)]
        context = context_ref[0, tile]
        grad_f = grad.astype(F32)
        grad_bands = both(grad, bands)
        context_grad = (tn(both(query, sides), grad_bands) * blocks).astype(BF16)
        part = nt(grad_bands, context)
        part = jnp.where(side > 0, part[:, LANES:], part[:, :LANES])
        query_grad = (
            part * SCALE + grad_f * conv_ref[:, lane(tile)].astype(F32)
        ).astype(BF16)
        soft_grad = nt(both(value, bands), context_grad)
        soft_grad = jnp.where(side > 0, soft_grad[:, LANES:], soft_grad[:, :LANES])
        soft_f = soft.astype(F32)
        inner = crop_reduce(ids, soft_f * soft_grad, jnp.sum, 0.0)
        keys_grad = (soft_f * (soft_grad - pick(ids, inner))).astype(BF16)
        value_part = nn(both(soft, sides), context_grad)
        value_part = jnp.where(band > 0, value_part[:, LANES:], value_part[:, :LANES])

        def read_row(row):
            part = pl.ds(SIDE * row, SIDE)
            return grad_ref[part, lane(tile)].astype(F32) * query_ref[part, lane(tile)].astype(F32)

        spread(read_row, reach, cut, mask_ref, grid_ref)
        other_ref[:PLACES, :] = value.astype(F32)
        conv_back_tile(reach, cut, grid_ref, crpe_ref, 3, tile, other_ref, out_ref, crpe_sum_ref)
        value_grad = (value_part + out_ref[:PLACES, :]).astype(BF16)
        three_ref[:, :LANES] = query_grad
        three_ref[:, LANES : 2 * LANES] = keys_grad
        three_ref[:, 2 * LANES :] = value_grad
        sum_ref[0:1, lane(tile)] += jnp.sum(query_grad.astype(F32), axis=0, keepdims=True)
        sum_ref[1:2, lane(tile)] += jnp.sum(value_grad.astype(F32), axis=0, keepdims=True)
        three = three_ref[...]
        qkv_grad_ref[shard] += tn(hidden, three)
        back = nt(three, qkv_ref[shard])
        if tile:
            norm_grad_ref[...] += back
        else:
            norm_grad_ref[...] = back
    norm_grad = norm_grad_ref[...]
    first = first_ref[...]
    center = row_mean(first)
    square = row_mean(first * first)
    inverse = lax.rsqrt(square - center * center + EPSILON)
    hat = (first - center) * inverse
    weighted = norm_grad * vec_ref[1:2, :]
    first_grad = second_grad_ref[...] + inverse * (
        weighted - row_mean(weighted) - hat * row_mean(weighted * hat)
    )
    first_grad_ref[...] = first_grad
    sum_ref[2:3, :] += jnp.sum(norm_grad * hat, axis=0, keepdims=True)
    sum_ref[3:4, :] += jnp.sum(norm_grad, axis=0, keepdims=True)
    sum_ref[4:5, :] += jnp.sum(first_grad, axis=0, keepdims=True)
    for move, piece_ref in enumerate((x0_ref, x1_ref, x2_ref, x3_ref)):
        start = pl.multiple_of(LANES * lax.bitwise_xor(me, move), LANES)
        norm_grad_ref[:, pl.ds(start, LANES)] = piece_ref[...].astype(F32)
    for tile in range(TILES):
        spread(
            lambda row: first_grad_ref[SIDE * row : SIDE * row + SIDE, lane(tile)],
            1, cut, mask_ref, grid_ref,
        )
        other_ref[:PLACES, :] = norm_grad_ref[:, lane(tile)]
        conv_back_tile(1, cut, grid_ref, cpe_ref, 1, tile, other_ref, out_ref, cpe_sum_ref)
        first_grad_ref[:, lane(tile)] += out_ref[:PLACES, :]
    for move, piece_ref in enumerate((out0_ref, out1_ref, out2_ref, out3_ref)):
        start = pl.multiple_of(LANES * lax.bitwise_xor(me, move), LANES)
        piece_ref[...] = first_grad_ref[:, pl.ds(start, LANES)].astype(BF16)


def back(cuts, me, x_parts, base, grad, query, value, soft, context, conv, first, hidden,
         second_grad, vec, qkv, crpe, cpe):
    rows = x_parts[0].shape[0]
    count = rows // PLACES
    wide = rows_spec(D, base)
    piece = rows_spec(LANES)
    return pl.pallas_call(
        lambda *refs: back_kernel(base, *refs),
        grid_spec=pltpu.PrefetchScalarGridSpec(
            num_scalar_prefetch=2,
            grid=(count,),
            in_specs=[piece] * 4 + [
                wide, wide, wide, wide, context_spec(base), wide, wide, wide, wide,
                whole(vec.shape), whole(qkv.shape), whole(crpe.shape), whole(cpe.shape),
            ],
            out_specs=[piece] * 4 + [
                whole(qkv.shape), whole((49, 8, D)), whole((9, 8, D)), whole((8, D)),
            ],
            scratch_shapes=[
                pltpu.VMEM((2, 7, SIDE, LANES), F32),
                pltpu.VMEM((7, GRID_ROWS * SIDE, LANES), F32),
                pltpu.VMEM((PLACES + SIDE, LANES), F32),
                pltpu.VMEM((PLACES + SIDE, LANES), F32),
                pltpu.VMEM((PLACES, 3 * LANES), BF16),
                pltpu.VMEM((PLACES, D), F32),
                pltpu.VMEM((PLACES, D), F32),
            ],
        ),
        out_shape=[like((rows, LANES), BF16)] * 4 + [
            like(qkv.shape, F32), like((49, 8, D), F32), like((9, 8, D), F32), like((8, D), F32),
        ],
        compiler_params=params(),
        cost_estimate=pl.CostEstimate(
            flops=rows * D * D * 64, bytes_accessed=count * 10**7, transcendentals=0
        ),
        name="back",
    )(cuts, me, *x_parts, grad, query, value, soft, context, conv, first, hidden, second_grad,
      vec, qkv, crpe, cpe)


def collect_kernel(me_ref, *refs):
    out_ref = refs[-1]
    for item, piece_ref in enumerate(refs[:-1]):

        @pl.when(pl.program_id(0) == item)
        def _():
            out_ref[...] = piece_ref[...].astype(F32)


def collect(me, pieces):
    parts = len(pieces[0])
    rows = pieces[0][0].shape[0]
    return pl.pallas_call(
        collect_kernel,
        grid_spec=pltpu.PrefetchScalarGridSpec(
            num_scalar_prefetch=1,
            grid=(4 * parts,),
            in_specs=[once((rows, LANES))] * (4 * parts),
            out_specs=pl.BlockSpec(
                (rows, LANES),
                lambda i, me: (lax.bitwise_xor(me[0], i // parts) * parts + i % parts, 0),
            ),
        ),
        out_shape=like((4 * parts * rows, LANES), F32),
        compiler_params=params(),
        name="collect",
    )(me, *[piece for move in pieces for piece in move])


HALVES = 2


def find_cuts(crop_ids):
    cut = jnp.sum((crop_ids[:, :, 0] < 2).astype(jnp.int32), axis=1)
    upper = jnp.sum((crop_ids[:, 0, :] == 0).astype(jnp.int32), axis=1)
    lower = jnp.sum((crop_ids[:, SIDE - 1, :] == 2).astype(jnp.int32), axis=1)
    return jnp.stack([cut, upper, lower], axis=1)


def reach_mask():
    head = jnp.arange(D, dtype=jnp.int32) // HEAD_DIM
    reach = 1 + (head >= 2).astype(jnp.int32) + (head >= 5).astype(jnp.int32)
    taps = jnp.arange(49, dtype=jnp.int32)
    ring = jnp.maximum(jnp.abs(taps // 7 - 3), jnp.abs(taps % 7 - 3))
    return (ring[:, None] <= reach[None, :]).astype(F32)


def forward_parts(me, cuts, x_halves, small, qkv):
    zero = jnp.zeros((D,), F32)
    vec = jnp.stack([small[58], small[59], small[60], small[61], small[62], zero, zero, zero])
    crpe = jnp.broadcast_to((small[9:58] * reach_mask())[:, None, :], (49, 8, D))
    cpe = jnp.broadcast_to(small[:9][:, None, :], (9, 8, D))
    kept = ()
    base = 0
    for x_parts in x_halves:
        kept = front(cuts, me, x_parts, base, kept, cpe, vec, qkv, crpe)
        base += x_parts[0].shape[0] // PLACES
    return kept, vec, crpe, cpe


def middle_parts(me, kept, cot_parts, small, bias, proj, fc1, fc2):
    zero = jnp.zeros((D,), F32)
    vec = jnp.stack([small[63], small[64], small[65], small[66], zero, zero, zero, zero])
    return middle(me, kept[7], kept[0], cot_parts, vec, bias, proj, fc1, fc2)


def body(
    block_in, crop_ids, cotangent, cpe_kernel, cpe_bias, norm1_gain, norm1_shift, qkv_weight,
    qv_bias, crpe_kernel, proj_weight, proj_bias, norm2_gain, norm2_shift, fc1_weight, fc1_bias,
    fc2_weight, fc2_bias,
):
    head = lax.axis_index("head")
    me = head.reshape(1).astype(jnp.int32)
    canvases = crop_ids.shape[0] // 4
    rows = canvases * PLACES
    cuts = find_cuts(lax.dynamic_slice_in_dim(crop_ids, head * canvases, canvases, 0))

    def swap(values, move):
        return lax.ppermute(values, "head", [(item, item ^ move) for item in range(4)])

    def take(values, move, part, parts):
        size = rows // parts
        start = lax.bitwise_xor(head, move) * rows + part * size
        return lax.dynamic_slice_in_dim(values, start, size, 0)

    def bring(values, part, parts):
        pieces = [take(values, move, part, parts) for move in range(4)]
        return [pieces[0]] + [swap(pieces[move], move) for move in (1, 2, 3)]

    def gather(shard):
        far = swap(shard, 2)
        near = swap(jnp.stack([shard, far]), 1)
        return jnp.stack([shard, near[0], far, near[1]])

    packed = jnp.concatenate([
        cpe_kernel, crpe_kernel, cpe_bias[None], norm1_gain[None], norm1_shift[None], qv_bias,
        proj_bias[None], norm2_gain[None], norm2_shift[None], fc2_bias[None],
    ]).astype(F32)
    small = lax.all_gather(packed, "head", axis=1, tiled=True)
    x_halves = [bring(block_in, 0, HALVES)]
    qkv = gather(qkv_weight.reshape(D, 3 * LANES))
    x_halves += [bring(block_in, part, HALVES) for part in range(1, HALVES)]
    proj = gather(proj_weight)
    cot_parts = bring(cotangent, 0, 1)
    fc1 = gather(fc1_weight)
    fc2 = gather(fc2_weight)
    bias = gather(fc1_bias.astype(F32).reshape(1, -1))

    kept, vec, crpe, cpe = forward_parts(me, cuts, x_halves, small, qkv)
    first, hidden, query, value, soft, context, conv, attended = kept
    results = middle_parts(me, kept, cot_parts, small, bias, proj, fc1, fc2)
    second_grad, att_grad, fc1_grad, fc2_grad, proj_grad, sums2, bias_grad = results[4:]
    out_parts = [[results[move] if move == 0 else swap(results[move], move)] for move in range(4)]

    def reduce_head(grads):
        near = swap(jnp.stack([grads[1], grads[3]]).astype(BF16), 1).astype(F32)
        far = swap((grads[2].astype(F32) + near[1]).astype(BF16), 2).astype(F32)
        return grads[0].astype(F32) + near[0] + far

    early = jnp.concatenate(
        [fc1_grad, fc2_grad, proj_grad], axis=1
    )
    early = lax.psum(reduce_head(early).astype(BF16), "dp")

    grad_parts = [[] for _ in range(4)]
    sums = []
    base = 0
    for x_parts in x_halves:
        back_results = back(
            cuts, me, x_parts, base, att_grad, query, value, soft, context, conv, first, hidden,
            second_grad, vec, qkv, crpe, cpe,
        )
        for move in range(4):
            piece = back_results[move]
            grad_parts[move].append(piece if move == 0 else swap(piece, move))
        sums.append(back_results[4:])
        base += x_parts[0].shape[0] // PLACES
    qkv_grad, crpe_sum, cpe_sum, sums1 = [sum(items[1:], items[0]) for items in zip(*sums)]
    small_grad = jnp.concatenate([
        jnp.sum(cpe_sum, axis=1), jnp.sum(crpe_sum, axis=1) * reach_mask(), sums1[4:5], sums1[2:4],
        sums1[0:2], sums2[3:4], sums2[1:3], sums2[0:1],
    ]).reshape(-1, 4, LANES).transpose(1, 0, 2)
    order = lax.bitwise_xor(head, jnp.arange(4, dtype=jnp.int32))
    small_grad = jnp.take(small_grad, order, axis=0)
    late = jnp.concatenate([
        qkv_grad.reshape(4, D * 3, LANES), small_grad, bias_grad.reshape(4, 4, LANES),
        jnp.zeros((4, 1, LANES), F32),
    ], axis=1)
    late = lax.psum(reduce_head(late), "dp")
    small_g = late[D * 3 : D * 3 + 67]
    early = early.astype(F32)
    return (
        collect(me, out_parts), collect(me, grad_parts),
        small_g[:9], small_g[58], small_g[59], small_g[60],
        late[: D * 3].reshape(D, 3, LANES), small_g[61:63], small_g[9:58],
        early[2 * D :], small_g[63], small_g[64], small_g[65],
        early[:D], late[D * 3 + 67 : D * 3 + 71].reshape(D), early[D : 2 * D], small_g[66],
    )


def solution(mesh):
    return jax.shard_map(
        body,
        mesh=mesh,
        in_specs=(
            P("dp", "head"), P("dp", None, None), P("dp", "head"), P(None, "head"), P("head"),
            P("head"), P("head"), P(None, None, "head"), P(None, "head"), P(None, "head"),
            P("head", None), P("head"), P("head"), P("head"), P(None, "head"), P("head"),
            P("head", None), P("head"),
        ),
        out_specs=(
            P("dp", "head"), P("dp", "head"), P(None, "head"), P("head"), P("head"), P("head"),
            P(None, None, "head"), P(None, "head"), P(None, "head"), P("head", None), P("head"),
            P("head"), P("head"), P(None, "head"), P("head"), P("head", None), P("head"),
        ),
        check_vma=False,
    )
```

```python
import jax
import jax.numpy as jnp
from jax import lax
from jax.experimental import pallas as pl
from jax.experimental.pallas import tpu as pltpu
from jax.sharding import PartitionSpec as P

D = 512
HEADS = 8
HEAD_DIM = 64
HIDDEN = 2048
SIDE = 16
PLACES = 256
LANES = 128
TILES = 4
REACH = (1, 2, 3, 3)
GAP = 3
GRID_ROWS = SIDE + 3 * GAP + 1
EPSILON = 1e-06
SCALE = HEAD_DIM ** (-0.5)
F32 = jnp.float32
BF16 = jnp.bfloat16


def dot(left, right, dims):
    return lax.dot_general(left, right, (dims, ((), ())), preferred_element_type=F32)


def nn(left, right):
    return dot(left, right, ((1,), (0,)))


def nt(left, right):
    return dot(left, right, ((1,), (1,)))


def tn(left, right):
    return dot(left, right, ((0,), (0,)))


def lane(tile):
    return pl.ds(LANES * tile, LANES)


def fill_masks(cut, col_cuts, mask_ref):
    col = lax.broadcasted_iota(jnp.int32, (SIDE, LANES), 0)
    for band in range(2):
        here = (col >= col_cuts[band]).astype(jnp.int32)
        for step in range(-3, 4):
            if step == 0:
                continue
            there = (col + step >= col_cuts[band]).astype(jnp.int32)
            good = (col + step >= 0) & (col + step < SIDE) & (here == there)
            mask_ref[band, step + 3] = jnp.where(good, 1.0, 0.0).astype(F32)


def place_ids(cut, col_cuts):
    place = lax.broadcasted_iota(jnp.int32, (PLACES, LANES), 0)
    row = lax.shift_right_logical(place, 4)
    col = lax.bitwise_and(place, 15)
    band = (row >= cut).astype(jnp.int32)
    col_cut = jnp.where(band > 0, col_cuts[1], col_cuts[0])
    side = (col >= col_cut).astype(jnp.int32)
    return band, side


def spread(read_row, reach, cut, mask_ref, grid_ref):
    zero = jnp.zeros((GAP * SIDE, LANES), F32)
    for step in range(-reach, reach + 1):
        start = pl.multiple_of(SIDE * (GAP + cut), SIDE)
        grid_ref[step + 3, pl.ds(start, GAP * SIDE), :] = zero
    for row in range(SIDE):
        lower = (row >= cut).astype(jnp.int32)
        start = pl.multiple_of(SIDE * (row + GAP + GAP * lower), SIDE)
        values = read_row(row)
        for step in range(-reach, reach + 1):
            moved = values
            if step != 0:
                moved = pltpu.roll(values, (-step) % SIDE, 0) * mask_ref[lower, step + 3]
            grid_ref[step + 3, pl.ds(start, SIDE), :] = moved


def pair_place(index, cut, upper_pairs, reach):
    lower = (index >= upper_pairs).astype(jnp.int32)
    row = 2 * index + lower * (cut - 2 * upper_pairs)
    base = row + GAP * lower + (GAP - reach)
    return lower, row, base


def conv_tile(reach, cut, grid_ref, taps_ref, tap_reach, tile, out_ref):
    upper_pairs = (cut + 1) // 2
    pairs = upper_pairs + (SIDE - cut + 1) // 2
    width = 2 * tap_reach + 1

    def body(index, carry):
        lower, row, base = pair_place(index, cut, upper_pairs, reach)
        total = [[None, None], [None, None]]
        for step in range(-reach, reach + 1):
            taps = [
                taps_ref[(dr + tap_reach) * width + step + tap_reach, :, lane(tile)]
                for dr in range(-reach, reach + 1)
            ]
            for place in range(2 * reach + 2):
                for half in range(2):
                    start = pl.multiple_of(SIDE * (base + place) + 8 * half, 8)
                    field = grid_ref[step + 3, pl.ds(start, 8), :]
                    for out in range(2):
                        tap = place - out
                        if 0 <= tap <= 2 * reach:
                            term = taps[tap] * field
                            old = total[out][half]
                            total[out][half] = term if old is None else old + term
        for out in range(2):
            for half in range(2):
                start = pl.multiple_of(SIDE * (row + out) + 8 * half, 8)
                out_ref[pl.ds(start, 8), :] = total[out][half]
        return carry

    lax.fori_loop(0, pairs, body, 0)


def conv_back_tile(reach, cut, grid_ref, taps_ref, tap_reach, tile, other_ref, out_ref, sum_ref):
    upper_pairs = (cut + 1) // 2
    pairs = upper_pairs + (SIDE - cut + 1) // 2
    width = 2 * tap_reach + 1

    def body(index, carry):
        lower, row, base = pair_place(index, cut, upper_pairs, reach)
        keep = jnp.where((lower == 0) & (row + 1 >= cut), 0.0, 1.0).astype(F32)
        other = []
        for out in range(2):
            halves = []
            for half in range(2):
                start = pl.multiple_of(SIDE * (row + out) + 8 * half, 8)
                value = other_ref[pl.ds(start, 8), :]
                halves.append(value * keep if out else value)
            other.append(halves)
        total = [[None, None], [None, None]]
        for step in range(-reach, reach + 1):
            sums = [None] * (2 * reach + 1)
            ids = [
                (tap_reach - dr) * width + tap_reach - step for dr in range(-reach, reach + 1)
            ]
            taps = [taps_ref[item, :, lane(tile)] for item in ids]
            for place in range(2 * reach + 2):
                for half in range(2):
                    start = pl.multiple_of(SIDE * (base + place) + 8 * half, 8)
                    field = grid_ref[step + 3, pl.ds(start, 8), :]
                    for out in range(2):
                        tap = place - out
                        if 0 <= tap <= 2 * reach:
                            term = taps[tap] * field
                            old = total[out][half]
                            total[out][half] = term if old is None else old + term
                            part = other[out][half] * field
                            old = sums[tap]
                            sums[tap] = part if old is None else old + part
            for tap in range(2 * reach + 1):
                sum_ref[ids[tap], :, lane(tile)] += sums[tap]
        for out in range(2):
            for half in range(2):
                start = pl.multiple_of(SIDE * (row + out) + 8 * half, 8)
                out_ref[pl.ds(start, 8), :] = total[out][half]
        return carry

    lax.fori_loop(0, pairs, body, 0)


def row_mean(values):
    return jnp.sum(values, axis=1, keepdims=True) * (1.0 / D)


def pick(ids, rows):
    out = rows[0]
    for crop in range(1, 4):
        out = jnp.where(ids >= crop, rows[crop], out)
    return out


def crop_reduce(ids, values, op, empty):
    return [op(jnp.where(ids == crop, values, empty), axis=0, keepdims=True) for crop in range(4)]


def head_block():
    row = lax.broadcasted_iota(jnp.int32, (2 * LANES, 2 * LANES), 0)
    col = lax.broadcasted_iota(jnp.int32, (2 * LANES, 2 * LANES), 1)
    same = lax.bitwise_and(row, HEAD_DIM) == lax.bitwise_and(col, HEAD_DIM)
    return jnp.where(same, 1.0, 0.0).astype(F32)


def both(values, masks):
    return jnp.concatenate([values * masks[0], values * masks[1]], axis=1)


def read_cuts(cuts_ref, base):
    step = pl.program_id(0) + base
    return cuts_ref[step, 0], (cuts_ref[step, 1], cuts_ref[step, 2])


def whole(shape):
    return pl.BlockSpec(shape, lambda *_: (0,) * len(shape))


def once(shape):
    return pl.BlockSpec(shape, lambda *_: (0,) * len(shape), pipeline_mode=pl.Buffered(1))


def rows_spec(width, base=0):
    return pl.BlockSpec((PLACES, width), lambda i, *_: (i + base, 0))


def context_spec(base):
    return pl.BlockSpec((1, TILES, 2 * LANES, 2 * LANES), lambda i, *_: (i + base, 0, 0, 0))


def like(shape, dtype):
    return jax.ShapeDtypeStruct(shape, dtype)


def params(**given):
    return pltpu.CompilerParams(vmem_limit_bytes=58 * 2**20, **given)


def front_kernel(base, kept, *refs):
    (cuts_ref, me_ref, x0_ref, x1_ref, x2_ref, x3_ref, cpe_ref, vec_ref, qkv_ref, crpe_ref) = refs[:10]
    (first_ref, hidden_ref, query_ref, value_ref, soft_ref, context_ref, conv_ref, attended_ref,
     mask_ref, grid_ref, out_ref, x_ref) = refs[10 + kept :]
    cut, col_cuts = read_cuts(cuts_ref, base)
    me = me_ref[0]

    @pl.when(pl.program_id(0) == 0)
    def _():
        grid_ref[...] = jnp.zeros_like(grid_ref)

    for move, piece_ref in enumerate((x0_ref, x1_ref, x2_ref, x3_ref)):
        start = pl.multiple_of(LANES * lax.bitwise_xor(me, move), LANES)
        x_ref[:, pl.ds(start, LANES)] = piece_ref[...].astype(F32)
    fill_masks(cut, col_cuts, mask_ref)
    for tile in range(TILES):
        spread(
            lambda row: x_ref[SIDE * row : SIDE * row + SIDE, lane(tile)],
            1, cut, mask_ref, grid_ref,
        )
        conv_tile(1, cut, grid_ref, cpe_ref, 1, tile, out_ref)
        first_ref[:, lane(tile)] = (
            x_ref[:, lane(tile)] + out_ref[:PLACES, :] + vec_ref[0:1, lane(tile)]
        )
    first = first_ref[...]
    center = row_mean(first)
    square = row_mean(first * first)
    inverse = lax.rsqrt(square - center * center + EPSILON)
    hidden = ((first - center) * inverse * vec_ref[1:2, :] + vec_ref[2:3, :]).astype(BF16)
    hidden_ref[...] = hidden
    band, side = place_ids(cut, col_cuts)
    ids = 2 * band + side
    sides = [(side == item).astype(F32).astype(BF16) for item in range(2)]
    bands = [(band == item).astype(F32).astype(BF16) for item in range(2)]
    blocks = head_block()
    for tile in range(TILES):
        reach = REACH[tile]
        three = nn(hidden, qkv_ref[lax.bitwise_xor(me, tile)])
        query = (three[:, :LANES] + vec_ref[3:4, lane(tile)]).astype(BF16)
        keys = three[:, LANES : 2 * LANES].astype(BF16).astype(F32)
        value = (three[:, 2 * LANES :] + vec_ref[4:5, lane(tile)]).astype(BF16)
        query_ref[:, lane(tile)] = query
        value_ref[:, lane(tile)] = value
        highest = crop_reduce(ids, keys, jnp.max, -1e30)
        powers = jnp.exp(keys - pick(ids, highest))
        totals = crop_reduce(ids, powers, jnp.sum, 0.0)
        soft = (powers * pick(ids, [1.0 / item for item in totals])).astype(BF16)
        soft_ref[:, lane(tile)] = soft
        context = (tn(both(soft, sides), both(value, bands)) * blocks).astype(BF16)
        context_ref[0, tile] = context
        factor = nn(both(query, sides), context)
        factor = jnp.where(band > 0, factor[:, LANES:], factor[:, :LANES])
        spread(
            lambda row: value_ref[SIDE * row : SIDE * row + SIDE, lane(tile)].astype(F32),
            reach, cut, mask_ref, grid_ref,
        )
        conv_tile(reach, cut, grid_ref, crpe_ref, 3, tile, out_ref)
        conv = out_ref[:PLACES, :]
        conv_ref[:, lane(tile)] = conv.astype(BF16)
        attended_ref[:, lane(tile)] = (factor * SCALE + query.astype(F32) * conv).astype(BF16)


def front(cuts, me, x_parts, base, kept, cpe, vec, qkv, crpe):
    count = x_parts[0].shape[0] // PLACES
    total = cuts.shape[0]
    rows = total * PLACES
    wide = rows_spec(D, base)
    flops = 2 * count * PLACES * D * D * 4
    return pl.pallas_call(
        lambda *refs: front_kernel(base, len(kept), *refs),
        grid_spec=pltpu.PrefetchScalarGridSpec(
            num_scalar_prefetch=2,
            grid=(count,),
            in_specs=[rows_spec(LANES)] * 4
            + [whole(cpe.shape), whole(vec.shape), whole(qkv.shape), whole(crpe.shape)]
            + [pl.BlockSpec(memory_space=pl.ANY)] * len(kept),
            out_specs=[wide, wide, wide, wide, wide, context_spec(base), wide, wide],
            scratch_shapes=[
                pltpu.VMEM((2, 7, SIDE, LANES), F32),
                pltpu.VMEM((7, GRID_ROWS * SIDE, LANES), F32),
                pltpu.VMEM((PLACES + SIDE, LANES), F32),
                pltpu.VMEM((PLACES, D), F32),
            ],
        ),
        out_shape=[
            like((rows, D), F32), like((rows, D), BF16), like((rows, D), BF16),
            like((rows, D), BF16), like((rows, D), BF16),
            like((total, TILES, 2 * LANES, 2 * LANES), BF16),
            like((rows, D), BF16), like((rows, D), BF16),
        ],
        input_output_aliases={10 + item: item for item in range(len(kept))},
        compiler_params=params(),
        cost_estimate=pl.CostEstimate(flops=flops * 6, bytes_accessed=count * 10**7, transcendentals=0),
        name="front",
    )(cuts, me, *x_parts, cpe, vec, qkv, crpe, *kept)


def gelu_both(pre):
    power = jnp.exp(pre * pre * -0.5)
    t = 1.0 / (1.0 + jnp.abs(pre) * (0.3275911 * 0.7071067811865476))
    poly = 0.5 * 1.061405429
    for item in (-1.453152027, 1.421413741, -0.284496736, 0.254829592):
        poly = poly * t + 0.5 * item
    tail = poly * t * power
    cdf = jnp.where(pre >= 0.0, 1.0 - tail, tail)
    return pre * cdf, cdf + pre * power * 0.3989422804014327


CHUNK = 256
BLOCK = 512


def middle_kernel(
    me_ref, attended_ref, first_ref, cot0_ref, cot1_ref, cot2_ref, cot3_ref, vec_ref, bias_ref,
    proj_ref, fc1_ref, fc2_ref,
    out0_ref, out1_ref, out2_ref, out3_ref, second_grad_ref, att_grad_ref, fc1_grad_ref,
    fc2_grad_ref, proj_grad_ref, sum_ref, bias_grad_ref,
    cot_ref, hat_ref, inverse_ref, hidden_ref, total_ref, back_ref, active_ref, pre_grad_ref,
):
    me = me_ref[0]
    step = pl.program_id(0)
    rows = attended_ref.shape[0]
    blocks = rows // BLOCK

    def part(index):
        return pl.ds(pl.multiple_of(BLOCK * index, BLOCK), BLOCK)

    @pl.when(step == 0)
    def _():
        sum_ref[...] = jnp.zeros_like(sum_ref)
        for move, piece_ref in enumerate((cot0_ref, cot1_ref, cot2_ref, cot3_ref)):
            start = pl.multiple_of(LANES * lax.bitwise_xor(me, move), LANES)
            cot_ref[:, pl.ds(start, LANES)] = piece_ref[...]

        def enter(index, carry):
            now = part(index)
            second = first_ref[now, :] + vec_ref[0:1, :]
            for tile in range(TILES):
                second += nn(attended_ref[now, lane(tile)], proj_ref[lax.bitwise_xor(me, tile)])
            center = row_mean(second)
            square = row_mean(second * second)
            inverse = lax.rsqrt(square - center * center + EPSILON)
            hat = (second - center) * inverse
            hidden_ref[now, :] = (hat * vec_ref[1:2, :] + vec_ref[2:3, :]).astype(BF16)
            hat_ref[now, :] = hat
            inverse_ref[now, :] = jnp.broadcast_to(inverse, (BLOCK, LANES))
            total_ref[now, :] = second + vec_ref[3:4, :]
            back_ref[now, :] = jnp.zeros((BLOCK, D), F32)
            sum_ref[0:1, :] += jnp.sum(cot_ref[now, :].astype(F32), axis=0, keepdims=True)
            return carry

        lax.fori_loop(0, blocks, enter, 0)

    bias_grad_ref[0] = jnp.zeros((1, CHUNK), F32)

    def chunk(index, carry):
        now = part(index)
        pre = nn(hidden_ref[now, :], fc1_ref[0]) + bias_ref[0]
        active, slope = gelu_both(pre)
        active = active.astype(BF16)
        active_ref[now, :] = active
        total_ref[now, :] += nn(active, fc2_ref[0])
        pre_grad_f = nt(cot_ref[now, :], fc2_ref[0]) * slope
        pre_grad = pre_grad_f.astype(BF16)
        pre_grad_ref[now, :] = pre_grad
        back_ref[now, :] += nt(pre_grad, fc1_ref[0])
        bias_grad_ref[0] += jnp.sum(pre_grad_f, axis=0, keepdims=True)
        return carry

    lax.fori_loop(0, blocks, chunk, 0)
    fc2_grad_ref[0] = tn(active_ref[...], cot_ref[...]).astype(fc2_grad_ref.dtype)
    fc1_grad_ref[0] = tn(hidden_ref[...], pre_grad_ref[...]).astype(fc1_grad_ref.dtype)

    @pl.when(step == pl.num_programs(0) - 1)
    def _():
        def leave(index, carry):
            now = part(index)
            for move, piece_ref in enumerate((out0_ref, out1_ref, out2_ref, out3_ref)):
                start = pl.multiple_of(LANES * lax.bitwise_xor(me, move), LANES)
                piece_ref[now, :] = total_ref[now, pl.ds(start, LANES)].astype(BF16)
            hat = hat_ref[now, :]
            norm_grad = back_ref[now, :]
            weighted = norm_grad * vec_ref[1:2, :]
            second_grad = cot_ref[now, :].astype(F32) + inverse_ref[now, 0:1] * (
                weighted - row_mean(weighted) - hat * row_mean(weighted * hat)
            )
            second_grad_ref[now, :] = second_grad
            low = second_grad.astype(BF16)
            hidden_ref[now, :] = low
            for tile in range(TILES):
                att_grad_ref[now, lane(tile)] = nt(low, proj_ref[lax.bitwise_xor(me, tile)]).astype(BF16)
            sum_ref[1:2, :] += jnp.sum(norm_grad * hat, axis=0, keepdims=True)
            sum_ref[2:3, :] += jnp.sum(norm_grad, axis=0, keepdims=True)
            sum_ref[3:4, :] += jnp.sum(low.astype(F32), axis=0, keepdims=True)
            return carry

        lax.fori_loop(0, blocks, leave, 0)
        for tile in range(TILES):
            proj_grad_ref[lax.bitwise_xor(me, tile)] = tn(
                attended_ref[:, lane(tile)], hidden_ref[...]
            ).astype(proj_grad_ref.dtype)


def middle(me, attended, first, cot_parts, vec, bias, proj, fc1, fc2):
    rows = attended.shape[0]
    split = fc1.shape[2] // CHUNK
    steps = 4 * split
    left = pl.BlockSpec((1, D, CHUNK), lambda i, *_: (i // split, 0, i % split))
    right = pl.BlockSpec((1, CHUNK, D), lambda i, *_: (i // split, i % split, 0))
    piece = once((rows, LANES))
    wide = once((rows, D))
    line = pl.BlockSpec((1, 1, CHUNK), lambda i, *_: (i // split, 0, i % split))
    return pl.pallas_call(
        middle_kernel,
        grid_spec=pltpu.PrefetchScalarGridSpec(
            num_scalar_prefetch=1,
            grid=(steps,),
            in_specs=[
                wide, wide, piece, piece, piece, piece, whole(vec.shape), line, once(proj.shape),
                left, right,
            ],
            out_specs=[
                piece, piece, piece, piece, wide, wide, left, right, once(proj.shape),
                whole((8, D)), line,
            ],
            scratch_shapes=[
                pltpu.VMEM((rows, D), BF16), pltpu.VMEM((rows, D), F32),
                pltpu.VMEM((rows, LANES), F32),
                pltpu.VMEM((rows, D), BF16), pltpu.VMEM((rows, D), F32),
                pltpu.VMEM((rows, D), F32), pltpu.VMEM((rows, CHUNK), BF16),
                pltpu.VMEM((rows, CHUNK), BF16),
            ],
        ),
        out_shape=[like((rows, LANES), BF16)] * 4 + [
            like((rows, D), F32), like((rows, D), BF16),
            like(fc1.shape, BF16), like(fc2.shape, BF16), like(proj.shape, BF16),
            like((8, D), F32), like(bias.shape, F32),
        ],
        compiler_params=params(),
        cost_estimate=pl.CostEstimate(flops=rows * D * D * 60, bytes_accessed=3 * 10**7, transcendentals=0),
        name="middle",
    )(me, attended, first, *cot_parts, vec, bias, proj, fc1, fc2)


def back_kernel(
    base,
    cuts_ref, me_ref, x0_ref, x1_ref, x2_ref, x3_ref,
    grad_ref, query_ref, value_ref, soft_ref, context_ref, conv_ref,
    first_ref, hidden_ref, second_grad_ref, vec_ref, qkv_ref, crpe_ref, cpe_ref,
    out0_ref, out1_ref, out2_ref, out3_ref, qkv_grad_ref, crpe_sum_ref, cpe_sum_ref, sum_ref,
    mask_ref, grid_ref, out_ref, other_ref, three_ref, first_grad_ref, norm_grad_ref,
):
    cut, col_cuts = read_cuts(cuts_ref, base)
    me = me_ref[0]

    @pl.when(pl.program_id(0) == 0)
    def _():
        grid_ref[...] = jnp.zeros_like(grid_ref)
        other_ref[...] = jnp.zeros_like(other_ref)
        qkv_grad_ref[...] = jnp.zeros_like(qkv_grad_ref)
        crpe_sum_ref[...] = jnp.zeros_like(crpe_sum_ref)
        cpe_sum_ref[...] = jnp.zeros_like(cpe_sum_ref)
        sum_ref[...] = jnp.zeros_like(sum_ref)

    fill_masks(cut, col_cuts, mask_ref)
    band, side = place_ids(cut, col_cuts)
    ids = 2 * band + side
    sides = [(side == item).astype(F32).astype(BF16) for item in range(2)]
    bands = [(band == item).astype(F32).astype(BF16) for item in range(2)]
    blocks = head_block() * SCALE
    hidden = hidden_ref[...]
    for tile in range(TILES):
        reach = REACH[tile]
        shard = lax.bitwise_xor(me, tile)
        grad = grad_ref[:, lane(tile)]
        query = query_ref[:, lane(tile)]
        value = value_ref[:, lane(tile)]
        soft = soft_ref[:, lane(tile)]
        context = context_ref[0, tile]
        grad_f = grad.astype(F32)
        grad_bands = both(grad, bands)
        context_grad = (tn(both(query, sides), grad_bands) * blocks).astype(BF16)
        part = nt(grad_bands, context)
        part = jnp.where(side > 0, part[:, LANES:], part[:, :LANES])
        query_grad = (
            part * SCALE + grad_f * conv_ref[:, lane(tile)].astype(F32)
        ).astype(BF16)
        soft_grad = nt(both(value, bands), context_grad)
        soft_grad = jnp.where(side > 0, soft_grad[:, LANES:], soft_grad[:, :LANES])
        soft_f = soft.astype(F32)
        inner = crop_reduce(ids, soft_f * soft_grad, jnp.sum, 0.0)
        keys_grad = (soft_f * (soft_grad - pick(ids, inner))).astype(BF16)
        value_part = nn(both(soft, sides), context_grad)
        value_part = jnp.where(band > 0, value_part[:, LANES:], value_part[:, :LANES])

        def read_row(row):
            part = pl.ds(SIDE * row, SIDE)
            return grad_ref[part, lane(tile)].astype(F32) * query_ref[part, lane(tile)].astype(F32)

        spread(read_row, reach, cut, mask_ref, grid_ref)
        other_ref[:PLACES, :] = value.astype(F32)
        conv_back_tile(reach, cut, grid_ref, crpe_ref, 3, tile, other_ref, out_ref, crpe_sum_ref)
        value_grad = (value_part + out_ref[:PLACES, :]).astype(BF16)
        three_ref[:, :LANES] = query_grad
        three_ref[:, LANES : 2 * LANES] = keys_grad
        three_ref[:, 2 * LANES :] = value_grad
        sum_ref[0:1, lane(tile)] += jnp.sum(query_grad.astype(F32), axis=0, keepdims=True)
        sum_ref[1:2, lane(tile)] += jnp.sum(value_grad.astype(F32), axis=0, keepdims=True)
        three = three_ref[...]
        qkv_grad_ref[shard] += tn(hidden, three)
        back = nt(three, qkv_ref[shard])
        if tile:
            norm_grad_ref[...] += back
        else:
            norm_grad_ref[...] = back
    norm_grad = norm_grad_ref[...]
    first = first_ref[...]
    center = row_mean(first)
    square = row_mean(first * first)
    inverse = lax.rsqrt(square - center * center + EPSILON)
    hat = (first - center) * inverse
    weighted = norm_grad * vec_ref[1:2, :]
    first_grad = second_grad_ref[...] + inverse * (
        weighted - row_mean(weighted) - hat * row_mean(weighted * hat)
    )
    first_grad_ref[...] = first_grad
    sum_ref[2:3, :] += jnp.sum(norm_grad * hat, axis=0, keepdims=True)
    sum_ref[3:4, :] += jnp.sum(norm_grad, axis=0, keepdims=True)
    sum_ref[4:5, :] += jnp.sum(first_grad, axis=0, keepdims=True)
    for move, piece_ref in enumerate((x0_ref, x1_ref, x2_ref, x3_ref)):
        start = pl.multiple_of(LANES * lax.bitwise_xor(me, move), LANES)
        norm_grad_ref[:, pl.ds(start, LANES)] = piece_ref[...].astype(F32)
    for tile in range(TILES):
        spread(
            lambda row: first_grad_ref[SIDE * row : SIDE * row + SIDE, lane(tile)],
            1, cut, mask_ref, grid_ref,
        )
        other_ref[:PLACES, :] = norm_grad_ref[:, lane(tile)]
        conv_back_tile(1, cut, grid_ref, cpe_ref, 1, tile, other_ref, out_ref, cpe_sum_ref)
        first_grad_ref[:, lane(tile)] += out_ref[:PLACES, :]
    for move, piece_ref in enumerate((out0_ref, out1_ref, out2_ref, out3_ref)):
        start = pl.multiple_of(LANES * lax.bitwise_xor(me, move), LANES)
        piece_ref[...] = first_grad_ref[:, pl.ds(start, LANES)].astype(BF16)


def back(cuts, me, x_parts, base, grad, query, value, soft, context, conv, first, hidden,
         second_grad, vec, qkv, crpe, cpe):
    rows = x_parts[0].shape[0]
    count = rows // PLACES
    wide = rows_spec(D, base)
    piece = rows_spec(LANES)
    return pl.pallas_call(
        lambda *refs: back_kernel(base, *refs),
        grid_spec=pltpu.PrefetchScalarGridSpec(
            num_scalar_prefetch=2,
            grid=(count,),
            in_specs=[piece] * 4 + [
                wide, wide, wide, wide, context_spec(base), wide, wide, wide, wide,
                whole(vec.shape), whole(qkv.shape), whole(crpe.shape), whole(cpe.shape),
            ],
            out_specs=[piece] * 4 + [
                whole(qkv.shape), whole((49, 8, D)), whole((9, 8, D)), whole((8, D)),
            ],
            scratch_shapes=[
                pltpu.VMEM((2, 7, SIDE, LANES), F32),
                pltpu.VMEM((7, GRID_ROWS * SIDE, LANES), F32),
                pltpu.VMEM((PLACES + SIDE, LANES), F32),
                pltpu.VMEM((PLACES + SIDE, LANES), F32),
                pltpu.VMEM((PLACES, 3 * LANES), BF16),
                pltpu.VMEM((PLACES, D), F32),
                pltpu.VMEM((PLACES, D), F32),
            ],
        ),
        out_shape=[like((rows, LANES), BF16)] * 4 + [
            like(qkv.shape, F32), like((49, 8, D), F32), like((9, 8, D), F32), like((8, D), F32),
        ],
        compiler_params=params(),
        cost_estimate=pl.CostEstimate(
            flops=rows * D * D * 64, bytes_accessed=count * 10**7, transcendentals=0
        ),
        name="back",
    )(cuts, me, *x_parts, grad, query, value, soft, context, conv, first, hidden, second_grad,
      vec, qkv, crpe, cpe)


def collect_kernel(me_ref, *refs):
    out_ref = refs[-1]
    for item, piece_ref in enumerate(refs[:-1]):

        @pl.when(pl.program_id(0) == item)
        def _():
            out_ref[...] = piece_ref[...].astype(F32)


def collect(me, pieces):
    parts = len(pieces[0])
    rows = pieces[0][0].shape[0]
    return pl.pallas_call(
        collect_kernel,
        grid_spec=pltpu.PrefetchScalarGridSpec(
            num_scalar_prefetch=1,
            grid=(4 * parts,),
            in_specs=[once((rows, LANES))] * (4 * parts),
            out_specs=pl.BlockSpec(
                (rows, LANES),
                lambda i, me: (lax.bitwise_xor(me[0], i // parts) * parts + i % parts, 0),
            ),
        ),
        out_shape=like((4 * parts * rows, LANES), F32),
        compiler_params=params(),
        name="collect",
    )(me, *[piece for move in pieces for piece in move])


MESH = pl.DeviceIdType.MESH
PIECE_ROWS = 128


def peer(move):
    return (lax.axis_index("dp"), lax.bitwise_xor(lax.axis_index("head"), move))


def meet(peers):
    barrier = pltpu.get_barrier_semaphore()
    for item in peers:
        pl.semaphore_signal(barrier, inc=1, device_id=item, device_id_type=MESH)
    pl.semaphore_wait(barrier, len(peers))


def remote(source, target, send, receive, device):
    return pltpu.make_async_remote_copy(
        src_ref=source, dst_ref=target, send_sem=send, recv_sem=receive,
        device_id=device, device_id_type=MESH,
    )


def entry_kernel(
    rows, size, x_ref, qkv_ref, small_ref,
    x1_ref, x2_ref, x3_ref, all_qkv_ref, all_small_ref,
    send, receive, local,
):
    head = lax.axis_index("head")
    meet([peer(move) for move in (1, 2, 3)])
    copies = []
    far = remote(qkv_ref, all_qkv_ref.at[2], send.at[0], receive.at[0], peer(2))
    far.start()
    near = remote(qkv_ref, all_qkv_ref.at[1], send.at[1], receive.at[1], peer(1))
    near.start()
    for move in (1, 2, 3):
        copies.append(
            remote(small_ref, all_small_ref.at[move], send.at[1 + move], receive.at[1 + move], peer(move))
        )
        copies[-1].start()
    for move, target in ((2, x2_ref), (3, x3_ref), (1, x1_ref)):
        start = pl.multiple_of(lax.bitwise_xor(head, move) * rows, PLACES)
        copies.append(
            remote(x_ref.at[pl.ds(start, size)], target, send.at[4 + move], receive.at[4 + move], peer(move))
        )
        copies[-1].start()
    mine = pltpu.make_async_copy(qkv_ref, all_qkv_ref.at[0], local.at[0])
    mine.start()
    mine_small = pltpu.make_async_copy(small_ref, all_small_ref.at[0], local.at[1])
    mine_small.start()
    far.wait_recv()
    relay = remote(all_qkv_ref.at[2], all_qkv_ref.at[3], send.at[8], receive.at[8], peer(1))
    relay.start()
    far.wait_send()
    near.wait()
    for copy in copies:
        copy.wait()
    relay.wait()
    mine.wait()
    mine_small.wait()


def entry(block_in, size, qkv, small):
    rows = block_in.shape[0] // 4
    hbm = pl.BlockSpec(memory_space=pl.ANY)
    return pl.pallas_call(
        lambda *refs: entry_kernel(rows, size, *refs),
        in_specs=[hbm] * 3,
        out_specs=[hbm] * 5,
        out_shape=[like((size, LANES), BF16)] * 3 + [
            like((4,) + qkv.shape, BF16), like((4,) + small.shape, F32),
        ],
        scratch_shapes=[
            pltpu.SemaphoreType.DMA((9,)), pltpu.SemaphoreType.DMA((9,)),
            pltpu.SemaphoreType.DMA((2,)),
        ],
        compiler_params=params(collective_id=1, has_side_effects=True),
        name="entry",
    )(block_in, qkv, small)


def plan_pieces(shapes, count):
    pieces = []
    for item, (rows, lanes) in enumerate(shapes):
        height = min(PIECE_ROWS, rows)
        unit = 16 * count
        padded = -(-height // unit) * unit
        for start in range(0, rows, height):
            pieces.append((item, start, height, padded, lanes))
    return pieces


def sum_steps(pieces, count, grad_refs, out_refs, near_refs, far_refs, own_refs, mid_refs, part_refs, send, receive):
    group = count // 2
    dp = lax.axis_index("dp")
    head = lax.axis_index("head")
    low, high = lax.rem(dp, 2), dp // 2
    made = {}

    def sems(piece, slot):
        return send.at[piece, slot], receive.at[piece, slot]

    def copy(key, source, target, slot, device):
        made[key] = remote(source, target, *sems(key[0], slot), device)
        made[key].start()

    def widths(piece):
        item, start, height, padded, lanes = pieces[piece]
        return grad_refs[item], pl.ds(start, height), height, padded, padded // 2, padded // count

    def to_core(piece):
        grad, span, *_ = widths(piece)
        copy((piece, "n1"), grad.at[1, span], near_refs[piece].at[0], 0, peer(1))
        copy((piece, "n3"), grad.at[3, span], near_refs[piece].at[1], 1, peer(1))

    def to_far(piece):
        grad, span, height, *_ = widths(piece)
        made[piece, "n3"].wait_recv()
        own_refs[piece][:height, :] = (
            grad[2, span, :].astype(F32) + near_refs[piece][1].astype(F32)
        ).astype(BF16)
        copy((piece, "far"), own_refs[piece].at[:height], far_refs[piece], 2, peer(2))

    def to_low(piece):
        grad, span, height, padded, half, _ = widths(piece)
        made[piece, "n1"].wait()
        made[piece, "n3"].wait_send()
        made[piece, "far"].wait()
        own_refs[piece][:height, :] = (
            grad[0, span, :].astype(F32) + near_refs[piece][0].astype(F32)
            + far_refs[piece][...].astype(F32)
        ).astype(BF16)
        if padded > height:
            own_refs[piece][height:, :] = jnp.zeros((padded - height, own_refs[piece].shape[1]), BF16)
        away = pl.multiple_of((1 - low) * half, half)
        copy(
            (piece, "low"), own_refs[piece].at[pl.ds(away, half)], mid_refs[piece].at[1], 3,
            (dp + 1 - 2 * low, head),
        )

    def to_high(piece):
        _, _, _, _, half, part = widths(piece)
        made[piece, "low"].wait()
        here = pl.multiple_of(low * half, half)
        mid_refs[piece][0] = (
            own_refs[piece][pl.ds(here, half), :].astype(F32) + mid_refs[piece][1].astype(F32)
        ).astype(BF16)
        for step in range(1, group):
            other = lax.rem(high + step, group)
            start = pl.multiple_of(other * part, part)
            copy(
                (piece, "high", step), mid_refs[piece].at[0, pl.ds(start, part)],
                part_refs[piece].at[step - 1], 3 + step, (other * 2 + low, head),
            )

    def share_high(piece):
        _, _, _, _, half, part = widths(piece)
        mine = pl.multiple_of(high * part, part)
        total = mid_refs[piece][0, pl.ds(mine, part), :].astype(F32)
        for step in range(1, group):
            made[piece, "high", step].wait()
            total += part_refs[piece][step - 1].astype(F32)
        spot = own_refs[piece].at[pl.ds(pl.multiple_of(low * half + high * part, part), part)]
        spot[...] = total.astype(BF16)
        for step in range(1, group):
            other = lax.rem(high + step, group)
            copy((piece, "share", step), spot, spot, 2 + group + step, (other * 2 + low, head))

    def share_low(piece):
        _, _, _, _, half, _ = widths(piece)
        for step in range(1, group):
            made[piece, "share", step].wait()
        here = own_refs[piece].at[pl.ds(pl.multiple_of(low * half, half), half)]
        copy((piece, "last"), here, here, 2 + 2 * group, (dp + 1 - 2 * low, head))

    def leave(piece):
        item, start, height, *_ = pieces[piece]
        made[piece, "last"].wait()
        out_refs[item][start : start + height, :] = own_refs[piece][:height, :].astype(F32)

    return [to_core, to_far, to_low, to_high, share_high, share_low, leave]


def sum_peers(count):
    dp, head = lax.axis_index("dp"), lax.axis_index("head")
    low, high = lax.rem(dp, 2), dp // 2
    group = count // 2
    return [peer(1), peer(2), (dp + 1 - 2 * low, head)] + [
        (lax.rem(high + step, group) * 2 + low, head) for step in range(1, group)
    ]


def sum_scratch(pieces, count):
    group = count // 2
    scratch = []
    for _, _, height, padded, lanes in pieces:
        scratch.append(pltpu.VMEM((2, height, lanes), BF16))
    for _, _, height, padded, lanes in pieces:
        scratch.append(pltpu.VMEM((height, lanes), BF16))
    for _, _, height, padded, lanes in pieces:
        scratch.append(pltpu.VMEM((padded, lanes), BF16))
    for _, _, height, padded, lanes in pieces:
        scratch.append(pltpu.VMEM((2, padded // 2, lanes), BF16))
    for _, _, height, padded, lanes in pieces:
        scratch.append(pltpu.VMEM((group - 1, padded // count, lanes), BF16))
    sems = pltpu.SemaphoreType.DMA((len(pieces), 3 + 2 * group))
    return scratch + [sems, sems]


def sum_kernel(pieces, count, segments, moves, *refs):
    refs = list(refs)

    def grab(number):
        taken = refs[:number]
        del refs[:number]
        return taken

    grads, sources = grab(segments), grab(moves)
    outs, targets = grab(segments), grab(moves)
    number = len(pieces)
    near, far, own, mid, part = (grab(number) for _ in range(5))
    send, receive = grab(2)
    meet(sum_peers(count) + ([peer(3)] if moves else []))
    copies = []
    if moves:
        extra_send, extra_receive = grab(2)
        for item, move in enumerate((2, 3, 1)):
            copies.append(
                remote(sources[move - 1], targets[move - 1], extra_send.at[item], extra_receive.at[item], peer(move))
            )
    steps = sum_steps(pieces, count, grads, outs, near, far, own, mid, part, send, receive)
    for time in range(number + len(steps) - 1):
        for stage in reversed(range(len(steps))):
            if 0 <= time - stage < number:
                steps[stage](time - stage)
        if time == 1:
            for copy in copies:
                copy.start()
    for copy in copies:
        copy.wait()


def sum_over_devices(grads, sources, identity):
    count = lax.axis_size("dp")
    shapes = [item.shape[1:] for item in grads]
    pieces = plan_pieces(shapes, count)
    vmem = pl.BlockSpec(memory_space=pltpu.VMEM)
    hbm = pl.BlockSpec(memory_space=pl.ANY)
    scratch = sum_scratch(pieces, count)
    if sources:
        scratch += [pltpu.SemaphoreType.DMA((3,)), pltpu.SemaphoreType.DMA((3,))]
    results = pl.pallas_call(
        lambda *refs: sum_kernel(pieces, count, len(grads), len(sources), *refs),
        in_specs=[vmem] * len(grads) + [hbm] * len(sources),
        out_specs=[vmem] * len(grads) + [hbm] * len(sources),
        out_shape=[like(shape, F32) for shape in shapes] + [like(item.shape, BF16) for item in sources],
        scratch_shapes=scratch,
        compiler_params=params(collective_id=identity, has_side_effects=True),
        name=f"sum{identity}",
    )(*grads, *sources)
    return results[: len(grads)], results[len(grads) :]


HALVES = 2


def find_cuts(crop_ids):
    cut = jnp.sum((crop_ids[:, :, 0] < 2).astype(jnp.int32), axis=1)
    upper = jnp.sum((crop_ids[:, 0, :] == 0).astype(jnp.int32), axis=1)
    lower = jnp.sum((crop_ids[:, SIDE - 1, :] == 2).astype(jnp.int32), axis=1)
    return jnp.stack([cut, upper, lower], axis=1)


def reach_mask():
    head = jnp.arange(D, dtype=jnp.int32) // HEAD_DIM
    reach = 1 + (head >= 2).astype(jnp.int32) + (head >= 5).astype(jnp.int32)
    taps = jnp.arange(49, dtype=jnp.int32)
    ring = jnp.maximum(jnp.abs(taps // 7 - 3), jnp.abs(taps % 7 - 3))
    return (ring[:, None] <= reach[None, :]).astype(F32)


def forward_parts(me, cuts, x_halves, small, qkv):
    zero = jnp.zeros((D,), F32)
    vec = jnp.stack([small[58], small[59], small[60], small[61], small[62], zero, zero, zero])
    crpe = jnp.broadcast_to((small[9:58] * reach_mask())[:, None, :], (49, 8, D))
    cpe = jnp.broadcast_to(small[:9][:, None, :], (9, 8, D))
    kept = ()
    base = 0
    for x_parts in x_halves:
        kept = front(cuts, me, x_parts, base, kept, cpe, vec, qkv, crpe)
        base += x_parts[0].shape[0] // PLACES
    return kept, vec, crpe, cpe


def middle_parts(me, kept, cot_parts, small, bias, proj, fc1, fc2):
    zero = jnp.zeros((D,), F32)
    vec = jnp.stack([small[63], small[64], small[65], small[66], zero, zero, zero, zero])
    return middle(me, kept[7], kept[0], cot_parts, vec, bias, proj, fc1, fc2)


def body(
    block_in, crop_ids, cotangent, cpe_kernel, cpe_bias, norm1_gain, norm1_shift, qkv_weight,
    qv_bias, crpe_kernel, proj_weight, proj_bias, norm2_gain, norm2_shift, fc1_weight, fc1_bias,
    fc2_weight, fc2_bias,
):
    head = lax.axis_index("head")
    me = head.reshape(1).astype(jnp.int32)
    canvases = crop_ids.shape[0] // 4
    rows = canvases * PLACES
    cuts = find_cuts(lax.dynamic_slice_in_dim(crop_ids, head * canvases, canvases, 0))

    def swap(values, move):
        return lax.ppermute(values, "head", [(item, item ^ move) for item in range(4)])

    def take(values, move, part, parts):
        size = rows // parts
        start = lax.bitwise_xor(head, move) * rows + part * size
        return lax.dynamic_slice_in_dim(values, start, size, 0)

    def bring(values, part, parts):
        pieces = [take(values, move, part, parts) for move in range(4)]
        return [pieces[0]] + [swap(pieces[move], move) for move in (1, 2, 3)]

    def gather(shard):
        far = swap(shard, 2)
        near = swap(jnp.stack([shard, far]), 1)
        return jnp.stack([shard, near[0], far, near[1]])

    packed = jnp.concatenate([
        cpe_kernel, crpe_kernel, cpe_bias[None], norm1_gain[None], norm1_shift[None], qv_bias,
        proj_bias[None], norm2_gain[None], norm2_shift[None], fc2_bias[None],
        fc1_bias.reshape(4, LANES), jnp.zeros((1, LANES), BF16),
    ]).astype(F32)
    part_rows = rows // HALVES
    order = lax.bitwise_xor(head, jnp.arange(4, dtype=jnp.int32))
    x1, x2, x3, qkv, small_all = entry(
        block_in, part_rows, qkv_weight.reshape(D, 3 * LANES), packed
    )
    x_halves = [[take(block_in, 0, 0, HALVES), x1, x2, x3]]
    block_in, proj_weight, cotangent, fc1_weight, fc2_weight, x_halves = lax.optimization_barrier(
        (block_in, proj_weight, cotangent, fc1_weight, fc2_weight, x_halves)
    )
    x_halves += [bring(block_in, part, HALVES) for part in range(1, HALVES)]
    cot_parts = bring(cotangent, 0, 1)
    proj = gather(proj_weight)
    fc1 = gather(fc1_weight)
    fc2 = gather(fc2_weight)
    small = jnp.take(small_all[:, :67], order, axis=0).transpose(1, 0, 2).reshape(67, D)
    bias = small_all[:, 67:71].reshape(4, 1, D)

    kept, vec, crpe, cpe = forward_parts(me, cuts, x_halves, small, qkv)
    first, hidden, query, value, soft, context, conv, attended = kept
    results = middle_parts(me, kept, cot_parts, small, bias, proj, fc1, fc2)
    second_grad, att_grad, fc1_grad, fc2_grad, proj_grad, sums2, bias_grad = results[4:]
    (fc1_own, fc2_own, proj_own), _ = sum_over_devices([fc1_grad, fc2_grad, proj_grad], [], 2)
    fc1_own, fc2_own, proj_own, att_grad, out_sent = lax.optimization_barrier(
        (fc1_own, fc2_own, proj_own, att_grad, list(results[:4]))
    )
    out_parts = [[out_sent[0]]] + [[swap(out_sent[move], move)] for move in (1, 2, 3)]

    grad_parts = [[] for _ in range(4)]
    sums = []
    base = 0
    for index, x_parts in enumerate(x_halves):
        back_results = back(
            cuts, me, x_parts, base, att_grad, query, value, soft, context, conv, first, hidden,
            second_grad, vec, qkv, crpe, cpe,
        )
        last = index == HALVES - 1
        for move in range(4):
            piece = back_results[move]
            grad_parts[move].append(piece if move == 0 or last else swap(piece, move))
        sums.append(back_results[4:])
        base += x_parts[0].shape[0] // PLACES
    qkv_grad, crpe_sum, cpe_sum, sums1 = [sum(items[1:], items[0]) for items in zip(*sums)]
    small_grad = jnp.concatenate([
        jnp.sum(cpe_sum, axis=1), jnp.sum(crpe_sum, axis=1) * reach_mask(), sums1[4:5], sums1[2:4],
        sums1[0:2], sums2[3:4], sums2[1:3], sums2[0:1],
    ]).reshape(-1, 4, LANES).transpose(1, 0, 2)
    small_grad = jnp.concatenate([
        jnp.take(small_grad, order, axis=0), bias_grad.reshape(4, 4, LANES),
        jnp.zeros((4, PIECE_ROWS - 71, LANES), F32),
    ], axis=1).astype(BF16)
    (qkv_own, small_own), last_parts = sum_over_devices(
        [qkv_grad.astype(BF16), small_grad], [grad_parts[move][-1] for move in (1, 2, 3)], 3
    )
    for move in (1, 2, 3):
        grad_parts[move][-1] = last_parts[move - 1]
    return (
        collect(me, out_parts), collect(me, grad_parts),
        small_own[:9], small_own[58], small_own[59], small_own[60],
        qkv_own.reshape(D, 3, LANES), small_own[61:63], small_own[9:58],
        proj_own, small_own[63], small_own[64], small_own[65],
        fc1_own, small_own[67:71].reshape(D), fc2_own, small_own[66],
    )


def solution(mesh):
    return jax.shard_map(
        body,
        mesh=mesh,
        in_specs=(
            P("dp", "head"), P("dp", None, None), P("dp", "head"), P(None, "head"), P("head"),
            P("head"), P("head"), P(None, None, "head"), P(None, "head"), P(None, "head"),
            P("head", None), P("head"), P("head"), P("head"), P(None, "head"), P("head"),
            P("head", None), P("head"),
        ),
        out_specs=(
            P("dp", "head"), P("dp", "head"), P(None, "head"), P("head"), P("head"), P("head"),
            P(None, None, "head"), P(None, "head"), P(None, "head"), P("head", None), P("head"),
            P("head"), P("head"), P(None, "head"), P("head"), P("head", None), P("head"),
        ),
        check_vma=False,
    )
```

```python
import jax
import jax.numpy as jnp
from jax import lax
from jax.experimental import pallas as pl
from jax.experimental.pallas import tpu as pltpu
from jax.sharding import PartitionSpec as P

D = 512
HEADS = 8
HEAD_DIM = 64
HIDDEN = 2048
SIDE = 16
PLACES = 256
LANES = 128
TILES = 4
REACH = (1, 2, 3, 3)
GAP = 3
GRID_ROWS = SIDE + 3 * GAP + 1
EPSILON = 1e-06
SCALE = HEAD_DIM ** (-0.5)
F32 = jnp.float32
BF16 = jnp.bfloat16


def dot(left, right, dims):
    return lax.dot_general(left, right, (dims, ((), ())), preferred_element_type=F32)


def nn(left, right):
    return dot(left, right, ((1,), (0,)))


def nt(left, right):
    return dot(left, right, ((1,), (1,)))


def tn(left, right):
    return dot(left, right, ((0,), (0,)))


def lane(tile):
    return pl.ds(LANES * tile, LANES)


def fill_masks(cut, col_cuts, mask_ref):
    col = lax.broadcasted_iota(jnp.int32, (SIDE, LANES), 0)
    for band in range(2):
        here = (col >= col_cuts[band]).astype(jnp.int32)
        for step in range(-3, 4):
            if step == 0:
                continue
            there = (col + step >= col_cuts[band]).astype(jnp.int32)
            good = (col + step >= 0) & (col + step < SIDE) & (here == there)
            mask_ref[band, step + 3] = jnp.where(good, 1.0, 0.0).astype(F32)


def place_ids(cut, col_cuts):
    place = lax.broadcasted_iota(jnp.int32, (PLACES, LANES), 0)
    row = lax.shift_right_logical(place, 4)
    col = lax.bitwise_and(place, 15)
    band = (row >= cut).astype(jnp.int32)
    col_cut = jnp.where(band > 0, col_cuts[1], col_cuts[0])
    side = (col >= col_cut).astype(jnp.int32)
    return band, side


def spread(read_row, reach, cut, mask_ref, grid_ref, plane):
    zero = jnp.zeros((GAP * SIDE, LANES), F32)
    for step in range(-reach, reach + 1):
        start = pl.multiple_of(SIDE * (GAP + cut), SIDE)
        grid_ref[plane + step, pl.ds(start, GAP * SIDE), :] = zero
    for row in range(SIDE):
        lower = (row >= cut).astype(jnp.int32)
        start = pl.multiple_of(SIDE * (row + GAP + GAP * lower), SIDE)
        values = read_row(row)
        for step in range(-reach, reach + 1):
            moved = values
            if step != 0:
                moved = pltpu.roll(values, (-step) % SIDE, 0) * mask_ref[lower, step + 3]
            grid_ref[plane + step, pl.ds(start, SIDE), :] = moved


def add_to(store, key, term):
    store[key] = term if key not in store else store[key] + term


def conv_tiles(items, reach, cut, grid_ref, taps_ref, tap_reach, out_ref):
    upper_pairs = (cut + 1) // 2
    pairs = upper_pairs + (SIDE - cut + 1) // 2
    width = 2 * tap_reach + 1
    chains = 3

    def body(index, carry):
        lower = (index >= upper_pairs).astype(jnp.int32)
        row = 2 * index + lower * (cut - 2 * upper_pairs)
        base = row + GAP * lower + (GAP - reach)
        for tile, plane in items:
            total = {}
            for step in range(-reach, reach + 1):
                taps = [
                    taps_ref[(dr + tap_reach) * width + step + tap_reach, :, lane(tile)]
                    for dr in range(-reach, reach + 1)
                ]
                for place in range(2 * reach + 2):
                    for half in range(2):
                        start = pl.multiple_of(SIDE * (base + place) + 8 * half, 8)
                        field = grid_ref[plane + step, pl.ds(start, 8), :]
                        for out in range(2):
                            tap = place - out
                            if 0 <= tap <= 2 * reach:
                                add_to(total, (out, half, step % chains), taps[tap] * field)
            for out in range(2):
                for half in range(2):
                    start = pl.multiple_of(SIDE * (row + out) + 8 * half, 8)
                    out_ref[pl.ds(start, 8), lane(tile)] = sum(
                        [total[out, half, chain] for chain in range(1, chains)], total[out, half, 0]
                    )
        return carry

    lax.fori_loop(0, pairs, body, 0)


def conv_back_tiles(items, reach, cut, grid_ref, taps_ref, tap_reach, other_ref, out_ref, sum_ref):
    upper_pairs = (cut + 1) // 2
    pairs = upper_pairs + (SIDE - cut + 1) // 2
    width = 2 * tap_reach + 1
    chains = 2

    def body(index, carry):
        lower = (index >= upper_pairs).astype(jnp.int32)
        row = 2 * index + lower * (cut - 2 * upper_pairs)
        base = row + GAP * lower + (GAP - reach)
        keep = jnp.where((lower == 0) & (row + 1 >= cut), 0.0, 1.0).astype(F32)
        for tile, plane in items:
            other = {}
            for out in range(2):
                for half in range(2):
                    start = pl.multiple_of(SIDE * (row + out) + 8 * half, 8)
                    value = other_ref[pl.ds(start, 8), lane(tile)]
                    other[out, half] = value * keep if out else value
            total = {}
            for step in range(-reach, reach + 1):
                sums = {}
                ids = [
                    (tap_reach - dr) * width + tap_reach - step for dr in range(-reach, reach + 1)
                ]
                taps = [taps_ref[item, :, lane(tile)] for item in ids]
                for place in range(2 * reach + 2):
                    for half in range(2):
                        start = pl.multiple_of(SIDE * (base + place) + 8 * half, 8)
                        field = grid_ref[plane + step, pl.ds(start, 8), :]
                        for out in range(2):
                            tap = place - out
                            if 0 <= tap <= 2 * reach:
                                add_to(total, (out, half, step % chains), taps[tap] * field)
                                add_to(sums, tap, other[out, half] * field)
                for tap in range(2 * reach + 1):
                    sum_ref[ids[tap], :, lane(tile)] += sums[tap]
            for out in range(2):
                for half in range(2):
                    start = pl.multiple_of(SIDE * (row + out) + 8 * half, 8)
                    out_ref[pl.ds(start, 8), lane(tile)] = sum(
                        [total[out, half, chain] for chain in range(1, chains)], total[out, half, 0]
                    )
        return carry

    lax.fori_loop(0, pairs, body, 0)


SMALL_ITEMS = tuple((tile, 3 * tile + 1) for tile in range(TILES))


def row_mean(values):
    return jnp.sum(values, axis=1, keepdims=True) * (1.0 / D)


def pick(ids, rows):
    out = rows[0]
    for crop in range(1, 4):
        out = jnp.where(ids >= crop, rows[crop], out)
    return out


def crop_reduce(ids, values, op, empty):
    return [op(jnp.where(ids == crop, values, empty), axis=0, keepdims=True) for crop in range(4)]


def head_block():
    row = lax.broadcasted_iota(jnp.int32, (2 * LANES, 2 * LANES), 0)
    col = lax.broadcasted_iota(jnp.int32, (2 * LANES, 2 * LANES), 1)
    same = lax.bitwise_and(row, HEAD_DIM) == lax.bitwise_and(col, HEAD_DIM)
    return jnp.where(same, 1.0, 0.0).astype(F32)


def both(values, masks):
    return jnp.concatenate([values * masks[0], values * masks[1]], axis=1)


def read_cuts(cuts_ref, base):
    step = pl.program_id(0) + base
    return cuts_ref[step, 0], (cuts_ref[step, 1], cuts_ref[step, 2])


def whole(shape):
    return pl.BlockSpec(shape, lambda *_: (0,) * len(shape))


def once(shape):
    return pl.BlockSpec(shape, lambda *_: (0,) * len(shape), pipeline_mode=pl.Buffered(1))


def rows_spec(width, base=0):
    return pl.BlockSpec((PLACES, width), lambda i, *_: (i + base, 0))


def context_spec(base):
    return pl.BlockSpec((1, TILES, 2 * LANES, 2 * LANES), lambda i, *_: (i + base, 0, 0, 0))


def like(shape, dtype):
    return jax.ShapeDtypeStruct(shape, dtype)


def params(**given):
    return pltpu.CompilerParams(vmem_limit_bytes=58 * 2**20, **given)


MESH = pl.DeviceIdType.MESH
PIECE_ROWS = 256
SMALL_ROWS = 128


def peer(move):
    return (lax.axis_index("dp"), lax.bitwise_xor(lax.axis_index("head"), move))


def meet(peers):
    barrier = pltpu.get_barrier_semaphore()
    for item in peers:
        pl.semaphore_signal(barrier, inc=1, device_id=item, device_id_type=MESH)
    pl.semaphore_wait(barrier, len(peers))


def remote(source, target, send, receive, device):
    return pltpu.make_async_remote_copy(
        src_ref=source, dst_ref=target, send_sem=send, recv_sem=receive,
        device_id=device, device_id_type=MESH,
    )


def plan_pieces(shapes, count):
    pieces = []
    for item, (rows, lanes) in enumerate(shapes):
        height = min(PIECE_ROWS, rows)
        for start in range(0, rows, height):
            pieces.append((item, start, height, padded_rows(height, count), lanes))
    return pieces


def padded_rows(height, count):
    unit = 16 * count
    return -(-height // unit) * unit


def place_on_dp():
    dp = lax.axis_index("dp")
    return dp, lax.rem(dp, 2), dp // 2


def low_peer():
    dp, low, _ = place_on_dp()
    return (dp + 1 - 2 * low, lax.axis_index("head"))


def high_peer(step, group):
    _, low, high = place_on_dp()
    return (lax.rem(high + step, group) * 2 + low, lax.axis_index("head"))


def aligned(index, size):
    return pl.ds(pl.multiple_of(index * size, size), size)


class HighSum:
    def __init__(self, count, mid, part, whole, got, send, receive, slot):
        self.group = count // 2
        self.got = got
        self.mid, self.part, self.whole = mid, part, whole
        self.send, self.receive, self.slot = send, receive, slot
        self.half = mid.shape[0]
        self.size = self.half // self.group

    def copy(self, source, target, slot, device):
        return remote(
            source, target, self.send.at[self.slot + slot], self.receive.at[self.slot + slot], device
        )

    def high(self, step):
        _, _, high = place_on_dp()
        other = lax.rem(high + step, self.group)
        return self.copy(
            self.mid.at[aligned(other, self.size)], self.part.at[step - 1], step - 1,
            high_peer(step, self.group),
        )

    def spot(self):
        dp, low, high = place_on_dp()
        return self.whole.at[aligned(low * self.group + high, self.size)]

    def share(self, step):
        spot = self.spot()
        return self.copy(spot, spot, self.group - 2 + step, high_peer(step, self.group))

    def last(self):
        _, low, _ = place_on_dp()
        here = self.whole.at[aligned(low, self.half)]
        return self.copy(here, self.got, 2 * self.group - 2, low_peer())

    def to_high(self):
        for step in range(1, self.group):
            self.high(step).start()

    def share_high(self):
        _, _, high = place_on_dp()
        total = self.mid[aligned(high, self.size), :].astype(F32)
        for step in range(1, self.group):
            self.high(step).wait()
            total += self.part[step - 1].astype(F32)
        self.spot()[...] = total.astype(BF16)
        for step in range(1, self.group):
            self.share(step).start()

    def share_low(self):
        for step in range(1, self.group):
            self.share(step).wait()
        self.last().start()

    def finish(self):
        _, low, _ = place_on_dp()
        self.last().wait()
        self.whole[aligned(1 - low, self.half), :] = self.got[...]


def high_slots(count):
    return count - 1


class FullSum:
    def __init__(self, count, grad, span, near, far, whole, mid, low, part, got, send, receive, slot):
        self.grad, self.span, self.near, self.far = grad, span, near, far
        self.whole, self.mid, self.low = whole, mid, low
        self.height = far.shape[0]
        self.send, self.receive, self.slot = send, receive, slot
        self.rest = HighSum(count, mid, part, whole, got, send, receive, slot + 4)

    def copy(self, source, target, slot, device):
        return remote(
            source, target, self.send.at[self.slot + slot], self.receive.at[self.slot + slot], device
        )

    def near_copy(self, item):
        return self.copy(
            self.grad.at[1 + 2 * item, self.span], self.near.at[item], item, peer(1)
        )

    def far_copy(self):
        return self.copy(self.whole.at[: self.height], self.far, 2, peer(2))

    def low_copy(self):
        _, low, _ = place_on_dp()
        return self.copy(self.whole.at[aligned(1 - low, self.mid.shape[0])], self.low, 3, low_peer())

    def to_core(self):
        self.near_copy(1).start()
        self.near_copy(0).start()

    def to_far(self):
        self.near_copy(1).wait()
        self.whole[: self.height, :] = (
            self.grad[2, self.span, :].astype(F32) + self.near[1].astype(F32)
        ).astype(BF16)
        self.far_copy().start()

    def to_low(self):
        self.near_copy(0).wait()
        self.far_copy().wait()
        self.whole[: self.height, :] = (
            self.grad[0, self.span, :].astype(F32) + self.near[0].astype(F32)
            + self.far[...].astype(F32)
        ).astype(BF16)
        rows = self.whole.shape[0]
        if rows > self.height:
            self.whole[self.height :, :] = jnp.zeros((rows - self.height, self.whole.shape[1]), BF16)
        self.low_copy().start()

    def to_high(self):
        _, low, _ = place_on_dp()
        self.low_copy().wait()
        half = self.mid.shape[0]
        self.mid[...] = (
            self.whole[aligned(low, half), :].astype(F32) + self.low[...].astype(F32)
        ).astype(BF16)
        self.rest.to_high()


def sum_scratch(pieces, count):
    scratch = []
    for _, _, height, padded, lanes in pieces:
        scratch += [
            pltpu.VMEM((2, height, lanes), BF16), pltpu.VMEM((height, lanes), BF16),
            pltpu.VMEM((padded, lanes), BF16), pltpu.VMEM((padded // 2, lanes), BF16),
            pltpu.VMEM((padded // 2, lanes), BF16),
            pltpu.VMEM((count // 2 - 1, padded // count, lanes), BF16),
            pltpu.VMEM((padded // 2, lanes), BF16),
        ]
    return scratch


def entry_kernel(
    rows, size, x_ref, qkv_ref, small_ref,
    x1_ref, x2_ref, x3_ref, all_qkv_ref, all_small_ref,
    send, receive, local,
):
    head = lax.axis_index("head")
    meet([peer(move) for move in (1, 2, 3)])
    copies = []
    far = remote(qkv_ref, all_qkv_ref.at[2], send.at[0], receive.at[0], peer(2))
    far.start()
    near = remote(qkv_ref, all_qkv_ref.at[1], send.at[1], receive.at[1], peer(1))
    near.start()
    for move in (1, 2, 3):
        copies.append(
            remote(small_ref, all_small_ref.at[move], send.at[1 + move], receive.at[1 + move], peer(move))
        )
        copies[-1].start()
    for move, target in ((2, x2_ref), (3, x3_ref), (1, x1_ref)):
        start = pl.multiple_of(lax.bitwise_xor(head, move) * rows, PLACES)
        copies.append(
            remote(x_ref.at[pl.ds(start, size)], target, send.at[4 + move], receive.at[4 + move], peer(move))
        )
        copies[-1].start()
    mine = pltpu.make_async_copy(qkv_ref, all_qkv_ref.at[0], local.at[0])
    mine.start()
    mine_small = pltpu.make_async_copy(small_ref, all_small_ref.at[0], local.at[1])
    mine_small.start()
    far.wait_recv()
    relay = remote(all_qkv_ref.at[2], all_qkv_ref.at[3], send.at[8], receive.at[8], peer(1))
    relay.start()
    far.wait_send()
    near.wait()
    for copy in copies:
        copy.wait()
    relay.wait()
    mine.wait()
    mine_small.wait()


def entry(block_in, size, qkv, small):
    rows = block_in.shape[0] // 4
    hbm = pl.BlockSpec(memory_space=pl.ANY)
    return pl.pallas_call(
        lambda *refs: entry_kernel(rows, size, *refs),
        in_specs=[hbm] * 3,
        out_specs=[hbm] * 5,
        out_shape=[like((size, LANES), BF16)] * 3 + [
            like((4,) + qkv.shape, BF16), like((4,) + small.shape, F32),
        ],
        scratch_shapes=[
            pltpu.SemaphoreType.DMA((9,)), pltpu.SemaphoreType.DMA((9,)),
            pltpu.SemaphoreType.DMA((2,)),
        ],
        compiler_params=params(collective_id=1, has_side_effects=True),
        name="entry",
    )(block_in, qkv, small)


def front_kernel(base, kept, *refs):
    (cuts_ref, me_ref, x0_ref, x1_ref, x2_ref, x3_ref, cpe_ref, vec_ref, qkv_ref, crpe_ref) = refs[:10]
    (first_ref, hidden_ref, query_ref, value_ref, soft_ref, context_ref, conv_ref, attended_ref,
     mask_ref, grid_ref, out_ref, x_ref) = refs[10 + kept :]
    cut, col_cuts = read_cuts(cuts_ref, base)
    me = me_ref[0]

    @pl.when(pl.program_id(0) == 0)
    def _():
        grid_ref[...] = jnp.zeros_like(grid_ref)

    for move, piece_ref in enumerate((x0_ref, x1_ref, x2_ref, x3_ref)):
        start = pl.multiple_of(LANES * lax.bitwise_xor(me, move), LANES)
        x_ref[:, pl.ds(start, LANES)] = piece_ref[...].astype(F32)
    fill_masks(cut, col_cuts, mask_ref)
    for tile, plane in SMALL_ITEMS:
        spread(
            lambda row: x_ref[SIDE * row : SIDE * row + SIDE, lane(tile)],
            1, cut, mask_ref, grid_ref, plane,
        )
    conv_tiles(SMALL_ITEMS, 1, cut, grid_ref, cpe_ref, 1, out_ref)
    first = x_ref[...] + out_ref[:PLACES, :] + vec_ref[0:1, :]
    first_ref[...] = first
    center = row_mean(first)
    square = row_mean(first * first)
    inverse = lax.rsqrt(square - center * center + EPSILON)
    hidden = ((first - center) * inverse * vec_ref[1:2, :] + vec_ref[2:3, :]).astype(BF16)
    hidden_ref[...] = hidden
    band, side = place_ids(cut, col_cuts)
    ids = 2 * band + side
    sides = [(side == item).astype(F32).astype(BF16) for item in range(2)]
    bands = [(band == item).astype(F32).astype(BF16) for item in range(2)]
    blocks = head_block()
    for tile in range(TILES):
        three = nn(hidden, qkv_ref[lax.bitwise_xor(me, tile)])
        query = (three[:, :LANES] + vec_ref[3:4, lane(tile)]).astype(BF16)
        keys = three[:, LANES : 2 * LANES].astype(BF16).astype(F32)
        value = (three[:, 2 * LANES :] + vec_ref[4:5, lane(tile)]).astype(BF16)
        query_ref[:, lane(tile)] = query
        value_ref[:, lane(tile)] = value
        highest = crop_reduce(ids, keys, jnp.max, -1e30)
        powers = jnp.exp(keys - pick(ids, highest))
        totals = crop_reduce(ids, powers, jnp.sum, 0.0)
        soft = (powers * pick(ids, [1.0 / item for item in totals])).astype(BF16)
        soft_ref[:, lane(tile)] = soft
        context = (tn(both(soft, sides), both(value, bands)) * blocks).astype(BF16)
        context_ref[0, tile] = context
        factor = nn(both(query, sides), context)
        x_ref[:, lane(tile)] = jnp.where(band > 0, factor[:, LANES:], factor[:, :LANES]) * SCALE
    for tile in range(TILES):
        spread(
            lambda row: value_ref[SIDE * row : SIDE * row + SIDE, lane(tile)].astype(F32),
            REACH[tile], cut, mask_ref, grid_ref, 3,
        )
        conv_tiles(((tile, 3),), REACH[tile], cut, grid_ref, crpe_ref, 3, out_ref)
    conv = out_ref[:PLACES, :]
    conv_ref[...] = conv.astype(BF16)
    attended_ref[...] = (x_ref[...] + query_ref[...].astype(F32) * conv).astype(BF16)


def front(cuts, me, x_parts, base, kept, cpe, vec, qkv, crpe):
    count = x_parts[0].shape[0] // PLACES
    total = cuts.shape[0]
    rows = total * PLACES
    wide = rows_spec(D, base)
    flops = 2 * count * PLACES * D * D * 4
    return pl.pallas_call(
        lambda *refs: front_kernel(base, len(kept), *refs),
        grid_spec=pltpu.PrefetchScalarGridSpec(
            num_scalar_prefetch=2,
            grid=(count,),
            in_specs=[rows_spec(LANES)] * 4
            + [whole(cpe.shape), whole(vec.shape), whole(qkv.shape), whole(crpe.shape)]
            + [pl.BlockSpec(memory_space=pl.ANY)] * len(kept),
            out_specs=[wide, wide, wide, wide, wide, context_spec(base), wide, wide],
            scratch_shapes=[
                pltpu.VMEM((2, 7, SIDE, LANES), F32),
                pltpu.VMEM((3 * TILES, GRID_ROWS * SIDE, LANES), F32),
                pltpu.VMEM((PLACES + SIDE, D), F32),
                pltpu.VMEM((PLACES, D), F32),
            ],
        ),
        out_shape=[
            like((rows, D), F32), like((rows, D), BF16), like((rows, D), BF16),
            like((rows, D), BF16), like((rows, D), BF16),
            like((total, TILES, 2 * LANES, 2 * LANES), BF16),
            like((rows, D), BF16), like((rows, D), BF16),
        ],
        input_output_aliases={10 + item: item for item in range(len(kept))},
        compiler_params=params(),
        cost_estimate=pl.CostEstimate(flops=flops * 6, bytes_accessed=count * 10**7, transcendentals=0),
        name="front",
    )(cuts, me, *x_parts, cpe, vec, qkv, crpe, *kept)


def gelu_both(pre):
    power = jnp.exp(pre * pre * -0.5)
    t = 1.0 / (1.0 + jnp.abs(pre) * (0.3275911 * 0.7071067811865476))
    poly = 0.5 * 1.061405429
    for item in (-1.453152027, 1.421413741, -0.284496736, 0.254829592):
        poly = poly * t + 0.5 * item
    tail = poly * t * power
    cdf = jnp.where(pre >= 0.0, 1.0 - tail, tail)
    return pre * cdf, cdf + pre * power * 0.3989422804014327


BLOCK = 512


def middle_kernel(
    count,
    attended_ref, first_ref, cot0_ref, cot1_ref, cot2_ref, cot3_ref, vec_ref, bias_ref,
    proj_ref, fc1_ref, fc2_ref,
    out0_ref, out1_ref, out2_ref, out3_ref, second_grad_ref, att_grad_ref, fc_mid_ref,
    proj_grad_ref, sum_ref, bias_grad_ref,
    cot_ref, hat_ref, inverse_ref, hidden_ref, total_ref, back_ref, active_ref, pre_grad_ref,
    grads_ref, near_ref, far_ref, own_ref, low_ref, send, receive,
):
    me = lax.axis_index("head")
    step = pl.program_id(0)
    rows = attended_ref.shape[0]
    blocks = rows // BLOCK
    _, low, _ = place_on_dp()
    half = low_ref.shape[1]

    def near(item, kind):
        return remote(
            grads_ref.at[2 * item, kind], near_ref.at[item, kind], send.at[2 * item + kind],
            receive.at[2 * item + kind], peer(1),
        )

    def far(kind):
        return remote(
            grads_ref.at[1, kind], far_ref.at[kind], send.at[4 + kind], receive.at[4 + kind], peer(2)
        )

    def to_low(kind):
        return remote(
            own_ref.at[kind, aligned(1 - low, half)], low_ref.at[kind], send.at[6 + kind],
            receive.at[6 + kind], low_peer(),
        )

    def part(index):
        return aligned(index, BLOCK)

    @pl.when(step == 0)
    def _():
        meet([peer(1), peer(2), low_peer()])
        own_ref[...] = jnp.zeros_like(own_ref)
        sum_ref[...] = jnp.zeros_like(sum_ref)
        for move, piece_ref in enumerate((cot0_ref, cot1_ref, cot2_ref, cot3_ref)):
            cot_ref[:, aligned(lax.bitwise_xor(me, move), LANES)] = piece_ref[...]

        def enter(index, carry):
            now = part(index)
            second = first_ref[now, :] + vec_ref[0:1, :]
            for tile in range(TILES):
                second += nn(attended_ref[now, lane(tile)], proj_ref[lax.bitwise_xor(me, tile)])
            center = row_mean(second)
            square = row_mean(second * second)
            inverse = lax.rsqrt(square - center * center + EPSILON)
            hat = (second - center) * inverse
            hidden_ref[now, :] = (hat * vec_ref[1:2, :] + vec_ref[2:3, :]).astype(BF16)
            hat_ref[now, :] = hat
            inverse_ref[now, :] = jnp.broadcast_to(inverse, (BLOCK, LANES))
            total_ref[now, :] = second + vec_ref[3:4, :]
            back_ref[now, :] = jnp.zeros((BLOCK, D), F32)
            sum_ref[0:1, :] += jnp.sum(cot_ref[now, :].astype(F32), axis=0, keepdims=True)
            return carry

        lax.fori_loop(0, blocks, enter, 0)

    bias_grad_ref[0] = jnp.zeros_like(bias_grad_ref[0])

    def chunk(index, carry):
        now = part(index)
        pre = nn(hidden_ref[now, :], fc1_ref[0]) + bias_ref[0]
        active, slope = gelu_both(pre)
        active = active.astype(BF16)
        active_ref[now, :] = active
        total_ref[now, :] += nn(active, fc2_ref[0])
        pre_grad_f = nt(cot_ref[now, :], fc2_ref[0]) * slope
        pre_grad = pre_grad_f.astype(BF16)
        pre_grad_ref[now, :] = pre_grad
        back_ref[now, :] += nt(pre_grad, fc1_ref[0])
        bias_grad_ref[0] += jnp.sum(pre_grad_f, axis=0, keepdims=True)
        return carry

    lax.fori_loop(0, blocks, chunk, 0)
    grads_ref[step, 0] = tn(hidden_ref[...], pre_grad_ref[...]).astype(BF16)
    grads_ref[step, 1] = tn(active_ref[...], cot_ref[...]).astype(BF16)

    @pl.when(step == 0)
    def _():
        for kind in range(2):
            near(0, kind).start()

    @pl.when(step == 1)
    def _():
        for kind in range(2):
            near(0, kind).wait()
            grads_ref[1, kind] = (
                grads_ref[1, kind].astype(F32) + near_ref[0, kind].astype(F32)
            ).astype(BF16)
            far(kind).start()

    @pl.when(step == 2)
    def _():
        for kind in range(2):
            near(1, kind).start()

    @pl.when(step == 3)
    def _():
        for kind in range(2):
            near(1, kind).wait()
            far(kind).wait()
            own_ref[kind, :D, :] = (
                grads_ref[3, kind].astype(F32) + near_ref[1, kind].astype(F32)
                + far_ref[kind].astype(F32)
            ).astype(BF16)
            to_low(kind).start()

        def leave(index, carry):
            now = part(index)
            for move, piece_ref in enumerate((out0_ref, out1_ref, out2_ref, out3_ref)):
                piece_ref[now, :] = total_ref[now, aligned(lax.bitwise_xor(me, move), LANES)].astype(BF16)
            hat = hat_ref[now, :]
            norm_grad = back_ref[now, :]
            weighted = norm_grad * vec_ref[1:2, :]
            second_grad = cot_ref[now, :].astype(F32) + inverse_ref[now, 0:1] * (
                weighted - row_mean(weighted) - hat * row_mean(weighted * hat)
            )
            second_grad_ref[now, :] = second_grad
            second_low = second_grad.astype(BF16)
            hidden_ref[now, :] = second_low
            for tile in range(TILES):
                att_grad_ref[now, lane(tile)] = nt(
                    second_low, proj_ref[lax.bitwise_xor(me, tile)]
                ).astype(BF16)
            sum_ref[1:2, :] += jnp.sum(norm_grad * hat, axis=0, keepdims=True)
            sum_ref[2:3, :] += jnp.sum(norm_grad, axis=0, keepdims=True)
            sum_ref[3:4, :] += jnp.sum(second_low.astype(F32), axis=0, keepdims=True)
            return carry

        lax.fori_loop(0, blocks, leave, 0)
        for tile in range(TILES):
            proj_grad_ref[lax.bitwise_xor(me, tile)] = tn(
                attended_ref[:, lane(tile)], hidden_ref[...]
            ).astype(BF16)
        for kind in range(2):
            to_low(kind).wait()
            fc_mid_ref[kind] = (
                own_ref[kind, aligned(low, half), :].astype(F32) + low_ref[kind].astype(F32)
            ).astype(BF16)


def middle(attended, first, cot_parts, vec, bias, proj, fc1, fc2):
    rows = attended.shape[0]
    count = lax.axis_size("dp")
    padded = padded_rows(D, count)
    shard = pl.BlockSpec((1, D, D), lambda i: (3 - i, 0, 0))
    piece = once((rows, LANES))
    wide = once((rows, D))
    line = pl.BlockSpec((1, 1, D), lambda i: (3 - i, 0, 0))
    return pl.pallas_call(
        lambda *refs: middle_kernel(count, *refs),
        grid=(4,),
        in_specs=[
            wide, wide, piece, piece, piece, piece, whole(vec.shape), line, once(proj.shape),
            shard, shard,
        ],
        out_specs=[
            piece, piece, piece, piece, wide, wide, once((2, padded // 2, D)), once(proj.shape),
            once((8, D)), line,
        ],
        out_shape=[like((rows, LANES), BF16)] * 4 + [
            like((rows, D), F32), like((rows, D), BF16), like((2, padded // 2, D), BF16),
            like(proj.shape, BF16), like((8, D), F32), like(bias.shape, F32),
        ],
        scratch_shapes=[
            pltpu.VMEM((rows, D), BF16), pltpu.VMEM((rows, D), F32),
            pltpu.VMEM((rows, LANES), F32),
            pltpu.VMEM((rows, D), BF16), pltpu.VMEM((rows, D), F32),
            pltpu.VMEM((rows, D), F32), pltpu.VMEM((rows, D), BF16),
            pltpu.VMEM((rows, D), BF16),
            pltpu.VMEM((4, 2, D, D), BF16), pltpu.VMEM((2, 2, D, D), BF16),
            pltpu.VMEM((2, D, D), BF16), pltpu.VMEM((2, padded, D), BF16),
            pltpu.VMEM((2, padded // 2, D), BF16),
            pltpu.SemaphoreType.DMA((8,)), pltpu.SemaphoreType.DMA((8,)),
        ],
        compiler_params=params(collective_id=2, has_side_effects=True),
        cost_estimate=pl.CostEstimate(flops=rows * D * D * 60, bytes_accessed=3 * 10**7, transcendentals=0),
        name="middle",
    )(attended, first, *cot_parts, vec, bias, proj, fc1, fc2)


def back_kernel(
    cuts_ref, me_ref, grad_ref, query_ref, value_ref, soft_ref, context_ref, conv_ref, hidden_ref,
    crpe_ref,
    three_ref, qkv_out_ref, crpe_sum_ref, sum_ref,
    mask_ref, grid_ref, out_ref, other_ref, value_part_ref, qkv_grad_ref,
):
    cut, col_cuts = read_cuts(cuts_ref, 0)
    me = me_ref[0]

    @pl.when(pl.program_id(0) == 0)
    def _():
        grid_ref[...] = jnp.zeros_like(grid_ref)
        other_ref[...] = jnp.zeros_like(other_ref)
        qkv_grad_ref[...] = jnp.zeros_like(qkv_grad_ref)
        crpe_sum_ref[...] = jnp.zeros_like(crpe_sum_ref)
        sum_ref[...] = jnp.zeros_like(sum_ref)

    fill_masks(cut, col_cuts, mask_ref)
    band, side = place_ids(cut, col_cuts)
    ids = 2 * band + side
    sides = [(side == item).astype(F32).astype(BF16) for item in range(2)]
    bands = [(band == item).astype(F32).astype(BF16) for item in range(2)]
    blocks = head_block() * SCALE
    for tile in range(TILES):
        grad = grad_ref[:, lane(tile)]
        query = query_ref[:, lane(tile)]
        value = value_ref[:, lane(tile)]
        soft = soft_ref[:, lane(tile)]
        context = context_ref[0, tile]
        grad_f = grad.astype(F32)
        grad_bands = both(grad, bands)
        context_grad = (tn(both(query, sides), grad_bands) * blocks).astype(BF16)
        part = nt(grad_bands, context)
        part = jnp.where(side > 0, part[:, LANES:], part[:, :LANES])
        query_grad = (
            part * SCALE + grad_f * conv_ref[:, lane(tile)].astype(F32)
        ).astype(BF16)
        soft_grad = nt(both(value, bands), context_grad)
        soft_grad = jnp.where(side > 0, soft_grad[:, LANES:], soft_grad[:, :LANES])
        soft_f = soft.astype(F32)
        inner = crop_reduce(ids, soft_f * soft_grad, jnp.sum, 0.0)
        keys_grad = (soft_f * (soft_grad - pick(ids, inner))).astype(BF16)
        value_part = nn(both(soft, sides), context_grad)
        value_part_ref[:, lane(tile)] = jnp.where(
            band > 0, value_part[:, LANES:], value_part[:, :LANES]
        )
        three_ref[tile, :, :LANES] = query_grad
        three_ref[tile, :, LANES : 2 * LANES] = keys_grad
        sum_ref[0:1, lane(tile)] += jnp.sum(query_grad.astype(F32), axis=0, keepdims=True)
    other_ref[:PLACES, :] = value_ref[...].astype(F32)
    for tile in range(TILES):

        def read_row(row):
            part = pl.ds(SIDE * row, SIDE)
            return grad_ref[part, lane(tile)].astype(F32) * query_ref[part, lane(tile)].astype(F32)

        spread(read_row, REACH[tile], cut, mask_ref, grid_ref, 3)
        conv_back_tiles(
            ((tile, 3),), REACH[tile], cut, grid_ref, crpe_ref, 3, other_ref, out_ref, crpe_sum_ref
        )
    hidden = hidden_ref[...]
    for tile in range(TILES):
        value_grad = (value_part_ref[:, lane(tile)] + out_ref[:PLACES, lane(tile)]).astype(BF16)
        three_ref[tile, :, 2 * LANES :] = value_grad
        sum_ref[1:2, lane(tile)] += jnp.sum(value_grad.astype(F32), axis=0, keepdims=True)
        qkv_grad_ref[lax.bitwise_xor(me, tile)] += tn(hidden, three_ref[tile])

    @pl.when(pl.program_id(0) == pl.num_programs(0) - 1)
    def _():
        qkv_out_ref[...] = qkv_grad_ref[...].astype(BF16)


def back(cuts, me, grad, query, value, soft, context, conv, hidden, crpe):
    rows = grad.shape[0]
    count = rows // PLACES
    wide = rows_spec(D)
    shards = (4, D, 3 * LANES)
    return pl.pallas_call(
        lambda *refs: back_kernel(*refs),
        grid_spec=pltpu.PrefetchScalarGridSpec(
            num_scalar_prefetch=2,
            grid=(count,),
            in_specs=[wide, wide, wide, wide, context_spec(0), wide, wide, whole(crpe.shape)],
            out_specs=[
                pl.BlockSpec((TILES, PLACES, 3 * LANES), lambda i, *_: (0, i, 0)),
                once(shards), whole((49, 8, D)), whole((8, D)),
            ],
            scratch_shapes=[
                pltpu.VMEM((2, 7, SIDE, LANES), F32),
                pltpu.VMEM((7, GRID_ROWS * SIDE, LANES), F32),
                pltpu.VMEM((PLACES + SIDE, D), F32),
                pltpu.VMEM((PLACES + SIDE, D), F32),
                pltpu.VMEM((PLACES, D), F32),
                pltpu.VMEM(shards, F32),
            ],
        ),
        out_shape=[
            like((TILES, rows, 3 * LANES), BF16), like(shards, BF16), like((49, 8, D), F32),
            like((8, D), F32),
        ],
        compiler_params=params(),
        cost_estimate=pl.CostEstimate(
            flops=rows * D * D * 64, bytes_accessed=count * 10**7, transcendentals=0
        ),
        name="back",
    )(cuts, me, grad, query, value, soft, context, conv, hidden, crpe)


def step_masks(cut, col_cuts):
    place = lax.broadcasted_iota(jnp.int32, (PLACES, LANES), 0)
    row = lax.shift_right_logical(place, 4)
    col = lax.bitwise_and(place, 15)
    col_cut = jnp.where(row >= cut, col_cuts[1], col_cuts[0])
    rows = {
        1: (row < SIDE - 1) & (row + 1 != cut),
        -1: (row > 0) & (row != cut),
    }
    cols = {
        1: (col < SIDE - 1) & (col + 1 != col_cut),
        -1: (col > 0) & (col != col_cut),
    }
    return [
        {key: jnp.where(mask, 1.0, 0.0).astype(F32) for key, mask in masks.items()}
        for masks in (rows, cols)
    ]


def shift_rows(values, step):
    if step == 0:
        return values
    zero = jnp.zeros((SIDE, values.shape[1]), values.dtype)
    if step > 0:
        return jnp.concatenate([values[SIDE:], zero], axis=0)
    return jnp.concatenate([zero, values[:-SIDE]], axis=0)


def shift_cols(values, masks, step):
    if step == 0:
        return values
    return pltpu.roll(values, (-step) % PLACES, 0) * masks[step]


LAST_ROWS = 16
STAGES = {"core": 0, "far": 1, "low": 3, "high": 4, "share": 5, "last": 6}
FC_STAGES = {"high": 0, "share": 2, "last": 4}


def tail_kernel(
    count, pieces,
    cuts_ref, x0_ref, x1_ref, x2_ref, x3_ref, three_ref, first_ref, second_grad_ref, vec_ref, qkv_ref,
    cpe_ref, fc_mid_in, qkv_grad_in, proj_grad_in, small_in,
    out0_ref, out1_ref, out2_ref, out3_ref, fc1_own_ref, fc2_own_ref, qkv_own_ref, proj_own_ref,
    small_own_ref, last_own_ref,
    x_ref, gone_ref, cpe_sum_ref, sum_ref, fc_part_ref, fc_whole_ref, fc_got_ref, mine_ref, first_got_ref,
    total_ref, second_got_ref, piece_send, piece_receive, send, receive, last_send, last_receive,
    fc_mid_ref, qkv_grad_ref, proj_grad_ref, small_ref, *buffers,
):
    me = lax.axis_index("head")
    dp = lax.axis_index("dp")
    step = pl.program_id(0)
    steps = pl.num_programs(0)
    slots = high_slots(count)
    fc_sums = [
        HighSum(
            count, fc_mid_ref.at[kind], fc_part_ref.at[kind], fc_whole_ref.at[kind],
            fc_got_ref.at[kind], send, receive, kind * slots,
        )
        for kind in range(2)
    ]
    sources = (qkv_grad_ref, proj_grad_ref, small_ref)
    targets = (qkv_own_ref, proj_own_ref, small_own_ref)
    sums = []
    for number, (item, start, height, padded, lanes) in enumerate(pieces):
        near, far, own, mid, low, part, got = buffers[7 * number : 7 * number + 7]
        sums.append(
            FullSum(
                count, sources[item], pl.ds(start, height), near, far, own, mid, low, part, got, send,
                receive, 2 * slots + number * (slots + 4),
            )
        )

    def piece_copy(index, move):
        target = (out1_ref, out2_ref, out3_ref)[move - 1]
        return remote(
            gone_ref.at[index, move - 1], target.at[aligned(index, PLACES)],
            piece_send.at[index, move - 1], piece_receive.at[index, move - 1], peer(move),
        )

    def first_copy(move):
        return remote(
            mine_ref.at[move], first_got_ref.at[move - 1], last_send.at[move - 1],
            last_receive.at[move - 1], peer(move),
        )

    def second_copy(hop):
        return remote(
            total_ref, second_got_ref.at[hop - 1], last_send.at[2 + hop], last_receive.at[2 + hop],
            (lax.rem(dp + hop, count), me),
        )

    @pl.when(step == 0)
    def _():
        meet(
            [peer(1), peer(2), peer(3)] + [(lax.rem(dp + hop, count), me) for hop in range(1, count)]
        )
        fc_mid_ref[...] = fc_mid_in[...]
        qkv_grad_ref[...] = qkv_grad_in[...]
        proj_grad_ref[...] = proj_grad_in[...]
        small_ref[...] = small_in[...]
        cpe_sum_ref[...] = jnp.zeros_like(cpe_sum_ref)
        sum_ref[...] = jnp.zeros_like(sum_ref)

    def at(when, action, items):
        @pl.when(step == when)
        def _():
            for item in items:
                action(item)

    at(STAGES["core"], lambda item: item.to_core(), sums)
    at(FC_STAGES["high"], lambda item: item.to_high(), fc_sums)
    at(STAGES["far"], lambda item: item.to_far(), sums)
    at(FC_STAGES["share"], lambda item: item.share_high(), fc_sums)
    at(STAGES["low"], lambda item: item.to_low(), sums)
    at(STAGES["high"], lambda item: item.to_high(), sums)
    at(FC_STAGES["last"], lambda item: item.share_low(), fc_sums)
    at(STAGES["share"], lambda item: item.rest.share_high(), sums)
    at(STAGES["last"], lambda item: item.rest.share_low(), sums)

    norm_grad = nt(three_ref[0], qkv_ref[lax.bitwise_xor(me, 0)])
    for tile in range(1, TILES):
        norm_grad += nt(three_ref[tile], qkv_ref[lax.bitwise_xor(me, tile)])
    first = first_ref[...]
    center = row_mean(first)
    square = row_mean(first * first)
    inverse = lax.rsqrt(square - center * center + EPSILON)
    hat = (first - center) * inverse
    weighted = norm_grad * vec_ref[1:2, :]
    first_grad = second_grad_ref[...] + inverse * (
        weighted - row_mean(weighted) - hat * row_mean(weighted * hat)
    )
    sum_ref[0:1, :] += jnp.sum(first_grad, axis=0, keepdims=True)
    sum_ref[1:2, :] += jnp.sum(norm_grad * hat, axis=0, keepdims=True)
    sum_ref[2:3, :] += jnp.sum(norm_grad, axis=0, keepdims=True)
    for move, piece_ref in enumerate((x0_ref, x1_ref, x2_ref, x3_ref)):
        x_ref[:, aligned(lax.bitwise_xor(me, move), LANES)] = piece_ref[...].astype(F32)
    rows, cols = step_masks(cuts_ref[step, 0], (cuts_ref[step, 1], cuts_ref[step, 2]))
    results = []
    for tile in range(TILES):
        field = first_grad[:, LANES * tile : LANES * (tile + 1)]
        other = x_ref[:, lane(tile)]
        others = {0: other, 1: shift_rows(other * rows[1], -1), -1: shift_rows(other * rows[-1], 1)}
        moved = [shift_cols(field, cols, col) for col in (-1, 0, 1)]
        result = field
        for row in (-1, 0, 1):
            line = None
            for col in (-1, 0, 1):
                tap = (1 - row) * 3 + 1 - col
                wide_tap = jnp.broadcast_to(cpe_ref[tap : tap + 1, lane(tile)], (PLACES, LANES))
                term = wide_tap * moved[col + 1]
                line = term if line is None else line + term
                product = others[row] * moved[col + 1]
                cpe_sum_ref[tap, :, lane(tile)] += jnp.sum(product.reshape(PLACES // 8, 8, LANES), axis=0)
            line = shift_rows(line, row)
            result = result + (line * rows[row] if row else line)
        results.append(result)
    result = jnp.concatenate(results, axis=1)
    x_ref[...] = result
    out0_ref[...] = x_ref[:, aligned(me, LANES)].astype(BF16)
    for move in (1, 2, 3):
        gone_ref[step, move - 1] = x_ref[:, aligned(lax.bitwise_xor(me, move), LANES)].astype(BF16)
    for move in (2, 3, 1):
        piece_copy(step, move).start()

    @pl.when(step == steps - 1)
    def _():
        sum_ref[3:12, :] = jnp.sum(cpe_sum_ref[...], axis=1)
        for move in range(4):
            mine_ref[move] = sum_ref[:, aligned(lax.bitwise_xor(me, move), LANES)]
        for move in (1, 2, 3):
            first_copy(move).start()
        for item in fc_sums:
            item.finish()
        fc1_own_ref[...] = fc_whole_ref[0, :D, :].astype(F32)
        fc2_own_ref[...] = fc_whole_ref[1, :D, :].astype(F32)
        total = mine_ref[0]
        for move in (1, 2, 3):
            first_copy(move).wait()
            total += first_got_ref[move - 1]
        total_ref[...] = total
        for hop in range(1, count):
            second_copy(hop).start()
        for piece, item in zip(pieces, sums):
            item.rest.finish()
            targets[piece[0]][piece[1] : piece[1] + piece[2], :] = item.whole[: piece[2], :].astype(F32)
        for hop in range(1, count):
            second_copy(hop).wait()
            total += second_got_ref[hop - 1]
        last_own_ref[...] = total

        def settle(index, carry):
            for move in (1, 2, 3):
                piece_copy(index, move).wait()
            return carry

        lax.fori_loop(0, steps, settle, 0)


def tail(cuts, x_parts, three, first, second_grad, vec, qkv, cpe, fc_mid, qkv_grad, proj_grad, small):
    rows = first.shape[0]
    canvases = rows // PLACES
    count = lax.axis_size("dp")
    segments = [qkv_grad, proj_grad, small]
    pieces = plan_pieces([item.shape[1:] for item in segments], count)
    slots = high_slots(count)
    wide = rows_spec(D)
    piece = rows_spec(LANES)
    hbm = pl.BlockSpec(memory_space=pl.ANY)
    half = fc_mid.shape[1]
    group = count // 2
    total_slots = 2 * slots + len(pieces) * (slots + 4)
    last = (LAST_ROWS, LANES)
    return pl.pallas_call(
        lambda *refs: tail_kernel(count, pieces, *refs),
        grid=(canvases,),
        in_specs=[pl.BlockSpec(memory_space=pltpu.SMEM)] + [piece] * 4 + [
            pl.BlockSpec((TILES, PLACES, 3 * LANES), lambda i: (0, i, 0)), wide, wide,
            once(vec.shape), once(qkv.shape), once(cpe.shape), once(fc_mid.shape),
        ] + [once(item.shape) for item in segments],
        out_specs=[piece, hbm, hbm, hbm, once((D, D)), once((D, D))]
        + [once(item.shape[1:]) for item in segments] + [once(last)],
        out_shape=[like((rows, LANES), BF16)] * 4 + [like((D, D), F32)] * 2
        + [like(item.shape[1:], F32) for item in segments] + [like(last, F32)],
        scratch_shapes=[
            pltpu.VMEM((PLACES, D), F32), pltpu.VMEM((canvases, 3, PLACES, LANES), BF16),
            pltpu.VMEM((9, 8, D), F32), pltpu.VMEM((LAST_ROWS, D), F32),
            pltpu.VMEM((2, group - 1, half // group, D), BF16), pltpu.VMEM((2, 2 * half, D), BF16),
            pltpu.VMEM((2, half, D), BF16),
            pltpu.VMEM((4,) + last, F32), pltpu.VMEM((3,) + last, F32), pltpu.VMEM(last, F32),
            pltpu.VMEM((count - 1,) + last, F32),
            pltpu.SemaphoreType.DMA((canvases, 3)), pltpu.SemaphoreType.DMA((canvases, 3)),
            pltpu.SemaphoreType.DMA((total_slots,)), pltpu.SemaphoreType.DMA((total_slots,)),
            pltpu.SemaphoreType.DMA((2 + count,)), pltpu.SemaphoreType.DMA((2 + count,)),
        ] + [pltpu.VMEM(item.shape, BF16) for item in [fc_mid] + segments]
        + sum_scratch(pieces, count),
        compiler_params=params(collective_id=3, has_side_effects=True),
        cost_estimate=pl.CostEstimate(
            flops=rows * D * D * 12, bytes_accessed=canvases * 3 * 10**6, transcendentals=0
        ),
        name="tail",
    )(cuts, *x_parts, three, first, second_grad, vec, qkv, cpe, fc_mid, *segments)


def collect_kernel(me_ref, *refs):
    out_ref = refs[-1]
    for item, piece_ref in enumerate(refs[:-1]):

        @pl.when(pl.program_id(0) == item)
        def _():
            out_ref[...] = piece_ref[...].astype(F32)


def collect(me, pieces):
    parts = len(pieces[0])
    rows = pieces[0][0].shape[0]
    return pl.pallas_call(
        collect_kernel,
        grid_spec=pltpu.PrefetchScalarGridSpec(
            num_scalar_prefetch=1,
            grid=(4 * parts,),
            in_specs=[once((rows, LANES))] * (4 * parts),
            out_specs=pl.BlockSpec(
                (rows, LANES),
                lambda i, me: (lax.bitwise_xor(me[0], i // parts) * parts + i % parts, 0),
            ),
        ),
        out_shape=like((4 * parts * rows, LANES), F32),
        compiler_params=params(),
        name="collect",
    )(me, *[piece for move in pieces for piece in move])


HALVES = 2


def find_cuts(crop_ids):
    cut = jnp.sum((crop_ids[:, :, 0] < 2).astype(jnp.int32), axis=1)
    upper = jnp.sum((crop_ids[:, 0, :] == 0).astype(jnp.int32), axis=1)
    lower = jnp.sum((crop_ids[:, SIDE - 1, :] == 2).astype(jnp.int32), axis=1)
    return jnp.stack([cut, upper, lower], axis=1)


def reach_mask():
    head = jnp.arange(D, dtype=jnp.int32) // HEAD_DIM
    reach = 1 + (head >= 2).astype(jnp.int32) + (head >= 5).astype(jnp.int32)
    taps = jnp.arange(49, dtype=jnp.int32)
    ring = jnp.maximum(jnp.abs(taps // 7 - 3), jnp.abs(taps % 7 - 3))
    return (ring[:, None] <= reach[None, :]).astype(F32)


def forward_parts(me, cuts, x_halves, small, qkv):
    zero = jnp.zeros((D,), F32)
    vec = jnp.stack([small[58], small[59], small[60], small[61], small[62], zero, zero, zero])
    crpe = jnp.broadcast_to((small[9:58] * reach_mask())[:, None, :], (49, 8, D))
    cpe = jnp.broadcast_to(small[:9][:, None, :], (9, 8, D))
    kept = ()
    base = 0
    for x_parts in x_halves:
        kept = front(cuts, me, x_parts, base, kept, cpe, vec, qkv, crpe)
        base += x_parts[0].shape[0] // PLACES
    return kept, vec, crpe, cpe


def middle_parts(kept, cot_parts, small, bias, proj, fc1, fc2):
    zero = jnp.zeros((D,), F32)
    vec = jnp.stack([small[63], small[64], small[65], small[66], zero, zero, zero, zero])
    return middle(kept[7], kept[0], cot_parts, vec, bias, proj, fc1, fc2)


def body(
    block_in, crop_ids, cotangent, cpe_kernel, cpe_bias, norm1_gain, norm1_shift, qkv_weight,
    qv_bias, crpe_kernel, proj_weight, proj_bias, norm2_gain, norm2_shift, fc1_weight, fc1_bias,
    fc2_weight, fc2_bias,
):
    head = lax.axis_index("head")
    me = head.reshape(1).astype(jnp.int32)
    canvases = crop_ids.shape[0] // 4
    rows = canvases * PLACES
    cuts = find_cuts(lax.dynamic_slice_in_dim(crop_ids, head * canvases, canvases, 0))

    def swap(values, move):
        return lax.ppermute(values, "head", [(item, item ^ move) for item in range(4)])

    def take(values, move, part, parts):
        size = rows // parts
        start = lax.bitwise_xor(head, move) * rows + part * size
        return lax.dynamic_slice_in_dim(values, start, size, 0)

    def bring(values, part, parts):
        pieces = [take(values, move, part, parts) for move in range(4)]
        return [pieces[0]] + [swap(pieces[move], move) for move in (1, 2, 3)]

    def gather(shard):
        far = swap(shard, 2)
        near = swap(jnp.stack([shard, far]), 1)
        return jnp.stack([shard, near[0], far, near[1]])

    packed = jnp.concatenate([
        cpe_kernel, crpe_kernel, cpe_bias[None], norm1_gain[None], norm1_shift[None], qv_bias,
        proj_bias[None], norm2_gain[None], norm2_shift[None], fc2_bias[None],
        fc1_bias.reshape(4, LANES), jnp.zeros((1, LANES), BF16),
    ]).astype(F32)
    part_rows = rows // HALVES
    order = lax.bitwise_xor(head, jnp.arange(4, dtype=jnp.int32))
    x1, x2, x3, qkv, small_all = entry(
        block_in, part_rows, qkv_weight.reshape(D, 3 * LANES), packed
    )
    x_halves = [[take(block_in, 0, 0, HALVES), x1, x2, x3]]
    block_in, proj_weight, cotangent, fc1_weight, fc2_weight, x_halves = lax.optimization_barrier(
        (block_in, proj_weight, cotangent, fc1_weight, fc2_weight, x_halves)
    )
    x_halves += [bring(block_in, part, HALVES) for part in range(1, HALVES)]
    cot_parts = bring(cotangent, 0, 1)
    proj = gather(proj_weight)
    fc1 = gather(fc1_weight)
    fc2 = gather(fc2_weight)
    small = jnp.take(small_all[:, :67], order, axis=0).transpose(1, 0, 2).reshape(67, D)
    bias = small_all[:, 67:71].reshape(4, 1, D)

    kept, vec, crpe, cpe = forward_parts(me, cuts, x_halves, small, qkv)
    first, hidden, query, value, soft, context, conv, attended = kept
    results = middle_parts(kept, cot_parts, small, bias, proj, fc1, fc2)
    second_grad, att_grad, fc_mid, proj_grad, sums2, bias_grad = results[4:]
    out_parts = [[results[0]]] + [[swap(results[move], move)] for move in (1, 2, 3)]
    three, qkv_grad, crpe_sum, sums1 = back(
        cuts, me, att_grad, query, value, soft, context, conv, hidden, crpe
    )
    small_grad = jnp.concatenate([
        jnp.sum(crpe_sum, axis=1) * reach_mask(), sums1[0:2], sums2[3:4], sums2[1:3], sums2[0:1],
    ])
    small_rows = small_grad.shape[0]
    small_grad = jnp.concatenate([
        jnp.take(small_grad.reshape(-1, 4, LANES).transpose(1, 0, 2), order, axis=0),
        bias_grad.reshape(4, 4, LANES), jnp.zeros((4, SMALL_ROWS - small_rows - 4, LANES), F32),
    ], axis=1).astype(BF16)
    x_parts = [jnp.concatenate([item[move] for item in x_halves]) for move in range(4)]
    results = tail(
        cuts, x_parts, three, first, second_grad, vec, qkv, small[:9], fc_mid, qkv_grad, proj_grad,
        small_grad,
    )
    fc1_own, fc2_own, qkv_own, proj_own, small_own, last_own = results[4:]
    return (
        collect(me, out_parts), collect(me, [[item] for item in results[:4]]),
        last_own[3:12], last_own[0], last_own[1], last_own[2],
        qkv_own.reshape(D, 3, LANES), small_own[49:51], small_own[:49],
        proj_own, small_own[51], small_own[52], small_own[53],
        fc1_own, small_own[55:59].reshape(D), fc2_own, small_own[54],
    )


def solution(mesh):
    return jax.shard_map(
        body,
        mesh=mesh,
        in_specs=(
            P("dp", "head"), P("dp", None, None), P("dp", "head"), P(None, "head"), P("head"),
            P("head"), P("head"), P(None, None, "head"), P(None, "head"), P(None, "head"),
            P("head", None), P("head"), P("head"), P("head"), P(None, "head"), P("head"),
            P("head", None), P("head"),
        ),
        out_specs=(
            P("dp", "head"), P("dp", "head"), P(None, "head"), P("head"), P("head"), P("head"),
            P(None, None, "head"), P(None, "head"), P(None, "head"), P("head", None), P("head"),
            P("head"), P("head"), P(None, "head"), P("head"), P("head", None), P("head"),
        ),
        check_vma=False,
    )
```

```python
import jax
import jax.numpy as jnp
from jax import lax
from jax.experimental import pallas as pl
from jax.experimental.pallas import tpu as pltpu
from jax.sharding import PartitionSpec as P

D = 512
HEADS = 8
HEAD_DIM = 64
HIDDEN = 2048
SIDE = 16
PLACES = 256
LANES = 128
TILES = 4
REACH = (1, 2, 3, 3)
GAP = 3
GRID_ROWS = SIDE + 3 * GAP + 1
EPSILON = 1e-06
SCALE = HEAD_DIM ** (-0.5)
F32 = jnp.float32
BF16 = jnp.bfloat16


def dot(left, right, dims):
    return lax.dot_general(left, right, (dims, ((), ())), preferred_element_type=F32)


def nn(left, right):
    return dot(left, right, ((1,), (0,)))


def nt(left, right):
    return dot(left, right, ((1,), (1,)))


def tn(left, right):
    return dot(left, right, ((0,), (0,)))


def lane(tile):
    return pl.ds(LANES * tile, LANES)


def fill_masks(cut, col_cuts, mask_ref):
    col = lax.broadcasted_iota(jnp.int32, (SIDE, LANES), 0)
    for band in range(2):
        here = (col >= col_cuts[band]).astype(jnp.int32)
        for step in range(-3, 4):
            if step == 0:
                continue
            there = (col + step >= col_cuts[band]).astype(jnp.int32)
            good = (col + step >= 0) & (col + step < SIDE) & (here == there)
            mask_ref[band, step + 3] = jnp.where(good, 1.0, 0.0).astype(F32)


def place_ids(cut, col_cuts):
    place = lax.broadcasted_iota(jnp.int32, (PLACES, LANES), 0)
    row = lax.shift_right_logical(place, 4)
    col = lax.bitwise_and(place, 15)
    band = (row >= cut).astype(jnp.int32)
    col_cut = jnp.where(band > 0, col_cuts[1], col_cuts[0])
    side = (col >= col_cut).astype(jnp.int32)
    return band, side


def spread(read_row, reach, cut, mask_ref, grid_ref, plane):
    zero = jnp.zeros((GAP * SIDE, LANES), F32)
    for step in range(-reach, reach + 1):
        start = pl.multiple_of(SIDE * (GAP + cut), SIDE)
        grid_ref[plane + step, pl.ds(start, GAP * SIDE), :] = zero
    for row in range(SIDE):
        lower = (row >= cut).astype(jnp.int32)
        start = pl.multiple_of(SIDE * (row + GAP + GAP * lower), SIDE)
        values = read_row(row)
        for step in range(-reach, reach + 1):
            moved = values
            if step != 0:
                moved = pltpu.roll(values, (-step) % SIDE, 0) * mask_ref[lower, step + 3]
            grid_ref[plane + step, pl.ds(start, SIDE), :] = moved


def add_to(store, key, term):
    store[key] = term if key not in store else store[key] + term


def conv_tiles(items, reach, cut, grid_ref, taps_ref, tap_reach, out_ref):
    upper_pairs = (cut + 1) // 2
    pairs = upper_pairs + (SIDE - cut + 1) // 2
    width = 2 * tap_reach + 1
    chains = 3

    def body(index, carry):
        lower = (index >= upper_pairs).astype(jnp.int32)
        row = 2 * index + lower * (cut - 2 * upper_pairs)
        base = row + GAP * lower + (GAP - reach)
        for tile, plane in items:
            total = {}
            for step in range(-reach, reach + 1):
                taps = [
                    taps_ref[(dr + tap_reach) * width + step + tap_reach, :, lane(tile)]
                    for dr in range(-reach, reach + 1)
                ]
                for place in range(2 * reach + 2):
                    for half in range(2):
                        start = pl.multiple_of(SIDE * (base + place) + 8 * half, 8)
                        field = grid_ref[plane + step, pl.ds(start, 8), :]
                        for out in range(2):
                            tap = place - out
                            if 0 <= tap <= 2 * reach:
                                add_to(total, (out, half, step % chains), taps[tap] * field)
            for out in range(2):
                for half in range(2):
                    start = pl.multiple_of(SIDE * (row + out) + 8 * half, 8)
                    out_ref[pl.ds(start, 8), lane(tile)] = sum(
                        [total[out, half, chain] for chain in range(1, chains)], total[out, half, 0]
                    )
        return carry

    lax.fori_loop(0, pairs, body, 0)


def conv_back_tiles(items, reach, cut, grid_ref, taps_ref, tap_reach, other_ref, out_ref, sum_ref):
    upper_pairs = (cut + 1) // 2
    pairs = upper_pairs + (SIDE - cut + 1) // 2
    width = 2 * tap_reach + 1
    chains = 2

    def body(index, carry):
        lower = (index >= upper_pairs).astype(jnp.int32)
        row = 2 * index + lower * (cut - 2 * upper_pairs)
        base = row + GAP * lower + (GAP - reach)
        keep = jnp.where((lower == 0) & (row + 1 >= cut), 0.0, 1.0).astype(F32)
        for tile, plane in items:
            other = {}
            for out in range(2):
                for half in range(2):
                    start = pl.multiple_of(SIDE * (row + out) + 8 * half, 8)
                    value = other_ref[pl.ds(start, 8), lane(tile)]
                    other[out, half] = value * keep if out else value
            total = {}
            for step in range(-reach, reach + 1):
                sums = {}
                ids = [
                    (tap_reach - dr) * width + tap_reach - step for dr in range(-reach, reach + 1)
                ]
                taps = [taps_ref[item, :, lane(tile)] for item in ids]
                for place in range(2 * reach + 2):
                    for half in range(2):
                        start = pl.multiple_of(SIDE * (base + place) + 8 * half, 8)
                        field = grid_ref[plane + step, pl.ds(start, 8), :]
                        for out in range(2):
                            tap = place - out
                            if 0 <= tap <= 2 * reach:
                                add_to(total, (out, half, step % chains), taps[tap] * field)
                                add_to(sums, tap, other[out, half] * field)
                for tap in range(2 * reach + 1):
                    sum_ref[ids[tap], :, lane(tile)] += sums[tap]
            for out in range(2):
                for half in range(2):
                    start = pl.multiple_of(SIDE * (row + out) + 8 * half, 8)
                    out_ref[pl.ds(start, 8), lane(tile)] = sum(
                        [total[out, half, chain] for chain in range(1, chains)], total[out, half, 0]
                    )
        return carry

    lax.fori_loop(0, pairs, body, 0)


SMALL_ITEMS = tuple((tile, 3 * tile + 1) for tile in range(TILES))


def row_mean(values):
    return jnp.sum(values, axis=1, keepdims=True) * (1.0 / D)


def pick(ids, rows):
    out = rows[0]
    for crop in range(1, 4):
        out = jnp.where(ids >= crop, rows[crop], out)
    return out


def crop_reduce(ids, values, op, empty):
    return [op(jnp.where(ids == crop, values, empty), axis=0, keepdims=True) for crop in range(4)]


def head_block():
    row = lax.broadcasted_iota(jnp.int32, (2 * LANES, 2 * LANES), 0)
    col = lax.broadcasted_iota(jnp.int32, (2 * LANES, 2 * LANES), 1)
    same = lax.bitwise_and(row, HEAD_DIM) == lax.bitwise_and(col, HEAD_DIM)
    return jnp.where(same, 1.0, 0.0).astype(F32)


def both(values, masks):
    return jnp.concatenate([values * masks[0], values * masks[1]], axis=1)


def read_cuts(ids_ref, canvases):
    canvas = lax.axis_index("head") * canvases + pl.program_id(0)

    def count(places, bound):
        return sum(jnp.where(ids_ref[canvas, place] < bound, 1, 0) for place in places)

    cut = count(range(0, PLACES, SIDE), 2)
    upper = count(range(SIDE), 1)
    lower = count(range(PLACES - SIDE, PLACES), 3)
    return cut, (upper, lower)


SMALL_SIZE = 72
(CPE, CRPE, CPE_BIAS, GAIN1, SHIFT1, QUERY_BIAS, VALUE_BIAS, PROJ_BIAS, GAIN2, SHIFT2, FC2_BIAS, FC1_BIAS) = (
    0, 9, 58, 59, 60, 61, 62, 63, 64, 65, 66, 67,
)


def spread_small(small_in, small_ref):
    me = lax.axis_index("head")
    for tile in range(TILES):
        small_ref[:, lane(tile)] = small_in[lax.bitwise_xor(me, tile)]


def outer_taps(tap):
    return max(abs(tap // 7 - 3), abs(tap % 7 - 3)) > 2


def keep_head(tap, tile, values):
    if tile != 2 or not outer_taps(tap):
        return values
    col = lax.broadcasted_iota(jnp.int32, values.shape, len(values.shape) - 1)
    return jnp.where(col < HEAD_DIM, 0.0, values)


def spread_taps(small_ref, row, count, masked, taps_ref):
    for tap in range(count):
        for tile in range(TILES):
            values = jnp.broadcast_to(small_ref[row + tap : row + tap + 1, lane(tile)], (8, LANES))
            taps_ref[tap, :, lane(tile)] = keep_head(tap, tile, values) if masked else values


def whole(shape):
    return pl.BlockSpec(shape, lambda *_: (0,) * len(shape))


def once(shape):
    return pl.BlockSpec(shape, lambda *_: (0,) * len(shape), pipeline_mode=pl.Buffered(1))


def rows_spec(width, base=0):
    return pl.BlockSpec((PLACES, width), lambda i, *_: (i + base, 0))


def context_spec(base):
    return pl.BlockSpec((1, TILES, 2 * LANES, 2 * LANES), lambda i, *_: (i + base, 0, 0, 0))


def like(shape, dtype):
    return jax.ShapeDtypeStruct(shape, dtype)


def params(**given):
    return pltpu.CompilerParams(vmem_limit_bytes=58 * 2**20, **given)


MESH = pl.DeviceIdType.MESH
PIECE_ROWS = 256
SMALL_ROWS = 128


def peer(move):
    return (lax.axis_index("dp"), lax.bitwise_xor(lax.axis_index("head"), move))


def meet(peers):
    barrier = pltpu.get_barrier_semaphore()
    for item in peers:
        pl.semaphore_signal(barrier, inc=1, device_id=item, device_id_type=MESH)
    pl.semaphore_wait(barrier, len(peers))


def remote(source, target, send, receive, device):
    return pltpu.make_async_remote_copy(
        src_ref=source, dst_ref=target, send_sem=send, recv_sem=receive,
        device_id=device, device_id_type=MESH,
    )


def plan_pieces(shapes, count):
    pieces = []
    for item, (rows, lanes) in enumerate(shapes):
        height = min(PIECE_ROWS, rows)
        for start in range(0, rows, height):
            pieces.append((item, start, height, padded_rows(height, count), lanes))
    return pieces


def padded_rows(height, count):
    unit = 16 * count
    return -(-height // unit) * unit


def place_on_dp():
    dp = lax.axis_index("dp")
    return dp, lax.rem(dp, 2), dp // 2


def low_peer():
    dp, low, _ = place_on_dp()
    return (dp + 1 - 2 * low, lax.axis_index("head"))


def high_peer(step, group):
    _, low, high = place_on_dp()
    return (lax.rem(high + step, group) * 2 + low, lax.axis_index("head"))


def aligned(index, size):
    return pl.ds(pl.multiple_of(index * size, size), size)


class HighSum:
    def __init__(self, count, mid, part, whole, got, send, receive, slot):
        self.group = count // 2
        self.got = got
        self.mid, self.part, self.whole = mid, part, whole
        self.send, self.receive, self.slot = send, receive, slot
        self.half = mid.shape[0]
        self.size = self.half // self.group

    def copy(self, source, target, slot, device):
        return remote(
            source, target, self.send.at[self.slot + slot], self.receive.at[self.slot + slot], device
        )

    def high(self, step):
        _, _, high = place_on_dp()
        other = lax.rem(high + step, self.group)
        return self.copy(
            self.mid.at[aligned(other, self.size)], self.part.at[step - 1], step - 1,
            high_peer(step, self.group),
        )

    def spot(self):
        dp, low, high = place_on_dp()
        return self.whole.at[aligned(low * self.group + high, self.size)]

    def share(self, step):
        spot = self.spot()
        return self.copy(spot, spot, self.group - 2 + step, high_peer(step, self.group))

    def last(self):
        _, low, _ = place_on_dp()
        here = self.whole.at[aligned(low, self.half)]
        return self.copy(here, self.got, 2 * self.group - 2, low_peer())

    def to_high(self):
        for step in range(1, self.group):
            self.high(step).start()

    def share_high(self):
        _, _, high = place_on_dp()
        total = self.mid[aligned(high, self.size), :].astype(F32)
        for step in range(1, self.group):
            self.high(step).wait()
            total += self.part[step - 1].astype(F32)
        self.spot()[...] = total.astype(BF16)
        for step in range(1, self.group):
            self.share(step).start()

    def share_low(self):
        for step in range(1, self.group):
            self.share(step).wait()
        self.last().start()

    def finish(self):
        _, low, _ = place_on_dp()
        self.last().wait()
        self.whole[aligned(1 - low, self.half), :] = self.got[...]


def high_slots(count):
    return count - 1


class FullSum:
    def __init__(self, count, grad, span, near, far, whole, mid, low, part, got, send, receive, slot):
        self.grad, self.span, self.near, self.far = grad, span, near, far
        self.whole, self.mid, self.low = whole, mid, low
        self.height = far.shape[0]
        self.send, self.receive, self.slot = send, receive, slot
        self.rest = HighSum(count, mid, part, whole, got, send, receive, slot + 4)

    def copy(self, source, target, slot, device):
        return remote(
            source, target, self.send.at[self.slot + slot], self.receive.at[self.slot + slot], device
        )

    def near_copy(self, item):
        return self.copy(
            self.grad.at[1 + 2 * item, self.span], self.near.at[item], item, peer(1)
        )

    def far_copy(self):
        return self.copy(self.whole.at[: self.height], self.far, 2, peer(2))

    def low_copy(self):
        _, low, _ = place_on_dp()
        return self.copy(self.whole.at[aligned(1 - low, self.mid.shape[0])], self.low, 3, low_peer())

    def to_core(self):
        self.near_copy(1).start()
        self.near_copy(0).start()

    def to_far(self):
        self.near_copy(1).wait()
        self.whole[: self.height, :] = (
            self.grad[2, self.span, :].astype(F32) + self.near[1].astype(F32)
        ).astype(BF16)
        self.far_copy().start()

    def to_low(self):
        self.near_copy(0).wait()
        self.far_copy().wait()
        self.whole[: self.height, :] = (
            self.grad[0, self.span, :].astype(F32) + self.near[0].astype(F32)
            + self.far[...].astype(F32)
        ).astype(BF16)
        rows = self.whole.shape[0]
        if rows > self.height:
            self.whole[self.height :, :] = jnp.zeros((rows - self.height, self.whole.shape[1]), BF16)
        self.low_copy().start()

    def to_high(self):
        _, low, _ = place_on_dp()
        self.low_copy().wait()
        half = self.mid.shape[0]
        self.mid[...] = (
            self.whole[aligned(low, half), :].astype(F32) + self.low[...].astype(F32)
        ).astype(BF16)
        self.rest.to_high()


def sum_scratch(pieces, count):
    scratch = []
    for _, _, height, padded, lanes in pieces:
        scratch += [
            pltpu.VMEM((2, height, lanes), BF16), pltpu.VMEM((height, lanes), BF16),
            pltpu.VMEM((padded, lanes), BF16), pltpu.VMEM((padded // 2, lanes), BF16),
            pltpu.VMEM((padded // 2, lanes), BF16),
            pltpu.VMEM((count // 2 - 1, padded // count, lanes), BF16),
            pltpu.VMEM((padded // 2, lanes), BF16),
        ]
    return scratch


def entry_kernel(
    rows, x_ref, qkv_ref, small_ref,
    x0_ref, x1_ref, x2_ref, x3_ref, all_qkv_ref, all_small_ref,
    send, receive, local,
):
    head = lax.axis_index("head")
    meet([peer(move) for move in (1, 2, 3)])
    far = remote(qkv_ref, all_qkv_ref.at[2], send.at[0], receive.at[0], peer(2))
    near = remote(qkv_ref, all_qkv_ref.at[1], send.at[1], receive.at[1], peer(1))
    copies = [near]
    for move in (1, 2, 3):
        copies.append(
            remote(small_ref, all_small_ref.at[move], send.at[1 + move], receive.at[1 + move], peer(move))
        )
    for move, target in ((2, x2_ref), (3, x3_ref), (1, x1_ref)):
        source = x_ref.at[aligned(lax.bitwise_xor(head, move), rows)]
        copies.append(remote(source, target, send.at[4 + move], receive.at[4 + move], peer(move)))
    mine = [
        pltpu.make_async_copy(qkv_ref, all_qkv_ref.at[0], local.at[0]),
        pltpu.make_async_copy(small_ref, all_small_ref.at[0], local.at[1]),
        pltpu.make_async_copy(x_ref.at[aligned(head, rows)], x0_ref, local.at[2]),
    ]
    far.start()
    for copy in copies + mine:
        copy.start()
    far.wait()
    relay = remote(all_qkv_ref.at[2], all_qkv_ref.at[3], send.at[8], receive.at[8], peer(1))
    relay.start()
    for copy in copies + mine:
        copy.wait()
    relay.wait()


def entry(block_in, qkv, small):
    rows = block_in.shape[0] // 4
    hbm = pl.BlockSpec(memory_space=pl.ANY)
    return pl.pallas_call(
        lambda *refs: entry_kernel(rows, *refs),
        in_specs=[hbm] * 3,
        out_specs=[hbm] * 6,
        out_shape=[like((rows, LANES), BF16)] * 4 + [
            like((4,) + qkv.shape, BF16), like((4,) + small.shape, F32),
        ],
        scratch_shapes=[
            pltpu.SemaphoreType.DMA((9,)), pltpu.SemaphoreType.DMA((9,)),
            pltpu.SemaphoreType.DMA((3,)),
        ],
        compiler_params=params(collective_id=1, has_side_effects=True),
        name="entry",
    )(block_in, qkv, small)


def front_kernel(
    canvases, ids_ref, x0_ref, x1_ref, x2_ref, x3_ref, small_in, qkv_ref,
    first_ref, hidden_ref, query_ref, value_ref, soft_ref, context_ref, conv_ref, attended_ref,
    mask_ref, grid_ref, out_ref, x_ref, small_ref, cpe_ref, crpe_ref,
):
    cut, col_cuts = read_cuts(ids_ref, canvases)
    me = lax.axis_index("head")

    @pl.when(pl.program_id(0) == 0)
    def _():
        grid_ref[...] = jnp.zeros_like(grid_ref)
        spread_small(small_in, small_ref)
        spread_taps(small_ref, CPE, 9, False, cpe_ref)
        spread_taps(small_ref, CRPE, 49, True, crpe_ref)

    for move, piece_ref in enumerate((x0_ref, x1_ref, x2_ref, x3_ref)):
        x_ref[:, aligned(lax.bitwise_xor(me, move), LANES)] = piece_ref[...].astype(F32)
    fill_masks(cut, col_cuts, mask_ref)
    for tile, plane in SMALL_ITEMS:
        spread(
            lambda row: x_ref[SIDE * row : SIDE * row + SIDE, lane(tile)],
            1, cut, mask_ref, grid_ref, plane,
        )
    conv_tiles(SMALL_ITEMS, 1, cut, grid_ref, cpe_ref, 1, out_ref)
    first = x_ref[...] + out_ref[:PLACES, :] + small_ref[CPE_BIAS : CPE_BIAS + 1, :]
    first_ref[...] = first
    center = row_mean(first)
    square = row_mean(first * first)
    inverse = lax.rsqrt(square - center * center + EPSILON)
    hidden = (
        (first - center) * inverse * small_ref[GAIN1 : GAIN1 + 1, :] + small_ref[SHIFT1 : SHIFT1 + 1, :]
    ).astype(BF16)
    hidden_ref[...] = hidden
    band, side = place_ids(cut, col_cuts)
    ids = 2 * band + side
    sides = [(side == item).astype(F32).astype(BF16) for item in range(2)]
    bands = [(band == item).astype(F32).astype(BF16) for item in range(2)]
    blocks = head_block()
    for tile in range(TILES):
        three = nn(hidden, qkv_ref[lax.bitwise_xor(me, tile)])
        query = (three[:, :LANES] + small_ref[QUERY_BIAS : QUERY_BIAS + 1, lane(tile)]).astype(BF16)
        keys = three[:, LANES : 2 * LANES].astype(BF16).astype(F32)
        value = (
            three[:, 2 * LANES :] + small_ref[VALUE_BIAS : VALUE_BIAS + 1, lane(tile)]
        ).astype(BF16)
        query_ref[:, lane(tile)] = query
        value_ref[:, lane(tile)] = value
        highest = crop_reduce(ids, keys, jnp.max, -1e30)
        powers = jnp.exp(keys - pick(ids, highest))
        totals = crop_reduce(ids, powers, jnp.sum, 0.0)
        soft = (powers * pick(ids, [1.0 / item for item in totals])).astype(BF16)
        soft_ref[:, lane(tile)] = soft
        context = (tn(both(soft, sides), both(value, bands)) * blocks).astype(BF16)
        context_ref[0, tile] = context
        factor = nn(both(query, sides), context)
        x_ref[:, lane(tile)] = jnp.where(band > 0, factor[:, LANES:], factor[:, :LANES]) * SCALE
    for tile in range(TILES):
        spread(
            lambda row: value_ref[SIDE * row : SIDE * row + SIDE, lane(tile)].astype(F32),
            REACH[tile], cut, mask_ref, grid_ref, 3,
        )
        conv_tiles(((tile, 3),), REACH[tile], cut, grid_ref, crpe_ref, 3, out_ref)
    conv = out_ref[:PLACES, :]
    conv_ref[...] = conv.astype(BF16)
    attended_ref[...] = (x_ref[...] + query_ref[...].astype(F32) * conv).astype(BF16)


def front(ids, x_parts, small, qkv):
    rows = x_parts[0].shape[0]
    count = rows // PLACES
    wide = rows_spec(D)
    return pl.pallas_call(
        lambda *refs: front_kernel(count, *refs),
        grid_spec=pltpu.PrefetchScalarGridSpec(
            num_scalar_prefetch=1,
            grid=(count,),
            in_specs=[rows_spec(LANES)] * 4 + [once(small.shape), once(qkv.shape)],
            out_specs=[wide, wide, wide, wide, wide, context_spec(0), wide, wide],
            scratch_shapes=[
                pltpu.VMEM((2, 7, SIDE, LANES), F32),
                pltpu.VMEM((3 * TILES, GRID_ROWS * SIDE, LANES), F32),
                pltpu.VMEM((PLACES + SIDE, D), F32),
                pltpu.VMEM((PLACES, D), F32),
                pltpu.VMEM((SMALL_SIZE, D), F32),
                pltpu.VMEM((9, 8, D), F32),
                pltpu.VMEM((49, 8, D), F32),
            ],
        ),
        out_shape=[
            like((rows, D), F32), like((rows, D), BF16), like((rows, D), BF16),
            like((rows, D), BF16), like((rows, D), BF16),
            like((count, TILES, 2 * LANES, 2 * LANES), BF16),
            like((rows, D), BF16), like((rows, D), BF16),
        ],
        compiler_params=params(),
        cost_estimate=pl.CostEstimate(
            flops=rows * D * D * 60, bytes_accessed=count * 10**7, transcendentals=0
        ),
        name="front",
    )(ids, *x_parts, small, qkv)


def gelu_both(pre):
    power = jnp.exp(pre * pre * -0.5)
    t = 1.0 / (1.0 + jnp.abs(pre) * (0.3275911 * 0.7071067811865476))
    poly = 0.5 * 1.061405429
    for item in (-1.453152027, 1.421413741, -0.284496736, 0.254829592):
        poly = poly * t + 0.5 * item
    tail = poly * t * power
    cdf = jnp.where(pre >= 0.0, 1.0 - tail, tail)
    return pre * cdf, cdf + pre * power * 0.3989422804014327


BLOCK = 512


def middle_kernel(
    count,
    attended_ref, first_ref, cot0_ref, cot1_ref, cot2_ref, cot3_ref, small_in, own_weights,
    far_weights,
    out0_ref, out1_ref, out2_ref, out3_ref, second_grad_ref, att_grad_ref, fc_mid_ref,
    proj_grad_ref, sum_ref, bias_grad_ref,
    cot_ref, hat_ref, inverse_ref, hidden_ref, total_ref, back_ref, active_ref, pre_grad_ref,
    grads_ref, near_ref, far_ref, own_ref, low_ref, small_ref, weights_ref, send, receive, fetch,
):
    me = lax.axis_index("head")
    step = pl.program_id(0)
    rows = attended_ref.shape[0]
    blocks = rows // BLOCK
    _, low, _ = place_on_dp()
    half = low_ref.shape[1]

    def near(item, kind):
        return remote(
            grads_ref.at[2 * item, kind], near_ref.at[item, kind], send.at[2 * item + kind],
            receive.at[2 * item + kind], peer(1),
        )

    def far(kind):
        return remote(
            grads_ref.at[1, kind], far_ref.at[kind], send.at[4 + kind], receive.at[4 + kind], peer(2)
        )

    def to_low(kind):
        return remote(
            own_ref.at[kind, aligned(1 - low, half)], low_ref.at[kind], send.at[6 + kind],
            receive.at[6 + kind], low_peer(),
        )

    def part(index):
        return aligned(index, BLOCK)

    shard = 3 - step
    fc1 = weights_ref.at[shard, :D]
    fc2 = weights_ref.at[shard, D : 2 * D]

    def proj(tile):
        return weights_ref[lax.bitwise_xor(me, tile), 2 * D :, :]

    def relay(number, source, target, part):
        return remote(
            source.at[part], weights_ref.at[target, part], send.at[8 + number], receive.at[8 + number],
            peer(1),
        )

    narrow, broad = pl.ds(2 * D, LANES), pl.ds(0, 2 * D)
    relays = [
        relay(0, own_weights, 1, narrow), relay(1, far_weights, 3, narrow),
        relay(2, far_weights, 3, broad), relay(3, own_weights, 1, broad),
    ]

    @pl.when(step == 0)
    def _():
        loads = [
            pltpu.make_async_copy(own_weights, weights_ref.at[0], fetch.at[0]),
            pltpu.make_async_copy(far_weights, weights_ref.at[2], fetch.at[1]),
        ]
        for load in loads:
            load.start()
        meet([peer(1), peer(2), low_peer()])
        for item in relays:
            item.start()
        spread_small(small_in, small_ref)
        own_ref[...] = jnp.zeros_like(own_ref)
        sum_ref[...] = jnp.zeros_like(sum_ref)
        for move, piece_ref in enumerate((cot0_ref, cot1_ref, cot2_ref, cot3_ref)):
            cot_ref[:, aligned(lax.bitwise_xor(me, move), LANES)] = piece_ref[...]
        for item in loads + relays[:2]:
            item.wait()

        def enter(index, carry):
            now = part(index)
            second = first_ref[now, :] + small_ref[PROJ_BIAS : PROJ_BIAS + 1, :]
            for tile in range(TILES):
                second += nn(attended_ref[now, lane(tile)], proj(tile))
            center = row_mean(second)
            square = row_mean(second * second)
            inverse = lax.rsqrt(square - center * center + EPSILON)
            hat = (second - center) * inverse
            hidden_ref[now, :] = (
                hat * small_ref[GAIN2 : GAIN2 + 1, :] + small_ref[SHIFT2 : SHIFT2 + 1, :]
            ).astype(BF16)
            hat_ref[now, :] = hat
            inverse_ref[now, :] = jnp.broadcast_to(inverse, (BLOCK, LANES))
            total_ref[now, :] = second + small_ref[FC2_BIAS : FC2_BIAS + 1, :]
            back_ref[now, :] = jnp.zeros((BLOCK, D), F32)
            sum_ref[3:4, :] += jnp.sum(cot_ref[now, :].astype(F32), axis=0, keepdims=True)
            return carry

        lax.fori_loop(0, blocks, enter, 0)
        for item in relays[2:]:
            item.wait()

    bias_grad_ref[0] = jnp.zeros_like(bias_grad_ref[0])

    def chunk(index, carry):
        now = part(index)
        bias = jnp.concatenate(
            [small_in[shard, FC1_BIAS + tile : FC1_BIAS + tile + 1, :] for tile in range(TILES)], axis=1
        )
        pre = nn(hidden_ref[now, :], fc1[...]) + bias
        active, slope = gelu_both(pre)
        active = active.astype(BF16)
        active_ref[now, :] = active
        total_ref[now, :] += nn(active, fc2[...])
        pre_grad_f = nt(cot_ref[now, :], fc2[...]) * slope
        pre_grad = pre_grad_f.astype(BF16)
        pre_grad_ref[now, :] = pre_grad
        back_ref[now, :] += nt(pre_grad, fc1[...])
        bias_grad_ref[0] += jnp.sum(pre_grad_f, axis=0, keepdims=True)
        return carry

    lax.fori_loop(0, blocks, chunk, 0)
    grads_ref[step, 0] = tn(hidden_ref[...], pre_grad_ref[...]).astype(BF16)
    grads_ref[step, 1] = tn(active_ref[...], cot_ref[...]).astype(BF16)

    @pl.when(step == 0)
    def _():
        for kind in range(2):
            near(0, kind).start()

    @pl.when(step == 1)
    def _():
        for kind in range(2):
            near(0, kind).wait()
            grads_ref[1, kind] = (
                grads_ref[1, kind].astype(F32) + near_ref[0, kind].astype(F32)
            ).astype(BF16)
            far(kind).start()

    @pl.when(step == 2)
    def _():
        for kind in range(2):
            near(1, kind).start()

    @pl.when(step == 3)
    def _():
        for kind in range(2):
            near(1, kind).wait()
            far(kind).wait()
            own_ref[kind, :D, :] = (
                grads_ref[3, kind].astype(F32) + near_ref[1, kind].astype(F32)
                + far_ref[kind].astype(F32)
            ).astype(BF16)
            to_low(kind).start()

        def leave(index, carry):
            now = part(index)
            for move, piece_ref in enumerate((out0_ref, out1_ref, out2_ref, out3_ref)):
                piece_ref[now, :] = total_ref[now, aligned(lax.bitwise_xor(me, move), LANES)].astype(BF16)
            hat = hat_ref[now, :]
            norm_grad = back_ref[now, :]
            weighted = norm_grad * small_ref[GAIN2 : GAIN2 + 1, :]
            second_grad = cot_ref[now, :].astype(F32) + inverse_ref[now, 0:1] * (
                weighted - row_mean(weighted) - hat * row_mean(weighted * hat)
            )
            second_grad_ref[now, :] = second_grad
            second_low = second_grad.astype(BF16)
            hidden_ref[now, :] = second_low
            for tile in range(TILES):
                att_grad_ref[now, lane(tile)] = nt(
                    second_low, proj(tile)
                ).astype(BF16)
            sum_ref[1:2, :] += jnp.sum(norm_grad * hat, axis=0, keepdims=True)
            sum_ref[2:3, :] += jnp.sum(norm_grad, axis=0, keepdims=True)
            sum_ref[0:1, :] += jnp.sum(second_low.astype(F32), axis=0, keepdims=True)
            return carry

        lax.fori_loop(0, blocks, leave, 0)
        for tile in range(TILES):
            proj_grad_ref[lax.bitwise_xor(me, tile)] = tn(
                attended_ref[:, lane(tile)], hidden_ref[...]
            ).astype(BF16)
        for kind in range(2):
            to_low(kind).wait()
            fc_mid_ref[kind] = (
                own_ref[kind, aligned(low, half), :].astype(F32) + low_ref[kind].astype(F32)
            ).astype(BF16)


def middle(attended, first, cot_parts, small, own_weights, far_weights):
    rows = attended.shape[0]
    count = lax.axis_size("dp")
    padded = padded_rows(D, count)
    hbm = pl.BlockSpec(memory_space=pl.ANY)
    proj_shape = (4, LANES, D)
    piece = once((rows, LANES))
    wide = once((rows, D))
    line = pl.BlockSpec((1, 1, D), lambda i: (3 - i, 0, 0))
    return pl.pallas_call(
        lambda *refs: middle_kernel(count, *refs),
        grid=(4,),
        in_specs=[
            wide, wide, piece, piece, piece, piece, once(small.shape), hbm, hbm,
        ],
        out_specs=[
            piece, piece, piece, piece, wide, wide, once((2, padded // 2, D)), once(proj_shape),
            once((8, D)), line,
        ],
        out_shape=[like((rows, LANES), BF16)] * 4 + [
            like((rows, D), F32), like((rows, D), BF16), like((2, padded // 2, D), BF16),
            like(proj_shape, BF16), like((8, D), F32), like((4, 1, D), F32),
        ],
        scratch_shapes=[
            pltpu.VMEM((rows, D), BF16), pltpu.VMEM((rows, D), F32),
            pltpu.VMEM((rows, LANES), F32),
            pltpu.VMEM((rows, D), BF16), pltpu.VMEM((rows, D), F32),
            pltpu.VMEM((rows, D), F32), pltpu.VMEM((rows, D), BF16),
            pltpu.VMEM((rows, D), BF16),
            pltpu.VMEM((4, 2, D, D), BF16), pltpu.VMEM((2, 2, D, D), BF16),
            pltpu.VMEM((2, D, D), BF16), pltpu.VMEM((2, padded, D), BF16),
            pltpu.VMEM((2, padded // 2, D), BF16),
            pltpu.VMEM((SMALL_SIZE, D), F32), pltpu.VMEM((4,) + own_weights.shape, BF16),
            pltpu.SemaphoreType.DMA((12,)), pltpu.SemaphoreType.DMA((12,)),
            pltpu.SemaphoreType.DMA((2,)),
        ],
        compiler_params=params(collective_id=2, has_side_effects=True),
        cost_estimate=pl.CostEstimate(flops=rows * D * D * 60, bytes_accessed=3 * 10**7, transcendentals=0),
        name="middle",
    )(attended, first, *cot_parts, small, own_weights, far_weights)


def back_kernel(
    canvases, ids_ref, grad_ref, query_ref, value_ref, soft_ref, context_ref, conv_ref, hidden_ref,
    small_in, middle_sum_ref, bias_grad_ref,
    three_ref, qkv_out_ref, small_out_ref,
    mask_ref, grid_ref, out_ref, other_ref, value_part_ref, qkv_grad_ref, small_ref, crpe_ref,
    crpe_sum_ref, sum_ref, late_ref,
):
    cut, col_cuts = read_cuts(ids_ref, canvases)
    me = lax.axis_index("head")

    @pl.when(pl.program_id(0) == 0)
    def _():
        grid_ref[...] = jnp.zeros_like(grid_ref)
        other_ref[...] = jnp.zeros_like(other_ref)
        qkv_grad_ref[...] = jnp.zeros_like(qkv_grad_ref)
        crpe_sum_ref[...] = jnp.zeros_like(crpe_sum_ref)
        sum_ref[...] = jnp.zeros_like(sum_ref)
        spread_small(small_in, small_ref)
        spread_taps(small_ref, CRPE, 49, True, crpe_ref)

    fill_masks(cut, col_cuts, mask_ref)
    band, side = place_ids(cut, col_cuts)
    ids = 2 * band + side
    sides = [(side == item).astype(F32).astype(BF16) for item in range(2)]
    bands = [(band == item).astype(F32).astype(BF16) for item in range(2)]
    blocks = head_block() * SCALE
    for tile in range(TILES):
        grad = grad_ref[:, lane(tile)]
        query = query_ref[:, lane(tile)]
        value = value_ref[:, lane(tile)]
        soft = soft_ref[:, lane(tile)]
        context = context_ref[0, tile]
        grad_f = grad.astype(F32)
        grad_bands = both(grad, bands)
        context_grad = (tn(both(query, sides), grad_bands) * blocks).astype(BF16)
        part = nt(grad_bands, context)
        part = jnp.where(side > 0, part[:, LANES:], part[:, :LANES])
        query_grad = (
            part * SCALE + grad_f * conv_ref[:, lane(tile)].astype(F32)
        ).astype(BF16)
        soft_grad = nt(both(value, bands), context_grad)
        soft_grad = jnp.where(side > 0, soft_grad[:, LANES:], soft_grad[:, :LANES])
        soft_f = soft.astype(F32)
        inner = crop_reduce(ids, soft_f * soft_grad, jnp.sum, 0.0)
        keys_grad = (soft_f * (soft_grad - pick(ids, inner))).astype(BF16)
        value_part = nn(both(soft, sides), context_grad)
        value_part_ref[:, lane(tile)] = jnp.where(
            band > 0, value_part[:, LANES:], value_part[:, :LANES]
        )
        three_ref[tile, :, :LANES] = query_grad
        three_ref[tile, :, LANES : 2 * LANES] = keys_grad
        sum_ref[0:1, lane(tile)] += jnp.sum(query_grad.astype(F32), axis=0, keepdims=True)
    other_ref[:PLACES, :] = value_ref[...].astype(F32)
    for tile in range(TILES):

        def read_row(row):
            part = pl.ds(SIDE * row, SIDE)
            return grad_ref[part, lane(tile)].astype(F32) * query_ref[part, lane(tile)].astype(F32)

        spread(read_row, REACH[tile], cut, mask_ref, grid_ref, 3)
        conv_back_tiles(
            ((tile, 3),), REACH[tile], cut, grid_ref, crpe_ref, 3, other_ref, out_ref, crpe_sum_ref
        )
    hidden = hidden_ref[...]
    for tile in range(TILES):
        value_grad = (value_part_ref[:, lane(tile)] + out_ref[:PLACES, lane(tile)]).astype(BF16)
        three_ref[tile, :, 2 * LANES :] = value_grad
        sum_ref[1:2, lane(tile)] += jnp.sum(value_grad.astype(F32), axis=0, keepdims=True)
        qkv_grad_ref[lax.bitwise_xor(me, tile)] += tn(hidden, three_ref[tile])

    @pl.when(pl.program_id(0) == pl.num_programs(0) - 1)
    def _():
        qkv_out_ref[...] = qkv_grad_ref[...].astype(BF16)
        late_ref[...] = jnp.zeros_like(late_ref)
        for tap in range(49):
            for tile in range(TILES):
                late_ref[tap : tap + 1, lane(tile)] = keep_head(
                    tap, tile, jnp.sum(crpe_sum_ref[tap, :, lane(tile)], axis=0, keepdims=True)
                )
        late_ref[49:51, :] = sum_ref[0:2, :]
        late_ref[51:55, :] = middle_sum_ref[0:4, :]
        for move in range(4):
            late = late_ref[:, aligned(lax.bitwise_xor(me, move), LANES)]
            small_out_ref[move] = late.astype(BF16)
            small_out_ref[move, 64:80, :] = jnp.concatenate(
                [bias_grad_ref[move, :, lane(tile)] for tile in range(TILES)]
                + [jnp.zeros((12, LANES), F32)],
                axis=0,
            ).astype(BF16)


def back(ids, grad, query, value, soft, context, conv, hidden, small, middle_sum, bias_grad):
    rows = grad.shape[0]
    count = rows // PLACES
    wide = rows_spec(D)
    shards = (4, D, 3 * LANES)
    late = (4, SMALL_ROWS, LANES)
    return pl.pallas_call(
        lambda *refs: back_kernel(count, *refs),
        grid_spec=pltpu.PrefetchScalarGridSpec(
            num_scalar_prefetch=1,
            grid=(count,),
            in_specs=[
                wide, wide, wide, wide, context_spec(0), wide, wide, once(small.shape),
                once(middle_sum.shape), once(bias_grad.shape),
            ],
            out_specs=[
                pl.BlockSpec((TILES, PLACES, 3 * LANES), lambda i, *_: (0, i, 0)),
                once(shards), once(late),
            ],
            scratch_shapes=[
                pltpu.VMEM((2, 7, SIDE, LANES), F32),
                pltpu.VMEM((7, GRID_ROWS * SIDE, LANES), F32),
                pltpu.VMEM((PLACES + SIDE, D), F32),
                pltpu.VMEM((PLACES + SIDE, D), F32),
                pltpu.VMEM((PLACES, D), F32),
                pltpu.VMEM(shards, F32),
                pltpu.VMEM((SMALL_SIZE, D), F32),
                pltpu.VMEM((49, 8, D), F32),
                pltpu.VMEM((49, 8, D), F32),
                pltpu.VMEM((8, D), F32),
                pltpu.VMEM((SMALL_ROWS, D), F32),
            ],
        ),
        out_shape=[
            like((TILES, rows, 3 * LANES), BF16), like(shards, BF16), like(late, BF16),
        ],
        compiler_params=params(),
        cost_estimate=pl.CostEstimate(
            flops=rows * D * D * 64, bytes_accessed=count * 10**7, transcendentals=0
        ),
        name="back",
    )(ids, grad, query, value, soft, context, conv, hidden, small, middle_sum, bias_grad)


def step_masks(cut, col_cuts):
    place = lax.broadcasted_iota(jnp.int32, (PLACES, LANES), 0)
    row = lax.shift_right_logical(place, 4)
    col = lax.bitwise_and(place, 15)
    col_cut = jnp.where(row >= cut, col_cuts[1], col_cuts[0])
    rows = {
        1: (row < SIDE - 1) & (row + 1 != cut),
        -1: (row > 0) & (row != cut),
    }
    cols = {
        1: (col < SIDE - 1) & (col + 1 != col_cut),
        -1: (col > 0) & (col != col_cut),
    }
    return [
        {key: jnp.where(mask, 1.0, 0.0).astype(F32) for key, mask in masks.items()}
        for masks in (rows, cols)
    ]


def shift_rows(values, step):
    if step == 0:
        return values
    zero = jnp.zeros((SIDE, values.shape[1]), values.dtype)
    if step > 0:
        return jnp.concatenate([values[SIDE:], zero], axis=0)
    return jnp.concatenate([zero, values[:-SIDE]], axis=0)


def shift_cols(values, masks, step):
    if step == 0:
        return values
    return pltpu.roll(values, (-step) % PLACES, 0) * masks[step]


LAST_ROWS = 16
STAGES = {"core": 0, "far": 1, "low": 3, "high": 4, "share": 5, "last": 6}
FC_STAGES = {"high": 0, "share": 2, "last": 4}


def tail_kernel(
    count, pieces,
    canvases, ids_ref, x0_ref, x1_ref, x2_ref, x3_ref, three_ref, first_ref, second_grad_ref, small_params,
    qkv_ref, fc_mid_in, qkv_grad_in, proj_grad_in, small_in,
    out0_ref, out1_ref, out2_ref, out3_ref, fc1_own_ref, fc2_own_ref, qkv_own_ref, proj_own_ref,
    small_own_ref, last_own_ref,
    x_ref, gone_ref, cpe_sum_ref, sum_ref, fc_part_ref, fc_whole_ref, fc_got_ref, mine_ref, first_got_ref,
    total_ref, second_got_ref, piece_send, piece_receive, send, receive, last_send, last_receive,
    cpe_ref, fc_mid_ref, qkv_grad_ref, proj_grad_ref, small_ref, *buffers,
):
    me = lax.axis_index("head")
    dp = lax.axis_index("dp")
    step = pl.program_id(0)
    steps = pl.num_programs(0)
    slots = high_slots(count)
    fc_sums = [
        HighSum(
            count, fc_mid_ref.at[kind], fc_part_ref.at[kind], fc_whole_ref.at[kind],
            fc_got_ref.at[kind], send, receive, kind * slots,
        )
        for kind in range(2)
    ]
    sources = (qkv_grad_ref, proj_grad_ref, small_ref)
    targets = (qkv_own_ref, proj_own_ref, small_own_ref)
    sums = []
    for number, (item, start, height, padded, lanes) in enumerate(pieces):
        near, far, own, mid, low, part, got = buffers[7 * number : 7 * number + 7]
        sums.append(
            FullSum(
                count, sources[item], pl.ds(start, height), near, far, own, mid, low, part, got, send,
                receive, 2 * slots + number * (slots + 4),
            )
        )

    def piece_copy(index, move):
        target = (out1_ref, out2_ref, out3_ref)[move - 1]
        return remote(
            gone_ref.at[index, move - 1], target.at[aligned(index, PLACES)],
            piece_send.at[index, move - 1], piece_receive.at[index, move - 1], peer(move),
        )

    def first_copy(move):
        return remote(
            mine_ref.at[move], first_got_ref.at[move - 1], last_send.at[move - 1],
            last_receive.at[move - 1], peer(move),
        )

    def second_copy(hop):
        return remote(
            total_ref, second_got_ref.at[hop - 1], last_send.at[2 + hop], last_receive.at[2 + hop],
            (lax.rem(dp + hop, count), me),
        )

    @pl.when(step == 0)
    def _():
        meet(
            [peer(1), peer(2), peer(3)] + [(lax.rem(dp + hop, count), me) for hop in range(1, count)]
        )
        spread_small(small_params, cpe_ref)
        fc_mid_ref[...] = fc_mid_in[...]
        qkv_grad_ref[...] = qkv_grad_in[...]
        proj_grad_ref[...] = proj_grad_in[...]
        small_ref[...] = small_in[...]
        cpe_sum_ref[...] = jnp.zeros_like(cpe_sum_ref)
        sum_ref[...] = jnp.zeros_like(sum_ref)

    def at(when, action, items):
        @pl.when(step == when)
        def _():
            for item in items:
                action(item)

    at(STAGES["core"], lambda item: item.to_core(), sums)
    at(FC_STAGES["high"], lambda item: item.to_high(), fc_sums)
    at(STAGES["far"], lambda item: item.to_far(), sums)
    at(FC_STAGES["share"], lambda item: item.share_high(), fc_sums)
    at(STAGES["low"], lambda item: item.to_low(), sums)
    at(STAGES["high"], lambda item: item.to_high(), sums)
    at(FC_STAGES["last"], lambda item: item.share_low(), fc_sums)
    at(STAGES["share"], lambda item: item.rest.share_high(), sums)
    at(STAGES["last"], lambda item: item.rest.share_low(), sums)

    norm_grad = nt(three_ref[0], qkv_ref[lax.bitwise_xor(me, 0)])
    for tile in range(1, TILES):
        norm_grad += nt(three_ref[tile], qkv_ref[lax.bitwise_xor(me, tile)])
    first = first_ref[...]
    center = row_mean(first)
    square = row_mean(first * first)
    inverse = lax.rsqrt(square - center * center + EPSILON)
    hat = (first - center) * inverse
    weighted = norm_grad * cpe_ref[GAIN1 : GAIN1 + 1, :]
    first_grad = second_grad_ref[...] + inverse * (
        weighted - row_mean(weighted) - hat * row_mean(weighted * hat)
    )
    sum_ref[0:1, :] += jnp.sum(first_grad, axis=0, keepdims=True)
    sum_ref[1:2, :] += jnp.sum(norm_grad * hat, axis=0, keepdims=True)
    sum_ref[2:3, :] += jnp.sum(norm_grad, axis=0, keepdims=True)
    for move, piece_ref in enumerate((x0_ref, x1_ref, x2_ref, x3_ref)):
        x_ref[:, aligned(lax.bitwise_xor(me, move), LANES)] = piece_ref[...].astype(F32)
    rows, cols = step_masks(*read_cuts(ids_ref, canvases))
    results = []
    for tile in range(TILES):
        field = first_grad[:, LANES * tile : LANES * (tile + 1)]
        other = x_ref[:, lane(tile)]
        others = {0: other, 1: shift_rows(other * rows[1], -1), -1: shift_rows(other * rows[-1], 1)}
        moved = [shift_cols(field, cols, col) for col in (-1, 0, 1)]
        result = field
        for row in (-1, 0, 1):
            line = None
            for col in (-1, 0, 1):
                tap = (1 - row) * 3 + 1 - col
                wide_tap = jnp.broadcast_to(cpe_ref[tap : tap + 1, lane(tile)], (PLACES, LANES))
                term = wide_tap * moved[col + 1]
                line = term if line is None else line + term
                product = others[row] * moved[col + 1]
                cpe_sum_ref[tap, :, lane(tile)] += jnp.sum(product.reshape(PLACES // 8, 8, LANES), axis=0)
            line = shift_rows(line, row)
            result = result + (line * rows[row] if row else line)
        results.append(result)
    result = jnp.concatenate(results, axis=1)
    x_ref[...] = result
    out0_ref[...] = x_ref[:, aligned(me, LANES)].astype(BF16)
    for move in (1, 2, 3):
        gone_ref[step, move - 1] = x_ref[:, aligned(lax.bitwise_xor(me, move), LANES)].astype(BF16)
    for move in (2, 3, 1):
        piece_copy(step, move).start()

    @pl.when(step == steps - 1)
    def _():
        sum_ref[3:12, :] = jnp.sum(cpe_sum_ref[...], axis=1)
        for move in range(4):
            mine_ref[move] = sum_ref[:, aligned(lax.bitwise_xor(me, move), LANES)]
        for move in (1, 2, 3):
            first_copy(move).start()
        for item in fc_sums:
            item.finish()
        fc1_own_ref[...] = fc_whole_ref[0, :D, :]
        fc2_own_ref[...] = fc_whole_ref[1, :D, :]
        total = mine_ref[0]
        for move in (1, 2, 3):
            first_copy(move).wait()
            total += first_got_ref[move - 1]
        total_ref[...] = total
        for hop in range(1, count):
            second_copy(hop).start()
        for piece, item in zip(pieces, sums):
            item.rest.finish()
            targets[piece[0]][piece[1] : piece[1] + piece[2], :] = item.whole[: piece[2], :]
        for hop in range(1, count):
            second_copy(hop).wait()
            total += second_got_ref[hop - 1]
        last_own_ref[...] = total

        def settle(index, carry):
            for move in (1, 2, 3):
                piece_copy(index, move).wait()
            return carry

        lax.fori_loop(0, steps, settle, 0)


def tail(ids, x_parts, three, first, second_grad, params_small, qkv, fc_mid, qkv_grad, proj_grad, small):
    rows = first.shape[0]
    canvases = rows // PLACES
    count = lax.axis_size("dp")
    segments = [qkv_grad, proj_grad, small]
    pieces = plan_pieces([item.shape[1:] for item in segments], count)
    slots = high_slots(count)
    wide = rows_spec(D)
    piece = rows_spec(LANES)
    hbm = pl.BlockSpec(memory_space=pl.ANY)
    half = fc_mid.shape[1]
    group = count // 2
    total_slots = 2 * slots + len(pieces) * (slots + 4)
    last = (LAST_ROWS, LANES)
    return pl.pallas_call(
        lambda *refs: tail_kernel(count, pieces, canvases, *refs),
        grid=(canvases,),
        in_specs=[pl.BlockSpec(memory_space=pltpu.SMEM)] + [piece] * 4 + [
            pl.BlockSpec((TILES, PLACES, 3 * LANES), lambda i: (0, i, 0)), wide, wide,
            once(params_small.shape), once(qkv.shape), once(fc_mid.shape),
        ] + [once(item.shape) for item in segments],
        out_specs=[piece, hbm, hbm, hbm, once((D, D)), once((D, D))]
        + [once(item.shape[1:]) for item in segments] + [once(last)],
        out_shape=[like((rows, LANES), BF16)] * 4 + [like((D, D), BF16)] * 2
        + [like(item.shape[1:], BF16) for item in segments] + [like(last, F32)],
        scratch_shapes=[
            pltpu.VMEM((PLACES, D), F32), pltpu.VMEM((canvases, 3, PLACES, LANES), BF16),
            pltpu.VMEM((9, 8, D), F32), pltpu.VMEM((LAST_ROWS, D), F32),
            pltpu.VMEM((2, group - 1, half // group, D), BF16), pltpu.VMEM((2, 2 * half, D), BF16),
            pltpu.VMEM((2, half, D), BF16),
            pltpu.VMEM((4,) + last, F32), pltpu.VMEM((3,) + last, F32), pltpu.VMEM(last, F32),
            pltpu.VMEM((count - 1,) + last, F32),
            pltpu.SemaphoreType.DMA((canvases, 3)), pltpu.SemaphoreType.DMA((canvases, 3)),
            pltpu.SemaphoreType.DMA((total_slots,)), pltpu.SemaphoreType.DMA((total_slots,)),
            pltpu.SemaphoreType.DMA((2 + count,)), pltpu.SemaphoreType.DMA((2 + count,)),
        ] + [pltpu.VMEM((SMALL_SIZE, D), F32)]
        + [pltpu.VMEM(item.shape, BF16) for item in [fc_mid] + segments]
        + sum_scratch(pieces, count),
        compiler_params=params(collective_id=3, has_side_effects=True),
        cost_estimate=pl.CostEstimate(
            flops=rows * D * D * 12, bytes_accessed=canvases * 3 * 10**6, transcendentals=0
        ),
        name="tail",
    )(ids, *x_parts, three, first, second_grad, params_small, qkv, fc_mid, *segments)


def collect_kernel(me_ref, *refs):
    out_ref = refs[-1]
    for item, piece_ref in enumerate(refs[:-1]):

        @pl.when(pl.program_id(0) == item)
        def _():
            out_ref[...] = piece_ref[...].astype(F32)


def collect(me, pieces):
    rows = pieces[0].shape[0]
    return pl.pallas_call(
        collect_kernel,
        grid_spec=pltpu.PrefetchScalarGridSpec(
            num_scalar_prefetch=1,
            grid=(4,),
            in_specs=[once((rows, LANES))] * 4,
            out_specs=pl.BlockSpec((rows, LANES), lambda i, me: (lax.bitwise_xor(me[0], i), 0)),
        ),
        out_shape=like((4 * rows, LANES), F32),
        compiler_params=params(),
        name="collect",
    )(me, *pieces)


def finish_kernel(
    me_ref, p0_ref, p1_ref, p2_ref, p3_ref, fc1_ref, fc2_ref, qkv_ref, proj_ref, small_ref, last_ref,
    grad_ref, cpe_ref, vectors_ref, qkv_out_ref, qv_ref, crpe_ref, proj_out_ref, fc1_out_ref,
    bias_ref, fc2_out_ref,
):
    for item, piece_ref in enumerate((p0_ref, p1_ref, p2_ref, p3_ref)):

        @pl.when(pl.program_id(0) == item)
        def _():
            grad_ref[...] = piece_ref[...].astype(F32)

    @pl.when(pl.program_id(0) == 0)
    def _():
        cpe_ref[...] = last_ref[3:12, :]
        small = small_ref[...].astype(F32)
        vectors_ref[...] = jnp.concatenate(
            [last_ref[0:3, :], small[51:55, :], jnp.zeros((1, LANES), F32)], axis=0
        )
        qkv_out_ref[...] = qkv_ref[...].astype(F32)
        qv_ref[...] = small[49:51, :]
        crpe_ref[...] = small[:49, :]
        proj_out_ref[...] = proj_ref[...].astype(F32)
        fc1_out_ref[...] = fc1_ref[...].astype(F32)
        bias_ref[...] = small[64:68, :]
        fc2_out_ref[...] = fc2_ref[...].astype(F32)


def finish(me, pieces, fc1, fc2, qkv, proj, small, last):
    rows = pieces[0].shape[0]
    shapes = [
        (9, LANES), (8, LANES), qkv.shape, (2, LANES), (49, LANES), proj.shape, fc1.shape,
        (4, LANES), fc2.shape,
    ]
    return pl.pallas_call(
        finish_kernel,
        grid_spec=pltpu.PrefetchScalarGridSpec(
            num_scalar_prefetch=1,
            grid=(4,),
            in_specs=[once((rows, LANES))] * 4
            + [once(item.shape) for item in (fc1, fc2, qkv, proj, small, last)],
            out_specs=[
                pl.BlockSpec((rows, LANES), lambda i, me: (lax.bitwise_xor(me[0], i), 0)),
            ] + [once(shape) for shape in shapes],
        ),
        out_shape=[like((4 * rows, LANES), F32)] + [like(shape, F32) for shape in shapes],
        compiler_params=params(),
        name="finish",
    )(me, *pieces, fc1, fc2, qkv, proj, small, last)


def body(
    block_in, crop_ids, cotangent, cpe_kernel, cpe_bias, norm1_gain, norm1_shift, qkv_weight,
    qv_bias, crpe_kernel, proj_weight, proj_bias, norm2_gain, norm2_shift, fc1_weight, fc1_bias,
    fc2_weight, fc2_bias,
):
    head = lax.axis_index("head")
    me = head.reshape(1).astype(jnp.int32)
    rows = block_in.shape[0] // 4
    ids = crop_ids.reshape(crop_ids.shape[0], PLACES)

    def swap(values, move):
        return lax.ppermute(values, "head", [(item, item ^ move) for item in range(4)])

    packed = jnp.concatenate([
        cpe_kernel, crpe_kernel, cpe_bias[None], norm1_gain[None], norm1_shift[None], qv_bias,
        proj_bias[None], norm2_gain[None], norm2_shift[None], fc2_bias[None],
        fc1_bias.reshape(4, LANES), jnp.zeros((1, LANES), BF16),
    ]).astype(F32)
    own_weights = jnp.concatenate([fc1_weight, fc2_weight, proj_weight])
    *x_parts, qkv, small = entry(block_in, qkv_weight.reshape(D, 3 * LANES), packed)
    own_weights, cotangent, x_parts = lax.optimization_barrier((own_weights, cotangent, x_parts))
    far_weights = swap(own_weights, 2)
    cot_pieces = [
        lax.dynamic_slice_in_dim(cotangent, lax.bitwise_xor(head, move) * rows, rows, 0)
        for move in range(4)
    ]
    cot_parts = [cot_pieces[0]] + [swap(cot_pieces[move], move) for move in (1, 2, 3)]

    first, hidden, query, value, soft, context, conv, attended = front(ids, x_parts, small, qkv)
    results = middle(attended, first, cot_parts, small, own_weights, far_weights)
    second_grad, att_grad, fc_mid, proj_grad, middle_sum, bias_grad = results[4:]
    out_parts = [results[0]] + [swap(results[move], move) for move in (1, 2, 3)]
    three, qkv_grad, small_grad = back(
        ids, att_grad, query, value, soft, context, conv, hidden, small, middle_sum, bias_grad
    )
    three, out_parts = lax.optimization_barrier((three, out_parts))
    results = tail(
        ids, x_parts, three, first, second_grad, small, qkv, fc_mid, qkv_grad, proj_grad, small_grad
    )
    (input_grad, cpe_g, vectors, qkv_g, qv_g, crpe_g, proj_g, fc1_g, bias_g, fc2_g) = finish(
        me, results[:4], *results[4:]
    )
    return (
        collect(me, out_parts), input_grad, cpe_g, vectors[0], vectors[1], vectors[2],
        qkv_g.reshape(D, 3, LANES), qv_g, crpe_g, proj_g, vectors[3], vectors[4], vectors[5],
        fc1_g, bias_g.reshape(D), fc2_g, vectors[6],
    )


def solution(mesh):
    return jax.shard_map(
        body,
        mesh=mesh,
        in_specs=(
            P("dp", "head"), P("dp", None, None), P("dp", "head"), P(None, "head"), P("head"),
            P("head"), P("head"), P(None, None, "head"), P(None, "head"), P(None, "head"),
            P("head", None), P("head"), P("head"), P("head"), P(None, "head"), P("head"),
            P("head", None), P("head"),
        ),
        out_specs=(
            P("dp", "head"), P("dp", "head"), P(None, "head"), P("head"), P("head"), P("head"),
            P(None, None, "head"), P(None, "head"), P(None, "head"), P("head", None), P("head"),
            P("head"), P("head"), P(None, "head"), P("head"), P("head", None), P("head"),
        ),
        check_vma=False,
    )
```

```python
import jax
import jax.numpy as jnp
from jax import lax
from jax.experimental import pallas as pl
from jax.experimental.pallas import tpu as pltpu
from jax.sharding import PartitionSpec as P

D = 512
HEADS = 8
HEAD_DIM = 64
HIDDEN = 2048
SIDE = 16
PLACES = 256
LANES = 128
TILES = 4
REACH = (1, 2, 3, 3)
GAP = 3
GRID_ROWS = SIDE + 3 * GAP + 1
EPSILON = 1e-06
SCALE = HEAD_DIM ** (-0.5)
F32 = jnp.float32
BF16 = jnp.bfloat16


def dot(left, right, dims):
    return lax.dot_general(left, right, (dims, ((), ())), preferred_element_type=F32)


def nn(left, right):
    return dot(left, right, ((1,), (0,)))


def nt(left, right):
    return dot(left, right, ((1,), (1,)))


def tn(left, right):
    return dot(left, right, ((0,), (0,)))


def lane(tile):
    return pl.ds(LANES * tile, LANES)


def fill_masks(cut, col_cuts, mask_ref):
    col = lax.broadcasted_iota(jnp.int32, (SIDE, LANES), 0)
    for band in range(2):
        here = (col >= col_cuts[band]).astype(jnp.int32)
        for step in range(-3, 4):
            if step == 0:
                continue
            there = (col + step >= col_cuts[band]).astype(jnp.int32)
            good = (col + step >= 0) & (col + step < SIDE) & (here == there)
            mask_ref[band, step + 3] = jnp.where(good, 1.0, 0.0).astype(F32)


def place_ids(cut, col_cuts):
    place = lax.broadcasted_iota(jnp.int32, (PLACES, LANES), 0)
    row = lax.shift_right_logical(place, 4)
    col = lax.bitwise_and(place, 15)
    band = (row >= cut).astype(jnp.int32)
    col_cut = jnp.where(band > 0, col_cuts[1], col_cuts[0])
    side = (col >= col_cut).astype(jnp.int32)
    return band, side


def spread(read_row, reach, cut, mask_ref, grid_ref, plane):
    zero = jnp.zeros((GAP * SIDE, LANES), F32)
    for step in range(-reach, reach + 1):
        start = pl.multiple_of(SIDE * (GAP + cut), SIDE)
        grid_ref[plane + step, pl.ds(start, GAP * SIDE), :] = zero
    for row in range(SIDE):
        lower = (row >= cut).astype(jnp.int32)
        start = pl.multiple_of(SIDE * (row + GAP + GAP * lower), SIDE)
        values = read_row(row)
        for step in range(-reach, reach + 1):
            moved = values
            if step != 0:
                moved = pltpu.roll(values, (-step) % SIDE, 0) * mask_ref[lower, step + 3]
            grid_ref[plane + step, pl.ds(start, SIDE), :] = moved


def add_to(store, key, term):
    store[key] = term if key not in store else store[key] + term


def over_bands(reach, cut, body):
    every = range(2 * reach + 2)
    for lower in range(2):
        first = cut if lower else 0
        height = SIDE - cut if lower else cut
        pairs = (height + 1) // 2
        shift = GAP * lower + GAP - reach

        def pair(index, places):
            row = first + 2 * index
            body(row, row + shift, first + height - 1, places)

        def inner(index, carry):
            pair(index, every)
            return carry

        pair(0, every[reach:])
        lax.fori_loop(1, pairs - 1, inner, 0)
        pair(pairs - 1, every[: reach + 2])


def conv_tiles(items, reach, cut, grid_ref, taps_ref, tap_reach, out_ref):
    width = 2 * tap_reach + 1
    chains = 3

    def body(row, base, last, places):
        for tile, plane in items:
            total = {}
            for step in range(-reach, reach + 1):
                taps = [
                    taps_ref[(dr + tap_reach) * width + step + tap_reach, :, lane(tile)]
                    for dr in range(-reach, reach + 1)
                ]
                for place in places:
                    for half in range(2):
                        start = pl.multiple_of(SIDE * (base + place) + 8 * half, 8)
                        field = grid_ref[plane + step, pl.ds(start, 8), :]
                        for out in range(2):
                            tap = place - out
                            if 0 <= tap <= 2 * reach:
                                add_to(total, (out, half, step % chains), taps[tap] * field)
            for out in range(2):
                for half in range(2):
                    start = pl.multiple_of(SIDE * (row + out) + 8 * half, 8)
                    out_ref[pl.ds(start, 8), lane(tile)] = sum(
                        [total[out, half, chain] for chain in range(1, chains)], total[out, half, 0]
                    )

    over_bands(reach, cut, body)


def conv_back_tiles(items, reach, cut, grid_ref, taps_ref, tap_reach, other_ref, out_ref, sum_ref):
    width = 2 * tap_reach + 1
    chains = 2

    def body(row, base, last, places):
        keep = jnp.where(row + 1 > last, 0.0, 1.0).astype(F32)
        for tile, plane in items:
            other = {}
            for out in range(2):
                for half in range(2):
                    start = pl.multiple_of(SIDE * (row + out) + 8 * half, 8)
                    value = other_ref[pl.ds(start, 8), lane(tile)]
                    other[out, half] = value * keep if out else value
            total = {}
            for step in range(-reach, reach + 1):
                sums = {}
                ids = [
                    (tap_reach - dr) * width + tap_reach - step for dr in range(-reach, reach + 1)
                ]
                taps = [taps_ref[item, :, lane(tile)] for item in ids]
                for place in places:
                    for half in range(2):
                        start = pl.multiple_of(SIDE * (base + place) + 8 * half, 8)
                        field = grid_ref[plane + step, pl.ds(start, 8), :]
                        for out in range(2):
                            tap = place - out
                            if 0 <= tap <= 2 * reach:
                                add_to(total, (out, half, step % chains), taps[tap] * field)
                                add_to(sums, tap, other[out, half] * field)
                for tap, part in sums.items():
                    sum_ref[ids[tap], :, lane(tile)] += part
            for out in range(2):
                for half in range(2):
                    start = pl.multiple_of(SIDE * (row + out) + 8 * half, 8)
                    out_ref[pl.ds(start, 8), lane(tile)] = sum(
                        [total[out, half, chain] for chain in range(1, chains)], total[out, half, 0]
                    )

    over_bands(reach, cut, body)


def row_mean(values):
    return jnp.sum(values, axis=1, keepdims=True) * (1.0 / D)


def pick(ids, rows):
    out = rows[0]
    for crop in range(1, 4):
        out = jnp.where(ids >= crop, rows[crop], out)
    return out


def crop_reduce(ids, values, op, empty):
    return [op(jnp.where(ids == crop, values, empty), axis=0, keepdims=True) for crop in range(4)]


def head_block():
    row = lax.broadcasted_iota(jnp.int32, (2 * LANES, 2 * LANES), 0)
    col = lax.broadcasted_iota(jnp.int32, (2 * LANES, 2 * LANES), 1)
    same = lax.bitwise_and(row, HEAD_DIM) == lax.bitwise_and(col, HEAD_DIM)
    return jnp.where(same, 1.0, 0.0).astype(F32)


def both(values, masks):
    return jnp.concatenate([values * masks[0], values * masks[1]], axis=1)


def read_cuts(ids_ref, canvases):
    canvas = lax.axis_index("head") * canvases + pl.program_id(0)

    def count(places, bound):
        return sum(jnp.where(ids_ref[canvas, place] < bound, 1, 0) for place in places)

    cut = count(range(0, PLACES, SIDE), 2)
    upper = count(range(SIDE), 1)
    lower = count(range(PLACES - SIDE, PLACES), 3)
    return cut, (upper, lower)


SMALL_SIZE = 72
(CPE, CRPE, CPE_BIAS, GAIN1, SHIFT1, QUERY_BIAS, VALUE_BIAS, PROJ_BIAS, GAIN2, SHIFT2, FC2_BIAS, FC1_BIAS) = (
    0, 9, 58, 59, 60, 61, 62, 63, 64, 65, 66, 67,
)


def spread_small(small_in, small_ref):
    me = lax.axis_index("head")
    for tile in range(TILES):
        small_ref[:, lane(tile)] = small_in[lax.bitwise_xor(me, tile)]


def outer_taps(tap):
    return max(abs(tap // 7 - 3), abs(tap % 7 - 3)) > 2


def keep_head(tap, tile, values):
    if tile != 2 or not outer_taps(tap):
        return values
    col = lax.broadcasted_iota(jnp.int32, values.shape, len(values.shape) - 1)
    return jnp.where(col < HEAD_DIM, 0.0, values)


def spread_taps(small_ref, row, count, masked, taps_ref):
    for tap in range(count):
        for tile in range(TILES):
            values = jnp.broadcast_to(small_ref[row + tap : row + tap + 1, lane(tile)], (8, LANES))
            taps_ref[tap, :, lane(tile)] = keep_head(tap, tile, values) if masked else values


def whole(shape):
    return pl.BlockSpec(shape, lambda *_: (0,) * len(shape))


def once(shape):
    return pl.BlockSpec(shape, lambda *_: (0,) * len(shape), pipeline_mode=pl.Buffered(1))


def rows_spec(width, base=0):
    return pl.BlockSpec((PLACES, width), lambda i, *_: (i + base, 0))


def context_spec(base):
    return pl.BlockSpec((1, TILES, 2 * LANES, 2 * LANES), lambda i, *_: (i + base, 0, 0, 0))


def like(shape, dtype):
    return jax.ShapeDtypeStruct(shape, dtype)


def params(**given):
    return pltpu.CompilerParams(vmem_limit_bytes=58 * 2**20, **given)


MESH = pl.DeviceIdType.MESH
PIECE_ROWS = 256
SMALL_ROWS = 128


def peer(move):
    return (lax.axis_index("dp"), lax.bitwise_xor(lax.axis_index("head"), move))


def meet(peers):
    barrier = pltpu.get_barrier_semaphore()
    for item in peers:
        pl.semaphore_signal(barrier, inc=1, device_id=item, device_id_type=MESH)
    pl.semaphore_wait(barrier, len(peers))


def remote(source, target, send, receive, device):
    return pltpu.make_async_remote_copy(
        src_ref=source, dst_ref=target, send_sem=send, recv_sem=receive,
        device_id=device, device_id_type=MESH,
    )


def plan_pieces(shapes, count):
    pieces = []
    for item, (rows, lanes) in enumerate(shapes):
        height = min(PIECE_ROWS, rows)
        for start in range(0, rows, height):
            pieces.append((item, start, height, padded_rows(height, count), lanes))
    return pieces


def padded_rows(height, count):
    unit = 16 * count
    return -(-height // unit) * unit


def place_on_dp():
    dp = lax.axis_index("dp")
    return dp, lax.rem(dp, 2), dp // 2


def low_peer():
    dp, low, _ = place_on_dp()
    return (dp + 1 - 2 * low, lax.axis_index("head"))


def high_peer(step, group):
    _, low, high = place_on_dp()
    return (lax.rem(high + step, group) * 2 + low, lax.axis_index("head"))


def aligned(index, size):
    return pl.ds(pl.multiple_of(index * size, size), size)


class HighSum:
    def __init__(self, count, mid, part, whole, got, send, receive, slot):
        self.group = count // 2
        self.got = got
        self.mid, self.part, self.whole = mid, part, whole
        self.send, self.receive, self.slot = send, receive, slot
        self.half = mid.shape[0]
        self.size = self.half // self.group

    def copy(self, source, target, slot, device):
        return remote(
            source, target, self.send.at[self.slot + slot], self.receive.at[self.slot + slot], device
        )

    def high(self, step):
        _, _, high = place_on_dp()
        other = lax.rem(high + step, self.group)
        return self.copy(
            self.mid.at[aligned(other, self.size)], self.part.at[step - 1], step - 1,
            high_peer(step, self.group),
        )

    def spot(self):
        dp, low, high = place_on_dp()
        return self.whole.at[aligned(low * self.group + high, self.size)]

    def share(self, step):
        spot = self.spot()
        return self.copy(spot, spot, self.group - 2 + step, high_peer(step, self.group))

    def last(self):
        _, low, _ = place_on_dp()
        here = self.whole.at[aligned(low, self.half)]
        return self.copy(here, self.got, 2 * self.group - 2, low_peer())

    def to_high(self):
        for step in range(1, self.group):
            self.high(step).start()

    def share_high(self):
        _, _, high = place_on_dp()
        total = self.mid[aligned(high, self.size), :].astype(F32)
        for step in range(1, self.group):
            self.high(step).wait()
            total += self.part[step - 1].astype(F32)
        self.spot()[...] = total.astype(BF16)
        for step in range(1, self.group):
            self.share(step).start()

    def share_low(self):
        for step in range(1, self.group):
            self.share(step).wait()
        self.last().start()

    def finish(self):
        _, low, _ = place_on_dp()
        self.last().wait()
        self.whole[aligned(1 - low, self.half), :] = self.got[...]


def high_slots(count):
    return count - 1


class FullSum:
    def __init__(self, count, grad, span, near, far, whole, mid, low, part, got, send, receive, slot):
        self.grad, self.span, self.near, self.far = grad, span, near, far
        self.whole, self.mid, self.low = whole, mid, low
        self.height = far.shape[0]
        self.send, self.receive, self.slot = send, receive, slot
        self.rest = HighSum(count, mid, part, whole, got, send, receive, slot + 4)

    def copy(self, source, target, slot, device):
        return remote(
            source, target, self.send.at[self.slot + slot], self.receive.at[self.slot + slot], device
        )

    def near_copy(self, item):
        return self.copy(
            self.grad.at[1 + 2 * item, self.span], self.near.at[item], item, peer(1)
        )

    def far_copy(self):
        return self.copy(self.whole.at[: self.height], self.far, 2, peer(2))

    def low_copy(self):
        _, low, _ = place_on_dp()
        return self.copy(self.whole.at[aligned(1 - low, self.mid.shape[0])], self.low, 3, low_peer())

    def to_core(self):
        self.near_copy(1).start()
        self.near_copy(0).start()

    def to_far(self):
        self.near_copy(1).wait()
        self.whole[: self.height, :] = (
            self.grad[2, self.span, :].astype(F32) + self.near[1].astype(F32)
        ).astype(BF16)
        self.far_copy().start()

    def to_low(self):
        self.near_copy(0).wait()
        self.far_copy().wait()
        self.whole[: self.height, :] = (
            self.grad[0, self.span, :].astype(F32) + self.near[0].astype(F32)
            + self.far[...].astype(F32)
        ).astype(BF16)
        rows = self.whole.shape[0]
        if rows > self.height:
            self.whole[self.height :, :] = jnp.zeros((rows - self.height, self.whole.shape[1]), BF16)
        self.low_copy().start()

    def to_high(self):
        _, low, _ = place_on_dp()
        self.low_copy().wait()
        half = self.mid.shape[0]
        self.mid[...] = (
            self.whole[aligned(low, half), :].astype(F32) + self.low[...].astype(F32)
        ).astype(BF16)
        self.rest.to_high()


def sum_scratch(pieces, count):
    scratch = []
    for _, _, height, padded, lanes in pieces:
        scratch += [
            pltpu.VMEM((2, height, lanes), BF16), pltpu.VMEM((height, lanes), BF16),
            pltpu.VMEM((padded, lanes), BF16), pltpu.VMEM((padded // 2, lanes), BF16),
            pltpu.VMEM((padded // 2, lanes), BF16),
            pltpu.VMEM((count // 2 - 1, padded // count, lanes), BF16),
            pltpu.VMEM((padded // 2, lanes), BF16),
        ]
    return scratch


def step_masks(cut, col_cuts):
    place = lax.broadcasted_iota(jnp.int32, (PLACES, LANES), 0)
    row = lax.shift_right_logical(place, 4)
    col = lax.bitwise_and(place, 15)
    col_cut = jnp.where(row >= cut, col_cuts[1], col_cuts[0])
    rows = {
        1: (row < SIDE - 1) & (row + 1 != cut),
        -1: (row > 0) & (row != cut),
    }
    cols = {
        1: (col < SIDE - 1) & (col + 1 != col_cut),
        -1: (col > 0) & (col != col_cut),
    }
    return [
        {key: jnp.where(mask, 1.0, 0.0).astype(F32) for key, mask in masks.items()}
        for masks in (rows, cols)
    ]


def shift_rows(values, step):
    if step == 0:
        return values
    zero = jnp.zeros((SIDE, values.shape[1]), values.dtype)
    if step > 0:
        return jnp.concatenate([values[SIDE:], zero], axis=0)
    return jnp.concatenate([zero, values[:-SIDE]], axis=0)


def shift_cols(values, masks, step):
    if step == 0:
        return values
    return pltpu.roll(values, (-step) % PLACES, 0) * masks[step]


def head_kernel(
    canvases, count, ids_ref, small_own, qkv_own, x_in, qkv_in, share_in,
    first_ref, hidden_ref, query_ref, key_ref, value_ref, x_out, qkv_ref, small_out, far_out,
    x_ref, landing_ref, mine_ref, small_ref, qkv_all, small_got, send, receive, weight_send, weight_receive,
    share_send, share_receive, local,
):
    me = lax.axis_index("head")
    step = pl.program_id(0)
    rows = canvases * PLACES

    def piece(index, move):
        start = pl.multiple_of(lax.bitwise_xor(me, move) * rows + index * PLACES, PLACES)
        return remote(
            x_in.at[pl.ds(start, PLACES)], landing_ref.at[index, move - 1], send.at[index, move - 1],
            receive.at[index, move - 1], peer(move),
        )

    def weight(number, source, target, move):
        return remote(source, target, weight_send.at[number], weight_receive.at[number], peer(move))

    far = weight(0, qkv_in, qkv_all.at[1], 2)
    near = weight(1, qkv_in, qkv_all.at[0], 1)
    relay = weight(2, qkv_all.at[1], qkv_all.at[2], 1)
    smalls = [weight(2 + move, small_got.at[0], small_got.at[move], move) for move in (1, 2, 3)]
    mine = pltpu.make_async_copy(x_in.at[aligned(me, rows)], mine_ref, local.at[0])
    dp = lax.axis_index("dp")
    spot = aligned(dp, share_in.shape[0] // count)
    share = remote(share_in.at[spot], far_out.at[spot], share_send.at[0], share_receive.at[0], peer(2))
    group = count // 2
    _, low, high = place_on_dp()
    spread_high = [
        remote(
            far_out.at[spot], far_out.at[spot], share_send.at[hop], share_receive.at[hop],
            high_peer(hop, group),
        )
        for hop in range(1, group)
    ]
    spread_low = []
    for hop in range(group):
        source = lax.rem(high - hop + group, group) * 2 + low
        there = aligned(source, share_in.shape[0] // count)
        spread_low.append(
            remote(
                far_out.at[there], far_out.at[there], share_send.at[group + hop],
                share_receive.at[group + hop], low_peer(),
            )
        )

    @pl.when(step == 0)
    def _():
        mine.start()
        small_got[0] = small_own[...]
        meet(
            [peer(move) for move in (1, 2, 3)] + [low_peer()]
            + [high_peer(hop, group) for hop in range(1, group)]
        )
        for item in smalls:
            item.start()
        share.start()
        for move in (2, 3, 1):
            piece(0, move).start()
        far.start()
        near.start()

        def send_piece(index, carry):
            for move in (2, 3, 1):
                piece(index, move).start()
            return carry

        lax.fori_loop(1, canvases, send_piece, 0)
        for item in smalls:
            item.wait()
        for move in range(4):
            small_ref[:, aligned(lax.bitwise_xor(me, move), LANES)] = small_got[move]
            small_out[move] = small_got[move]
        mine.wait()

    for hop in range(1, group):

        @pl.when(step == min(1 + hop, canvases - 1))
        def _():
            spread_high[hop - 1].wait()
            spread_low[hop].start()

    @pl.when(step == canvases - 1)
    def _():
        for item in spread_low:
            item.wait()

    x_ref[:, aligned(me, LANES)] = mine_ref[aligned(step, PLACES), :].astype(F32)
    for move in (1, 2, 3):
        piece(step, move).wait()
        x_ref[:, aligned(lax.bitwise_xor(me, move), LANES)] = landing_ref[step, move - 1].astype(F32)
    rows_mask, cols_mask = step_masks(*read_cuts(ids_ref, canvases))
    for tile in range(TILES):
        field = x_ref[:, lane(tile)]
        moved = [shift_cols(field, cols_mask, col) for col in (-1, 0, 1)]
        result = field + small_ref[CPE_BIAS : CPE_BIAS + 1, lane(tile)]
        for row in (-1, 0, 1):
            line = None
            for col in (-1, 0, 1):
                tap = CPE + (row + 1) * 3 + col + 1
                term = jnp.broadcast_to(small_ref[tap : tap + 1, lane(tile)], (PLACES, LANES)) * moved[col + 1]
                line = term if line is None else line + term
            line = shift_rows(line, row)
            result = result + (line * rows_mask[row] if row else line)
        first_ref[:, lane(tile)] = result
    x_out[...] = x_ref[...].astype(BF16)
    first = first_ref[...]
    center = row_mean(first)
    square = row_mean(first * first)
    inverse = lax.rsqrt(square - center * center + EPSILON)
    hidden = (
        (first - center) * inverse * small_ref[GAIN1 : GAIN1 + 1, :] + small_ref[SHIFT1 : SHIFT1 + 1, :]
    ).astype(BF16)
    hidden_ref[...] = hidden

    @pl.when(step == 0)
    def _():
        share.wait()
        for item in spread_high + spread_low[:1]:
            item.start()
        far.wait()
        relay.start()
        near.wait()
        relay.wait()
        qkv_ref[0] = qkv_own[...]
        for move in (1, 2, 3):
            qkv_ref[move] = qkv_all[move - 1]

    for tile in range(TILES):
        three = nn(hidden, qkv_ref[lax.bitwise_xor(me, tile)])
        query_ref[:, lane(tile)] = (
            three[:, :LANES] + small_ref[QUERY_BIAS : QUERY_BIAS + 1, lane(tile)]
        ).astype(BF16)
        key_ref[:, lane(tile)] = three[:, LANES : 2 * LANES].astype(BF16)
        value_ref[:, lane(tile)] = (
            three[:, 2 * LANES :] + small_ref[VALUE_BIAS : VALUE_BIAS + 1, lane(tile)]
        ).astype(BF16)


def head_part(ids, small, qkv, block_in, share):
    count = lax.axis_size("dp")
    rows = block_in.shape[0] // 4
    canvases = rows // PLACES
    wide = rows_spec(D)
    hbm = pl.BlockSpec(memory_space=pl.ANY)
    return pl.pallas_call(
        lambda *refs: head_kernel(canvases, count, *refs),
        grid=(canvases,),
        in_specs=[
            pl.BlockSpec(memory_space=pltpu.SMEM), once(small.shape), once(qkv.shape), hbm, hbm, hbm,
        ],
        out_specs=[wide] * 6 + [once((4,) + qkv.shape), once((4,) + small.shape), hbm],
        out_shape=[like((rows, D), F32)] + [like((rows, D), BF16)] * 5 + [
            like((4,) + qkv.shape, BF16), like((4,) + small.shape, F32), like(share.shape, BF16),
        ],
        scratch_shapes=[
            pltpu.VMEM((PLACES, D), F32), pltpu.VMEM((canvases, 3, PLACES, LANES), BF16),
            pltpu.VMEM((rows, LANES), BF16), pltpu.VMEM((SMALL_SIZE, D), F32),
            pltpu.VMEM((3,) + qkv.shape, BF16), pltpu.VMEM((4,) + small.shape, F32),
            pltpu.SemaphoreType.DMA((canvases, 3)), pltpu.SemaphoreType.DMA((canvases, 3)),
            pltpu.SemaphoreType.DMA((6,)), pltpu.SemaphoreType.DMA((6,)),
            pltpu.SemaphoreType.DMA((count,)), pltpu.SemaphoreType.DMA((count,)),
            pltpu.SemaphoreType.DMA((1,)),
        ],
        compiler_params=params(collective_id=1, has_side_effects=True),
        name="head",
    )(ids, small, qkv, block_in, qkv, share)


def front_kernel(
    canvases, ids_ref, query_ref, key_ref, value_ref, small_in,
    soft_ref, context_ref, conv_ref, attended_ref,
    mask_ref, grid_ref, out_ref, x_ref, small_ref, crpe_ref,
):
    cut, col_cuts = read_cuts(ids_ref, canvases)

    @pl.when(pl.program_id(0) == 0)
    def _():
        grid_ref[...] = jnp.zeros_like(grid_ref)
        spread_small(small_in, small_ref)
        spread_taps(small_ref, CRPE, 49, True, crpe_ref)

    fill_masks(cut, col_cuts, mask_ref)
    band, side = place_ids(cut, col_cuts)
    ids = 2 * band + side
    sides = [(side == item).astype(F32).astype(BF16) for item in range(2)]
    bands = [(band == item).astype(F32).astype(BF16) for item in range(2)]
    blocks = head_block()
    for tile in range(TILES):
        query = query_ref[:, lane(tile)]
        keys = key_ref[:, lane(tile)].astype(F32)
        value = value_ref[:, lane(tile)]
        highest = crop_reduce(ids, keys, jnp.max, -1e30)
        powers = jnp.exp(keys - pick(ids, highest))
        totals = crop_reduce(ids, powers, jnp.sum, 0.0)
        soft = (powers * pick(ids, [1.0 / item for item in totals])).astype(BF16)
        soft_ref[:, lane(tile)] = soft
        context = (tn(both(soft, sides), both(value, bands)) * blocks).astype(BF16)
        context_ref[0, tile] = context
        factor = nn(both(query, sides), context)
        x_ref[:, lane(tile)] = jnp.where(band > 0, factor[:, LANES:], factor[:, :LANES]) * SCALE
    for tile in range(TILES):
        spread(
            lambda row: value_ref[SIDE * row : SIDE * row + SIDE, lane(tile)].astype(F32),
            REACH[tile], cut, mask_ref, grid_ref, 3,
        )
        conv_tiles(((tile, 3),), REACH[tile], cut, grid_ref, crpe_ref, 3, out_ref)
    conv = out_ref[:PLACES, :]
    conv_ref[...] = conv.astype(BF16)
    attended_ref[...] = (x_ref[...] + query_ref[...].astype(F32) * conv).astype(BF16)


def front(ids, query, key, value, small):
    rows = query.shape[0]
    count = rows // PLACES
    wide = rows_spec(D)
    return pl.pallas_call(
        lambda *refs: front_kernel(count, *refs),
        grid_spec=pltpu.PrefetchScalarGridSpec(
            num_scalar_prefetch=1,
            grid=(count,),
            in_specs=[wide, wide, wide, once(small.shape)],
            out_specs=[wide, context_spec(0), wide, wide],
            scratch_shapes=[
                pltpu.VMEM((2, 7, SIDE, LANES), F32),
                pltpu.VMEM((7, GRID_ROWS * SIDE, LANES), F32),
                pltpu.VMEM((PLACES + SIDE, D), F32),
                pltpu.VMEM((PLACES, D), F32),
                pltpu.VMEM((SMALL_SIZE, D), F32),
                pltpu.VMEM((49, 8, D), F32),
            ],
        ),
        out_shape=[
            like((rows, D), BF16), like((count, TILES, 2 * LANES, 2 * LANES), BF16),
            like((rows, D), BF16), like((rows, D), BF16),
        ],
        compiler_params=params(),
        cost_estimate=pl.CostEstimate(
            flops=rows * D * D * 40, bytes_accessed=count * 10**7, transcendentals=0
        ),
        name="front",
    )(ids, query, key, value, small)


def gelu_both(pre):
    power = jnp.exp(pre * pre * -0.5)
    t = 1.0 / (1.0 + jnp.abs(pre) * (0.3275911 * 0.7071067811865476))
    poly = 0.5 * 1.061405429
    for item in (-1.453152027, 1.421413741, -0.284496736, 0.254829592):
        poly = poly * t + 0.5 * item
    tail = poly * t * power
    cdf = jnp.where(pre >= 0.0, 1.0 - tail, tail)
    return pre * cdf, cdf + pre * power * 0.3989422804014327


BLOCK = 1024


def middle_kernel(
    count,
    attended_ref, first_ref, cot0_ref, cot1_ref, cot2_ref, cot3_ref, small_in, own_weights,
    far_weights,
    out0_ref, out1_ref, out2_ref, out3_ref, second_grad_ref, att_grad_ref, fc_mid_ref,
    proj_grad_ref, sum_ref, bias_grad_ref,
    cot_ref, hat_ref, inverse_ref, hidden_ref, total_ref, back_ref, active_ref, pre_grad_ref,
    grads_ref, near_ref, far_ref, own_ref, low_ref, small_ref, weights_ref, send, receive, fetch,
):
    me = lax.axis_index("head")
    step = pl.program_id(0)
    rows = attended_ref.shape[0]
    blocks = rows // BLOCK
    _, low, _ = place_on_dp()
    half = low_ref.shape[1]

    def near(item, kind):
        return remote(
            grads_ref.at[2 * item, kind], near_ref.at[item, kind], send.at[2 * item + kind],
            receive.at[2 * item + kind], peer(1),
        )

    def far(kind):
        return remote(
            grads_ref.at[1, kind], far_ref.at[kind], send.at[4 + kind], receive.at[4 + kind], peer(2)
        )

    def to_low(kind):
        return remote(
            own_ref.at[kind, aligned(1 - low, half)], low_ref.at[kind], send.at[6 + kind],
            receive.at[6 + kind], low_peer(),
        )

    def part(index):
        return aligned(index, BLOCK)

    shard = 3 - step
    fc1 = weights_ref.at[shard, :D]
    fc2 = weights_ref.at[shard, D : 2 * D]

    def proj(tile):
        return weights_ref[lax.bitwise_xor(me, tile), 2 * D : 2 * D + LANES, :]

    def relay(number, source, target, part):
        return remote(
            source.at[part], weights_ref.at[target, part], send.at[8 + number], receive.at[8 + number],
            peer(1),
        )

    narrow, broad = pl.ds(2 * D, LANES), pl.ds(0, 2 * D)
    relays = [
        relay(0, own_weights, 1, narrow), relay(1, far_weights, 3, narrow),
        relay(2, far_weights, 3, broad), relay(3, own_weights, 1, broad),
    ]

    @pl.when(step == 0)
    def _():
        loads = [
            pltpu.make_async_copy(own_weights.at[pl.ds(0, 2 * D + LANES)], weights_ref.at[0], fetch.at[0]),
            pltpu.make_async_copy(far_weights.at[pl.ds(0, 2 * D + LANES)], weights_ref.at[2], fetch.at[1]),
        ]
        for move, piece_ref in enumerate((cot0_ref, cot1_ref, cot2_ref, cot3_ref)):
            spot = cot_ref.at[:, aligned(lax.bitwise_xor(me, move), LANES)]
            loads.append(pltpu.make_async_copy(piece_ref, spot, fetch.at[2 + move]))
        for load in loads:
            load.start()
        meet([peer(1), peer(2), low_peer()])
        for item in relays:
            item.start()
        spread_small(small_in, small_ref)
        own_ref[...] = jnp.zeros_like(own_ref)
        sum_ref[...] = jnp.zeros_like(sum_ref)
        for item in loads + relays[:2]:
            item.wait()

        def enter(index, carry):
            now = part(index)
            second = first_ref[now, :] + small_ref[PROJ_BIAS : PROJ_BIAS + 1, :]
            for tile in range(TILES):
                second += nn(attended_ref[now, lane(tile)], proj(tile))
            center = row_mean(second)
            square = row_mean(second * second)
            inverse = lax.rsqrt(square - center * center + EPSILON)
            hat = (second - center) * inverse
            hidden_ref[now, :] = (
                hat * small_ref[GAIN2 : GAIN2 + 1, :] + small_ref[SHIFT2 : SHIFT2 + 1, :]
            ).astype(BF16)
            hat_ref[now, :] = hat
            inverse_ref[now, :] = jnp.broadcast_to(inverse, (BLOCK, LANES))
            total_ref[now, :] = second + small_ref[FC2_BIAS : FC2_BIAS + 1, :]
            back_ref[now, :] = jnp.zeros((BLOCK, D), F32)
            sum_ref[3:4, :] += jnp.sum(cot_ref[now, :].astype(F32), axis=0, keepdims=True)
            return carry

        lax.fori_loop(0, blocks, enter, 0)
        for item in relays[2:]:
            item.wait()

    bias_grad_ref[0] = jnp.zeros_like(bias_grad_ref[0])

    def chunk(index, carry):
        now = part(index)
        bias = jnp.concatenate(
            [small_in[shard, FC1_BIAS + tile : FC1_BIAS + tile + 1, :] for tile in range(TILES)], axis=1
        )
        pre = nn(hidden_ref[now, :], fc1[...]) + bias
        active, slope = gelu_both(pre)
        active = active.astype(BF16)
        active_ref[now, :] = active
        total_ref[now, :] += nn(active, fc2[...])
        pre_grad_f = nt(cot_ref[now, :], fc2[...]) * slope
        pre_grad = pre_grad_f.astype(BF16)
        pre_grad_ref[now, :] = pre_grad
        back_ref[now, :] += nt(pre_grad, fc1[...])
        bias_grad_ref[0] += jnp.sum(pre_grad_f, axis=0, keepdims=True)
        return carry

    lax.fori_loop(0, blocks, chunk, 0)
    grads_ref[step, 0] = tn(hidden_ref[...], pre_grad_ref[...]).astype(BF16)
    grads_ref[step, 1] = tn(active_ref[...], cot_ref[...]).astype(BF16)

    @pl.when(step == 0)
    def _():
        for kind in range(2):
            near(0, kind).start()

    @pl.when(step == 1)
    def _():
        for kind in range(2):
            near(0, kind).wait()
            grads_ref[1, kind] = (
                grads_ref[1, kind].astype(F32) + near_ref[0, kind].astype(F32)
            ).astype(BF16)
            far(kind).start()

    @pl.when(step == 2)
    def _():
        for kind in range(2):
            near(1, kind).start()

    @pl.when(step == 3)
    def _():
        for kind in range(2):
            near(1, kind).wait()
            far(kind).wait()
            own_ref[kind, :D, :] = (
                grads_ref[3, kind].astype(F32) + near_ref[1, kind].astype(F32)
                + far_ref[kind].astype(F32)
            ).astype(BF16)
            to_low(kind).start()

        def leave(index, carry):
            now = part(index)
            for move, piece_ref in enumerate((out0_ref, out1_ref, out2_ref, out3_ref)):
                piece_ref[now, :] = total_ref[now, aligned(lax.bitwise_xor(me, move), LANES)].astype(BF16)
            hat = hat_ref[now, :]
            norm_grad = back_ref[now, :]
            weighted = norm_grad * small_ref[GAIN2 : GAIN2 + 1, :]
            second_grad = cot_ref[now, :].astype(F32) + inverse_ref[now, 0:1] * (
                weighted - row_mean(weighted) - hat * row_mean(weighted * hat)
            )
            second_grad_ref[now, :] = second_grad
            second_low = second_grad.astype(BF16)
            hidden_ref[now, :] = second_low
            for tile in range(TILES):
                att_grad_ref[now, lane(tile)] = nt(
                    second_low, proj(tile)
                ).astype(BF16)
            sum_ref[1:2, :] += jnp.sum(norm_grad * hat, axis=0, keepdims=True)
            sum_ref[2:3, :] += jnp.sum(norm_grad, axis=0, keepdims=True)
            sum_ref[0:1, :] += jnp.sum(second_low.astype(F32), axis=0, keepdims=True)
            return carry

        lax.fori_loop(0, blocks, leave, 0)
        for tile in range(TILES):
            proj_grad_ref[lax.bitwise_xor(me, tile)] = tn(
                attended_ref[:, lane(tile)], hidden_ref[...]
            ).astype(BF16)
        for kind in range(2):
            to_low(kind).wait()
            fc_mid_ref[kind] = (
                own_ref[kind, aligned(low, half), :].astype(F32) + low_ref[kind].astype(F32)
            ).astype(BF16)


def middle(attended, first, cot_parts, small, own_weights, far_weights):
    rows = attended.shape[0]
    count = lax.axis_size("dp")
    padded = padded_rows(D, count)
    hbm = pl.BlockSpec(memory_space=pl.ANY)
    proj_shape = (4, LANES, D)
    piece = once((rows, LANES))
    wide = once((rows, D))
    line = pl.BlockSpec((1, 1, D), lambda i: (3 - i, 0, 0))
    return pl.pallas_call(
        lambda *refs: middle_kernel(count, *refs),
        grid=(4,),
        in_specs=[
            wide, wide, hbm, hbm, hbm, hbm, once(small.shape), hbm, hbm,
        ],
        out_specs=[
            piece, piece, piece, piece, wide, wide, once((2, padded // 2, D)), once(proj_shape),
            once((8, D)), line,
        ],
        out_shape=[like((rows, LANES), BF16)] * 4 + [
            like((rows, D), F32), like((rows, D), BF16), like((2, padded // 2, D), BF16),
            like(proj_shape, BF16), like((8, D), F32), like((4, 1, D), F32),
        ],
        scratch_shapes=[
            pltpu.VMEM((rows, D), BF16), pltpu.VMEM((rows, D), F32),
            pltpu.VMEM((rows, LANES), F32),
            pltpu.VMEM((rows, D), BF16), pltpu.VMEM((rows, D), F32),
            pltpu.VMEM((rows, D), F32), pltpu.VMEM((rows, D), BF16),
            pltpu.VMEM((rows, D), BF16),
            pltpu.VMEM((4, 2, D, D), BF16), pltpu.VMEM((2, 2, D, D), BF16),
            pltpu.VMEM((2, D, D), BF16), pltpu.VMEM((2, padded, D), BF16),
            pltpu.VMEM((2, padded // 2, D), BF16),
            pltpu.VMEM((SMALL_SIZE, D), F32), pltpu.VMEM((4, 2 * D + LANES, D), BF16),
            pltpu.SemaphoreType.DMA((12,)), pltpu.SemaphoreType.DMA((12,)),
            pltpu.SemaphoreType.DMA((6,)),
        ],
        compiler_params=params(collective_id=2, has_side_effects=True),
        cost_estimate=pl.CostEstimate(flops=rows * D * D * 60, bytes_accessed=3 * 10**7, transcendentals=0),
        name="middle",
    )(attended, first, *cot_parts, small, own_weights, far_weights)


def back_kernel(
    canvases, ids_ref, grad_ref, query_ref, value_ref, soft_ref, context_ref, conv_ref, hidden_ref,
    small_in, middle_sum_ref, bias_grad_ref,
    three_ref, qkv_out_ref, small_out_ref,
    mask_ref, grid_ref, out_ref, other_ref, value_part_ref, qkv_grad_ref, small_ref, crpe_ref,
    crpe_sum_ref, sum_ref, late_ref,
):
    cut, col_cuts = read_cuts(ids_ref, canvases)
    me = lax.axis_index("head")

    @pl.when(pl.program_id(0) == 0)
    def _():
        grid_ref[...] = jnp.zeros_like(grid_ref)
        other_ref[...] = jnp.zeros_like(other_ref)
        qkv_grad_ref[...] = jnp.zeros_like(qkv_grad_ref)
        crpe_sum_ref[...] = jnp.zeros_like(crpe_sum_ref)
        sum_ref[...] = jnp.zeros_like(sum_ref)
        spread_small(small_in, small_ref)
        spread_taps(small_ref, CRPE, 49, True, crpe_ref)

    fill_masks(cut, col_cuts, mask_ref)
    band, side = place_ids(cut, col_cuts)
    ids = 2 * band + side
    sides = [(side == item).astype(F32).astype(BF16) for item in range(2)]
    bands = [(band == item).astype(F32).astype(BF16) for item in range(2)]
    blocks = head_block() * SCALE
    for tile in range(TILES):
        grad = grad_ref[:, lane(tile)]
        query = query_ref[:, lane(tile)]
        value = value_ref[:, lane(tile)]
        soft = soft_ref[:, lane(tile)]
        context = context_ref[0, tile]
        grad_f = grad.astype(F32)
        grad_bands = both(grad, bands)
        context_grad = (tn(both(query, sides), grad_bands) * blocks).astype(BF16)
        part = nt(grad_bands, context)
        part = jnp.where(side > 0, part[:, LANES:], part[:, :LANES])
        query_grad = (
            part * SCALE + grad_f * conv_ref[:, lane(tile)].astype(F32)
        ).astype(BF16)
        soft_grad = nt(both(value, bands), context_grad)
        soft_grad = jnp.where(side > 0, soft_grad[:, LANES:], soft_grad[:, :LANES])
        soft_f = soft.astype(F32)
        inner = crop_reduce(ids, soft_f * soft_grad, jnp.sum, 0.0)
        keys_grad = (soft_f * (soft_grad - pick(ids, inner))).astype(BF16)
        value_part = nn(both(soft, sides), context_grad)
        value_part_ref[:, lane(tile)] = jnp.where(
            band > 0, value_part[:, LANES:], value_part[:, :LANES]
        )
        three_ref[tile, :, :LANES] = query_grad
        three_ref[tile, :, LANES : 2 * LANES] = keys_grad
        sum_ref[0:1, lane(tile)] += jnp.sum(query_grad.astype(F32), axis=0, keepdims=True)
    other_ref[:PLACES, :] = value_ref[...].astype(F32)
    for tile in range(TILES):

        def read_row(row):
            part = pl.ds(SIDE * row, SIDE)
            return grad_ref[part, lane(tile)].astype(F32) * query_ref[part, lane(tile)].astype(F32)

        spread(read_row, REACH[tile], cut, mask_ref, grid_ref, 3)
        conv_back_tiles(
            ((tile, 3),), REACH[tile], cut, grid_ref, crpe_ref, 3, other_ref, out_ref, crpe_sum_ref
        )
    hidden = hidden_ref[...]
    for tile in range(TILES):
        value_grad = (value_part_ref[:, lane(tile)] + out_ref[:PLACES, lane(tile)]).astype(BF16)
        three_ref[tile, :, 2 * LANES :] = value_grad
        sum_ref[1:2, lane(tile)] += jnp.sum(value_grad.astype(F32), axis=0, keepdims=True)
        qkv_grad_ref[lax.bitwise_xor(me, tile)] += tn(hidden, three_ref[tile])

    @pl.when(pl.program_id(0) == pl.num_programs(0) - 1)
    def _():
        qkv_out_ref[...] = qkv_grad_ref[...].astype(BF16)
        late_ref[...] = jnp.zeros_like(late_ref)
        for tap in range(49):
            for tile in range(TILES):
                late_ref[tap : tap + 1, lane(tile)] = keep_head(
                    tap, tile, jnp.sum(crpe_sum_ref[tap, :, lane(tile)], axis=0, keepdims=True)
                )
        late_ref[49:51, :] = sum_ref[0:2, :]
        late_ref[51:55, :] = middle_sum_ref[0:4, :]
        for move in range(4):
            late = late_ref[:, aligned(lax.bitwise_xor(me, move), LANES)]
            small_out_ref[move] = late.astype(BF16)
            small_out_ref[move, 64:80, :] = jnp.concatenate(
                [bias_grad_ref[move, :, lane(tile)] for tile in range(TILES)]
                + [jnp.zeros((12, LANES), F32)],
                axis=0,
            ).astype(BF16)


def back(ids, grad, query, value, soft, context, conv, hidden, small, middle_sum, bias_grad):
    rows = grad.shape[0]
    count = rows // PLACES
    wide = rows_spec(D)
    shards = (4, D, 3 * LANES)
    late = (4, SMALL_ROWS, LANES)
    return pl.pallas_call(
        lambda *refs: back_kernel(count, *refs),
        grid_spec=pltpu.PrefetchScalarGridSpec(
            num_scalar_prefetch=1,
            grid=(count,),
            in_specs=[
                wide, wide, wide, wide, context_spec(0), wide, wide, once(small.shape),
                once(middle_sum.shape), once(bias_grad.shape),
            ],
            out_specs=[
                pl.BlockSpec((TILES, PLACES, 3 * LANES), lambda i, *_: (0, i, 0)),
                once(shards), once(late),
            ],
            scratch_shapes=[
                pltpu.VMEM((2, 7, SIDE, LANES), F32),
                pltpu.VMEM((7, GRID_ROWS * SIDE, LANES), F32),
                pltpu.VMEM((PLACES + SIDE, D), F32),
                pltpu.VMEM((PLACES + SIDE, D), F32),
                pltpu.VMEM((PLACES, D), F32),
                pltpu.VMEM(shards, F32),
                pltpu.VMEM((SMALL_SIZE, D), F32),
                pltpu.VMEM((49, 8, D), F32),
                pltpu.VMEM((49, 8, D), F32),
                pltpu.VMEM((8, D), F32),
                pltpu.VMEM((SMALL_ROWS, D), F32),
            ],
        ),
        out_shape=[
            like((TILES, rows, 3 * LANES), BF16), like(shards, BF16), like(late, BF16),
        ],
        compiler_params=params(),
        cost_estimate=pl.CostEstimate(
            flops=rows * D * D * 64, bytes_accessed=count * 10**7, transcendentals=0
        ),
        name="back",
    )(ids, grad, query, value, soft, context, conv, hidden, small, middle_sum, bias_grad)


LAST_ROWS = 16
STAGES = ((0, 1, 2, 3, 4, 5), (0, 1, 3, 4, 5, 6), (0, 1, 4, 6, 7, 8), (0, 1, 5, 7, 8, 9))
FC_STAGES = ((0, 2, 4), (1, 4, 6))


def tail_kernel(
    count, pieces,
    canvases, ids_ref, x_in, three_ref, first_ref, second_grad_ref, small_params,
    qkv_ref, fc_mid_in, small_in, proj_grad_in, qkv_grad_in,
    out0_ref, out1_ref, out2_ref, out3_ref, fc1_own_ref, fc2_own_ref, small_own_ref, proj_own_ref,
    qkv_own_ref, last_own_ref,
    x_ref, gone_ref, cpe_sum_ref, sum_ref, fc_part_ref, fc_whole_ref, fc_got_ref, mine_ref, first_got_ref,
    total_ref, second_got_ref, piece_send, piece_receive, send, receive, last_send, last_receive,
    cpe_ref, fc_mid_ref, small_ref, proj_grad_ref, qkv_grad_ref, *buffers,
):
    me = lax.axis_index("head")
    dp = lax.axis_index("dp")
    step = pl.program_id(0)
    steps = pl.num_programs(0)
    slots = high_slots(count)
    fc_sums = [
        HighSum(
            count, fc_mid_ref.at[kind], fc_part_ref.at[kind], fc_whole_ref.at[kind],
            fc_got_ref.at[kind], send, receive, kind * slots,
        )
        for kind in range(2)
    ]
    sources = (small_ref, proj_grad_ref, qkv_grad_ref)
    targets = (small_own_ref, proj_own_ref, qkv_own_ref)
    sums = []
    for number, (item, start, height, padded, lanes) in enumerate(pieces):
        near, far, own, mid, low, part, got = buffers[7 * number : 7 * number + 7]
        sums.append(
            FullSum(
                count, sources[item], pl.ds(start, height), near, far, own, mid, low, part, got, send,
                receive, 2 * slots + number * (slots + 4),
            )
        )

    def piece_copy(index, move):
        target = (out1_ref, out2_ref, out3_ref)[move - 1]
        return remote(
            gone_ref.at[index, move - 1], target.at[aligned(index, PLACES)],
            piece_send.at[index, move - 1], piece_receive.at[index, move - 1], peer(move),
        )

    def first_copy(move):
        return remote(
            mine_ref.at[move], first_got_ref.at[move - 1], last_send.at[move - 1],
            last_receive.at[move - 1], peer(move),
        )

    def second_copy(hop):
        return remote(
            total_ref, second_got_ref.at[hop - 1], last_send.at[2 + hop], last_receive.at[2 + hop],
            (lax.rem(dp + hop, count), me),
        )

    @pl.when(step == 0)
    def _():
        meet(
            [peer(1), peer(2), peer(3)] + [(lax.rem(dp + hop, count), me) for hop in range(1, count)]
        )
        spread_small(small_params, cpe_ref)
        fc_mid_ref[...] = fc_mid_in[...]
        qkv_grad_ref[...] = qkv_grad_in[...]
        proj_grad_ref[...] = proj_grad_in[...]
        small_ref[...] = small_in[...]
        cpe_sum_ref[...] = jnp.zeros_like(cpe_sum_ref)
        sum_ref[...] = jnp.zeros_like(sum_ref)

    events = []
    for item, slots_of in zip(sums, STAGES):
        actions = (
            item.to_core, item.to_far, item.to_low, item.to_high, item.rest.share_high, item.rest.share_low,
        )
        events += list(zip(slots_of, actions))
    for item, slots_of in zip(fc_sums, FC_STAGES):
        events += list(zip(slots_of, (item.to_high, item.share_high, item.share_low)))

    def run(when):
        for slot, action in events:
            if slot == when:
                action()

    for when in range(canvases):
        pl.when(step == when)(lambda: run(when))

    norm_grad = nt(three_ref[0], qkv_ref[lax.bitwise_xor(me, 0)])
    for tile in range(1, TILES):
        norm_grad += nt(three_ref[tile], qkv_ref[lax.bitwise_xor(me, tile)])
    first = first_ref[...]
    center = row_mean(first)
    square = row_mean(first * first)
    inverse = lax.rsqrt(square - center * center + EPSILON)
    hat = (first - center) * inverse
    weighted = norm_grad * cpe_ref[GAIN1 : GAIN1 + 1, :]
    first_grad = second_grad_ref[...] + inverse * (
        weighted - row_mean(weighted) - hat * row_mean(weighted * hat)
    )
    sum_ref[0:1, :] += jnp.sum(first_grad, axis=0, keepdims=True)
    sum_ref[1:2, :] += jnp.sum(norm_grad * hat, axis=0, keepdims=True)
    sum_ref[2:3, :] += jnp.sum(norm_grad, axis=0, keepdims=True)
    x_ref[...] = x_in[...].astype(F32)
    rows, cols = step_masks(*read_cuts(ids_ref, canvases))
    results = []
    for tile in range(TILES):
        field = first_grad[:, LANES * tile : LANES * (tile + 1)]
        other = x_ref[:, lane(tile)]
        others = {0: other, 1: shift_rows(other * rows[1], -1), -1: shift_rows(other * rows[-1], 1)}
        moved = [shift_cols(field, cols, col) for col in (-1, 0, 1)]
        result = field
        for row in (-1, 0, 1):
            line = None
            for col in (-1, 0, 1):
                tap = (1 - row) * 3 + 1 - col
                wide_tap = jnp.broadcast_to(cpe_ref[tap : tap + 1, lane(tile)], (PLACES, LANES))
                term = wide_tap * moved[col + 1]
                line = term if line is None else line + term
                product = others[row] * moved[col + 1]
                cpe_sum_ref[tap, :, lane(tile)] += jnp.sum(product.reshape(PLACES // 8, 8, LANES), axis=0)
            line = shift_rows(line, row)
            result = result + (line * rows[row] if row else line)
        results.append(result)
    result = jnp.concatenate(results, axis=1)
    x_ref[...] = result
    out0_ref[...] = x_ref[:, aligned(me, LANES)].astype(BF16)
    for move in (1, 2, 3):
        gone_ref[step, move - 1] = x_ref[:, aligned(lax.bitwise_xor(me, move), LANES)].astype(BF16)
    late = canvases // 2

    @pl.when(step >= late)
    def _():
        for item in range(2):
            for move in (2, 3, 1):
                piece_copy(2 * (step - late) + item, move).start()

    @pl.when(step == steps - 1)
    def _():
        sum_ref[3:12, :] = jnp.sum(cpe_sum_ref[...], axis=1)
        for move in range(4):
            mine_ref[move] = sum_ref[:, aligned(lax.bitwise_xor(me, move), LANES)]
        for move in (1, 2, 3):
            first_copy(move).start()
        run(canvases)
        total = mine_ref[0]
        for move in (1, 2, 3):
            first_copy(move).wait()
            total += first_got_ref[move - 1]
        total_ref[...] = total
        for hop in range(1, count):
            second_copy(hop).start()
        run(canvases + 1)
        for item in fc_sums:
            item.finish()
        fc1_own_ref[...] = fc_whole_ref[0, :D, :]
        fc2_own_ref[...] = fc_whole_ref[1, :D, :]
        for hop in range(1, count):
            second_copy(hop).wait()
            total += second_got_ref[hop - 1]
        last_own_ref[...] = total
        for piece, item in zip(pieces, sums):
            item.rest.finish()
            targets[piece[0]][piece[1] : piece[1] + piece[2], :] = item.whole[: piece[2], :]

        def settle(index, carry):
            for move in (1, 2, 3):
                piece_copy(index, move).wait()
            return carry

        lax.fori_loop(0, steps, settle, 0)


def tail(ids, x, three, first, second_grad, params_small, qkv, fc_mid, qkv_grad, proj_grad, small):
    rows = first.shape[0]
    canvases = rows // PLACES
    count = lax.axis_size("dp")
    segments = [small, proj_grad, qkv_grad]
    pieces = plan_pieces([item.shape[1:] for item in segments], count)
    slots = high_slots(count)
    wide = rows_spec(D)
    piece = rows_spec(LANES)
    hbm = pl.BlockSpec(memory_space=pl.ANY)
    half = fc_mid.shape[1]
    group = count // 2
    total_slots = 2 * slots + len(pieces) * (slots + 4)
    last = (LAST_ROWS, LANES)
    return pl.pallas_call(
        lambda *refs: tail_kernel(count, pieces, canvases, *refs),
        grid=(canvases,),
        in_specs=[pl.BlockSpec(memory_space=pltpu.SMEM), wide] + [
            pl.BlockSpec((TILES, PLACES, 3 * LANES), lambda i: (0, i, 0)), wide, wide,
            once(params_small.shape), once(qkv.shape), once(fc_mid.shape),
        ] + [once(item.shape) for item in segments],
        out_specs=[piece, hbm, hbm, hbm, once((D, D)), once((D, D))]
        + [once(item.shape[1:]) for item in segments] + [once(last)],
        out_shape=[like((rows, LANES), BF16)] * 4 + [like((D, D), BF16)] * 2
        + [like(item.shape[1:], BF16) for item in segments] + [like(last, F32)],
        scratch_shapes=[
            pltpu.VMEM((PLACES, D), F32), pltpu.VMEM((canvases, 3, PLACES, LANES), BF16),
            pltpu.VMEM((9, 8, D), F32), pltpu.VMEM((LAST_ROWS, D), F32),
            pltpu.VMEM((2, group - 1, half // group, D), BF16), pltpu.VMEM((2, 2 * half, D), BF16),
            pltpu.VMEM((2, half, D), BF16),
            pltpu.VMEM((4,) + last, F32), pltpu.VMEM((3,) + last, F32), pltpu.VMEM(last, F32),
            pltpu.VMEM((count - 1,) + last, F32),
            pltpu.SemaphoreType.DMA((canvases, 3)), pltpu.SemaphoreType.DMA((canvases, 3)),
            pltpu.SemaphoreType.DMA((total_slots,)), pltpu.SemaphoreType.DMA((total_slots,)),
            pltpu.SemaphoreType.DMA((2 + count,)), pltpu.SemaphoreType.DMA((2 + count,)),
        ] + [pltpu.VMEM((SMALL_SIZE, D), F32)]
        + [pltpu.VMEM(item.shape, BF16) for item in [fc_mid] + segments]
        + sum_scratch(pieces, count),
        compiler_params=params(collective_id=3, has_side_effects=True),
        cost_estimate=pl.CostEstimate(
            flops=rows * D * D * 12, bytes_accessed=canvases * 3 * 10**6, transcendentals=0
        ),
        name="tail",
    )(ids, x, three, first, second_grad, params_small, qkv, fc_mid, *segments)


def collect_kernel(me_ref, *refs):
    out_ref = refs[-1]
    for item, piece_ref in enumerate(refs[:-1]):

        @pl.when(pl.program_id(0) == item)
        def _():
            out_ref[...] = piece_ref[...].astype(F32)


def collect(me, pieces):
    rows = pieces[0].shape[0]
    return pl.pallas_call(
        collect_kernel,
        grid_spec=pltpu.PrefetchScalarGridSpec(
            num_scalar_prefetch=1,
            grid=(4,),
            in_specs=[once((rows, LANES))] * 4,
            out_specs=pl.BlockSpec((rows, LANES), lambda i, me: (lax.bitwise_xor(me[0], i), 0)),
        ),
        out_shape=like((4 * rows, LANES), F32),
        compiler_params=params(),
        name="collect",
    )(me, *pieces)


def finish_kernel(
    me_ref, p0_ref, p1_ref, p2_ref, p3_ref, fc1_ref, fc2_ref, small_ref, proj_ref, qkv_ref, last_ref,
    grad_ref, cpe_ref, vectors_ref, qkv_out_ref, qv_ref, crpe_ref, proj_out_ref, fc1_out_ref,
    bias_ref, fc2_out_ref,
):
    for item, piece_ref in enumerate((p0_ref, p1_ref, p2_ref, p3_ref)):

        @pl.when(pl.program_id(0) == item)
        def _():
            grad_ref[...] = piece_ref[...].astype(F32)

    @pl.when(pl.program_id(0) == 0)
    def _():
        cpe_ref[...] = last_ref[3:12, :]
        small = small_ref[...].astype(F32)
        vectors_ref[...] = jnp.concatenate(
            [last_ref[0:3, :], small[51:55, :], jnp.zeros((1, LANES), F32)], axis=0
        )
        qkv_out_ref[...] = qkv_ref[...].astype(F32)
        qv_ref[...] = small[49:51, :]
        crpe_ref[...] = small[:49, :]
        proj_out_ref[...] = proj_ref[...].astype(F32)
        fc1_out_ref[...] = fc1_ref[...].astype(F32)
        bias_ref[...] = small[64:68, :]
        fc2_out_ref[...] = fc2_ref[...].astype(F32)


def finish(me, pieces, fc1, fc2, small, proj, qkv, last):
    rows = pieces[0].shape[0]
    shapes = [
        (9, LANES), (8, LANES), qkv.shape, (2, LANES), (49, LANES), proj.shape, fc1.shape,
        (4, LANES), fc2.shape,
    ]
    return pl.pallas_call(
        finish_kernel,
        grid_spec=pltpu.PrefetchScalarGridSpec(
            num_scalar_prefetch=1,
            grid=(4,),
            in_specs=[once((rows, LANES))] * 4
            + [once(item.shape) for item in (fc1, fc2, small, proj, qkv, last)],
            out_specs=[
                pl.BlockSpec((rows, LANES), lambda i, me: (lax.bitwise_xor(me[0], i), 0)),
            ] + [once(shape) for shape in shapes],
        ),
        out_shape=[like((4 * rows, LANES), F32)] + [like(shape, F32) for shape in shapes],
        compiler_params=params(),
        name="finish",
    )(me, *pieces, fc1, fc2, small, proj, qkv, last)


def body(
    block_in, crop_ids, cotangent, cpe_kernel, cpe_bias, norm1_gain, norm1_shift, qkv_weight,
    qv_bias, crpe_kernel, proj_weight, proj_bias, norm2_gain, norm2_shift, fc1_weight, fc1_bias,
    fc2_weight, fc2_bias,
):
    head = lax.axis_index("head")
    me = head.reshape(1).astype(jnp.int32)
    rows = block_in.shape[0] // 4
    ids = crop_ids.reshape(crop_ids.shape[0], PLACES)

    def swap(values, move):
        return lax.ppermute(values, "head", [(item, item ^ move) for item in range(4)])

    packed = jnp.concatenate([
        cpe_kernel, crpe_kernel, cpe_bias[None], norm1_gain[None], norm1_shift[None], qv_bias,
        proj_bias[None], norm2_gain[None], norm2_shift[None], fc2_bias[None],
        fc1_bias.reshape(4, LANES), jnp.zeros((1, LANES), BF16),
    ]).astype(F32)
    own_weights = jnp.concatenate([fc1_weight, fc2_weight, proj_weight])
    extra = padded_rows(own_weights.shape[0], lax.axis_size("dp")) - own_weights.shape[0]
    if extra:
        own_weights = jnp.pad(own_weights, ((0, extra), (0, 0)))
    first, hidden, query, key, value, x, qkv, small, far_weights = head_part(
        ids, packed, qkv_weight.reshape(D, 3 * LANES), block_in, own_weights
    )
    cotangent, query = lax.optimization_barrier((cotangent, query))
    cot_pieces = [
        lax.dynamic_slice_in_dim(cotangent, lax.bitwise_xor(head, move) * rows, rows, 0)
        for move in range(4)
    ]
    cot_parts = [cot_pieces[0]] + [swap(cot_pieces[move], move) for move in (1, 2, 3)]

    soft, context, conv, attended = front(ids, query, key, value, small)
    results = middle(attended, first, cot_parts, small, own_weights, far_weights)
    second_grad, att_grad, fc_mid, proj_grad, middle_sum, bias_grad = results[4:]
    out_parts = [results[0]] + [swap(results[move], move) for move in (1, 2, 3)]
    three, qkv_grad, small_grad = back(
        ids, att_grad, query, value, soft, context, conv, hidden, small, middle_sum, bias_grad
    )
    three, out_parts = lax.optimization_barrier((three, out_parts))
    results = tail(
        ids, x, three, first, second_grad, small, qkv, fc_mid, qkv_grad, proj_grad, small_grad
    )
    (input_grad, cpe_g, vectors, qkv_g, qv_g, crpe_g, proj_g, fc1_g, bias_g, fc2_g) = finish(
        me, results[:4], *results[4:]
    )
    return (
        collect(me, out_parts), input_grad, cpe_g, vectors[0], vectors[1], vectors[2],
        qkv_g.reshape(D, 3, LANES), qv_g, crpe_g, proj_g, vectors[3], vectors[4], vectors[5],
        fc1_g, bias_g.reshape(D), fc2_g, vectors[6],
    )


def solution(mesh):
    return jax.shard_map(
        body,
        mesh=mesh,
        in_specs=(
            P("dp", "head"), P("dp", None, None), P("dp", "head"), P(None, "head"), P("head"),
            P("head"), P("head"), P(None, None, "head"), P(None, "head"), P(None, "head"),
            P("head", None), P("head"), P("head"), P("head"), P(None, "head"), P("head"),
            P("head", None), P("head"),
        ),
        out_specs=(
            P("dp", "head"), P("dp", "head"), P(None, "head"), P("head"), P("head"), P("head"),
            P(None, None, "head"), P(None, "head"), P(None, "head"), P("head", None), P("head"),
            P("head"), P("head"), P(None, "head"), P("head"), P("head", None), P("head"),
        ),
        check_vma=False,
    )
```

```python
import jax
import jax.numpy as jnp
from jax import lax
from jax.experimental import pallas as pl
from jax.experimental.pallas import tpu as pltpu
from jax.sharding import PartitionSpec as P

D = 512
HEADS = 8
HEAD_DIM = 64
HIDDEN = 2048
SIDE = 16
PLACES = 256
LANES = 128
TILES = 4
REACH = (1, 2, 3, 3)
GAP = 3
GRID_ROWS = SIDE + 3 * GAP + 1
EPSILON = 1e-06
SCALE = HEAD_DIM ** (-0.5)
F32 = jnp.float32
BF16 = jnp.bfloat16


def dot(left, right, dims):
    return lax.dot_general(left, right, (dims, ((), ())), preferred_element_type=F32)


def nn(left, right):
    return dot(left, right, ((1,), (0,)))


def nt(left, right):
    return dot(left, right, ((1,), (1,)))


def tn(left, right):
    return dot(left, right, ((0,), (0,)))


def lane(tile):
    return pl.ds(LANES * tile, LANES)


def fill_masks(cut, col_cuts, mask_ref):
    col = lax.broadcasted_iota(jnp.int32, (SIDE, LANES), 0)
    for band in range(2):
        here = (col >= col_cuts[band]).astype(jnp.int32)
        for step in range(-3, 4):
            if step == 0:
                continue
            there = (col + step >= col_cuts[band]).astype(jnp.int32)
            good = (col + step >= 0) & (col + step < SIDE) & (here == there)
            mask_ref[band, step + 3] = jnp.where(good, 1.0, 0.0).astype(F32)


def place_ids(cut, col_cuts):
    place = lax.broadcasted_iota(jnp.int32, (PLACES, LANES), 0)
    row = lax.shift_right_logical(place, 4)
    col = lax.bitwise_and(place, 15)
    band = (row >= cut).astype(jnp.int32)
    col_cut = jnp.where(band > 0, col_cuts[1], col_cuts[0])
    side = (col >= col_cut).astype(jnp.int32)
    return band, side


def spread(read_row, reach, cut, mask_ref, grid_ref, plane):
    zero = jnp.zeros((GAP * SIDE, LANES), F32)
    for step in range(-reach, reach + 1):
        start = pl.multiple_of(SIDE * (GAP + cut), SIDE)
        grid_ref[plane + step, pl.ds(start, GAP * SIDE), :] = zero
    for row in range(SIDE):
        lower = (row >= cut).astype(jnp.int32)
        start = pl.multiple_of(SIDE * (row + GAP + GAP * lower), SIDE)
        values = read_row(row)
        for step in range(-reach, reach + 1):
            moved = values
            if step != 0:
                moved = pltpu.roll(values, (-step) % SIDE, 0) * mask_ref[lower, step + 3]
            grid_ref[plane + step, pl.ds(start, SIDE), :] = moved


def add_to(store, key, term):
    store[key] = term if key not in store else store[key] + term


def over_bands(reach, cut, body):
    every = range(2 * reach + 2)
    for lower in range(2):
        first = cut if lower else 0
        height = SIDE - cut if lower else cut
        pairs = (height + 1) // 2
        shift = GAP * lower + GAP - reach

        def pair(index, places):
            row = first + 2 * index
            body(row, row + shift, first + height - 1, places)

        def inner(index, carry):
            pair(index, every)
            return carry

        pair(0, every[reach:])
        lax.fori_loop(1, pairs - 1, inner, 0)
        pair(pairs - 1, every[: reach + 2])


def conv_tiles(items, reach, cut, grid_ref, taps_ref, tap_reach, out_ref):
    width = 2 * tap_reach + 1
    chains = 3

    def body(row, base, last, places):
        for tile, plane in items:
            total = {}
            for step in range(-reach, reach + 1):
                taps = [
                    taps_ref[(dr + tap_reach) * width + step + tap_reach, :, lane(tile)]
                    for dr in range(-reach, reach + 1)
                ]
                for place in places:
                    for half in range(2):
                        start = pl.multiple_of(SIDE * (base + place) + 8 * half, 8)
                        field = grid_ref[plane + step, pl.ds(start, 8), :]
                        for out in range(2):
                            tap = place - out
                            if 0 <= tap <= 2 * reach:
                                add_to(total, (out, half, step % chains), taps[tap] * field)
            for out in range(2):
                for half in range(2):
                    start = pl.multiple_of(SIDE * (row + out) + 8 * half, 8)
                    out_ref[pl.ds(start, 8), lane(tile)] = sum(
                        [total[out, half, chain] for chain in range(1, chains)], total[out, half, 0]
                    )

    over_bands(reach, cut, body)


def conv_back_tiles(items, reach, cut, grid_ref, taps_ref, tap_reach, other_ref, out_ref, sum_ref):
    width = 2 * tap_reach + 1
    chains = 2

    def body(row, base, last, places):
        keep = jnp.where(row + 1 > last, 0.0, 1.0).astype(F32)
        for tile, plane in items:
            other = {}
            for out in range(2):
                for half in range(2):
                    start = pl.multiple_of(SIDE * (row + out) + 8 * half, 8)
                    value = other_ref[pl.ds(start, 8), lane(tile)]
                    other[out, half] = value * keep if out else value
            total = {}
            for step in range(-reach, reach + 1):
                sums = {}
                ids = [
                    (tap_reach - dr) * width + tap_reach - step for dr in range(-reach, reach + 1)
                ]
                taps = [taps_ref[item, :, lane(tile)] for item in ids]
                for place in places:
                    for half in range(2):
                        start = pl.multiple_of(SIDE * (base + place) + 8 * half, 8)
                        field = grid_ref[plane + step, pl.ds(start, 8), :]
                        for out in range(2):
                            tap = place - out
                            if 0 <= tap <= 2 * reach:
                                add_to(total, (out, half, step % chains), taps[tap] * field)
                                add_to(sums, tap, other[out, half] * field)
                for tap, part in sums.items():
                    sum_ref[ids[tap], :, lane(tile)] += part
            for out in range(2):
                for half in range(2):
                    start = pl.multiple_of(SIDE * (row + out) + 8 * half, 8)
                    out_ref[pl.ds(start, 8), lane(tile)] = sum(
                        [total[out, half, chain] for chain in range(1, chains)], total[out, half, 0]
                    )

    over_bands(reach, cut, body)


def row_mean(values):
    return jnp.sum(values, axis=1, keepdims=True) * (1.0 / D)


def pick(ids, rows):
    out = rows[0]
    for crop in range(1, 4):
        out = jnp.where(ids >= crop, rows[crop], out)
    return out


def crop_reduce(ids, values, op, empty):
    return [op(jnp.where(ids == crop, values, empty), axis=0, keepdims=True) for crop in range(4)]


def head_block():
    row = lax.broadcasted_iota(jnp.int32, (2 * LANES, 2 * LANES), 0)
    col = lax.broadcasted_iota(jnp.int32, (2 * LANES, 2 * LANES), 1)
    same = lax.bitwise_and(row, HEAD_DIM) == lax.bitwise_and(col, HEAD_DIM)
    return jnp.where(same, 1.0, 0.0).astype(F32)


def both(values, masks):
    return jnp.concatenate([values * masks[0], values * masks[1]], axis=1)


def read_cuts(ids_ref, canvases):
    canvas = lax.axis_index("head") * canvases + pl.program_id(0)

    def count(places, bound):
        return sum(jnp.where(ids_ref[canvas, place] < bound, 1, 0) for place in places)

    cut = count(range(0, PLACES, SIDE), 2)
    upper = count(range(SIDE), 1)
    lower = count(range(PLACES - SIDE, PLACES), 3)
    return cut, (upper, lower)


SMALL_SIZE = 72
(CPE, CRPE, CPE_BIAS, GAIN1, SHIFT1, QUERY_BIAS, VALUE_BIAS, PROJ_BIAS, GAIN2, SHIFT2, FC2_BIAS, FC1_BIAS) = (
    0, 9, 58, 59, 60, 61, 62, 63, 64, 65, 66, 67,
)


def spread_small(small_in, small_ref):
    me = lax.axis_index("head")
    for tile in range(TILES):
        small_ref[:, lane(tile)] = small_in[lax.bitwise_xor(me, tile)]


def outer_taps(tap):
    return max(abs(tap // 7 - 3), abs(tap % 7 - 3)) > 2


def keep_head(tap, tile, values):
    if tile != 2 or not outer_taps(tap):
        return values
    col = lax.broadcasted_iota(jnp.int32, values.shape, len(values.shape) - 1)
    return jnp.where(col < HEAD_DIM, 0.0, values)


def spread_taps(small_ref, row, count, masked, taps_ref):
    for tap in range(count):
        for tile in range(TILES):
            values = jnp.broadcast_to(small_ref[row + tap : row + tap + 1, lane(tile)], (8, LANES))
            taps_ref[tap, :, lane(tile)] = keep_head(tap, tile, values) if masked else values


def whole(shape):
    return pl.BlockSpec(shape, lambda *_: (0,) * len(shape))


def once(shape):
    return pl.BlockSpec(shape, lambda *_: (0,) * len(shape), pipeline_mode=pl.Buffered(1))


def rows_spec(width, base=0):
    return pl.BlockSpec((PLACES, width), lambda i, *_: (i + base, 0))


def context_spec(base):
    return pl.BlockSpec((1, TILES, 2 * LANES, 2 * LANES), lambda i, *_: (i + base, 0, 0, 0))


def like(shape, dtype):
    return jax.ShapeDtypeStruct(shape, dtype)


def params(**given):
    return pltpu.CompilerParams(vmem_limit_bytes=58 * 2**20, **given)


MESH = pl.DeviceIdType.MESH
PIECE_ROWS = 256
SMALL_ROWS = 128


def peer(move):
    return (lax.axis_index("dp"), lax.bitwise_xor(lax.axis_index("head"), move))


def meet(peers):
    barrier = pltpu.get_barrier_semaphore()
    for item in peers:
        pl.semaphore_signal(barrier, inc=1, device_id=item, device_id_type=MESH)
    pl.semaphore_wait(barrier, len(peers))


def remote(source, target, send, receive, device):
    return pltpu.make_async_remote_copy(
        src_ref=source, dst_ref=target, send_sem=send, recv_sem=receive,
        device_id=device, device_id_type=MESH,
    )


def plan_pieces(shapes, count):
    pieces = []
    for item, (rows, lanes) in enumerate(shapes):
        height = min(PIECE_ROWS, rows)
        for start in range(0, rows, height):
            pieces.append((item, start, height, padded_rows(height, count), lanes))
    return pieces


def padded_rows(height, count):
    unit = 16 * count
    return -(-height // unit) * unit


def place_on_dp():
    dp = lax.axis_index("dp")
    return dp, lax.rem(dp, 2), dp // 2


def low_peer():
    dp, low, _ = place_on_dp()
    return (dp + 1 - 2 * low, lax.axis_index("head"))


def high_peer(step, group):
    _, low, high = place_on_dp()
    return (lax.rem(high + step, group) * 2 + low, lax.axis_index("head"))


def aligned(index, size):
    return pl.ds(pl.multiple_of(index * size, size), size)


class HighSum:
    def __init__(self, count, mid, part, whole, got, send, receive, slot):
        self.group = count // 2
        self.got = got
        self.mid, self.part, self.whole = mid, part, whole
        self.send, self.receive, self.slot = send, receive, slot
        self.half = mid.shape[0]
        self.size = self.half // self.group

    def copy(self, source, target, slot, device):
        return remote(
            source, target, self.send.at[self.slot + slot], self.receive.at[self.slot + slot], device
        )

    def high(self, step):
        _, _, high = place_on_dp()
        other = lax.rem(high + step, self.group)
        return self.copy(
            self.mid.at[aligned(other, self.size)], self.part.at[step - 1], step - 1,
            high_peer(step, self.group),
        )

    def spot(self):
        dp, low, high = place_on_dp()
        return self.whole.at[aligned(low * self.group + high, self.size)]

    def share(self, step):
        spot = self.spot()
        return self.copy(spot, spot, self.group - 2 + step, high_peer(step, self.group))

    def last(self):
        _, low, _ = place_on_dp()
        here = self.whole.at[aligned(low, self.half)]
        return self.copy(here, self.got, 2 * self.group - 2, low_peer())

    def to_high(self):
        for step in range(1, self.group):
            self.high(step).start()

    def share_high(self):
        _, _, high = place_on_dp()
        total = self.mid[aligned(high, self.size), :].astype(F32)
        for step in range(1, self.group):
            self.high(step).wait()
            total += self.part[step - 1].astype(F32)
        self.spot()[...] = total.astype(BF16)
        for step in range(1, self.group):
            self.share(step).start()

    def share_low(self):
        for step in range(1, self.group):
            self.share(step).wait()
        self.last().start()

    def finish(self):
        _, low, _ = place_on_dp()
        self.last().wait()
        self.whole[aligned(1 - low, self.half), :] = self.got[...]


def high_slots(count):
    return count - 1


class FullSum:
    def __init__(self, count, grad, span, near, far, whole, mid, low, part, got, send, receive, slot):
        self.grad, self.span, self.near, self.far = grad, span, near, far
        self.whole, self.mid, self.low = whole, mid, low
        self.height = far.shape[0]
        self.send, self.receive, self.slot = send, receive, slot
        self.rest = HighSum(count, mid, part, whole, got, send, receive, slot + 4)

    def copy(self, source, target, slot, device):
        return remote(
            source, target, self.send.at[self.slot + slot], self.receive.at[self.slot + slot], device
        )

    def near_copy(self, item):
        return self.copy(
            self.grad.at[1 + 2 * item, self.span], self.near.at[item], item, peer(1)
        )

    def far_copy(self):
        return self.copy(self.whole.at[: self.height], self.far, 2, peer(2))

    def low_copy(self):
        _, low, _ = place_on_dp()
        return self.copy(self.whole.at[aligned(1 - low, self.mid.shape[0])], self.low, 3, low_peer())

    def to_core(self):
        self.near_copy(1).start()
        self.near_copy(0).start()

    def to_far(self):
        self.near_copy(1).wait()
        self.whole[: self.height, :] = (
            self.grad[2, self.span, :].astype(F32) + self.near[1].astype(F32)
        ).astype(BF16)
        self.far_copy().start()

    def to_low(self):
        self.near_copy(0).wait()
        self.far_copy().wait()
        self.whole[: self.height, :] = (
            self.grad[0, self.span, :].astype(F32) + self.near[0].astype(F32)
            + self.far[...].astype(F32)
        ).astype(BF16)
        rows = self.whole.shape[0]
        if rows > self.height:
            self.whole[self.height :, :] = jnp.zeros((rows - self.height, self.whole.shape[1]), BF16)
        self.low_copy().start()

    def to_high(self):
        _, low, _ = place_on_dp()
        self.low_copy().wait()
        half = self.mid.shape[0]
        self.mid[...] = (
            self.whole[aligned(low, half), :].astype(F32) + self.low[...].astype(F32)
        ).astype(BF16)
        self.rest.to_high()


def sum_scratch(pieces, count):
    scratch = []
    for _, _, height, padded, lanes in pieces:
        scratch += [
            pltpu.VMEM((2, height, lanes), BF16), pltpu.VMEM((height, lanes), BF16),
            pltpu.VMEM((padded, lanes), BF16), pltpu.VMEM((padded // 2, lanes), BF16),
            pltpu.VMEM((padded // 2, lanes), BF16),
            pltpu.VMEM((count // 2 - 1, padded // count, lanes), BF16),
            pltpu.VMEM((padded // 2, lanes), BF16),
        ]
    return scratch


def step_masks(cut, col_cuts):
    place = lax.broadcasted_iota(jnp.int32, (PLACES, LANES), 0)
    row = lax.shift_right_logical(place, 4)
    col = lax.bitwise_and(place, 15)
    col_cut = jnp.where(row >= cut, col_cuts[1], col_cuts[0])
    rows = {
        1: (row < SIDE - 1) & (row + 1 != cut),
        -1: (row > 0) & (row != cut),
    }
    cols = {
        1: (col < SIDE - 1) & (col + 1 != col_cut),
        -1: (col > 0) & (col != col_cut),
    }
    return [
        {key: jnp.where(mask, 1.0, 0.0).astype(F32) for key, mask in masks.items()}
        for masks in (rows, cols)
    ]


def shift_rows(values, step):
    if step == 0:
        return values
    zero = jnp.zeros((SIDE, values.shape[1]), values.dtype)
    if step > 0:
        return jnp.concatenate([values[SIDE:], zero], axis=0)
    return jnp.concatenate([zero, values[:-SIDE]], axis=0)


def shift_cols(values, masks, step):
    if step == 0:
        return values
    return pltpu.roll(values, (-step) % PLACES, 0) * masks[step]


def head_kernel(
    canvases, count, ids_ref, small_own, qkv_own, x_in, qkv_in, share_in,
    first_ref, hidden_ref, query_ref, key_ref, value_ref, x_out, qkv_ref, small_out, far_out,
    x_ref, landing_ref, mine_ref, small_ref, qkv_all, small_got, send, receive, weight_send, weight_receive,
    share_send, share_receive, local,
):
    me = lax.axis_index("head")
    step = pl.program_id(0)
    rows = canvases * PLACES

    def piece(index, move):
        start = pl.multiple_of(lax.bitwise_xor(me, move) * rows + index * PLACES, PLACES)
        return remote(
            x_in.at[pl.ds(start, PLACES)], landing_ref.at[index, move - 1], send.at[index, move - 1],
            receive.at[index, move - 1], peer(move),
        )

    def weight(number, source, target, move):
        return remote(source, target, weight_send.at[number], weight_receive.at[number], peer(move))

    far = weight(0, qkv_in, qkv_all.at[1], 2)
    near = weight(1, qkv_in, qkv_all.at[0], 1)
    relay = weight(2, qkv_all.at[1], qkv_all.at[2], 1)
    smalls = [weight(2 + move, small_got.at[0], small_got.at[move], move) for move in (1, 2, 3)]
    mine = pltpu.make_async_copy(x_in.at[aligned(me, rows)], mine_ref, local.at[0])
    dp = lax.axis_index("dp")
    spot = aligned(dp, share_in.shape[0] // count)
    share = remote(share_in.at[spot], far_out.at[spot], share_send.at[0], share_receive.at[0], peer(2))
    group = count // 2
    _, low, high = place_on_dp()
    spread_high = [
        remote(
            far_out.at[spot], far_out.at[spot], share_send.at[hop], share_receive.at[hop],
            high_peer(hop, group),
        )
        for hop in range(1, group)
    ]
    spread_low = []
    for hop in range(group):
        source = lax.rem(high - hop + group, group) * 2 + low
        there = aligned(source, share_in.shape[0] // count)
        spread_low.append(
            remote(
                far_out.at[there], far_out.at[there], share_send.at[group + hop],
                share_receive.at[group + hop], low_peer(),
            )
        )

    @pl.when(step == 0)
    def _():
        mine.start()
        small_got[0] = small_own[...]
        meet(
            [peer(move) for move in (1, 2, 3)] + [low_peer()]
            + [high_peer(hop, group) for hop in range(1, group)]
        )
        for item in smalls:
            item.start()
        share.start()
        for move in (2, 3, 1):
            piece(0, move).start()
        far.start()
        near.start()

        def send_piece(index, carry):
            for move in (2, 3, 1):
                piece(index, move).start()
            return carry

        lax.fori_loop(1, canvases, send_piece, 0)
        for item in smalls:
            item.wait()
        for move in range(4):
            small_ref[:, aligned(lax.bitwise_xor(me, move), LANES)] = small_got[move]
            small_out[move] = small_got[move]
        mine.wait()

    for hop in range(1, group):

        @pl.when(step == min(1 + hop, canvases - 1))
        def _():
            spread_high[hop - 1].wait()
            spread_low[hop].start()

    @pl.when(step == canvases - 1)
    def _():
        for item in spread_low:
            item.wait()

    x_ref[:, aligned(me, LANES)] = mine_ref[aligned(step, PLACES), :].astype(F32)
    for move in (1, 2, 3):
        piece(step, move).wait()
        x_ref[:, aligned(lax.bitwise_xor(me, move), LANES)] = landing_ref[step, move - 1].astype(F32)
    rows_mask, cols_mask = step_masks(*read_cuts(ids_ref, canvases))
    for tile in range(TILES):
        field = x_ref[:, lane(tile)]
        moved = [shift_cols(field, cols_mask, col) for col in (-1, 0, 1)]
        result = field + small_ref[CPE_BIAS : CPE_BIAS + 1, lane(tile)]
        for row in (-1, 0, 1):
            line = None
            for col in (-1, 0, 1):
                tap = CPE + (row + 1) * 3 + col + 1
                term = jnp.broadcast_to(small_ref[tap : tap + 1, lane(tile)], (PLACES, LANES)) * moved[col + 1]
                line = term if line is None else line + term
            line = shift_rows(line, row)
            result = result + (line * rows_mask[row] if row else line)
        first_ref[:, lane(tile)] = result
    x_out[...] = x_ref[...].astype(BF16)
    first = first_ref[...]
    center = row_mean(first)
    square = row_mean(first * first)
    inverse = lax.rsqrt(square - center * center + EPSILON)
    hidden = (
        (first - center) * inverse * small_ref[GAIN1 : GAIN1 + 1, :] + small_ref[SHIFT1 : SHIFT1 + 1, :]
    ).astype(BF16)
    hidden_ref[...] = hidden

    @pl.when(step == 0)
    def _():
        share.wait()
        for item in spread_high + spread_low[:1]:
            item.start()
        far.wait()
        relay.start()
        near.wait()
        relay.wait()
        qkv_ref[0] = qkv_own[...]
        for move in (1, 2, 3):
            qkv_ref[move] = qkv_all[move - 1]

    for tile in range(TILES):
        three = nn(hidden, qkv_ref[lax.bitwise_xor(me, tile)])
        query_ref[:, lane(tile)] = (
            three[:, :LANES] + small_ref[QUERY_BIAS : QUERY_BIAS + 1, lane(tile)]
        ).astype(BF16)
        key_ref[:, lane(tile)] = three[:, LANES : 2 * LANES].astype(BF16)
        value_ref[:, lane(tile)] = (
            three[:, 2 * LANES :] + small_ref[VALUE_BIAS : VALUE_BIAS + 1, lane(tile)]
        ).astype(BF16)


def head_part(ids, small, qkv, block_in, share):
    count = lax.axis_size("dp")
    rows = block_in.shape[0] // 4
    canvases = rows // PLACES
    wide = rows_spec(D)
    hbm = pl.BlockSpec(memory_space=pl.ANY)
    return pl.pallas_call(
        lambda *refs: head_kernel(canvases, count, *refs),
        grid=(canvases,),
        in_specs=[
            pl.BlockSpec(memory_space=pltpu.SMEM), once(small.shape), once(qkv.shape), hbm, hbm, hbm,
        ],
        out_specs=[wide] * 6 + [once((4,) + qkv.shape), once((4,) + small.shape), hbm],
        out_shape=[like((rows, D), F32)] + [like((rows, D), BF16)] * 5 + [
            like((4,) + qkv.shape, BF16), like((4,) + small.shape, F32), like(share.shape, BF16),
        ],
        scratch_shapes=[
            pltpu.VMEM((PLACES, D), F32), pltpu.VMEM((canvases, 3, PLACES, LANES), BF16),
            pltpu.VMEM((rows, LANES), BF16), pltpu.VMEM((SMALL_SIZE, D), F32),
            pltpu.VMEM((3,) + qkv.shape, BF16), pltpu.VMEM((4,) + small.shape, F32),
            pltpu.SemaphoreType.DMA((canvases, 3)), pltpu.SemaphoreType.DMA((canvases, 3)),
            pltpu.SemaphoreType.DMA((6,)), pltpu.SemaphoreType.DMA((6,)),
            pltpu.SemaphoreType.DMA((count,)), pltpu.SemaphoreType.DMA((count,)),
            pltpu.SemaphoreType.DMA((1,)),
        ],
        compiler_params=params(collective_id=1, has_side_effects=True),
        name="head",
    )(ids, small, qkv, block_in, qkv, share)


def front_kernel(
    canvases, ids_ref, query_ref, key_ref, value_ref, small_in,
    soft_ref, context_ref, conv_ref, attended_ref,
    mask_ref, grid_ref, out_ref, x_ref, small_ref, crpe_ref,
):
    cut, col_cuts = read_cuts(ids_ref, canvases)

    @pl.when(pl.program_id(0) == 0)
    def _():
        grid_ref[...] = jnp.zeros_like(grid_ref)
        spread_small(small_in, small_ref)
        spread_taps(small_ref, CRPE, 49, True, crpe_ref)

    fill_masks(cut, col_cuts, mask_ref)
    band, side = place_ids(cut, col_cuts)
    ids = 2 * band + side
    sides = [(side == item).astype(F32).astype(BF16) for item in range(2)]
    bands = [(band == item).astype(F32).astype(BF16) for item in range(2)]
    blocks = head_block()
    for tile in range(TILES):
        query = query_ref[:, lane(tile)]
        keys = key_ref[:, lane(tile)].astype(F32)
        value = value_ref[:, lane(tile)]
        highest = crop_reduce(ids, keys, jnp.max, -1e30)
        powers = jnp.exp(keys - pick(ids, highest))
        totals = crop_reduce(ids, powers, jnp.sum, 0.0)
        soft = (powers * pick(ids, [1.0 / item for item in totals])).astype(BF16)
        soft_ref[:, lane(tile)] = soft
        context = (tn(both(soft, sides), both(value, bands)) * blocks).astype(BF16)
        context_ref[0, tile] = context
        factor = nn(both(query, sides), context)
        x_ref[:, lane(tile)] = jnp.where(band > 0, factor[:, LANES:], factor[:, :LANES]) * SCALE
    for tile in range(TILES):
        spread(
            lambda row: value_ref[SIDE * row : SIDE * row + SIDE, lane(tile)].astype(F32),
            REACH[tile], cut, mask_ref, grid_ref, 3,
        )
        conv_tiles(((tile, 3),), REACH[tile], cut, grid_ref, crpe_ref, 3, out_ref)
    conv = out_ref[:PLACES, :]
    conv_ref[...] = conv.astype(BF16)
    attended_ref[...] = (x_ref[...] + query_ref[...].astype(F32) * conv).astype(BF16)


def front(ids, query, key, value, small):
    rows = query.shape[0]
    count = rows // PLACES
    wide = rows_spec(D)
    return pl.pallas_call(
        lambda *refs: front_kernel(count, *refs),
        grid_spec=pltpu.PrefetchScalarGridSpec(
            num_scalar_prefetch=1,
            grid=(count,),
            in_specs=[wide, wide, wide, once(small.shape)],
            out_specs=[wide, context_spec(0), wide, wide],
            scratch_shapes=[
                pltpu.VMEM((2, 7, SIDE, LANES), F32),
                pltpu.VMEM((7, GRID_ROWS * SIDE, LANES), F32),
                pltpu.VMEM((PLACES + SIDE, D), F32),
                pltpu.VMEM((PLACES, D), F32),
                pltpu.VMEM((SMALL_SIZE, D), F32),
                pltpu.VMEM((49, 8, D), F32),
            ],
        ),
        out_shape=[
            like((rows, D), BF16), like((count, TILES, 2 * LANES, 2 * LANES), BF16),
            like((rows, D), BF16), like((rows, D), BF16),
        ],
        compiler_params=params(),
        cost_estimate=pl.CostEstimate(
            flops=rows * D * D * 40, bytes_accessed=count * 10**7, transcendentals=0
        ),
        name="front",
    )(ids, query, key, value, small)


def gelu_both(pre):
    power = jnp.exp(pre * pre * -0.5)
    t = 1.0 / (1.0 + jnp.abs(pre) * (0.3275911 * 0.7071067811865476))
    poly = 0.5 * 1.061405429
    for item in (-1.453152027, 1.421413741, -0.284496736, 0.254829592):
        poly = poly * t + 0.5 * item
    tail = poly * t * power
    cdf = jnp.where(pre >= 0.0, 1.0 - tail, tail)
    return pre * cdf, cdf + pre * power * 0.3989422804014327


BLOCK = 1024


def middle_kernel(
    count,
    attended_ref, first_ref, cot0_ref, cot1_ref, cot2_ref, cot3_ref, small_in, own_weights,
    far_weights,
    out0_ref, out1_ref, out2_ref, out3_ref, second_grad_ref, att_grad_ref, fc_mid_ref,
    proj_grad_ref, sum_ref, bias_grad_ref,
    cot_ref, hat_ref, inverse_ref, hidden_ref, total_ref, back_ref, active_ref, pre_grad_ref,
    grads_ref, near_ref, far_ref, own_ref, low_ref, small_ref, weights_ref, send, receive, fetch,
):
    me = lax.axis_index("head")
    step = pl.program_id(0)
    rows = attended_ref.shape[0]
    blocks = rows // BLOCK
    _, low, _ = place_on_dp()
    half = low_ref.shape[1]

    def near(item, kind):
        return remote(
            grads_ref.at[2 * item, kind], near_ref.at[item, kind], send.at[2 * item + kind],
            receive.at[2 * item + kind], peer(1),
        )

    def far(kind):
        return remote(
            grads_ref.at[1, kind], far_ref.at[kind], send.at[4 + kind], receive.at[4 + kind], peer(2)
        )

    def to_low(kind):
        return remote(
            own_ref.at[kind, aligned(1 - low, half)], low_ref.at[kind], send.at[6 + kind],
            receive.at[6 + kind], low_peer(),
        )

    def part(index):
        return aligned(index, BLOCK)

    shard = 3 - step
    fc1 = weights_ref.at[shard, :D]
    fc2 = weights_ref.at[shard, D : 2 * D]

    def proj(tile):
        return weights_ref[lax.bitwise_xor(me, tile), 2 * D : 2 * D + LANES, :]

    def relay(number, source, target, part):
        return remote(
            source.at[part], weights_ref.at[target, part], send.at[8 + number], receive.at[8 + number],
            peer(1),
        )

    narrow, broad = pl.ds(2 * D, LANES), pl.ds(0, 2 * D)
    relays = [
        relay(0, own_weights, 1, narrow), relay(1, far_weights, 3, narrow),
        relay(2, far_weights, 3, broad), relay(3, own_weights, 1, broad),
    ]

    @pl.when(step == 0)
    def _():
        loads = [
            pltpu.make_async_copy(own_weights.at[pl.ds(0, 2 * D + LANES)], weights_ref.at[0], fetch.at[0]),
            pltpu.make_async_copy(far_weights.at[pl.ds(0, 2 * D + LANES)], weights_ref.at[2], fetch.at[1]),
        ]
        for move, piece_ref in enumerate((cot0_ref, cot1_ref, cot2_ref, cot3_ref)):
            spot = cot_ref.at[:, aligned(lax.bitwise_xor(me, move), LANES)]
            loads.append(pltpu.make_async_copy(piece_ref, spot, fetch.at[2 + move]))
        for load in loads:
            load.start()
        meet([peer(1), peer(2), low_peer()])
        for item in relays:
            item.start()
        spread_small(small_in, small_ref)
        own_ref[...] = jnp.zeros_like(own_ref)
        sum_ref[...] = jnp.zeros_like(sum_ref)
        for item in loads + relays[:2]:
            item.wait()

        def enter(index, carry):
            now = part(index)
            second = first_ref[now, :] + small_ref[PROJ_BIAS : PROJ_BIAS + 1, :]
            for tile in range(TILES):
                second += nn(attended_ref[now, lane(tile)], proj(tile))
            center = row_mean(second)
            square = row_mean(second * second)
            inverse = lax.rsqrt(square - center * center + EPSILON)
            hat = (second - center) * inverse
            hidden_ref[now, :] = (
                hat * small_ref[GAIN2 : GAIN2 + 1, :] + small_ref[SHIFT2 : SHIFT2 + 1, :]
            ).astype(BF16)
            hat_ref[now, :] = hat
            inverse_ref[now, :] = jnp.broadcast_to(inverse, (BLOCK, LANES))
            total_ref[now, :] = second + small_ref[FC2_BIAS : FC2_BIAS + 1, :]
            back_ref[now, :] = jnp.zeros((BLOCK, D), F32)
            sum_ref[3:4, :] += jnp.sum(cot_ref[now, :].astype(F32), axis=0, keepdims=True)
            return carry

        lax.fori_loop(0, blocks, enter, 0)
        for item in relays[2:]:
            item.wait()

    bias_grad_ref[0] = jnp.zeros_like(bias_grad_ref[0])

    def chunk(index, carry):
        now = part(index)
        bias = jnp.concatenate(
            [small_in[shard, FC1_BIAS + tile : FC1_BIAS + tile + 1, :] for tile in range(TILES)], axis=1
        )
        pre = nn(hidden_ref[now, :], fc1[...]) + bias
        active, slope = gelu_both(pre)
        active = active.astype(BF16)
        active_ref[now, :] = active
        total_ref[now, :] += nn(active, fc2[...])
        pre_grad_f = nt(cot_ref[now, :], fc2[...]) * slope
        pre_grad = pre_grad_f.astype(BF16)
        pre_grad_ref[now, :] = pre_grad
        back_ref[now, :] += nt(pre_grad, fc1[...])
        bias_grad_ref[0] += jnp.sum(pre_grad_f, axis=0, keepdims=True)
        return carry

    lax.fori_loop(0, blocks, chunk, 0)
    grads_ref[step, 0] = tn(hidden_ref[...], pre_grad_ref[...]).astype(BF16)
    grads_ref[step, 1] = tn(active_ref[...], cot_ref[...]).astype(BF16)

    @pl.when(step == 0)
    def _():
        for kind in range(2):
            near(0, kind).start()

    @pl.when(step == 1)
    def _():
        for kind in range(2):
            near(0, kind).wait()
            grads_ref[1, kind] = (
                grads_ref[1, kind].astype(F32) + near_ref[0, kind].astype(F32)
            ).astype(BF16)
            far(kind).start()

    @pl.when(step == 2)
    def _():
        for kind in range(2):
            near(1, kind).start()

    @pl.when(step == 3)
    def _():
        for kind in range(2):
            near(1, kind).wait()
            far(kind).wait()
            own_ref[kind, :D, :] = (
                grads_ref[3, kind].astype(F32) + near_ref[1, kind].astype(F32)
                + far_ref[kind].astype(F32)
            ).astype(BF16)
            to_low(kind).start()

        def leave(index, carry):
            now = part(index)
            for move, piece_ref in enumerate((out0_ref, out1_ref, out2_ref, out3_ref)):
                piece_ref[now, :] = total_ref[now, aligned(lax.bitwise_xor(me, move), LANES)].astype(BF16)
            hat = hat_ref[now, :]
            norm_grad = back_ref[now, :]
            weighted = norm_grad * small_ref[GAIN2 : GAIN2 + 1, :]
            second_grad = cot_ref[now, :].astype(F32) + inverse_ref[now, 0:1] * (
                weighted - row_mean(weighted) - hat * row_mean(weighted * hat)
            )
            second_grad_ref[now, :] = second_grad
            second_low = second_grad.astype(BF16)
            hidden_ref[now, :] = second_low
            for tile in range(TILES):
                att_grad_ref[now, lane(tile)] = nt(
                    second_low, proj(tile)
                ).astype(BF16)
            sum_ref[1:2, :] += jnp.sum(norm_grad * hat, axis=0, keepdims=True)
            sum_ref[2:3, :] += jnp.sum(norm_grad, axis=0, keepdims=True)
            sum_ref[0:1, :] += jnp.sum(second_low.astype(F32), axis=0, keepdims=True)
            return carry

        lax.fori_loop(0, blocks, leave, 0)
        for tile in range(TILES):
            proj_grad_ref[lax.bitwise_xor(me, tile)] = tn(
                attended_ref[:, lane(tile)], hidden_ref[...]
            ).astype(BF16)
        for kind in range(2):
            to_low(kind).wait()
            fc_mid_ref[kind] = (
                own_ref[kind, aligned(low, half), :].astype(F32) + low_ref[kind].astype(F32)
            ).astype(BF16)


def middle(attended, first, cot_parts, small, own_weights, far_weights):
    rows = attended.shape[0]
    count = lax.axis_size("dp")
    padded = padded_rows(D, count)
    hbm = pl.BlockSpec(memory_space=pl.ANY)
    proj_shape = (4, LANES, D)
    piece = once((rows, LANES))
    wide = once((rows, D))
    line = pl.BlockSpec((1, 1, D), lambda i: (3 - i, 0, 0))
    return pl.pallas_call(
        lambda *refs: middle_kernel(count, *refs),
        grid=(4,),
        in_specs=[
            wide, wide, hbm, hbm, hbm, hbm, once(small.shape), hbm, hbm,
        ],
        out_specs=[
            piece, piece, piece, piece, wide, wide, once((2, padded // 2, D)), once(proj_shape),
            once((8, D)), line,
        ],
        out_shape=[like((rows, LANES), BF16)] * 4 + [
            like((rows, D), F32), like((rows, D), BF16), like((2, padded // 2, D), BF16),
            like(proj_shape, BF16), like((8, D), F32), like((4, 1, D), F32),
        ],
        scratch_shapes=[
            pltpu.VMEM((rows, D), BF16), pltpu.VMEM((rows, D), F32),
            pltpu.VMEM((rows, LANES), F32),
            pltpu.VMEM((rows, D), BF16), pltpu.VMEM((rows, D), F32),
            pltpu.VMEM((rows, D), F32), pltpu.VMEM((rows, D), BF16),
            pltpu.VMEM((rows, D), BF16),
            pltpu.VMEM((4, 2, D, D), BF16), pltpu.VMEM((2, 2, D, D), BF16),
            pltpu.VMEM((2, D, D), BF16), pltpu.VMEM((2, padded, D), BF16),
            pltpu.VMEM((2, padded // 2, D), BF16),
            pltpu.VMEM((SMALL_SIZE, D), F32), pltpu.VMEM((4, 2 * D + LANES, D), BF16),
            pltpu.SemaphoreType.DMA((12,)), pltpu.SemaphoreType.DMA((12,)),
            pltpu.SemaphoreType.DMA((6,)),
        ],
        compiler_params=params(collective_id=2, has_side_effects=True),
        cost_estimate=pl.CostEstimate(flops=rows * D * D * 60, bytes_accessed=3 * 10**7, transcendentals=0),
        name="middle",
    )(attended, first, *cot_parts, small, own_weights, far_weights)


def back_kernel(
    canvases, ids_ref, grad_ref, query_ref, value_ref, soft_ref, context_ref, conv_ref, hidden_ref,
    small_in, middle_sum_ref, bias_grad_ref,
    three_ref, qkv_out_ref, small_out_ref,
    mask_ref, grid_ref, out_ref, other_ref, value_part_ref, qkv_grad_ref, small_ref, crpe_ref,
    crpe_sum_ref, sum_ref, late_ref,
):
    cut, col_cuts = read_cuts(ids_ref, canvases)
    me = lax.axis_index("head")

    @pl.when(pl.program_id(0) == 0)
    def _():
        grid_ref[...] = jnp.zeros_like(grid_ref)
        other_ref[...] = jnp.zeros_like(other_ref)
        qkv_grad_ref[...] = jnp.zeros_like(qkv_grad_ref)
        crpe_sum_ref[...] = jnp.zeros_like(crpe_sum_ref)
        sum_ref[...] = jnp.zeros_like(sum_ref)
        spread_small(small_in, small_ref)
        spread_taps(small_ref, CRPE, 49, True, crpe_ref)

    fill_masks(cut, col_cuts, mask_ref)
    band, side = place_ids(cut, col_cuts)
    ids = 2 * band + side
    sides = [(side == item).astype(F32).astype(BF16) for item in range(2)]
    bands = [(band == item).astype(F32).astype(BF16) for item in range(2)]
    blocks = head_block() * SCALE
    for tile in range(TILES):
        grad = grad_ref[:, lane(tile)]
        query = query_ref[:, lane(tile)]
        value = value_ref[:, lane(tile)]
        soft = soft_ref[:, lane(tile)]
        context = context_ref[0, tile]
        grad_f = grad.astype(F32)
        grad_bands = both(grad, bands)
        context_grad = (tn(both(query, sides), grad_bands) * blocks).astype(BF16)
        part = nt(grad_bands, context)
        part = jnp.where(side > 0, part[:, LANES:], part[:, :LANES])
        query_grad = (
            part * SCALE + grad_f * conv_ref[:, lane(tile)].astype(F32)
        ).astype(BF16)
        soft_grad = nt(both(value, bands), context_grad)
        soft_grad = jnp.where(side > 0, soft_grad[:, LANES:], soft_grad[:, :LANES])
        soft_f = soft.astype(F32)
        inner = crop_reduce(ids, soft_f * soft_grad, jnp.sum, 0.0)
        keys_grad = (soft_f * (soft_grad - pick(ids, inner))).astype(BF16)
        value_part = nn(both(soft, sides), context_grad)
        value_part_ref[:, lane(tile)] = jnp.where(
            band > 0, value_part[:, LANES:], value_part[:, :LANES]
        )
        three_ref[tile, :, :LANES] = query_grad
        three_ref[tile, :, LANES : 2 * LANES] = keys_grad
        sum_ref[0:1, lane(tile)] += jnp.sum(query_grad.astype(F32), axis=0, keepdims=True)
    other_ref[:PLACES, :] = value_ref[...].astype(F32)
    for tile in range(TILES):

        def read_row(row):
            part = pl.ds(SIDE * row, SIDE)
            return grad_ref[part, lane(tile)].astype(F32) * query_ref[part, lane(tile)].astype(F32)

        spread(read_row, REACH[tile], cut, mask_ref, grid_ref, 3)
        conv_back_tiles(
            ((tile, 3),), REACH[tile], cut, grid_ref, crpe_ref, 3, other_ref, out_ref, crpe_sum_ref
        )
    hidden = hidden_ref[...]
    for tile in range(TILES):
        value_grad = (value_part_ref[:, lane(tile)] + out_ref[:PLACES, lane(tile)]).astype(BF16)
        three_ref[tile, :, 2 * LANES :] = value_grad
        sum_ref[1:2, lane(tile)] += jnp.sum(value_grad.astype(F32), axis=0, keepdims=True)
        qkv_grad_ref[lax.bitwise_xor(me, tile)] += tn(hidden, three_ref[tile])

    @pl.when(pl.program_id(0) == pl.num_programs(0) - 1)
    def _():
        qkv_out_ref[...] = qkv_grad_ref[...].astype(BF16)
        late_ref[...] = jnp.zeros_like(late_ref)
        for tap in range(49):
            for tile in range(TILES):
                late_ref[tap : tap + 1, lane(tile)] = keep_head(
                    tap, tile, jnp.sum(crpe_sum_ref[tap, :, lane(tile)], axis=0, keepdims=True)
                )
        late_ref[49:51, :] = sum_ref[0:2, :]
        late_ref[51:55, :] = middle_sum_ref[0:4, :]
        for move in range(4):
            late = late_ref[:, aligned(lax.bitwise_xor(me, move), LANES)]
            small_out_ref[move] = late.astype(BF16)
            small_out_ref[move, 64:80, :] = jnp.concatenate(
                [bias_grad_ref[move, :, lane(tile)] for tile in range(TILES)]
                + [jnp.zeros((12, LANES), F32)],
                axis=0,
            ).astype(BF16)


def back(ids, grad, query, value, soft, context, conv, hidden, small, middle_sum, bias_grad):
    rows = grad.shape[0]
    count = rows // PLACES
    wide = rows_spec(D)
    shards = (4, D, 3 * LANES)
    late = (4, SMALL_ROWS, LANES)
    return pl.pallas_call(
        lambda *refs: back_kernel(count, *refs),
        grid_spec=pltpu.PrefetchScalarGridSpec(
            num_scalar_prefetch=1,
            grid=(count,),
            in_specs=[
                wide, wide, wide, wide, context_spec(0), wide, wide, once(small.shape),
                once(middle_sum.shape), once(bias_grad.shape),
            ],
            out_specs=[
                pl.BlockSpec((TILES, PLACES, 3 * LANES), lambda i, *_: (0, i, 0)),
                once(shards), once(late),
            ],
            scratch_shapes=[
                pltpu.VMEM((2, 7, SIDE, LANES), F32),
                pltpu.VMEM((7, GRID_ROWS * SIDE, LANES), F32),
                pltpu.VMEM((PLACES + SIDE, D), F32),
                pltpu.VMEM((PLACES + SIDE, D), F32),
                pltpu.VMEM((PLACES, D), F32),
                pltpu.VMEM(shards, F32),
                pltpu.VMEM((SMALL_SIZE, D), F32),
                pltpu.VMEM((49, 8, D), F32),
                pltpu.VMEM((49, 8, D), F32),
                pltpu.VMEM((8, D), F32),
                pltpu.VMEM((SMALL_ROWS, D), F32),
            ],
        ),
        out_shape=[
            like((TILES, rows, 3 * LANES), BF16), like(shards, BF16), like(late, BF16),
        ],
        compiler_params=params(),
        cost_estimate=pl.CostEstimate(
            flops=rows * D * D * 64, bytes_accessed=count * 10**7, transcendentals=0
        ),
        name="back",
    )(ids, grad, query, value, soft, context, conv, hidden, small, middle_sum, bias_grad)


LAST_ROWS = 16
STAGES = ((0, 1, 2, 3, 4, 5), (0, 1, 3, 4, 5, 6), (0, 1, 4, 6, 7, 8), (0, 1, 5, 7, 8, 9))
FC_STAGES = ((0, 3, 6), (2, 5, 8))


def tail_kernel(
    count, pieces,
    canvases, ids_ref, x_in, three_ref, first_ref, second_grad_ref, small_params,
    qkv_ref, fc_mid_in, small_in, proj_grad_in, qkv_grad_in,
    out0_ref, out1_ref, out2_ref, out3_ref, fc1_own_ref, fc2_own_ref, small_own_ref, proj_own_ref,
    qkv_own_ref, last_own_ref,
    x_ref, gone_ref, cpe_sum_ref, sum_ref, fc_part_ref, fc_whole_ref, fc_got_ref, mine_ref, first_got_ref,
    total_ref, second_got_ref, piece_send, piece_receive, send, receive, last_send, last_receive,
    cpe_ref, fc_mid_ref, small_ref, proj_grad_ref, qkv_grad_ref, *buffers,
):
    me = lax.axis_index("head")
    dp = lax.axis_index("dp")
    step = pl.program_id(0)
    steps = pl.num_programs(0)
    slots = high_slots(count)
    fc_sums = [
        HighSum(
            count, fc_mid_ref.at[kind], fc_part_ref.at[kind], fc_whole_ref.at[kind],
            fc_got_ref.at[kind], send, receive, kind * slots,
        )
        for kind in range(2)
    ]
    sources = (small_ref, proj_grad_ref, qkv_grad_ref)
    targets = (small_own_ref, proj_own_ref, qkv_own_ref)
    sums = []
    for number, (item, start, height, padded, lanes) in enumerate(pieces):
        near, far, own, mid, low, part, got = buffers[7 * number : 7 * number + 7]
        sums.append(
            FullSum(
                count, sources[item], pl.ds(start, height), near, far, own, mid, low, part, got, send,
                receive, 2 * slots + number * (slots + 4),
            )
        )

    def piece_copy(index, move):
        target = (out1_ref, out2_ref, out3_ref)[move - 1]
        return remote(
            gone_ref.at[index, move - 1], target.at[aligned(index, PLACES)],
            piece_send.at[index, move - 1], piece_receive.at[index, move - 1], peer(move),
        )

    def first_copy(move):
        return remote(
            mine_ref.at[move], first_got_ref.at[move - 1], last_send.at[move - 1],
            last_receive.at[move - 1], peer(move),
        )

    def second_copy(hop):
        return remote(
            total_ref, second_got_ref.at[hop - 1], last_send.at[2 + hop], last_receive.at[2 + hop],
            (lax.rem(dp + hop, count), me),
        )

    @pl.when(step == 0)
    def _():
        meet(
            [peer(1), peer(2), peer(3)] + [(lax.rem(dp + hop, count), me) for hop in range(1, count)]
        )
        spread_small(small_params, cpe_ref)
        fc_mid_ref[...] = fc_mid_in[...]
        qkv_grad_ref[...] = qkv_grad_in[...]
        proj_grad_ref[...] = proj_grad_in[...]
        small_ref[...] = small_in[...]
        cpe_sum_ref[...] = jnp.zeros_like(cpe_sum_ref)
        sum_ref[...] = jnp.zeros_like(sum_ref)

    events = []
    for item, slots_of in zip(sums, STAGES):
        actions = (
            item.to_core, item.to_far, item.to_low, item.to_high, item.rest.share_high, item.rest.share_low,
        )
        events += list(zip(slots_of, actions))
    for item, slots_of in zip(fc_sums, FC_STAGES):
        events += list(zip(slots_of, (item.to_high, item.share_high, item.share_low)))

    def run(when):
        for slot, action in events:
            if slot == when:
                action()

    for when in range(canvases):
        pl.when(step == when)(lambda: run(when))

    norm_grad = nt(three_ref[0], qkv_ref[lax.bitwise_xor(me, 0)])
    for tile in range(1, TILES):
        norm_grad += nt(three_ref[tile], qkv_ref[lax.bitwise_xor(me, tile)])
    first = first_ref[...]
    center = row_mean(first)
    square = row_mean(first * first)
    inverse = lax.rsqrt(square - center * center + EPSILON)
    hat = (first - center) * inverse
    weighted = norm_grad * cpe_ref[GAIN1 : GAIN1 + 1, :]
    first_grad = second_grad_ref[...] + inverse * (
        weighted - row_mean(weighted) - hat * row_mean(weighted * hat)
    )
    sum_ref[0:1, :] += jnp.sum(first_grad, axis=0, keepdims=True)
    sum_ref[1:2, :] += jnp.sum(norm_grad * hat, axis=0, keepdims=True)
    sum_ref[2:3, :] += jnp.sum(norm_grad, axis=0, keepdims=True)
    x_ref[...] = x_in[...].astype(F32)
    rows, cols = step_masks(*read_cuts(ids_ref, canvases))
    results = []
    for tile in range(TILES):
        field = first_grad[:, LANES * tile : LANES * (tile + 1)]
        other = x_ref[:, lane(tile)]
        others = {0: other, 1: shift_rows(other * rows[1], -1), -1: shift_rows(other * rows[-1], 1)}
        moved = [shift_cols(field, cols, col) for col in (-1, 0, 1)]
        result = field
        for row in (-1, 0, 1):
            line = None
            for col in (-1, 0, 1):
                tap = (1 - row) * 3 + 1 - col
                wide_tap = jnp.broadcast_to(cpe_ref[tap : tap + 1, lane(tile)], (PLACES, LANES))
                term = wide_tap * moved[col + 1]
                line = term if line is None else line + term
                product = others[row] * moved[col + 1]
                cpe_sum_ref[tap, :, lane(tile)] += jnp.sum(product.reshape(PLACES // 8, 8, LANES), axis=0)
            line = shift_rows(line, row)
            result = result + (line * rows[row] if row else line)
        results.append(result)
    result = jnp.concatenate(results, axis=1)
    x_ref[...] = result
    out0_ref[...] = x_ref[:, aligned(me, LANES)].astype(BF16)
    for move in (1, 2, 3):
        gone_ref[step, move - 1] = x_ref[:, aligned(lax.bitwise_xor(me, move), LANES)].astype(BF16)
    for move in (2, 3, 1):
        piece_copy(step, move).start()

    @pl.when(step == steps - 1)
    def _():
        sum_ref[3:12, :] = jnp.sum(cpe_sum_ref[...], axis=1)
        for move in range(4):
            mine_ref[move] = sum_ref[:, aligned(lax.bitwise_xor(me, move), LANES)]
        for move in (1, 2, 3):
            first_copy(move).start()
        run(canvases)
        total = mine_ref[0]
        for move in (1, 2, 3):
            first_copy(move).wait()
            total += first_got_ref[move - 1]
        total_ref[...] = total
        for hop in range(1, count):
            second_copy(hop).start()
        run(canvases + 1)
        for item in fc_sums:
            item.finish()
        fc1_own_ref[...] = fc_whole_ref[0, :D, :]
        fc2_own_ref[...] = fc_whole_ref[1, :D, :]
        for hop in range(1, count):
            second_copy(hop).wait()
            total += second_got_ref[hop - 1]
        last_own_ref[...] = total
        for piece, item in zip(pieces, sums):
            item.rest.finish()
            targets[piece[0]][piece[1] : piece[1] + piece[2], :] = item.whole[: piece[2], :]

        def settle(index, carry):
            for move in (1, 2, 3):
                piece_copy(index, move).wait()
            return carry

        lax.fori_loop(0, steps, settle, 0)


def tail(ids, x, three, first, second_grad, params_small, qkv, fc_mid, qkv_grad, proj_grad, small):
    rows = first.shape[0]
    canvases = rows // PLACES
    count = lax.axis_size("dp")
    segments = [small, proj_grad, qkv_grad]
    pieces = plan_pieces([item.shape[1:] for item in segments], count)
    slots = high_slots(count)
    wide = rows_spec(D)
    piece = rows_spec(LANES)
    hbm = pl.BlockSpec(memory_space=pl.ANY)
    half = fc_mid.shape[1]
    group = count // 2
    total_slots = 2 * slots + len(pieces) * (slots + 4)
    last = (LAST_ROWS, LANES)
    return pl.pallas_call(
        lambda *refs: tail_kernel(count, pieces, canvases, *refs),
        grid=(canvases,),
        in_specs=[pl.BlockSpec(memory_space=pltpu.SMEM), wide] + [
            pl.BlockSpec((TILES, PLACES, 3 * LANES), lambda i: (0, i, 0)), wide, wide,
            once(params_small.shape), once(qkv.shape), once(fc_mid.shape),
        ] + [once(item.shape) for item in segments],
        out_specs=[piece, hbm, hbm, hbm, once((D, D)), once((D, D))]
        + [once(item.shape[1:]) for item in segments] + [once(last)],
        out_shape=[like((rows, LANES), BF16)] * 4 + [like((D, D), BF16)] * 2
        + [like(item.shape[1:], BF16) for item in segments] + [like(last, F32)],
        scratch_shapes=[
            pltpu.VMEM((PLACES, D), F32), pltpu.VMEM((canvases, 3, PLACES, LANES), BF16),
            pltpu.VMEM((9, 8, D), F32), pltpu.VMEM((LAST_ROWS, D), F32),
            pltpu.VMEM((2, group - 1, half // group, D), BF16), pltpu.VMEM((2, 2 * half, D), BF16),
            pltpu.VMEM((2, half, D), BF16),
            pltpu.VMEM((4,) + last, F32), pltpu.VMEM((3,) + last, F32), pltpu.VMEM(last, F32),
            pltpu.VMEM((count - 1,) + last, F32),
            pltpu.SemaphoreType.DMA((canvases, 3)), pltpu.SemaphoreType.DMA((canvases, 3)),
            pltpu.SemaphoreType.DMA((total_slots,)), pltpu.SemaphoreType.DMA((total_slots,)),
            pltpu.SemaphoreType.DMA((2 + count,)), pltpu.SemaphoreType.DMA((2 + count,)),
        ] + [pltpu.VMEM((SMALL_SIZE, D), F32)]
        + [pltpu.VMEM(item.shape, BF16) for item in [fc_mid] + segments]
        + sum_scratch(pieces, count),
        compiler_params=params(collective_id=3, has_side_effects=True),
        cost_estimate=pl.CostEstimate(
            flops=rows * D * D * 12, bytes_accessed=canvases * 3 * 10**6, transcendentals=0
        ),
        name="tail",
    )(ids, x, three, first, second_grad, params_small, qkv, fc_mid, *segments)


def collect_kernel(me_ref, *refs):
    out_ref = refs[-1]
    for item, piece_ref in enumerate(refs[:-1]):

        @pl.when(pl.program_id(0) == item)
        def _():
            out_ref[...] = piece_ref[...].astype(F32)


def collect(me, pieces):
    rows = pieces[0].shape[0]
    return pl.pallas_call(
        collect_kernel,
        grid_spec=pltpu.PrefetchScalarGridSpec(
            num_scalar_prefetch=1,
            grid=(4,),
            in_specs=[once((rows, LANES))] * 4,
            out_specs=pl.BlockSpec((rows, LANES), lambda i, me: (lax.bitwise_xor(me[0], i), 0)),
        ),
        out_shape=like((4 * rows, LANES), F32),
        compiler_params=params(),
        name="collect",
    )(me, *pieces)


def finish_kernel(
    me_ref, p0_ref, p1_ref, p2_ref, p3_ref, fc1_ref, fc2_ref, small_ref, proj_ref, qkv_ref, last_ref,
    grad_ref, cpe_ref, vectors_ref, qkv_out_ref, qv_ref, crpe_ref, proj_out_ref, fc1_out_ref,
    bias_ref, fc2_out_ref,
):
    for item, piece_ref in enumerate((p0_ref, p1_ref, p2_ref, p3_ref)):

        @pl.when(pl.program_id(0) == item)
        def _():
            grad_ref[...] = piece_ref[...].astype(F32)

    @pl.when(pl.program_id(0) == 0)
    def _():
        cpe_ref[...] = last_ref[3:12, :]
        small = small_ref[...].astype(F32)
        vectors_ref[...] = jnp.concatenate(
            [last_ref[0:3, :], small[51:55, :], jnp.zeros((1, LANES), F32)], axis=0
        )
        qkv_out_ref[...] = qkv_ref[...].astype(F32)
        qv_ref[...] = small[49:51, :]
        crpe_ref[...] = small[:49, :]
        proj_out_ref[...] = proj_ref[...].astype(F32)
        fc1_out_ref[...] = fc1_ref[...].astype(F32)
        bias_ref[...] = small[64:68, :]
        fc2_out_ref[...] = fc2_ref[...].astype(F32)


def finish(me, pieces, fc1, fc2, small, proj, qkv, last):
    rows = pieces[0].shape[0]
    shapes = [
        (9, LANES), (8, LANES), qkv.shape, (2, LANES), (49, LANES), proj.shape, fc1.shape,
        (4, LANES), fc2.shape,
    ]
    return pl.pallas_call(
        finish_kernel,
        grid_spec=pltpu.PrefetchScalarGridSpec(
            num_scalar_prefetch=1,
            grid=(4,),
            in_specs=[once((rows, LANES))] * 4
            + [once(item.shape) for item in (fc1, fc2, small, proj, qkv, last)],
            out_specs=[
                pl.BlockSpec((rows, LANES), lambda i, me: (lax.bitwise_xor(me[0], i), 0)),
            ] + [once(shape) for shape in shapes],
        ),
        out_shape=[like((4 * rows, LANES), F32)] + [like(shape, F32) for shape in shapes],
        compiler_params=params(),
        name="finish",
    )(me, *pieces, fc1, fc2, small, proj, qkv, last)


def body(
    block_in, crop_ids, cotangent, cpe_kernel, cpe_bias, norm1_gain, norm1_shift, qkv_weight,
    qv_bias, crpe_kernel, proj_weight, proj_bias, norm2_gain, norm2_shift, fc1_weight, fc1_bias,
    fc2_weight, fc2_bias,
):
    head = lax.axis_index("head")
    me = head.reshape(1).astype(jnp.int32)
    rows = block_in.shape[0] // 4
    ids = crop_ids.reshape(crop_ids.shape[0], PLACES)

    def swap(values, move):
        return lax.ppermute(values, "head", [(item, item ^ move) for item in range(4)])

    packed = jnp.concatenate([
        cpe_kernel, crpe_kernel, cpe_bias[None], norm1_gain[None], norm1_shift[None], qv_bias,
        proj_bias[None], norm2_gain[None], norm2_shift[None], fc2_bias[None],
        fc1_bias.reshape(4, LANES), jnp.zeros((1, LANES), BF16),
    ]).astype(F32)
    own_weights = jnp.concatenate([fc1_weight, fc2_weight, proj_weight])
    extra = padded_rows(own_weights.shape[0], lax.axis_size("dp")) - own_weights.shape[0]
    if extra:
        own_weights = jnp.pad(own_weights, ((0, extra), (0, 0)))
    first, hidden, query, key, value, x, qkv, small, far_weights = head_part(
        ids, packed, qkv_weight.reshape(D, 3 * LANES), block_in, own_weights
    )
    cotangent, query = lax.optimization_barrier((cotangent, query))
    cot_pieces = [
        lax.dynamic_slice_in_dim(cotangent, lax.bitwise_xor(head, move) * rows, rows, 0)
        for move in range(4)
    ]
    cot_parts = [cot_pieces[0]] + [swap(cot_pieces[move], move) for move in (1, 2, 3)]

    soft, context, conv, attended = front(ids, query, key, value, small)
    results = middle(attended, first, cot_parts, small, own_weights, far_weights)
    second_grad, att_grad, fc_mid, proj_grad, middle_sum, bias_grad = results[4:]
    out_parts = [results[0]] + [swap(results[move], move) for move in (1, 2, 3)]
    three, qkv_grad, small_grad = back(
        ids, att_grad, query, value, soft, context, conv, hidden, small, middle_sum, bias_grad
    )
    three, out_parts = lax.optimization_barrier((three, out_parts))
    results = tail(
        ids, x, three, first, second_grad, small, qkv, fc_mid, qkv_grad, proj_grad, small_grad
    )
    (input_grad, cpe_g, vectors, qkv_g, qv_g, crpe_g, proj_g, fc1_g, bias_g, fc2_g) = finish(
        me, results[:4], *results[4:]
    )
    return (
        collect(me, out_parts), input_grad, cpe_g, vectors[0], vectors[1], vectors[2],
        qkv_g.reshape(D, 3, LANES), qv_g, crpe_g, proj_g, vectors[3], vectors[4], vectors[5],
        fc1_g, bias_g.reshape(D), fc2_g, vectors[6],
    )


def solution(mesh):
    return jax.shard_map(
        body,
        mesh=mesh,
        in_specs=(
            P("dp", "head"), P("dp", None, None), P("dp", "head"), P(None, "head"), P("head"),
            P("head"), P("head"), P(None, None, "head"), P(None, "head"), P(None, "head"),
            P("head", None), P("head"), P("head"), P("head"), P(None, "head"), P("head"),
            P("head", None), P("head"),
        ),
        out_specs=(
            P("dp", "head"), P("dp", "head"), P(None, "head"), P("head"), P("head"), P("head"),
            P(None, None, "head"), P(None, "head"), P(None, "head"), P("head", None), P("head"),
            P("head"), P("head"), P(None, "head"), P("head"), P("head", None), P("head"),
        ),
        check_vma=False,
    )
```

```python
import jax
import jax.numpy as jnp
from jax import lax
from jax.experimental import pallas as pl
from jax.experimental.pallas import tpu as pltpu
from jax.sharding import PartitionSpec as P

D = 512
HEADS = 8
HEAD_DIM = 64
HIDDEN = 2048
SIDE = 16
PLACES = 256
LANES = 128
TILES = 4
REACH = (1, 2, 3, 3)
GAP = 3
GRID_ROWS = SIDE + 3 * GAP + 1
EPSILON = 1e-06
SCALE = HEAD_DIM ** (-0.5)
F32 = jnp.float32
BF16 = jnp.bfloat16


def dot(left, right, dims):
    return lax.dot_general(left, right, (dims, ((), ())), preferred_element_type=F32)


def nn(left, right):
    return dot(left, right, ((1,), (0,)))


def nt(left, right):
    return dot(left, right, ((1,), (1,)))


def tn(left, right):
    return dot(left, right, ((0,), (0,)))


def lane(tile):
    return pl.ds(LANES * tile, LANES)


def fill_masks(cut, col_cuts, mask_ref):
    col = lax.broadcasted_iota(jnp.int32, (SIDE, LANES), 0)
    for band in range(2):
        here = (col >= col_cuts[band]).astype(jnp.int32)
        for step in range(-3, 4):
            if step == 0:
                continue
            there = (col + step >= col_cuts[band]).astype(jnp.int32)
            good = (col + step >= 0) & (col + step < SIDE) & (here == there)
            mask_ref[band, step + 3] = jnp.where(good, 1.0, 0.0).astype(F32)


def place_ids(cut, col_cuts):
    place = lax.broadcasted_iota(jnp.int32, (PLACES, LANES), 0)
    row = lax.shift_right_logical(place, 4)
    col = lax.bitwise_and(place, 15)
    band = (row >= cut).astype(jnp.int32)
    col_cut = jnp.where(band > 0, col_cuts[1], col_cuts[0])
    side = (col >= col_cut).astype(jnp.int32)
    return band, side


def spread(read_row, reach, cut, mask_ref, grid_ref, plane):
    zero = jnp.zeros((GAP * SIDE, LANES), F32)
    for step in range(-reach, reach + 1):
        start = pl.multiple_of(SIDE * (GAP + cut), SIDE)
        grid_ref[plane + step, pl.ds(start, GAP * SIDE), :] = zero
    for row in range(SIDE):
        lower = (row >= cut).astype(jnp.int32)
        start = pl.multiple_of(SIDE * (row + GAP + GAP * lower), SIDE)
        values = read_row(row)
        for step in range(-reach, reach + 1):
            moved = values
            if step != 0:
                moved = pltpu.roll(values, (-step) % SIDE, 0) * mask_ref[lower, step + 3]
            grid_ref[plane + step, pl.ds(start, SIDE), :] = moved


def add_to(store, key, term):
    store[key] = term if key not in store else store[key] + term


def over_bands(reach, cut, body):
    every = range(2 * reach + 2)
    for lower in range(2):
        first = cut if lower else 0
        height = SIDE - cut if lower else cut
        pairs = (height + 1) // 2
        shift = GAP * lower + GAP - reach

        def pair(index, places):
            row = first + 2 * index
            body(row, row + shift, first + height - 1, places)

        def inner(index, carry):
            pair(index, every)
            return carry

        pair(0, every[reach:])
        lax.fori_loop(1, pairs - 1, inner, 0)
        pair(pairs - 1, every[: reach + 2])


def conv_tiles(items, reach, cut, grid_ref, taps_ref, tap_reach, out_ref):
    width = 2 * tap_reach + 1
    chains = 3

    def body(row, base, last, places):
        for tile, plane in items:
            total = {}
            for step in range(-reach, reach + 1):
                taps = [
                    taps_ref[(dr + tap_reach) * width + step + tap_reach, :, lane(tile)]
                    for dr in range(-reach, reach + 1)
                ]
                for place in places:
                    for half in range(2):
                        start = pl.multiple_of(SIDE * (base + place) + 8 * half, 8)
                        field = grid_ref[plane + step, pl.ds(start, 8), :]
                        for out in range(2):
                            tap = place - out
                            if 0 <= tap <= 2 * reach:
                                add_to(total, (out, half, step % chains), taps[tap] * field)
            for out in range(2):
                for half in range(2):
                    start = pl.multiple_of(SIDE * (row + out) + 8 * half, 8)
                    out_ref[pl.ds(start, 8), lane(tile)] = sum(
                        [total[out, half, chain] for chain in range(1, chains)], total[out, half, 0]
                    )

    over_bands(reach, cut, body)


def conv_back_tiles(items, reach, cut, grid_ref, taps_ref, tap_reach, other_ref, out_ref, sum_ref):
    width = 2 * tap_reach + 1
    chains = 2

    def body(row, base, last, places):
        keep = jnp.where(row + 1 > last, 0.0, 1.0).astype(F32)
        for tile, plane in items:
            other = {}
            for out in range(2):
                for half in range(2):
                    start = pl.multiple_of(SIDE * (row + out) + 8 * half, 8)
                    value = other_ref[pl.ds(start, 8), lane(tile)]
                    other[out, half] = value * keep if out else value
            total = {}
            for step in range(-reach, reach + 1):
                sums = {}
                ids = [
                    (tap_reach - dr) * width + tap_reach - step for dr in range(-reach, reach + 1)
                ]
                taps = [taps_ref[item, :, lane(tile)] for item in ids]
                for place in places:
                    for half in range(2):
                        start = pl.multiple_of(SIDE * (base + place) + 8 * half, 8)
                        field = grid_ref[plane + step, pl.ds(start, 8), :]
                        for out in range(2):
                            tap = place - out
                            if 0 <= tap <= 2 * reach:
                                add_to(total, (out, half, step % chains), taps[tap] * field)
                                add_to(sums, tap, other[out, half] * field)
                for tap, part in sums.items():
                    sum_ref[ids[tap], :, lane(tile)] += part
            for out in range(2):
                for half in range(2):
                    start = pl.multiple_of(SIDE * (row + out) + 8 * half, 8)
                    out_ref[pl.ds(start, 8), lane(tile)] = sum(
                        [total[out, half, chain] for chain in range(1, chains)], total[out, half, 0]
                    )

    over_bands(reach, cut, body)


def row_mean(values):
    return jnp.sum(values, axis=1, keepdims=True) * (1.0 / D)


def pick(ids, rows):
    out = rows[0]
    for crop in range(1, 4):
        out = jnp.where(ids >= crop, rows[crop], out)
    return out


def crop_reduce(ids, values, op, empty):
    return [op(jnp.where(ids == crop, values, empty), axis=0, keepdims=True) for crop in range(4)]


def head_block():
    row = lax.broadcasted_iota(jnp.int32, (2 * LANES, 2 * LANES), 0)
    col = lax.broadcasted_iota(jnp.int32, (2 * LANES, 2 * LANES), 1)
    same = lax.bitwise_and(row, HEAD_DIM) == lax.bitwise_and(col, HEAD_DIM)
    return jnp.where(same, 1.0, 0.0).astype(F32)


def both(values, masks):
    return jnp.concatenate([values * masks[0], values * masks[1]], axis=1)


def read_cuts(ids_ref, canvases):
    canvas = lax.axis_index("head") * canvases + pl.program_id(0)

    def count(places, bound):
        return sum(jnp.where(ids_ref[canvas, place] < bound, 1, 0) for place in places)

    cut = count(range(0, PLACES, SIDE), 2)
    upper = count(range(SIDE), 1)
    lower = count(range(PLACES - SIDE, PLACES), 3)
    return cut, (upper, lower)


SMALL_SIZE = 72
(CPE, CRPE, CPE_BIAS, GAIN1, SHIFT1, QUERY_BIAS, VALUE_BIAS, PROJ_BIAS, GAIN2, SHIFT2, FC2_BIAS, FC1_BIAS) = (
    0, 9, 58, 59, 60, 61, 62, 63, 64, 65, 66, 67,
)


def spread_small(small_in, small_ref):
    me = lax.axis_index("head")
    for tile in range(TILES):
        small_ref[:, lane(tile)] = small_in[lax.bitwise_xor(me, tile)]


def outer_taps(tap):
    return max(abs(tap // 7 - 3), abs(tap % 7 - 3)) > 2


def keep_head(tap, tile, values):
    if tile != 2 or not outer_taps(tap):
        return values
    col = lax.broadcasted_iota(jnp.int32, values.shape, len(values.shape) - 1)
    return jnp.where(col < HEAD_DIM, 0.0, values)


def spread_taps(small_ref, row, count, masked, taps_ref):
    for tap in range(count):
        for tile in range(TILES):
            values = jnp.broadcast_to(small_ref[row + tap : row + tap + 1, lane(tile)], (8, LANES))
            taps_ref[tap, :, lane(tile)] = keep_head(tap, tile, values) if masked else values


def whole(shape):
    return pl.BlockSpec(shape, lambda *_: (0,) * len(shape))


def once(shape):
    return pl.BlockSpec(shape, lambda *_: (0,) * len(shape), pipeline_mode=pl.Buffered(1))


def rows_spec(width, base=0):
    return pl.BlockSpec((PLACES, width), lambda i, *_: (i + base, 0))


def context_spec(base):
    return pl.BlockSpec((1, TILES, 2 * LANES, 2 * LANES), lambda i, *_: (i + base, 0, 0, 0))


def like(shape, dtype):
    return jax.ShapeDtypeStruct(shape, dtype)


def params(**given):
    return pltpu.CompilerParams(vmem_limit_bytes=58 * 2**20, **given)


MESH = pl.DeviceIdType.MESH
PIECE_ROWS = 256
SMALL_ROWS = 128


def peer(move):
    return (lax.axis_index("dp"), lax.bitwise_xor(lax.axis_index("head"), move))


def meet(peers):
    barrier = pltpu.get_barrier_semaphore()
    for item in peers:
        pl.semaphore_signal(barrier, inc=1, device_id=item, device_id_type=MESH)
    pl.semaphore_wait(barrier, len(peers))


def remote(source, target, send, receive, device):
    return pltpu.make_async_remote_copy(
        src_ref=source, dst_ref=target, send_sem=send, recv_sem=receive,
        device_id=device, device_id_type=MESH,
    )


def plan_pieces(shapes, count):
    pieces = []
    for item, (rows, lanes) in enumerate(shapes):
        height = min(PIECE_ROWS, rows)
        for start in range(0, rows, height):
            pieces.append((item, start, height, padded_rows(height, count), lanes))
    return pieces


def padded_rows(height, count):
    unit = 16 * count
    return -(-height // unit) * unit


def place_on_dp():
    dp = lax.axis_index("dp")
    return dp, lax.rem(dp, 2), dp // 2


def low_peer():
    dp, low, _ = place_on_dp()
    return (dp + 1 - 2 * low, lax.axis_index("head"))


def high_peer(step, group):
    _, low, high = place_on_dp()
    return (lax.rem(high + step, group) * 2 + low, lax.axis_index("head"))


def aligned(index, size):
    return pl.ds(pl.multiple_of(index * size, size), size)


class HighSum:
    def __init__(self, count, mid, part, whole, got, send, receive, slot):
        self.group = count // 2
        self.got = got
        self.mid, self.part, self.whole = mid, part, whole
        self.send, self.receive, self.slot = send, receive, slot
        self.half = mid.shape[0]
        self.size = self.half // self.group

    def copy(self, source, target, slot, device):
        return remote(
            source, target, self.send.at[self.slot + slot], self.receive.at[self.slot + slot], device
        )

    def high(self, step):
        _, _, high = place_on_dp()
        other = lax.rem(high + step, self.group)
        return self.copy(
            self.mid.at[aligned(other, self.size)], self.part.at[step - 1], step - 1,
            high_peer(step, self.group),
        )

    def spot(self):
        dp, low, high = place_on_dp()
        return self.whole.at[aligned(low * self.group + high, self.size)]

    def share(self, step):
        spot = self.spot()
        return self.copy(spot, spot, self.group - 2 + step, high_peer(step, self.group))

    def last(self):
        _, low, _ = place_on_dp()
        here = self.whole.at[aligned(low, self.half)]
        return self.copy(here, self.got, 2 * self.group - 2, low_peer())

    def to_high(self):
        for step in range(1, self.group):
            self.high(step).start()

    def share_high(self):
        _, _, high = place_on_dp()
        total = self.mid[aligned(high, self.size), :].astype(F32)
        for step in range(1, self.group):
            self.high(step).wait()
            total += self.part[step - 1].astype(F32)
        self.spot()[...] = total.astype(BF16)
        for step in range(1, self.group):
            self.share(step).start()

    def share_low(self):
        for step in range(1, self.group):
            self.share(step).wait()
        self.last().start()

    def finish(self):
        _, low, _ = place_on_dp()
        self.last().wait()
        self.whole[aligned(1 - low, self.half), :] = self.got[...]


def high_slots(count):
    return count - 1


class FullSum:
    def __init__(self, count, grad, span, near, far, whole, mid, low, part, got, send, receive, slot):
        self.grad, self.span, self.near, self.far = grad, span, near, far
        self.whole, self.mid, self.low = whole, mid, low
        self.height = far.shape[0]
        self.send, self.receive, self.slot = send, receive, slot
        self.rest = HighSum(count, mid, part, whole, got, send, receive, slot + 4)

    def copy(self, source, target, slot, device):
        return remote(
            source, target, self.send.at[self.slot + slot], self.receive.at[self.slot + slot], device
        )

    def near_copy(self, item):
        return self.copy(
            self.grad.at[1 + 2 * item, self.span], self.near.at[item], item, peer(1)
        )

    def far_copy(self):
        return self.copy(self.whole.at[: self.height], self.far, 2, peer(2))

    def low_copy(self):
        _, low, _ = place_on_dp()
        return self.copy(self.whole.at[aligned(1 - low, self.mid.shape[0])], self.low, 3, low_peer())

    def to_core(self):
        self.near_copy(1).start()
        self.near_copy(0).start()

    def to_far(self):
        self.near_copy(1).wait()
        self.whole[: self.height, :] = (
            self.grad[2, self.span, :].astype(F32) + self.near[1].astype(F32)
        ).astype(BF16)
        self.far_copy().start()

    def to_low(self):
        self.near_copy(0).wait()
        self.far_copy().wait()
        self.whole[: self.height, :] = (
            self.grad[0, self.span, :].astype(F32) + self.near[0].astype(F32)
            + self.far[...].astype(F32)
        ).astype(BF16)
        rows = self.whole.shape[0]
        if rows > self.height:
            self.whole[self.height :, :] = jnp.zeros((rows - self.height, self.whole.shape[1]), BF16)
        self.low_copy().start()

    def to_high(self):
        _, low, _ = place_on_dp()
        self.low_copy().wait()
        half = self.mid.shape[0]
        self.mid[...] = (
            self.whole[aligned(low, half), :].astype(F32) + self.low[...].astype(F32)
        ).astype(BF16)
        self.rest.to_high()


def sum_scratch(pieces, count):
    scratch = []
    for _, _, height, padded, lanes in pieces:
        scratch += [
            pltpu.VMEM((2, height, lanes), BF16), pltpu.VMEM((height, lanes), BF16),
            pltpu.VMEM((padded, lanes), BF16), pltpu.VMEM((padded // 2, lanes), BF16),
            pltpu.VMEM((padded // 2, lanes), BF16),
            pltpu.VMEM((count // 2 - 1, padded // count, lanes), BF16),
            pltpu.VMEM((padded // 2, lanes), BF16),
        ]
    return scratch


def step_masks(cut, col_cuts):
    place = lax.broadcasted_iota(jnp.int32, (PLACES, LANES), 0)
    row = lax.shift_right_logical(place, 4)
    col = lax.bitwise_and(place, 15)
    col_cut = jnp.where(row >= cut, col_cuts[1], col_cuts[0])
    rows = {
        1: (row < SIDE - 1) & (row + 1 != cut),
        -1: (row > 0) & (row != cut),
    }
    cols = {
        1: (col < SIDE - 1) & (col + 1 != col_cut),
        -1: (col > 0) & (col != col_cut),
    }
    return [
        {key: jnp.where(mask, 1.0, 0.0).astype(F32) for key, mask in masks.items()}
        for masks in (rows, cols)
    ]


def shift_rows(values, step):
    if step == 0:
        return values
    zero = jnp.zeros((SIDE, values.shape[1]), values.dtype)
    if step > 0:
        return jnp.concatenate([values[SIDE:], zero], axis=0)
    return jnp.concatenate([zero, values[:-SIDE]], axis=0)


def shift_cols(values, masks, step):
    if step == 0:
        return values
    return pltpu.roll(values, (-step) % PLACES, 0) * masks[step]


def head_kernel(
    canvases, count, ids_ref, small_own, qkv_own, x_in, qkv_in, share_in,
    first_ref, hidden_ref, query_ref, key_ref, value_ref, x_out, qkv_ref, small_out, far_out,
    x_ref, landing_ref, mine_ref, small_ref, qkv_all, small_got, send, receive, weight_send, weight_receive,
    share_send, share_receive, local,
):
    me = lax.axis_index("head")
    step = pl.program_id(0)
    rows = canvases * PLACES

    def piece(index, move):
        start = pl.multiple_of(lax.bitwise_xor(me, move) * rows + index * PLACES, PLACES)
        return remote(
            x_in.at[pl.ds(start, PLACES)], landing_ref.at[index, move - 1], send.at[index, move - 1],
            receive.at[index, move - 1], peer(move),
        )

    def weight(number, source, target, move):
        return remote(source, target, weight_send.at[number], weight_receive.at[number], peer(move))

    far = weight(0, qkv_in, qkv_all.at[1], 2)
    near = weight(1, qkv_in, qkv_all.at[0], 1)
    relay = weight(2, qkv_all.at[1], qkv_all.at[2], 1)
    smalls = [weight(2 + move, small_got.at[0], small_got.at[move], move) for move in (1, 2, 3)]
    mine = pltpu.make_async_copy(x_in.at[aligned(me, rows)], mine_ref, local.at[0])
    dp = lax.axis_index("dp")
    spot = aligned(dp, share_in.shape[0] // count)
    share = remote(share_in.at[spot], far_out.at[spot], share_send.at[0], share_receive.at[0], peer(2))
    group = count // 2
    _, low, high = place_on_dp()
    spread_high = [
        remote(
            far_out.at[spot], far_out.at[spot], share_send.at[hop], share_receive.at[hop],
            high_peer(hop, group),
        )
        for hop in range(1, group)
    ]
    spread_low = []
    for hop in range(group):
        source = lax.rem(high - hop + group, group) * 2 + low
        there = aligned(source, share_in.shape[0] // count)
        spread_low.append(
            remote(
                far_out.at[there], far_out.at[there], share_send.at[group + hop],
                share_receive.at[group + hop], low_peer(),
            )
        )

    @pl.when(step == 0)
    def _():
        mine.start()
        small_got[0] = small_own[...]
        meet(
            [peer(move) for move in (1, 2, 3)] + [low_peer()]
            + [high_peer(hop, group) for hop in range(1, group)]
        )
        for item in smalls:
            item.start()
        share.start()
        for move in (2, 3, 1):
            piece(0, move).start()
        far.start()
        near.start()

        def send_piece(index, carry):
            for move in (2, 3, 1):
                piece(index, move).start()
            return carry

        lax.fori_loop(1, canvases, send_piece, 0)
        for item in smalls:
            item.wait()
        for move in range(4):
            small_ref[:, aligned(lax.bitwise_xor(me, move), LANES)] = small_got[move]
            small_out[move] = small_got[move]
        mine.wait()

    for hop in range(1, group):

        @pl.when(step == min(1 + hop, canvases - 1))
        def _():
            spread_high[hop - 1].wait()
            spread_low[hop].start()

    @pl.when(step == canvases - 1)
    def _():
        for item in spread_low:
            item.wait()

    x_ref[:, aligned(me, LANES)] = mine_ref[aligned(step, PLACES), :].astype(F32)
    for move in (1, 2, 3):
        piece(step, move).wait()
        x_ref[:, aligned(lax.bitwise_xor(me, move), LANES)] = landing_ref[step, move - 1].astype(F32)
    rows_mask, cols_mask = step_masks(*read_cuts(ids_ref, canvases))
    for tile in range(TILES):
        field = x_ref[:, lane(tile)]
        moved = [shift_cols(field, cols_mask, col) for col in (-1, 0, 1)]
        result = field + small_ref[CPE_BIAS : CPE_BIAS + 1, lane(tile)]
        for row in (-1, 0, 1):
            line = None
            for col in (-1, 0, 1):
                tap = CPE + (row + 1) * 3 + col + 1
                term = jnp.broadcast_to(small_ref[tap : tap + 1, lane(tile)], (PLACES, LANES)) * moved[col + 1]
                line = term if line is None else line + term
            line = shift_rows(line, row)
            result = result + (line * rows_mask[row] if row else line)
        first_ref[:, lane(tile)] = result
    x_out[...] = x_ref[...].astype(BF16)
    first = first_ref[...]
    center = row_mean(first)
    square = row_mean(first * first)
    inverse = lax.rsqrt(square - center * center + EPSILON)
    hidden = (
        (first - center) * inverse * small_ref[GAIN1 : GAIN1 + 1, :] + small_ref[SHIFT1 : SHIFT1 + 1, :]
    ).astype(BF16)
    hidden_ref[...] = hidden

    @pl.when(step == 0)
    def _():
        share.wait()
        for item in spread_high + spread_low[:1]:
            item.start()
        far.wait()
        relay.start()
        near.wait()
        relay.wait()
        qkv_ref[0] = qkv_own[...]
        for move in (1, 2, 3):
            qkv_ref[move] = qkv_all[move - 1]

    for tile in range(TILES):
        three = nn(hidden, qkv_ref[lax.bitwise_xor(me, tile)])
        query_ref[:, lane(tile)] = (
            three[:, :LANES] + small_ref[QUERY_BIAS : QUERY_BIAS + 1, lane(tile)]
        ).astype(BF16)
        key_ref[:, lane(tile)] = three[:, LANES : 2 * LANES].astype(BF16)
        value_ref[:, lane(tile)] = (
            three[:, 2 * LANES :] + small_ref[VALUE_BIAS : VALUE_BIAS + 1, lane(tile)]
        ).astype(BF16)


def head_part(ids, small, qkv, block_in, share):
    count = lax.axis_size("dp")
    rows = block_in.shape[0] // 4
    canvases = rows // PLACES
    wide = rows_spec(D)
    hbm = pl.BlockSpec(memory_space=pl.ANY)
    return pl.pallas_call(
        lambda *refs: head_kernel(canvases, count, *refs),
        grid=(canvases,),
        in_specs=[
            pl.BlockSpec(memory_space=pltpu.SMEM), once(small.shape), once(qkv.shape), hbm, hbm, hbm,
        ],
        out_specs=[wide] * 6 + [once((4,) + qkv.shape), once((4,) + small.shape), hbm],
        out_shape=[like((rows, D), F32)] + [like((rows, D), BF16)] * 5 + [
            like((4,) + qkv.shape, BF16), like((4,) + small.shape, F32), like(share.shape, BF16),
        ],
        scratch_shapes=[
            pltpu.VMEM((PLACES, D), F32), pltpu.VMEM((canvases, 3, PLACES, LANES), BF16),
            pltpu.VMEM((rows, LANES), BF16), pltpu.VMEM((SMALL_SIZE, D), F32),
            pltpu.VMEM((3,) + qkv.shape, BF16), pltpu.VMEM((4,) + small.shape, F32),
            pltpu.SemaphoreType.DMA((canvases, 3)), pltpu.SemaphoreType.DMA((canvases, 3)),
            pltpu.SemaphoreType.DMA((6,)), pltpu.SemaphoreType.DMA((6,)),
            pltpu.SemaphoreType.DMA((count,)), pltpu.SemaphoreType.DMA((count,)),
            pltpu.SemaphoreType.DMA((1,)),
        ],
        compiler_params=params(collective_id=1, has_side_effects=True),
        name="head",
    )(ids, small, qkv, block_in, qkv, share)


def front_kernel(
    canvases, ids_ref, query_ref, key_ref, value_ref, small_in,
    soft_ref, context_ref, conv_ref, attended_ref,
    mask_ref, grid_ref, out_ref, x_ref, small_ref, crpe_ref,
):
    cut, col_cuts = read_cuts(ids_ref, canvases)

    @pl.when(pl.program_id(0) == 0)
    def _():
        grid_ref[...] = jnp.zeros_like(grid_ref)
        spread_small(small_in, small_ref)
        spread_taps(small_ref, CRPE, 49, True, crpe_ref)

    fill_masks(cut, col_cuts, mask_ref)
    band, side = place_ids(cut, col_cuts)
    ids = 2 * band + side
    sides = [(side == item).astype(F32).astype(BF16) for item in range(2)]
    bands = [(band == item).astype(F32).astype(BF16) for item in range(2)]
    blocks = head_block()
    for tile in range(TILES):
        query = query_ref[:, lane(tile)]
        keys = key_ref[:, lane(tile)].astype(F32)
        value = value_ref[:, lane(tile)]
        highest = crop_reduce(ids, keys, jnp.max, -1e30)
        powers = jnp.exp(keys - pick(ids, highest))
        totals = crop_reduce(ids, powers, jnp.sum, 0.0)
        soft = (powers * pick(ids, [1.0 / item for item in totals])).astype(BF16)
        soft_ref[:, lane(tile)] = soft
        context = (tn(both(soft, sides), both(value, bands)) * blocks).astype(BF16)
        context_ref[0, tile] = context
        factor = nn(both(query, sides), context)
        x_ref[:, lane(tile)] = jnp.where(band > 0, factor[:, LANES:], factor[:, :LANES]) * SCALE
    for tile in range(TILES):
        spread(
            lambda row: value_ref[SIDE * row : SIDE * row + SIDE, lane(tile)].astype(F32),
            REACH[tile], cut, mask_ref, grid_ref, 3,
        )
        conv_tiles(((tile, 3),), REACH[tile], cut, grid_ref, crpe_ref, 3, out_ref)
    conv = out_ref[:PLACES, :]
    conv_ref[...] = conv.astype(BF16)
    attended_ref[...] = (x_ref[...] + query_ref[...].astype(F32) * conv).astype(BF16)


def front(ids, query, key, value, small):
    rows = query.shape[0]
    count = rows // PLACES
    wide = rows_spec(D)
    return pl.pallas_call(
        lambda *refs: front_kernel(count, *refs),
        grid_spec=pltpu.PrefetchScalarGridSpec(
            num_scalar_prefetch=1,
            grid=(count,),
            in_specs=[wide, wide, wide, once(small.shape)],
            out_specs=[wide, context_spec(0), wide, wide],
            scratch_shapes=[
                pltpu.VMEM((2, 7, SIDE, LANES), F32),
                pltpu.VMEM((7, GRID_ROWS * SIDE, LANES), F32),
                pltpu.VMEM((PLACES + SIDE, D), F32),
                pltpu.VMEM((PLACES, D), F32),
                pltpu.VMEM((SMALL_SIZE, D), F32),
                pltpu.VMEM((49, 8, D), F32),
            ],
        ),
        out_shape=[
            like((rows, D), BF16), like((count, TILES, 2 * LANES, 2 * LANES), BF16),
            like((rows, D), BF16), like((rows, D), BF16),
        ],
        compiler_params=params(),
        cost_estimate=pl.CostEstimate(
            flops=rows * D * D * 40, bytes_accessed=count * 10**7, transcendentals=0
        ),
        name="front",
    )(ids, query, key, value, small)


def gelu_both(pre):
    power = jnp.exp(pre * pre * -0.5)
    t = 1.0 / (1.0 + jnp.abs(pre) * (0.3275911 * 0.7071067811865476))
    poly = 0.5 * 1.061405429
    for item in (-1.453152027, 1.421413741, -0.284496736, 0.254829592):
        poly = poly * t + 0.5 * item
    tail = poly * t * power
    cdf = jnp.where(pre >= 0.0, 1.0 - tail, tail)
    return pre * cdf, cdf + pre * power * 0.3989422804014327


BLOCK = 1024


def middle_kernel(
    count,
    attended_ref, first_ref, cot0_ref, cot1_ref, cot2_ref, cot3_ref, small_in, own_weights,
    far_weights,
    out0_ref, out1_ref, out2_ref, out3_ref, second_grad_ref, att_grad_ref, fc_mid_ref,
    proj_grad_ref, sum_ref, bias_grad_ref,
    cot_ref, hat_ref, inverse_ref, hidden_ref, total_ref, back_ref, active_ref, pre_grad_ref,
    grads_ref, near_ref, far_ref, own_ref, low_ref, small_ref, weights_ref, send, receive, fetch,
):
    me = lax.axis_index("head")
    step = pl.program_id(0)
    rows = attended_ref.shape[0]
    blocks = rows // BLOCK
    _, low, _ = place_on_dp()
    half = low_ref.shape[1]

    def near(item, kind):
        return remote(
            grads_ref.at[2 * item, kind], near_ref.at[item, kind], send.at[2 * item + kind],
            receive.at[2 * item + kind], peer(1),
        )

    def far(kind):
        return remote(
            grads_ref.at[1, kind], far_ref.at[kind], send.at[4 + kind], receive.at[4 + kind], peer(2)
        )

    def to_low(kind):
        return remote(
            own_ref.at[kind, aligned(1 - low, half)], low_ref.at[kind], send.at[6 + kind],
            receive.at[6 + kind], low_peer(),
        )

    def part(index):
        return aligned(index, BLOCK)

    shard = 3 - step
    fc1 = weights_ref.at[shard, :D]
    fc2 = weights_ref.at[shard, D : 2 * D]

    def proj(tile):
        return weights_ref[lax.bitwise_xor(me, tile), 2 * D : 2 * D + LANES, :]

    def relay(number, source, target, part):
        return remote(
            source.at[part], weights_ref.at[target, part], send.at[8 + number], receive.at[8 + number],
            peer(1),
        )

    narrow, broad = pl.ds(2 * D, LANES), pl.ds(0, 2 * D)
    relays = [
        relay(0, own_weights, 1, narrow), relay(1, far_weights, 3, narrow),
        relay(2, far_weights, 3, broad), relay(3, own_weights, 1, broad),
    ]

    @pl.when(step == 0)
    def _():
        loads = [
            pltpu.make_async_copy(own_weights.at[pl.ds(0, 2 * D + LANES)], weights_ref.at[0], fetch.at[0]),
            pltpu.make_async_copy(far_weights.at[pl.ds(0, 2 * D + LANES)], weights_ref.at[2], fetch.at[1]),
        ]
        for move, piece_ref in enumerate((cot0_ref, cot1_ref, cot2_ref, cot3_ref)):
            spot = cot_ref.at[:, aligned(lax.bitwise_xor(me, move), LANES)]
            loads.append(pltpu.make_async_copy(piece_ref, spot, fetch.at[2 + move]))
        for load in loads:
            load.start()
        meet([peer(1), peer(2), low_peer()])
        for item in relays:
            item.start()
        spread_small(small_in, small_ref)
        own_ref[...] = jnp.zeros_like(own_ref)
        sum_ref[...] = jnp.zeros_like(sum_ref)
        for item in loads + relays[:2]:
            item.wait()

        def enter(index, carry):
            now = part(index)
            second = first_ref[now, :] + small_ref[PROJ_BIAS : PROJ_BIAS + 1, :]
            for tile in range(TILES):
                second += nn(attended_ref[now, lane(tile)], proj(tile))
            center = row_mean(second)
            square = row_mean(second * second)
            inverse = lax.rsqrt(square - center * center + EPSILON)
            hat = (second - center) * inverse
            hidden_ref[now, :] = (
                hat * small_ref[GAIN2 : GAIN2 + 1, :] + small_ref[SHIFT2 : SHIFT2 + 1, :]
            ).astype(BF16)
            hat_ref[now, :] = hat
            inverse_ref[now, :] = jnp.broadcast_to(inverse, (BLOCK, LANES))
            total_ref[now, :] = second + small_ref[FC2_BIAS : FC2_BIAS + 1, :]
            back_ref[now, :] = jnp.zeros((BLOCK, D), F32)
            sum_ref[3:4, :] += jnp.sum(cot_ref[now, :].astype(F32), axis=0, keepdims=True)
            return carry

        lax.fori_loop(0, blocks, enter, 0)
        for item in relays[2:]:
            item.wait()

    bias_grad_ref[0] = jnp.zeros_like(bias_grad_ref[0])

    def chunk(index, carry):
        now = part(index)
        bias = jnp.concatenate(
            [small_in[shard, FC1_BIAS + tile : FC1_BIAS + tile + 1, :] for tile in range(TILES)], axis=1
        )
        pre = nn(hidden_ref[now, :], fc1[...]) + bias
        active, slope = gelu_both(pre)
        active = active.astype(BF16)
        active_ref[now, :] = active
        total_ref[now, :] += nn(active, fc2[...])
        pre_grad_f = nt(cot_ref[now, :], fc2[...]) * slope
        pre_grad = pre_grad_f.astype(BF16)
        pre_grad_ref[now, :] = pre_grad
        back_ref[now, :] += nt(pre_grad, fc1[...])
        bias_grad_ref[0] += jnp.sum(pre_grad_f, axis=0, keepdims=True)
        return carry

    lax.fori_loop(0, blocks, chunk, 0)
    grads_ref[step, 0] = tn(hidden_ref[...], pre_grad_ref[...]).astype(BF16)
    grads_ref[step, 1] = tn(active_ref[...], cot_ref[...]).astype(BF16)

    @pl.when(step == 0)
    def _():
        for kind in range(2):
            near(0, kind).start()

    @pl.when(step == 1)
    def _():
        for kind in range(2):
            near(0, kind).wait()
            grads_ref[1, kind] = (
                grads_ref[1, kind].astype(F32) + near_ref[0, kind].astype(F32)
            ).astype(BF16)
            far(kind).start()

    @pl.when(step == 2)
    def _():
        for kind in range(2):
            near(1, kind).start()

    @pl.when(step == 3)
    def _():
        for kind in range(2):
            near(1, kind).wait()
            far(kind).wait()
            own_ref[kind, :D, :] = (
                grads_ref[3, kind].astype(F32) + near_ref[1, kind].astype(F32)
                + far_ref[kind].astype(F32)
            ).astype(BF16)
            to_low(kind).start()

        def leave(index, carry):
            now = part(index)
            for move, piece_ref in enumerate((out0_ref, out1_ref, out2_ref, out3_ref)):
                piece_ref[now, :] = total_ref[now, aligned(lax.bitwise_xor(me, move), LANES)].astype(BF16)
            hat = hat_ref[now, :]
            norm_grad = back_ref[now, :]
            weighted = norm_grad * small_ref[GAIN2 : GAIN2 + 1, :]
            second_grad = cot_ref[now, :].astype(F32) + inverse_ref[now, 0:1] * (
                weighted - row_mean(weighted) - hat * row_mean(weighted * hat)
            )
            second_grad_ref[now, :] = second_grad
            second_low = second_grad.astype(BF16)
            hidden_ref[now, :] = second_low
            for tile in range(TILES):
                att_grad_ref[now, lane(tile)] = nt(
                    second_low, proj(tile)
                ).astype(BF16)
            sum_ref[1:2, :] += jnp.sum(norm_grad * hat, axis=0, keepdims=True)
            sum_ref[2:3, :] += jnp.sum(norm_grad, axis=0, keepdims=True)
            sum_ref[0:1, :] += jnp.sum(second_low.astype(F32), axis=0, keepdims=True)
            return carry

        lax.fori_loop(0, blocks, leave, 0)
        for tile in range(TILES):
            proj_grad_ref[lax.bitwise_xor(me, tile)] = tn(
                attended_ref[:, lane(tile)], hidden_ref[...]
            ).astype(BF16)
        for kind in range(2):
            to_low(kind).wait()
            fc_mid_ref[kind] = (
                own_ref[kind, aligned(low, half), :].astype(F32) + low_ref[kind].astype(F32)
            ).astype(BF16)


def middle(attended, first, cot_parts, small, own_weights, far_weights):
    rows = attended.shape[0]
    count = lax.axis_size("dp")
    padded = padded_rows(D, count)
    hbm = pl.BlockSpec(memory_space=pl.ANY)
    proj_shape = (4, LANES, D)
    piece = once((rows, LANES))
    wide = once((rows, D))
    line = pl.BlockSpec((1, 1, D), lambda i: (3 - i, 0, 0))
    return pl.pallas_call(
        lambda *refs: middle_kernel(count, *refs),
        grid=(4,),
        in_specs=[
            wide, wide, hbm, hbm, hbm, hbm, once(small.shape), hbm, hbm,
        ],
        out_specs=[
            piece, piece, piece, piece, wide, wide, once((2, padded // 2, D)), once(proj_shape),
            once((8, D)), line,
        ],
        out_shape=[like((rows, LANES), BF16)] * 4 + [
            like((rows, D), F32), like((rows, D), BF16), like((2, padded // 2, D), BF16),
            like(proj_shape, BF16), like((8, D), F32), like((4, 1, D), F32),
        ],
        scratch_shapes=[
            pltpu.VMEM((rows, D), BF16), pltpu.VMEM((rows, D), F32),
            pltpu.VMEM((rows, LANES), F32),
            pltpu.VMEM((rows, D), BF16), pltpu.VMEM((rows, D), F32),
            pltpu.VMEM((rows, D), F32), pltpu.VMEM((rows, D), BF16),
            pltpu.VMEM((rows, D), BF16),
            pltpu.VMEM((4, 2, D, D), BF16), pltpu.VMEM((2, 2, D, D), BF16),
            pltpu.VMEM((2, D, D), BF16), pltpu.VMEM((2, padded, D), BF16),
            pltpu.VMEM((2, padded // 2, D), BF16),
            pltpu.VMEM((SMALL_SIZE, D), F32), pltpu.VMEM((4, 2 * D + LANES, D), BF16),
            pltpu.SemaphoreType.DMA((12,)), pltpu.SemaphoreType.DMA((12,)),
            pltpu.SemaphoreType.DMA((6,)),
        ],
        compiler_params=params(collective_id=2, has_side_effects=True),
        cost_estimate=pl.CostEstimate(flops=rows * D * D * 60, bytes_accessed=3 * 10**7, transcendentals=0),
        name="middle",
    )(attended, first, *cot_parts, small, own_weights, far_weights)


def back_kernel(
    canvases, ids_ref, grad_ref, query_ref, value_ref, soft_ref, context_ref, conv_ref, hidden_ref,
    small_in, middle_sum_ref, bias_grad_ref,
    three_ref, qkv_out_ref, small_out_ref,
    mask_ref, grid_ref, out_ref, other_ref, value_part_ref, qkv_grad_ref, small_ref, crpe_ref,
    crpe_sum_ref, sum_ref, late_ref,
):
    cut, col_cuts = read_cuts(ids_ref, canvases)
    me = lax.axis_index("head")

    @pl.when(pl.program_id(0) == 0)
    def _():
        grid_ref[...] = jnp.zeros_like(grid_ref)
        other_ref[...] = jnp.zeros_like(other_ref)
        qkv_grad_ref[...] = jnp.zeros_like(qkv_grad_ref)
        crpe_sum_ref[...] = jnp.zeros_like(crpe_sum_ref)
        sum_ref[...] = jnp.zeros_like(sum_ref)
        spread_small(small_in, small_ref)
        spread_taps(small_ref, CRPE, 49, True, crpe_ref)

    fill_masks(cut, col_cuts, mask_ref)
    band, side = place_ids(cut, col_cuts)
    ids = 2 * band + side
    sides = [(side == item).astype(F32).astype(BF16) for item in range(2)]
    bands = [(band == item).astype(F32).astype(BF16) for item in range(2)]
    blocks = head_block() * SCALE
    for tile in range(TILES):
        grad = grad_ref[:, lane(tile)]
        query = query_ref[:, lane(tile)]
        value = value_ref[:, lane(tile)]
        soft = soft_ref[:, lane(tile)]
        context = context_ref[0, tile]
        grad_f = grad.astype(F32)
        grad_bands = both(grad, bands)
        context_grad = (tn(both(query, sides), grad_bands) * blocks).astype(BF16)
        part = nt(grad_bands, context)
        part = jnp.where(side > 0, part[:, LANES:], part[:, :LANES])
        query_grad = (
            part * SCALE + grad_f * conv_ref[:, lane(tile)].astype(F32)
        ).astype(BF16)
        soft_grad = nt(both(value, bands), context_grad)
        soft_grad = jnp.where(side > 0, soft_grad[:, LANES:], soft_grad[:, :LANES])
        soft_f = soft.astype(F32)
        inner = crop_reduce(ids, soft_f * soft_grad, jnp.sum, 0.0)
        keys_grad = (soft_f * (soft_grad - pick(ids, inner))).astype(BF16)
        value_part = nn(both(soft, sides), context_grad)
        value_part_ref[:, lane(tile)] = jnp.where(
            band > 0, value_part[:, LANES:], value_part[:, :LANES]
        )
        three_ref[tile, :, :LANES] = query_grad
        three_ref[tile, :, LANES : 2 * LANES] = keys_grad
        sum_ref[0:1, lane(tile)] += jnp.sum(query_grad.astype(F32), axis=0, keepdims=True)
    other_ref[:PLACES, :] = value_ref[...].astype(F32)
    for tile in range(TILES):

        def read_row(row):
            part = pl.ds(SIDE * row, SIDE)
            return grad_ref[part, lane(tile)].astype(F32) * query_ref[part, lane(tile)].astype(F32)

        spread(read_row, REACH[tile], cut, mask_ref, grid_ref, 3)
        conv_back_tiles(
            ((tile, 3),), REACH[tile], cut, grid_ref, crpe_ref, 3, other_ref, out_ref, crpe_sum_ref
        )
    hidden = hidden_ref[...]
    for tile in range(TILES):
        value_grad = (value_part_ref[:, lane(tile)] + out_ref[:PLACES, lane(tile)]).astype(BF16)
        three_ref[tile, :, 2 * LANES :] = value_grad
        sum_ref[1:2, lane(tile)] += jnp.sum(value_grad.astype(F32), axis=0, keepdims=True)
        qkv_grad_ref[lax.bitwise_xor(me, tile)] += tn(hidden, three_ref[tile])

    @pl.when(pl.program_id(0) == pl.num_programs(0) - 1)
    def _():
        qkv_out_ref[...] = qkv_grad_ref[...].astype(BF16)
        late_ref[...] = jnp.zeros_like(late_ref)
        for tap in range(49):
            for tile in range(TILES):
                late_ref[tap : tap + 1, lane(tile)] = keep_head(
                    tap, tile, jnp.sum(crpe_sum_ref[tap, :, lane(tile)], axis=0, keepdims=True)
                )
        late_ref[49:51, :] = sum_ref[0:2, :]
        late_ref[51:55, :] = middle_sum_ref[0:4, :]
        for move in range(4):
            late = late_ref[:, aligned(lax.bitwise_xor(me, move), LANES)]
            small_out_ref[move] = late.astype(BF16)
            small_out_ref[move, 64:80, :] = jnp.concatenate(
                [bias_grad_ref[move, :, lane(tile)] for tile in range(TILES)]
                + [jnp.zeros((12, LANES), F32)],
                axis=0,
            ).astype(BF16)


def back(ids, grad, query, value, soft, context, conv, hidden, small, middle_sum, bias_grad):
    rows = grad.shape[0]
    count = rows // PLACES
    wide = rows_spec(D)
    shards = (4, D, 3 * LANES)
    late = (4, SMALL_ROWS, LANES)
    return pl.pallas_call(
        lambda *refs: back_kernel(count, *refs),
        grid_spec=pltpu.PrefetchScalarGridSpec(
            num_scalar_prefetch=1,
            grid=(count,),
            in_specs=[
                wide, wide, wide, wide, context_spec(0), wide, wide, once(small.shape),
                once(middle_sum.shape), once(bias_grad.shape),
            ],
            out_specs=[
                pl.BlockSpec((TILES, PLACES, 3 * LANES), lambda i, *_: (0, i, 0)),
                once(shards), once(late),
            ],
            scratch_shapes=[
                pltpu.VMEM((2, 7, SIDE, LANES), F32),
                pltpu.VMEM((7, GRID_ROWS * SIDE, LANES), F32),
                pltpu.VMEM((PLACES + SIDE, D), F32),
                pltpu.VMEM((PLACES + SIDE, D), F32),
                pltpu.VMEM((PLACES, D), F32),
                pltpu.VMEM(shards, F32),
                pltpu.VMEM((SMALL_SIZE, D), F32),
                pltpu.VMEM((49, 8, D), F32),
                pltpu.VMEM((49, 8, D), F32),
                pltpu.VMEM((8, D), F32),
                pltpu.VMEM((SMALL_ROWS, D), F32),
            ],
        ),
        out_shape=[
            like((TILES, rows, 3 * LANES), BF16), like(shards, BF16), like(late, BF16),
        ],
        compiler_params=params(),
        cost_estimate=pl.CostEstimate(
            flops=rows * D * D * 64, bytes_accessed=count * 10**7, transcendentals=0
        ),
        name="back",
    )(ids, grad, query, value, soft, context, conv, hidden, small, middle_sum, bias_grad)


LAST_ROWS = 16
STAGES = ((0, 1, 2, 3, 4, 5), (0, 1, 3, 4, 5, 6), (0, 1, 4, 6, 7, 8), (0, 1, 5, 7, 8, 9))
FC_STAGES = ((0, 2, 4), (1, 4, 6))


def tail_kernel(
    count, pieces,
    canvases, ids_ref, x_in, three_ref, first_ref, second_grad_ref, small_params,
    qkv_ref, fc_mid_in, small_in, proj_grad_in, qkv_grad_in,
    out0_ref, out1_ref, out2_ref, out3_ref, fc1_own_ref, fc2_own_ref, small_own_ref, proj_own_ref,
    qkv_own_ref, last_own_ref,
    x_ref, gone_ref, cpe_sum_ref, sum_ref, fc_part_ref, fc_whole_ref, fc_got_ref, mine_ref, first_got_ref,
    total_ref, second_got_ref, piece_send, piece_receive, send, receive, last_send, last_receive,
    cpe_ref, fc_mid_ref, small_ref, proj_grad_ref, qkv_grad_ref, *buffers,
):
    me = lax.axis_index("head")
    dp = lax.axis_index("dp")
    step = pl.program_id(0)
    steps = pl.num_programs(0)
    slots = high_slots(count)
    fc_sums = [
        HighSum(
            count, fc_mid_ref.at[kind], fc_part_ref.at[kind], fc_whole_ref.at[kind],
            fc_got_ref.at[kind], send, receive, kind * slots,
        )
        for kind in range(2)
    ]
    sources = (small_ref, proj_grad_ref, qkv_grad_ref)
    targets = (small_own_ref, proj_own_ref, qkv_own_ref)
    sums = []
    for number, (item, start, height, padded, lanes) in enumerate(pieces):
        near, far, own, mid, low, part, got = buffers[7 * number : 7 * number + 7]
        sums.append(
            FullSum(
                count, sources[item], pl.ds(start, height), near, far, own, mid, low, part, got, send,
                receive, 2 * slots + number * (slots + 4),
            )
        )

    def piece_copy(index, move):
        target = (out1_ref, out2_ref, out3_ref)[move - 1]
        return remote(
            gone_ref.at[index, move - 1], target.at[aligned(index, PLACES)],
            piece_send.at[index, move - 1], piece_receive.at[index, move - 1], peer(move),
        )

    def first_copy(move):
        return remote(
            mine_ref.at[move], first_got_ref.at[move - 1], last_send.at[move - 1],
            last_receive.at[move - 1], peer(move),
        )

    def second_copy(hop):
        return remote(
            total_ref, second_got_ref.at[hop - 1], last_send.at[2 + hop], last_receive.at[2 + hop],
            (lax.rem(dp + hop, count), me),
        )

    @pl.when(step == 0)
    def _():
        meet(
            [peer(1), peer(2), peer(3)] + [(lax.rem(dp + hop, count), me) for hop in range(1, count)]
        )
        spread_small(small_params, cpe_ref)
        fc_mid_ref[...] = fc_mid_in[...]
        qkv_grad_ref[...] = qkv_grad_in[...]
        proj_grad_ref[...] = proj_grad_in[...]
        small_ref[...] = small_in[...]
        cpe_sum_ref[...] = jnp.zeros_like(cpe_sum_ref)
        sum_ref[...] = jnp.zeros_like(sum_ref)

    events = []
    for item, slots_of in zip(sums, STAGES):
        actions = (
            item.to_core, item.to_far, item.to_low, item.to_high, item.rest.share_high, item.rest.share_low,
        )
        events += list(zip(slots_of, actions))
    for item, slots_of in zip(fc_sums, FC_STAGES):
        events += list(zip(slots_of, (item.to_high, item.share_high, item.share_low)))

    def run(when):
        for slot, action in events:
            if slot == when:
                action()

    for when in range(canvases):
        pl.when(step == when)(lambda: run(when))

    norm_grad = nt(three_ref[0], qkv_ref[lax.bitwise_xor(me, 0)])
    for tile in range(1, TILES):
        norm_grad += nt(three_ref[tile], qkv_ref[lax.bitwise_xor(me, tile)])
    first = first_ref[...]
    center = row_mean(first)
    square = row_mean(first * first)
    inverse = lax.rsqrt(square - center * center + EPSILON)
    hat = (first - center) * inverse
    weighted = norm_grad * cpe_ref[GAIN1 : GAIN1 + 1, :]
    first_grad = second_grad_ref[...] + inverse * (
        weighted - row_mean(weighted) - hat * row_mean(weighted * hat)
    )
    sum_ref[0:1, :] += jnp.sum(first_grad, axis=0, keepdims=True)
    sum_ref[1:2, :] += jnp.sum(norm_grad * hat, axis=0, keepdims=True)
    sum_ref[2:3, :] += jnp.sum(norm_grad, axis=0, keepdims=True)
    x_ref[...] = x_in[...].astype(F32)
    rows, cols = step_masks(*read_cuts(ids_ref, canvases))
    results = []
    for tile in range(TILES):
        field = first_grad[:, LANES * tile : LANES * (tile + 1)]
        other = x_ref[:, lane(tile)]
        others = {0: other, 1: shift_rows(other * rows[1], -1), -1: shift_rows(other * rows[-1], 1)}
        moved = [shift_cols(field, cols, col) for col in (-1, 0, 1)]
        result = field
        for row in (-1, 0, 1):
            line = None
            for col in (-1, 0, 1):
                tap = (1 - row) * 3 + 1 - col
                wide_tap = jnp.broadcast_to(cpe_ref[tap : tap + 1, lane(tile)], (PLACES, LANES))
                term = wide_tap * moved[col + 1]
                line = term if line is None else line + term
                product = others[row] * moved[col + 1]
                cpe_sum_ref[tap, :, lane(tile)] += jnp.sum(product.reshape(PLACES // 8, 8, LANES), axis=0)
            line = shift_rows(line, row)
            result = result + (line * rows[row] if row else line)
        results.append(result)
    result = jnp.concatenate(results, axis=1)
    x_ref[...] = result
    out0_ref[...] = x_ref[:, aligned(me, LANES)].astype(BF16)
    for move in (1, 2, 3):
        gone_ref[step, move - 1] = x_ref[:, aligned(lax.bitwise_xor(me, move), LANES)].astype(BF16)
    for move in (2, 3, 1):
        piece_copy(step, move).start()

    @pl.when(step == steps - 1)
    def _():
        sum_ref[3:12, :] = jnp.sum(cpe_sum_ref[...], axis=1)
        for move in range(4):
            mine_ref[move] = sum_ref[:, aligned(lax.bitwise_xor(me, move), LANES)]
        for move in (1, 2, 3):
            first_copy(move).start()
        run(canvases)
        total = mine_ref[0]
        for move in (1, 2, 3):
            first_copy(move).wait()
            total += first_got_ref[move - 1]
        total_ref[...] = total
        for hop in range(1, count):
            second_copy(hop).start()
        run(canvases + 1)
        for item in fc_sums:
            item.finish()
        fc1_own_ref[...] = fc_whole_ref[0, :D, :]
        fc2_own_ref[...] = fc_whole_ref[1, :D, :]
        for hop in range(1, count):
            second_copy(hop).wait()
            total += second_got_ref[hop - 1]
        last_own_ref[...] = total
        for piece, item in zip(pieces, sums):
            item.rest.finish()
            targets[piece[0]][piece[1] : piece[1] + piece[2], :] = item.whole[: piece[2], :]

        def settle(index, carry):
            for move in (1, 2, 3):
                piece_copy(index, move).wait()
            return carry

        lax.fori_loop(0, steps, settle, 0)


def tail(ids, x, three, first, second_grad, params_small, qkv, fc_mid, qkv_grad, proj_grad, small):
    rows = first.shape[0]
    canvases = rows // PLACES
    count = lax.axis_size("dp")
    segments = [small, proj_grad, qkv_grad]
    pieces = plan_pieces([item.shape[1:] for item in segments], count)
    slots = high_slots(count)
    wide = rows_spec(D)
    piece = rows_spec(LANES)
    hbm = pl.BlockSpec(memory_space=pl.ANY)
    half = fc_mid.shape[1]
    group = count // 2
    total_slots = 2 * slots + len(pieces) * (slots + 4)
    last = (LAST_ROWS, LANES)
    return pl.pallas_call(
        lambda *refs: tail_kernel(count, pieces, canvases, *refs),
        grid=(canvases,),
        in_specs=[pl.BlockSpec(memory_space=pltpu.SMEM), wide] + [
            pl.BlockSpec((TILES, PLACES, 3 * LANES), lambda i: (0, i, 0)), wide, wide,
            once(params_small.shape), once(qkv.shape), once(fc_mid.shape),
        ] + [once(item.shape) for item in segments],
        out_specs=[piece, hbm, hbm, hbm, once((D, D)), once((D, D))]
        + [once(item.shape[1:]) for item in segments] + [once(last)],
        out_shape=[like((rows, LANES), BF16)] * 4 + [like((D, D), BF16)] * 2
        + [like(item.shape[1:], BF16) for item in segments] + [like(last, F32)],
        scratch_shapes=[
            pltpu.VMEM((PLACES, D), F32), pltpu.VMEM((canvases, 3, PLACES, LANES), BF16),
            pltpu.VMEM((9, 8, D), F32), pltpu.VMEM((LAST_ROWS, D), F32),
            pltpu.VMEM((2, group - 1, half // group, D), BF16), pltpu.VMEM((2, 2 * half, D), BF16),
            pltpu.VMEM((2, half, D), BF16),
            pltpu.VMEM((4,) + last, F32), pltpu.VMEM((3,) + last, F32), pltpu.VMEM(last, F32),
            pltpu.VMEM((count - 1,) + last, F32),
            pltpu.SemaphoreType.DMA((canvases, 3)), pltpu.SemaphoreType.DMA((canvases, 3)),
            pltpu.SemaphoreType.DMA((total_slots,)), pltpu.SemaphoreType.DMA((total_slots,)),
            pltpu.SemaphoreType.DMA((2 + count,)), pltpu.SemaphoreType.DMA((2 + count,)),
        ] + [pltpu.VMEM((SMALL_SIZE, D), F32)]
        + [pltpu.VMEM(item.shape, BF16) for item in [fc_mid] + segments]
        + sum_scratch(pieces, count),
        compiler_params=params(collective_id=3, has_side_effects=True),
        cost_estimate=pl.CostEstimate(
            flops=rows * D * D * 12, bytes_accessed=canvases * 3 * 10**6, transcendentals=0
        ),
        name="tail",
    )(ids, x, three, first, second_grad, params_small, qkv, fc_mid, *segments)


def collect_kernel(me_ref, *refs):
    out_ref = refs[-1]
    for item, piece_ref in enumerate(refs[:-1]):

        @pl.when(pl.program_id(0) == item)
        def _():
            out_ref[...] = piece_ref[...].astype(F32)


def collect(me, pieces):
    rows = pieces[0].shape[0]
    return pl.pallas_call(
        collect_kernel,
        grid_spec=pltpu.PrefetchScalarGridSpec(
            num_scalar_prefetch=1,
            grid=(4,),
            in_specs=[once((rows, LANES))] * 4,
            out_specs=pl.BlockSpec((rows, LANES), lambda i, me: (lax.bitwise_xor(me[0], i), 0)),
        ),
        out_shape=like((4 * rows, LANES), F32),
        compiler_params=params(),
        name="collect",
    )(me, *pieces)


def finish_kernel(
    me_ref, p0_ref, p1_ref, p2_ref, p3_ref, fc1_ref, fc2_ref, small_ref, proj_ref, qkv_ref, last_ref,
    grad_ref, cpe_ref, vectors_ref, qkv_out_ref, qv_ref, crpe_ref, proj_out_ref, fc1_out_ref,
    bias_ref, fc2_out_ref,
):
    for item, piece_ref in enumerate((p0_ref, p1_ref, p2_ref, p3_ref)):

        @pl.when(pl.program_id(0) == item)
        def _():
            grad_ref[...] = piece_ref[...].astype(F32)

    @pl.when(pl.program_id(0) == 0)
    def _():
        cpe_ref[...] = last_ref[3:12, :]
        small = small_ref[...].astype(F32)
        vectors_ref[...] = jnp.concatenate(
            [last_ref[0:3, :], small[51:55, :], jnp.zeros((1, LANES), F32)], axis=0
        )
        qkv_out_ref[...] = qkv_ref[...].astype(F32)
        qv_ref[...] = small[49:51, :]
        crpe_ref[...] = small[:49, :]
        proj_out_ref[...] = proj_ref[...].astype(F32)
        fc1_out_ref[...] = fc1_ref[...].astype(F32)
        bias_ref[...] = small[64:68, :]
        fc2_out_ref[...] = fc2_ref[...].astype(F32)


def finish(me, pieces, fc1, fc2, small, proj, qkv, last):
    rows = pieces[0].shape[0]
    shapes = [
        (9, LANES), (8, LANES), qkv.shape, (2, LANES), (49, LANES), proj.shape, fc1.shape,
        (4, LANES), fc2.shape,
    ]
    return pl.pallas_call(
        finish_kernel,
        grid_spec=pltpu.PrefetchScalarGridSpec(
            num_scalar_prefetch=1,
            grid=(4,),
            in_specs=[once((rows, LANES))] * 4
            + [once(item.shape) for item in (fc1, fc2, small, proj, qkv, last)],
            out_specs=[
                pl.BlockSpec((rows, LANES), lambda i, me: (lax.bitwise_xor(me[0], i), 0)),
            ] + [once(shape) for shape in shapes],
        ),
        out_shape=[like((4 * rows, LANES), F32)] + [like(shape, F32) for shape in shapes],
        compiler_params=params(),
        name="finish",
    )(me, *pieces, fc1, fc2, small, proj, qkv, last)


def body(
    block_in, crop_ids, cotangent, cpe_kernel, cpe_bias, norm1_gain, norm1_shift, qkv_weight,
    qv_bias, crpe_kernel, proj_weight, proj_bias, norm2_gain, norm2_shift, fc1_weight, fc1_bias,
    fc2_weight, fc2_bias,
):
    head = lax.axis_index("head")
    me = head.reshape(1).astype(jnp.int32)
    rows = block_in.shape[0] // 4
    ids = crop_ids.reshape(crop_ids.shape[0], PLACES)

    def swap(values, move):
        return lax.ppermute(values, "head", [(item, item ^ move) for item in range(4)])

    packed = jnp.concatenate([
        cpe_kernel, crpe_kernel, cpe_bias[None], norm1_gain[None], norm1_shift[None], qv_bias,
        proj_bias[None], norm2_gain[None], norm2_shift[None], fc2_bias[None],
        fc1_bias.reshape(4, LANES), jnp.zeros((1, LANES), BF16),
    ]).astype(F32)
    own_weights = jnp.concatenate([fc1_weight, fc2_weight, proj_weight])
    extra = padded_rows(own_weights.shape[0], lax.axis_size("dp")) - own_weights.shape[0]
    if extra:
        own_weights = jnp.pad(own_weights, ((0, extra), (0, 0)))
    first, hidden, query, key, value, x, qkv, small, far_weights = head_part(
        ids, packed, qkv_weight.reshape(D, 3 * LANES), block_in, own_weights
    )
    cotangent, query = lax.optimization_barrier((cotangent, query))
    cot_pieces = [
        lax.dynamic_slice_in_dim(cotangent, lax.bitwise_xor(head, move) * rows, rows, 0)
        for move in range(4)
    ]
    cot_parts = [cot_pieces[0]] + [swap(cot_pieces[move], move) for move in (1, 2, 3)]

    soft, context, conv, attended = front(ids, query, key, value, small)
    results = middle(attended, first, cot_parts, small, own_weights, far_weights)
    second_grad, att_grad, fc_mid, proj_grad, middle_sum, bias_grad = results[4:]
    out_parts = [results[0]] + [swap(results[move], move) for move in (1, 2, 3)]
    three, qkv_grad, small_grad = back(
        ids, att_grad, query, value, soft, context, conv, hidden, small, middle_sum, bias_grad
    )
    three, out_parts = lax.optimization_barrier((three, out_parts))
    results = tail(
        ids, x, three, first, second_grad, small, qkv, fc_mid, qkv_grad, proj_grad, small_grad
    )
    (input_grad, cpe_g, vectors, qkv_g, qv_g, crpe_g, proj_g, fc1_g, bias_g, fc2_g) = finish(
        me, results[:4], *results[4:]
    )
    return (
        collect(me, out_parts), input_grad, cpe_g, vectors[0], vectors[1], vectors[2],
        qkv_g.reshape(D, 3, LANES), qv_g, crpe_g, proj_g, vectors[3], vectors[4], vectors[5],
        fc1_g, bias_g.reshape(D), fc2_g, vectors[6],
    )


def solution(mesh):
    return jax.shard_map(
        body,
        mesh=mesh,
        in_specs=(
            P("dp", "head"), P("dp", None, None), P("dp", "head"), P(None, "head"), P("head"),
            P("head"), P("head"), P(None, None, "head"), P(None, "head"), P(None, "head"),
            P("head", None), P("head"), P("head"), P("head"), P(None, "head"), P("head"),
            P("head", None), P("head"),
        ),
        out_specs=(
            P("dp", "head"), P("dp", "head"), P(None, "head"), P("head"), P("head"), P("head"),
            P(None, None, "head"), P(None, "head"), P(None, "head"), P("head", None), P("head"),
            P("head"), P("head"), P(None, "head"), P("head"), P("head", None), P("head"),
        ),
        check_vma=False,
    )
```

```python
import jax
import jax.numpy as jnp
from jax import lax
from jax.experimental import pallas as pl
from jax.experimental.pallas import tpu as pltpu
from jax.sharding import PartitionSpec as P

D = 512
HEADS = 8
HEAD_DIM = 64
HIDDEN = 2048
SIDE = 16
PLACES = 256
LANES = 128
TILES = 4
REACH = (1, 2, 3, 3)
GAP = 3
GRID_ROWS = SIDE + 3 * GAP + 1
EPSILON = 1e-06
SCALE = HEAD_DIM ** (-0.5)
F32 = jnp.float32
BF16 = jnp.bfloat16


def dot(left, right, dims):
    return lax.dot_general(left, right, (dims, ((), ())), preferred_element_type=F32)


def nn(left, right):
    return dot(left, right, ((1,), (0,)))


def nt(left, right):
    return dot(left, right, ((1,), (1,)))


def tn(left, right):
    return dot(left, right, ((0,), (0,)))


def lane(tile):
    return pl.ds(LANES * tile, LANES)


def fill_masks(cut, col_cuts, mask_ref):
    col = lax.broadcasted_iota(jnp.int32, (SIDE, LANES), 0)
    for band in range(2):
        here = (col >= col_cuts[band]).astype(jnp.int32)
        for step in range(-3, 4):
            if step == 0:
                continue
            there = (col + step >= col_cuts[band]).astype(jnp.int32)
            good = (col + step >= 0) & (col + step < SIDE) & (here == there)
            mask_ref[band, step + 3] = jnp.where(good, 1.0, 0.0).astype(F32)


def place_ids(cut, col_cuts):
    place = lax.broadcasted_iota(jnp.int32, (PLACES, LANES), 0)
    row = lax.shift_right_logical(place, 4)
    col = lax.bitwise_and(place, 15)
    band = (row >= cut).astype(jnp.int32)
    col_cut = jnp.where(band > 0, col_cuts[1], col_cuts[0])
    side = (col >= col_cut).astype(jnp.int32)
    return band, side


def spread(read_row, reach, cut, mask_ref, grid_ref, plane):
    zero = jnp.zeros((GAP * SIDE, LANES), F32)
    for step in range(-reach, reach + 1):
        start = pl.multiple_of(SIDE * (GAP + cut), SIDE)
        grid_ref[plane + step, pl.ds(start, GAP * SIDE), :] = zero
    for row in range(SIDE):
        lower = (row >= cut).astype(jnp.int32)
        start = pl.multiple_of(SIDE * (row + GAP + GAP * lower), SIDE)
        values = read_row(row)
        for step in range(-reach, reach + 1):
            moved = values
            if step != 0:
                moved = pltpu.roll(values, (-step) % SIDE, 0) * mask_ref[lower, step + 3]
            grid_ref[plane + step, pl.ds(start, SIDE), :] = moved


def add_to(store, key, term):
    store[key] = term if key not in store else store[key] + term


def over_bands(reach, cut, body):
    every = range(2 * reach + 2)
    for lower in range(2):
        first = cut if lower else 0
        height = SIDE - cut if lower else cut
        pairs = (height + 1) // 2
        shift = GAP * lower + GAP - reach

        def pair(index, places):
            row = first + 2 * index
            body(row, row + shift, first + height - 1, places)

        def inner(index, carry):
            pair(index, every)
            return carry

        pair(0, every[reach:])
        lax.fori_loop(1, pairs - 1, inner, 0)
        pair(pairs - 1, every[: reach + 2])


def conv_tiles(items, reach, cut, grid_ref, taps_ref, tap_reach, out_ref):
    width = 2 * tap_reach + 1
    chains = 3

    def body(row, base, last, places):
        for tile, plane in items:
            total = {}
            for step in range(-reach, reach + 1):
                taps = [
                    taps_ref[(dr + tap_reach) * width + step + tap_reach, :, lane(tile)]
                    for dr in range(-reach, reach + 1)
                ]
                for place in places:
                    for half in range(2):
                        start = pl.multiple_of(SIDE * (base + place) + 8 * half, 8)
                        field = grid_ref[plane + step, pl.ds(start, 8), :]
                        for out in range(2):
                            tap = place - out
                            if 0 <= tap <= 2 * reach:
                                add_to(total, (out, half, step % chains), taps[tap] * field)
            for out in range(2):
                for half in range(2):
                    start = pl.multiple_of(SIDE * (row + out) + 8 * half, 8)
                    out_ref[pl.ds(start, 8), lane(tile)] = sum(
                        [total[out, half, chain] for chain in range(1, chains)], total[out, half, 0]
                    )

    over_bands(reach, cut, body)


def conv_back_tiles(items, reach, cut, grid_ref, taps_ref, tap_reach, other_ref, out_ref, sum_ref):
    width = 2 * tap_reach + 1
    chains = 2

    def body(row, base, last, places):
        keep = jnp.where(row + 1 > last, 0.0, 1.0).astype(F32)
        for tile, plane in items:
            other = {}
            for out in range(2):
                for half in range(2):
                    start = pl.multiple_of(SIDE * (row + out) + 8 * half, 8)
                    value = other_ref[pl.ds(start, 8), lane(tile)]
                    other[out, half] = value * keep if out else value
            total = {}
            for step in range(-reach, reach + 1):
                sums = {}
                ids = [
                    (tap_reach - dr) * width + tap_reach - step for dr in range(-reach, reach + 1)
                ]
                taps = [taps_ref[item, :, lane(tile)] for item in ids]
                for place in places:
                    for half in range(2):
                        start = pl.multiple_of(SIDE * (base + place) + 8 * half, 8)
                        field = grid_ref[plane + step, pl.ds(start, 8), :]
                        for out in range(2):
                            tap = place - out
                            if 0 <= tap <= 2 * reach:
                                add_to(total, (out, half, step % chains), taps[tap] * field)
                                add_to(sums, tap, other[out, half] * field)
                for tap, part in sums.items():
                    sum_ref[ids[tap], :, lane(tile)] += part
            for out in range(2):
                for half in range(2):
                    start = pl.multiple_of(SIDE * (row + out) + 8 * half, 8)
                    out_ref[pl.ds(start, 8), lane(tile)] = sum(
                        [total[out, half, chain] for chain in range(1, chains)], total[out, half, 0]
                    )

    over_bands(reach, cut, body)


def row_mean(values):
    return jnp.sum(values, axis=1, keepdims=True) * (1.0 / D)


def pick(ids, rows):
    out = rows[0]
    for crop in range(1, 4):
        out = jnp.where(ids >= crop, rows[crop], out)
    return out


def crop_reduce(ids, values, op, empty):
    return [op(jnp.where(ids == crop, values, empty), axis=0, keepdims=True) for crop in range(4)]


def head_block():
    row = lax.broadcasted_iota(jnp.int32, (2 * LANES, 2 * LANES), 0)
    col = lax.broadcasted_iota(jnp.int32, (2 * LANES, 2 * LANES), 1)
    same = lax.bitwise_and(row, HEAD_DIM) == lax.bitwise_and(col, HEAD_DIM)
    return jnp.where(same, 1.0, 0.0).astype(F32)


def both(values, masks):
    return jnp.concatenate([values * masks[0], values * masks[1]], axis=1)


def read_cuts(ids_ref, canvases):
    canvas = lax.axis_index("head") * canvases + pl.program_id(0)

    def count(places, bound):
        return sum(jnp.where(ids_ref[canvas, place] < bound, 1, 0) for place in places)

    cut = count(range(0, PLACES, SIDE), 2)
    upper = count(range(SIDE), 1)
    lower = count(range(PLACES - SIDE, PLACES), 3)
    return cut, (upper, lower)


SMALL_SIZE = 72
(CPE, CRPE, CPE_BIAS, GAIN1, SHIFT1, QUERY_BIAS, VALUE_BIAS, PROJ_BIAS, GAIN2, SHIFT2, FC2_BIAS, FC1_BIAS) = (
    0, 9, 58, 59, 60, 61, 62, 63, 64, 65, 66, 67,
)


def spread_small(small_in, small_ref):
    me = lax.axis_index("head")
    for tile in range(TILES):
        small_ref[:, lane(tile)] = small_in[lax.bitwise_xor(me, tile)]


def outer_taps(tap):
    return max(abs(tap // 7 - 3), abs(tap % 7 - 3)) > 2


def keep_head(tap, tile, values):
    if tile != 2 or not outer_taps(tap):
        return values
    col = lax.broadcasted_iota(jnp.int32, values.shape, len(values.shape) - 1)
    return jnp.where(col < HEAD_DIM, 0.0, values)


def spread_taps(small_ref, row, count, masked, taps_ref):
    for tap in range(count):
        for tile in range(TILES):
            values = jnp.broadcast_to(small_ref[row + tap : row + tap + 1, lane(tile)], (8, LANES))
            taps_ref[tap, :, lane(tile)] = keep_head(tap, tile, values) if masked else values


def whole(shape):
    return pl.BlockSpec(shape, lambda *_: (0,) * len(shape))


def once(shape):
    return pl.BlockSpec(shape, lambda *_: (0,) * len(shape), pipeline_mode=pl.Buffered(1))


def rows_spec(width, base=0):
    return pl.BlockSpec((PLACES, width), lambda i, *_: (i + base, 0))


def context_spec(base):
    return pl.BlockSpec((1, TILES, 2 * LANES, 2 * LANES), lambda i, *_: (i + base, 0, 0, 0))


def like(shape, dtype):
    return jax.ShapeDtypeStruct(shape, dtype)


def params(**given):
    return pltpu.CompilerParams(vmem_limit_bytes=58 * 2**20, **given)


MESH = pl.DeviceIdType.MESH
PIECE_ROWS = 256
SMALL_ROWS = 128


def peer(move):
    return (lax.axis_index("dp"), lax.bitwise_xor(lax.axis_index("head"), move))


def meet(peers):
    barrier = pltpu.get_barrier_semaphore()
    for item in peers:
        pl.semaphore_signal(barrier, inc=1, device_id=item, device_id_type=MESH)
    pl.semaphore_wait(barrier, len(peers))


def remote(source, target, send, receive, device):
    return pltpu.make_async_remote_copy(
        src_ref=source, dst_ref=target, send_sem=send, recv_sem=receive,
        device_id=device, device_id_type=MESH,
    )


def plan_pieces(shapes, count):
    pieces = []
    for item, (rows, lanes) in enumerate(shapes):
        height = min(PIECE_ROWS, rows)
        for start in range(0, rows, height):
            pieces.append((item, start, height, padded_rows(height, count), lanes))
    return pieces


def padded_rows(height, count):
    unit = 16 * count
    return -(-height // unit) * unit


def place_on_dp():
    dp = lax.axis_index("dp")
    return dp, lax.rem(dp, 2), dp // 2


def low_peer():
    dp, low, _ = place_on_dp()
    return (dp + 1 - 2 * low, lax.axis_index("head"))


def high_peer(step, group):
    _, low, high = place_on_dp()
    return (lax.rem(high + step, group) * 2 + low, lax.axis_index("head"))


def aligned(index, size):
    return pl.ds(pl.multiple_of(index * size, size), size)


class HighSum:
    def __init__(self, count, mid, part, whole, got, send, receive, slot):
        self.group = count // 2
        self.got = got
        self.mid, self.part, self.whole = mid, part, whole
        self.send, self.receive, self.slot = send, receive, slot
        self.half = mid.shape[0]
        self.size = self.half // self.group

    def copy(self, source, target, slot, device):
        return remote(
            source, target, self.send.at[self.slot + slot], self.receive.at[self.slot + slot], device
        )

    def high(self, step):
        _, _, high = place_on_dp()
        other = lax.rem(high + step, self.group)
        return self.copy(
            self.mid.at[aligned(other, self.size)], self.part.at[step - 1], step - 1,
            high_peer(step, self.group),
        )

    def spot(self):
        dp, low, high = place_on_dp()
        return self.whole.at[aligned(low * self.group + high, self.size)]

    def share(self, step):
        spot = self.spot()
        return self.copy(spot, spot, self.group - 2 + step, high_peer(step, self.group))

    def last(self):
        _, low, _ = place_on_dp()
        here = self.whole.at[aligned(low, self.half)]
        return self.copy(here, self.got, 2 * self.group - 2, low_peer())

    def to_high(self):
        for step in range(1, self.group):
            self.high(step).start()

    def share_high(self):
        _, _, high = place_on_dp()
        total = self.mid[aligned(high, self.size), :].astype(F32)
        for step in range(1, self.group):
            self.high(step).wait()
            total += self.part[step - 1].astype(F32)
        self.spot()[...] = total.astype(BF16)
        for step in range(1, self.group):
            self.share(step).start()

    def share_low(self):
        for step in range(1, self.group):
            self.share(step).wait()
        self.last().start()

    def finish(self):
        _, low, _ = place_on_dp()
        self.last().wait()
        self.whole[aligned(1 - low, self.half), :] = self.got[...]


def high_slots(count):
    return count - 1


class FullSum:
    def __init__(self, count, grad, span, near, far, whole, mid, low, part, got, send, receive, slot):
        self.grad, self.span, self.near, self.far = grad, span, near, far
        self.whole, self.mid, self.low = whole, mid, low
        self.height = far.shape[0]
        self.send, self.receive, self.slot = send, receive, slot
        self.rest = HighSum(count, mid, part, whole, got, send, receive, slot + 4)

    def copy(self, source, target, slot, device):
        return remote(
            source, target, self.send.at[self.slot + slot], self.receive.at[self.slot + slot], device
        )

    def near_copy(self, item):
        return self.copy(
            self.grad.at[1 + 2 * item, self.span], self.near.at[item], item, peer(1)
        )

    def far_copy(self):
        return self.copy(self.whole.at[: self.height], self.far, 2, peer(2))

    def low_copy(self):
        _, low, _ = place_on_dp()
        return self.copy(self.whole.at[aligned(1 - low, self.mid.shape[0])], self.low, 3, low_peer())

    def to_core(self):
        self.near_copy(1).start()
        self.near_copy(0).start()

    def to_far(self):
        self.near_copy(1).wait()
        self.whole[: self.height, :] = (
            self.grad[2, self.span, :].astype(F32) + self.near[1].astype(F32)
        ).astype(BF16)
        self.far_copy().start()

    def to_low(self):
        self.near_copy(0).wait()
        self.far_copy().wait()
        self.whole[: self.height, :] = (
            self.grad[0, self.span, :].astype(F32) + self.near[0].astype(F32)
            + self.far[...].astype(F32)
        ).astype(BF16)
        rows = self.whole.shape[0]
        if rows > self.height:
            self.whole[self.height :, :] = jnp.zeros((rows - self.height, self.whole.shape[1]), BF16)
        self.low_copy().start()

    def to_high(self):
        _, low, _ = place_on_dp()
        self.low_copy().wait()
        half = self.mid.shape[0]
        self.mid[...] = (
            self.whole[aligned(low, half), :].astype(F32) + self.low[...].astype(F32)
        ).astype(BF16)
        self.rest.to_high()


def sum_scratch(pieces, count):
    scratch = []
    for _, _, height, padded, lanes in pieces:
        scratch += [
            pltpu.VMEM((2, height, lanes), BF16), pltpu.VMEM((height, lanes), BF16),
            pltpu.VMEM((padded, lanes), BF16), pltpu.VMEM((padded // 2, lanes), BF16),
            pltpu.VMEM((padded // 2, lanes), BF16),
            pltpu.VMEM((count // 2 - 1, padded // count, lanes), BF16),
            pltpu.VMEM((padded // 2, lanes), BF16),
        ]
    return scratch


def step_masks(cut, col_cuts):
    place = lax.broadcasted_iota(jnp.int32, (PLACES, LANES), 0)
    row = lax.shift_right_logical(place, 4)
    col = lax.bitwise_and(place, 15)
    col_cut = jnp.where(row >= cut, col_cuts[1], col_cuts[0])
    rows = {
        1: (row < SIDE - 1) & (row + 1 != cut),
        -1: (row > 0) & (row != cut),
    }
    cols = {
        1: (col < SIDE - 1) & (col + 1 != col_cut),
        -1: (col > 0) & (col != col_cut),
    }
    return [
        {key: jnp.where(mask, 1.0, 0.0).astype(F32) for key, mask in masks.items()}
        for masks in (rows, cols)
    ]


def shift_rows(values, step):
    if step == 0:
        return values
    zero = jnp.zeros((SIDE, values.shape[1]), values.dtype)
    if step > 0:
        return jnp.concatenate([values[SIDE:], zero], axis=0)
    return jnp.concatenate([zero, values[:-SIDE]], axis=0)


def shift_cols(values, masks, step):
    if step == 0:
        return values
    return pltpu.roll(values, (-step) % PLACES, 0) * masks[step]


def head_kernel(
    canvases, count, ids_ref, small_own, qkv_own, x_in, qkv_in, share_in,
    first_ref, hidden_ref, query_ref, key_ref, value_ref, x_out, qkv_ref, small_out, far_out,
    x_ref, landing_ref, mine_ref, small_ref, qkv_all, small_got, send, receive, weight_send, weight_receive,
    share_send, share_receive, local,
):
    me = lax.axis_index("head")
    step = pl.program_id(0)
    rows = canvases * PLACES

    def piece(index, move):
        start = pl.multiple_of(lax.bitwise_xor(me, move) * rows + index * PLACES, PLACES)
        return remote(
            x_in.at[pl.ds(start, PLACES)], landing_ref.at[index, move - 1], send.at[index, move - 1],
            receive.at[index, move - 1], peer(move),
        )

    def weight(number, source, target, move):
        return remote(source, target, weight_send.at[number], weight_receive.at[number], peer(move))

    far = weight(0, qkv_in, qkv_all.at[1], 2)
    near = weight(1, qkv_in, qkv_all.at[0], 1)
    relay = weight(2, qkv_all.at[1], qkv_all.at[2], 1)
    smalls = [weight(2 + move, small_got.at[0], small_got.at[move], move) for move in (1, 2, 3)]
    mine = pltpu.make_async_copy(x_in.at[aligned(me, rows)], mine_ref, local.at[0])
    dp = lax.axis_index("dp")
    spot = aligned(dp, share_in.shape[0] // count)
    share = remote(share_in.at[spot], far_out.at[spot], share_send.at[0], share_receive.at[0], peer(2))
    group = count // 2
    _, low, high = place_on_dp()
    spread_high = [
        remote(
            far_out.at[spot], far_out.at[spot], share_send.at[hop], share_receive.at[hop],
            high_peer(hop, group),
        )
        for hop in range(1, group)
    ]
    spread_low = []
    for hop in range(group):
        source = lax.rem(high - hop + group, group) * 2 + low
        there = aligned(source, share_in.shape[0] // count)
        spread_low.append(
            remote(
                far_out.at[there], far_out.at[there], share_send.at[group + hop],
                share_receive.at[group + hop], low_peer(),
            )
        )

    @pl.when(step == 0)
    def _():
        mine.start()
        small_got[0] = small_own[...]
        meet(
            [peer(move) for move in (1, 2, 3)] + [low_peer()]
            + [high_peer(hop, group) for hop in range(1, group)]
        )
        for item in smalls:
            item.start()
        share.start()
        for move in (2, 3, 1):
            piece(0, move).start()
        far.start()
        near.start()

        def send_piece(index, carry):
            for move in (2, 3, 1):
                piece(index, move).start()
            return carry

        lax.fori_loop(1, canvases, send_piece, 0)
        for item in smalls:
            item.wait()
        for move in range(4):
            small_ref[:, aligned(lax.bitwise_xor(me, move), LANES)] = small_got[move]
            small_out[move] = small_got[move]
        mine.wait()

    for hop in range(1, group):

        @pl.when(step == min(1 + hop, canvases - 1))
        def _():
            spread_high[hop - 1].wait()
            spread_low[hop].start()

    @pl.when(step == canvases - 1)
    def _():
        for item in spread_low:
            item.wait()

    x_ref[:, aligned(me, LANES)] = mine_ref[aligned(step, PLACES), :].astype(F32)
    for move in (1, 2, 3):
        piece(step, move).wait()
        x_ref[:, aligned(lax.bitwise_xor(me, move), LANES)] = landing_ref[step, move - 1].astype(F32)
    rows_mask, cols_mask = step_masks(*read_cuts(ids_ref, canvases))
    for tile in range(TILES):
        field = x_ref[:, lane(tile)]
        moved = [shift_cols(field, cols_mask, col) for col in (-1, 0, 1)]
        result = field + small_ref[CPE_BIAS : CPE_BIAS + 1, lane(tile)]
        for row in (-1, 0, 1):
            line = None
            for col in (-1, 0, 1):
                tap = CPE + (row + 1) * 3 + col + 1
                term = jnp.broadcast_to(small_ref[tap : tap + 1, lane(tile)], (PLACES, LANES)) * moved[col + 1]
                line = term if line is None else line + term
            line = shift_rows(line, row)
            result = result + (line * rows_mask[row] if row else line)
        first_ref[:, lane(tile)] = result
    x_out[...] = x_ref[...].astype(BF16)
    first = first_ref[...]
    center = row_mean(first)
    square = row_mean(first * first)
    inverse = lax.rsqrt(square - center * center + EPSILON)
    hidden = (
        (first - center) * inverse * small_ref[GAIN1 : GAIN1 + 1, :] + small_ref[SHIFT1 : SHIFT1 + 1, :]
    ).astype(BF16)
    hidden_ref[...] = hidden

    @pl.when(step == 0)
    def _():
        share.wait()
        for item in spread_high + spread_low[:1]:
            item.start()
        far.wait()
        relay.start()
        near.wait()
        relay.wait()
        qkv_ref[0] = qkv_own[...]
        for move in (1, 2, 3):
            qkv_ref[move] = qkv_all[move - 1]

    for tile in range(TILES):
        three = nn(hidden, qkv_ref[lax.bitwise_xor(me, tile)])
        query_ref[:, lane(tile)] = (
            three[:, :LANES] + small_ref[QUERY_BIAS : QUERY_BIAS + 1, lane(tile)]
        ).astype(BF16)
        key_ref[:, lane(tile)] = three[:, LANES : 2 * LANES].astype(BF16)
        value_ref[:, lane(tile)] = (
            three[:, 2 * LANES :] + small_ref[VALUE_BIAS : VALUE_BIAS + 1, lane(tile)]
        ).astype(BF16)


def head_part(ids, small, qkv, block_in, share):
    count = lax.axis_size("dp")
    rows = block_in.shape[0] // 4
    canvases = rows // PLACES
    wide = rows_spec(D)
    hbm = pl.BlockSpec(memory_space=pl.ANY)
    return pl.pallas_call(
        lambda *refs: head_kernel(canvases, count, *refs),
        grid=(canvases,),
        in_specs=[
            pl.BlockSpec(memory_space=pltpu.SMEM), once(small.shape), once(qkv.shape), hbm, hbm, hbm,
        ],
        out_specs=[wide] * 6 + [once((4,) + qkv.shape), once((4,) + small.shape), hbm],
        out_shape=[like((rows, D), F32)] + [like((rows, D), BF16)] * 5 + [
            like((4,) + qkv.shape, BF16), like((4,) + small.shape, F32), like(share.shape, BF16),
        ],
        scratch_shapes=[
            pltpu.VMEM((PLACES, D), F32), pltpu.VMEM((canvases, 3, PLACES, LANES), BF16),
            pltpu.VMEM((rows, LANES), BF16), pltpu.VMEM((SMALL_SIZE, D), F32),
            pltpu.VMEM((3,) + qkv.shape, BF16), pltpu.VMEM((4,) + small.shape, F32),
            pltpu.SemaphoreType.DMA((canvases, 3)), pltpu.SemaphoreType.DMA((canvases, 3)),
            pltpu.SemaphoreType.DMA((6,)), pltpu.SemaphoreType.DMA((6,)),
            pltpu.SemaphoreType.DMA((count,)), pltpu.SemaphoreType.DMA((count,)),
            pltpu.SemaphoreType.DMA((1,)),
        ],
        compiler_params=params(collective_id=1, has_side_effects=True),
        name="head",
    )(ids, small, qkv, block_in, qkv, share)


def front_kernel(
    canvases, ids_ref, query_ref, key_ref, value_ref, small_in,
    soft_ref, context_ref, conv_ref, attended_ref,
    mask_ref, grid_ref, out_ref, x_ref, small_ref, crpe_ref,
):
    cut, col_cuts = read_cuts(ids_ref, canvases)

    @pl.when(pl.program_id(0) == 0)
    def _():
        grid_ref[...] = jnp.zeros_like(grid_ref)
        spread_small(small_in, small_ref)
        spread_taps(small_ref, CRPE, 49, True, crpe_ref)

    fill_masks(cut, col_cuts, mask_ref)
    band, side = place_ids(cut, col_cuts)
    ids = 2 * band + side
    sides = [(side == item).astype(F32).astype(BF16) for item in range(2)]
    bands = [(band == item).astype(F32).astype(BF16) for item in range(2)]
    blocks = head_block()
    for tile in range(TILES):
        query = query_ref[:, lane(tile)]
        keys = key_ref[:, lane(tile)].astype(F32)
        value = value_ref[:, lane(tile)]
        highest = crop_reduce(ids, keys, jnp.max, -1e30)
        powers = jnp.exp(keys - pick(ids, highest))
        totals = crop_reduce(ids, powers, jnp.sum, 0.0)
        soft = (powers * pick(ids, [1.0 / item for item in totals])).astype(BF16)
        soft_ref[:, lane(tile)] = soft
        context = (tn(both(soft, sides), both(value, bands)) * blocks).astype(BF16)
        context_ref[0, tile] = context
        factor = nn(both(query, sides), context)
        x_ref[:, lane(tile)] = jnp.where(band > 0, factor[:, LANES:], factor[:, :LANES]) * SCALE
    for tile in range(TILES):
        spread(
            lambda row: value_ref[SIDE * row : SIDE * row + SIDE, lane(tile)].astype(F32),
            REACH[tile], cut, mask_ref, grid_ref, 3,
        )
        conv_tiles(((tile, 3),), REACH[tile], cut, grid_ref, crpe_ref, 3, out_ref)
    conv = out_ref[:PLACES, :]
    conv_ref[...] = conv.astype(BF16)
    attended_ref[...] = (x_ref[...] + query_ref[...].astype(F32) * conv).astype(BF16)


def front(ids, query, key, value, small):
    rows = query.shape[0]
    count = rows // PLACES
    wide = rows_spec(D)
    return pl.pallas_call(
        lambda *refs: front_kernel(count, *refs),
        grid_spec=pltpu.PrefetchScalarGridSpec(
            num_scalar_prefetch=1,
            grid=(count,),
            in_specs=[wide, wide, wide, once(small.shape)],
            out_specs=[wide, context_spec(0), wide, wide],
            scratch_shapes=[
                pltpu.VMEM((2, 7, SIDE, LANES), F32),
                pltpu.VMEM((7, GRID_ROWS * SIDE, LANES), F32),
                pltpu.VMEM((PLACES + SIDE, D), F32),
                pltpu.VMEM((PLACES, D), F32),
                pltpu.VMEM((SMALL_SIZE, D), F32),
                pltpu.VMEM((49, 8, D), F32),
            ],
        ),
        out_shape=[
            like((rows, D), BF16), like((count, TILES, 2 * LANES, 2 * LANES), BF16),
            like((rows, D), BF16), like((rows, D), BF16),
        ],
        compiler_params=params(),
        cost_estimate=pl.CostEstimate(
            flops=rows * D * D * 40, bytes_accessed=count * 10**7, transcendentals=0
        ),
        name="front",
    )(ids, query, key, value, small)


def gelu_both(pre):
    power = jnp.exp(pre * pre * -0.5)
    t = 1.0 / (1.0 + jnp.abs(pre) * (0.3275911 * 0.7071067811865476))
    poly = 0.5 * 1.061405429
    for item in (-1.453152027, 1.421413741, -0.284496736, 0.254829592):
        poly = poly * t + 0.5 * item
    tail = poly * t * power
    cdf = jnp.where(pre >= 0.0, 1.0 - tail, tail)
    return pre * cdf, cdf + pre * power * 0.3989422804014327


BLOCK = 1024


def middle_kernel(
    count,
    attended_ref, first_ref, cot0_ref, cot1_ref, cot2_ref, cot3_ref, small_in, own_weights,
    far_weights,
    out0_ref, out1_ref, out2_ref, out3_ref, second_grad_ref, att_grad_ref, fc_mid_ref,
    proj_grad_ref, sum_ref, bias_grad_ref,
    cot_ref, hat_ref, inverse_ref, hidden_ref, total_ref, back_ref, active_ref, pre_grad_ref,
    grads_ref, near_ref, far_ref, own_ref, low_ref, small_ref, weights_ref, send, receive, fetch,
):
    me = lax.axis_index("head")
    step = pl.program_id(0)
    rows = attended_ref.shape[0]
    blocks = rows // BLOCK
    _, low, _ = place_on_dp()
    half = low_ref.shape[1]

    def near(item, kind):
        return remote(
            grads_ref.at[2 * item, kind], near_ref.at[item, kind], send.at[2 * item + kind],
            receive.at[2 * item + kind], peer(1),
        )

    def far(kind):
        return remote(
            grads_ref.at[1, kind], far_ref.at[kind], send.at[4 + kind], receive.at[4 + kind], peer(2)
        )

    def to_low(kind):
        return remote(
            own_ref.at[kind, aligned(1 - low, half)], low_ref.at[kind], send.at[6 + kind],
            receive.at[6 + kind], low_peer(),
        )

    def part(index):
        return aligned(index, BLOCK)

    shard = 3 - step
    fc1 = weights_ref.at[shard, :D]
    fc2 = weights_ref.at[shard, D : 2 * D]

    def proj(tile):
        return weights_ref[lax.bitwise_xor(me, tile), 2 * D : 2 * D + LANES, :]

    def relay(number, source, target, part):
        return remote(
            source.at[part], weights_ref.at[target, part], send.at[8 + number], receive.at[8 + number],
            peer(1),
        )

    narrow, broad = pl.ds(2 * D, LANES), pl.ds(0, 2 * D)
    relays = [
        relay(0, own_weights, 1, narrow), relay(1, far_weights, 3, narrow),
        relay(2, far_weights, 3, broad), relay(3, own_weights, 1, broad),
    ]

    @pl.when(step == 0)
    def _():
        loads = [
            pltpu.make_async_copy(own_weights.at[pl.ds(0, 2 * D + LANES)], weights_ref.at[0], fetch.at[0]),
            pltpu.make_async_copy(far_weights.at[pl.ds(0, 2 * D + LANES)], weights_ref.at[2], fetch.at[1]),
        ]
        for move, piece_ref in enumerate((cot0_ref, cot1_ref, cot2_ref, cot3_ref)):
            spot = cot_ref.at[:, aligned(lax.bitwise_xor(me, move), LANES)]
            loads.append(pltpu.make_async_copy(piece_ref, spot, fetch.at[2 + move]))
        for load in loads:
            load.start()
        meet([peer(1), peer(2), low_peer()])
        for item in relays:
            item.start()
        spread_small(small_in, small_ref)
        own_ref[...] = jnp.zeros_like(own_ref)
        sum_ref[...] = jnp.zeros_like(sum_ref)
        for item in loads + relays[:2]:
            item.wait()

        def enter(index, carry):
            now = part(index)
            second = first_ref[now, :] + small_ref[PROJ_BIAS : PROJ_BIAS + 1, :]
            for tile in range(TILES):
                second += nn(attended_ref[now, lane(tile)], proj(tile))
            center = row_mean(second)
            square = row_mean(second * second)
            inverse = lax.rsqrt(square - center * center + EPSILON)
            hat = (second - center) * inverse
            hidden_ref[now, :] = (
                hat * small_ref[GAIN2 : GAIN2 + 1, :] + small_ref[SHIFT2 : SHIFT2 + 1, :]
            ).astype(BF16)
            hat_ref[now, :] = hat
            inverse_ref[now, :] = jnp.broadcast_to(inverse, (BLOCK, LANES))
            total_ref[now, :] = second + small_ref[FC2_BIAS : FC2_BIAS + 1, :]
            back_ref[now, :] = jnp.zeros((BLOCK, D), F32)
            sum_ref[3:4, :] += jnp.sum(cot_ref[now, :].astype(F32), axis=0, keepdims=True)
            return carry

        lax.fori_loop(0, blocks, enter, 0)
        for item in relays[2:]:
            item.wait()

    bias_grad_ref[0] = jnp.zeros_like(bias_grad_ref[0])

    def chunk(index, carry):
        now = part(index)
        bias = jnp.concatenate(
            [small_in[shard, FC1_BIAS + tile : FC1_BIAS + tile + 1, :] for tile in range(TILES)], axis=1
        )
        pre = nn(hidden_ref[now, :], fc1[...]) + bias
        active, slope = gelu_both(pre)
        active = active.astype(BF16)
        active_ref[now, :] = active
        total_ref[now, :] += nn(active, fc2[...])
        pre_grad_f = nt(cot_ref[now, :], fc2[...]) * slope
        pre_grad = pre_grad_f.astype(BF16)
        pre_grad_ref[now, :] = pre_grad
        back_ref[now, :] += nt(pre_grad, fc1[...])
        bias_grad_ref[0] += jnp.sum(pre_grad_f, axis=0, keepdims=True)
        return carry

    lax.fori_loop(0, blocks, chunk, 0)
    grads_ref[step, 0] = tn(hidden_ref[...], pre_grad_ref[...]).astype(BF16)
    grads_ref[step, 1] = tn(active_ref[...], cot_ref[...]).astype(BF16)

    @pl.when(step == 0)
    def _():
        for kind in range(2):
            near(0, kind).start()

    @pl.when(step == 1)
    def _():
        for kind in range(2):
            near(0, kind).wait()
            grads_ref[1, kind] = (
                grads_ref[1, kind].astype(F32) + near_ref[0, kind].astype(F32)
            ).astype(BF16)
            far(kind).start()

    @pl.when(step == 2)
    def _():
        for kind in range(2):
            near(1, kind).start()

    @pl.when(step == 3)
    def _():
        for kind in range(2):
            near(1, kind).wait()
            far(kind).wait()
            own_ref[kind, :D, :] = (
                grads_ref[3, kind].astype(F32) + near_ref[1, kind].astype(F32)
                + far_ref[kind].astype(F32)
            ).astype(BF16)
            to_low(kind).start()

        def leave(index, carry):
            now = part(index)
            for move, piece_ref in enumerate((out0_ref, out1_ref, out2_ref, out3_ref)):
                piece_ref[now, :] = total_ref[now, aligned(lax.bitwise_xor(me, move), LANES)].astype(BF16)
            hat = hat_ref[now, :]
            norm_grad = back_ref[now, :]
            weighted = norm_grad * small_ref[GAIN2 : GAIN2 + 1, :]
            second_grad = cot_ref[now, :].astype(F32) + inverse_ref[now, 0:1] * (
                weighted - row_mean(weighted) - hat * row_mean(weighted * hat)
            )
            second_grad_ref[now, :] = second_grad
            second_low = second_grad.astype(BF16)
            hidden_ref[now, :] = second_low
            for tile in range(TILES):
                att_grad_ref[now, lane(tile)] = nt(
                    second_low, proj(tile)
                ).astype(BF16)
            sum_ref[1:2, :] += jnp.sum(norm_grad * hat, axis=0, keepdims=True)
            sum_ref[2:3, :] += jnp.sum(norm_grad, axis=0, keepdims=True)
            sum_ref[0:1, :] += jnp.sum(second_low.astype(F32), axis=0, keepdims=True)
            return carry

        lax.fori_loop(0, blocks, leave, 0)
        for tile in range(TILES):
            proj_grad_ref[lax.bitwise_xor(me, tile)] = tn(
                attended_ref[:, lane(tile)], hidden_ref[...]
            ).astype(BF16)
        for kind in range(2):
            to_low(kind).wait()
            fc_mid_ref[kind] = (
                own_ref[kind, aligned(low, half), :].astype(F32) + low_ref[kind].astype(F32)
            ).astype(BF16)


def middle(attended, first, cot_parts, small, own_weights, far_weights):
    rows = attended.shape[0]
    count = lax.axis_size("dp")
    padded = padded_rows(D, count)
    hbm = pl.BlockSpec(memory_space=pl.ANY)
    proj_shape = (4, LANES, D)
    piece = once((rows, LANES))
    wide = once((rows, D))
    line = pl.BlockSpec((1, 1, D), lambda i: (3 - i, 0, 0))
    return pl.pallas_call(
        lambda *refs: middle_kernel(count, *refs),
        grid=(4,),
        in_specs=[
            wide, wide, hbm, hbm, hbm, hbm, once(small.shape), hbm, hbm,
        ],
        out_specs=[
            piece, piece, piece, piece, wide, wide, once((2, padded // 2, D)), once(proj_shape),
            once((8, D)), line,
        ],
        out_shape=[like((rows, LANES), BF16)] * 4 + [
            like((rows, D), F32), like((rows, D), BF16), like((2, padded // 2, D), BF16),
            like(proj_shape, BF16), like((8, D), F32), like((4, 1, D), F32),
        ],
        scratch_shapes=[
            pltpu.VMEM((rows, D), BF16), pltpu.VMEM((rows, D), F32),
            pltpu.VMEM((rows, LANES), F32),
            pltpu.VMEM((rows, D), BF16), pltpu.VMEM((rows, D), F32),
            pltpu.VMEM((rows, D), F32), pltpu.VMEM((rows, D), BF16),
            pltpu.VMEM((rows, D), BF16),
            pltpu.VMEM((4, 2, D, D), BF16), pltpu.VMEM((2, 2, D, D), BF16),
            pltpu.VMEM((2, D, D), BF16), pltpu.VMEM((2, padded, D), BF16),
            pltpu.VMEM((2, padded // 2, D), BF16),
            pltpu.VMEM((SMALL_SIZE, D), F32), pltpu.VMEM((4, 2 * D + LANES, D), BF16),
            pltpu.SemaphoreType.DMA((12,)), pltpu.SemaphoreType.DMA((12,)),
            pltpu.SemaphoreType.DMA((6,)),
        ],
        compiler_params=params(collective_id=2, has_side_effects=True),
        cost_estimate=pl.CostEstimate(flops=rows * D * D * 60, bytes_accessed=3 * 10**7, transcendentals=0),
        name="middle",
    )(attended, first, *cot_parts, small, own_weights, far_weights)


def back_kernel(
    canvases, ids_ref, grad_ref, query_ref, value_ref, soft_ref, context_ref, conv_ref, hidden_ref,
    small_in, middle_sum_ref, bias_grad_ref,
    three_ref, qkv_out_ref, small_out_ref,
    mask_ref, grid_ref, out_ref, other_ref, value_part_ref, qkv_grad_ref, small_ref, crpe_ref,
    crpe_sum_ref, sum_ref, late_ref,
):
    cut, col_cuts = read_cuts(ids_ref, canvases)
    me = lax.axis_index("head")

    @pl.when(pl.program_id(0) == 0)
    def _():
        grid_ref[...] = jnp.zeros_like(grid_ref)
        other_ref[...] = jnp.zeros_like(other_ref)
        qkv_grad_ref[...] = jnp.zeros_like(qkv_grad_ref)
        crpe_sum_ref[...] = jnp.zeros_like(crpe_sum_ref)
        sum_ref[...] = jnp.zeros_like(sum_ref)
        spread_small(small_in, small_ref)
        spread_taps(small_ref, CRPE, 49, True, crpe_ref)

    fill_masks(cut, col_cuts, mask_ref)
    band, side = place_ids(cut, col_cuts)
    ids = 2 * band + side
    sides = [(side == item).astype(F32).astype(BF16) for item in range(2)]
    bands = [(band == item).astype(F32).astype(BF16) for item in range(2)]
    blocks = head_block() * SCALE
    for tile in range(TILES):
        grad = grad_ref[:, lane(tile)]
        query = query_ref[:, lane(tile)]
        value = value_ref[:, lane(tile)]
        soft = soft_ref[:, lane(tile)]
        context = context_ref[0, tile]
        grad_f = grad.astype(F32)
        grad_bands = both(grad, bands)
        context_grad = (tn(both(query, sides), grad_bands) * blocks).astype(BF16)
        part = nt(grad_bands, context)
        part = jnp.where(side > 0, part[:, LANES:], part[:, :LANES])
        query_grad = (
            part * SCALE + grad_f * conv_ref[:, lane(tile)].astype(F32)
        ).astype(BF16)
        soft_grad = nt(both(value, bands), context_grad)
        soft_grad = jnp.where(side > 0, soft_grad[:, LANES:], soft_grad[:, :LANES])
        soft_f = soft.astype(F32)
        inner = crop_reduce(ids, soft_f * soft_grad, jnp.sum, 0.0)
        keys_grad = (soft_f * (soft_grad - pick(ids, inner))).astype(BF16)
        value_part = nn(both(soft, sides), context_grad)
        value_part_ref[:, lane(tile)] = jnp.where(
            band > 0, value_part[:, LANES:], value_part[:, :LANES]
        )
        three_ref[tile, :, :LANES] = query_grad
        three_ref[tile, :, LANES : 2 * LANES] = keys_grad
        sum_ref[0:1, lane(tile)] += jnp.sum(query_grad.astype(F32), axis=0, keepdims=True)
    other_ref[:PLACES, :] = value_ref[...].astype(F32)
    for tile in range(TILES):

        def read_row(row):
            part = pl.ds(SIDE * row, SIDE)
            return grad_ref[part, lane(tile)].astype(F32) * query_ref[part, lane(tile)].astype(F32)

        spread(read_row, REACH[tile], cut, mask_ref, grid_ref, 3)
        conv_back_tiles(
            ((tile, 3),), REACH[tile], cut, grid_ref, crpe_ref, 3, other_ref, out_ref, crpe_sum_ref
        )
    hidden = hidden_ref[...]
    for tile in range(TILES):
        value_grad = (value_part_ref[:, lane(tile)] + out_ref[:PLACES, lane(tile)]).astype(BF16)
        three_ref[tile, :, 2 * LANES :] = value_grad
        sum_ref[1:2, lane(tile)] += jnp.sum(value_grad.astype(F32), axis=0, keepdims=True)
        qkv_grad_ref[lax.bitwise_xor(me, tile)] += tn(hidden, three_ref[tile])

    @pl.when(pl.program_id(0) == pl.num_programs(0) - 1)
    def _():
        qkv_out_ref[...] = qkv_grad_ref[...].astype(BF16)
        late_ref[...] = jnp.zeros_like(late_ref)
        for tap in range(49):
            for tile in range(TILES):
                late_ref[tap : tap + 1, lane(tile)] = keep_head(
                    tap, tile, jnp.sum(crpe_sum_ref[tap, :, lane(tile)], axis=0, keepdims=True)
                )
        late_ref[49:51, :] = sum_ref[0:2, :]
        late_ref[51:55, :] = middle_sum_ref[0:4, :]
        for move in range(4):
            late = late_ref[:, aligned(lax.bitwise_xor(me, move), LANES)]
            small_out_ref[move] = late.astype(BF16)
            small_out_ref[move, 64:80, :] = jnp.concatenate(
                [bias_grad_ref[move, :, lane(tile)] for tile in range(TILES)]
                + [jnp.zeros((12, LANES), F32)],
                axis=0,
            ).astype(BF16)


def back(ids, grad, query, value, soft, context, conv, hidden, small, middle_sum, bias_grad):
    rows = grad.shape[0]
    count = rows // PLACES
    wide = rows_spec(D)
    shards = (4, D, 3 * LANES)
    late = (4, SMALL_ROWS, LANES)
    return pl.pallas_call(
        lambda *refs: back_kernel(count, *refs),
        grid_spec=pltpu.PrefetchScalarGridSpec(
            num_scalar_prefetch=1,
            grid=(count,),
            in_specs=[
                wide, wide, wide, wide, context_spec(0), wide, wide, once(small.shape),
                once(middle_sum.shape), once(bias_grad.shape),
            ],
            out_specs=[
                pl.BlockSpec((TILES, PLACES, 3 * LANES), lambda i, *_: (0, i, 0)),
                once(shards), once(late),
            ],
            scratch_shapes=[
                pltpu.VMEM((2, 7, SIDE, LANES), F32),
                pltpu.VMEM((7, GRID_ROWS * SIDE, LANES), F32),
                pltpu.VMEM((PLACES + SIDE, D), F32),
                pltpu.VMEM((PLACES + SIDE, D), F32),
                pltpu.VMEM((PLACES, D), F32),
                pltpu.VMEM(shards, F32),
                pltpu.VMEM((SMALL_SIZE, D), F32),
                pltpu.VMEM((49, 8, D), F32),
                pltpu.VMEM((49, 8, D), F32),
                pltpu.VMEM((8, D), F32),
                pltpu.VMEM((SMALL_ROWS, D), F32),
            ],
        ),
        out_shape=[
            like((TILES, rows, 3 * LANES), BF16), like(shards, BF16), like(late, BF16),
        ],
        compiler_params=params(),
        cost_estimate=pl.CostEstimate(
            flops=rows * D * D * 64, bytes_accessed=count * 10**7, transcendentals=0
        ),
        name="back",
    )(ids, grad, query, value, soft, context, conv, hidden, small, middle_sum, bias_grad)


LAST_ROWS = 16
STAGES = ((0, 1, 2, 3, 4, 5), (0, 1, 3, 4, 5, 6), (0, 1, 3, 5, 6, 7), (0, 1, 4, 6, 7, 8))
FC_STAGES = ((0, 2, 4), (1, 4, 6))


def tail_kernel(
    count, pieces,
    canvases, ids_ref, x_in, three_ref, first_ref, second_grad_ref, small_params,
    qkv_ref, fc_mid_in, small_in, proj_grad_in, qkv_grad_in,
    out0_ref, out1_ref, out2_ref, out3_ref, fc1_own_ref, fc2_own_ref, small_own_ref, proj_own_ref,
    qkv_own_ref, last_own_ref,
    x_ref, gone_ref, cpe_sum_ref, sum_ref, fc_part_ref, fc_whole_ref, fc_got_ref, mine_ref, first_got_ref,
    total_ref, second_got_ref, piece_send, piece_receive, send, receive, last_send, last_receive,
    cpe_ref, fc_mid_ref, small_ref, proj_grad_ref, qkv_grad_ref, *buffers,
):
    me = lax.axis_index("head")
    dp = lax.axis_index("dp")
    step = pl.program_id(0)
    steps = pl.num_programs(0)
    slots = high_slots(count)
    fc_sums = [
        HighSum(
            count, fc_mid_ref.at[kind], fc_part_ref.at[kind], fc_whole_ref.at[kind],
            fc_got_ref.at[kind], send, receive, kind * slots,
        )
        for kind in range(2)
    ]
    sources = (small_ref, proj_grad_ref, qkv_grad_ref)
    targets = (small_own_ref, proj_own_ref, qkv_own_ref)
    sums = []
    for number, (item, start, height, padded, lanes) in enumerate(pieces):
        near, far, own, mid, low, part, got = buffers[7 * number : 7 * number + 7]
        sums.append(
            FullSum(
                count, sources[item], pl.ds(start, height), near, far, own, mid, low, part, got, send,
                receive, 2 * slots + number * (slots + 4),
            )
        )

    def piece_copy(index, move):
        target = (out1_ref, out2_ref, out3_ref)[move - 1]
        return remote(
            gone_ref.at[index, move - 1], target.at[aligned(index, PLACES)],
            piece_send.at[index, move - 1], piece_receive.at[index, move - 1], peer(move),
        )

    def first_copy(move):
        return remote(
            mine_ref.at[move], first_got_ref.at[move - 1], last_send.at[move - 1],
            last_receive.at[move - 1], peer(move),
        )

    def second_copy(hop):
        return remote(
            total_ref, second_got_ref.at[hop - 1], last_send.at[2 + hop], last_receive.at[2 + hop],
            (lax.rem(dp + hop, count), me),
        )

    @pl.when(step == 0)
    def _():
        meet(
            [peer(1), peer(2), peer(3)] + [(lax.rem(dp + hop, count), me) for hop in range(1, count)]
        )
        spread_small(small_params, cpe_ref)
        fc_mid_ref[...] = fc_mid_in[...]
        qkv_grad_ref[...] = qkv_grad_in[...]
        proj_grad_ref[...] = proj_grad_in[...]
        small_ref[...] = small_in[...]
        cpe_sum_ref[...] = jnp.zeros_like(cpe_sum_ref)
        sum_ref[...] = jnp.zeros_like(sum_ref)

    events = []
    for item, slots_of in zip(sums, STAGES):
        actions = (
            item.to_core, item.to_far, item.to_low, item.to_high, item.rest.share_high, item.rest.share_low,
        )
        events += list(zip(slots_of, actions))
    for item, slots_of in zip(fc_sums, FC_STAGES):
        events += list(zip(slots_of, (item.to_high, item.share_high, item.share_low)))

    def run(when):
        for slot, action in events:
            if slot == when:
                action()

    for when in range(canvases):
        pl.when(step == when)(lambda: run(when))

    norm_grad = nt(three_ref[0], qkv_ref[lax.bitwise_xor(me, 0)])
    for tile in range(1, TILES):
        norm_grad += nt(three_ref[tile], qkv_ref[lax.bitwise_xor(me, tile)])
    first = first_ref[...]
    center = row_mean(first)
    square = row_mean(first * first)
    inverse = lax.rsqrt(square - center * center + EPSILON)
    hat = (first - center) * inverse
    weighted = norm_grad * cpe_ref[GAIN1 : GAIN1 + 1, :]
    first_grad = second_grad_ref[...] + inverse * (
        weighted - row_mean(weighted) - hat * row_mean(weighted * hat)
    )
    sum_ref[0:1, :] += jnp.sum(first_grad, axis=0, keepdims=True)
    sum_ref[1:2, :] += jnp.sum(norm_grad * hat, axis=0, keepdims=True)
    sum_ref[2:3, :] += jnp.sum(norm_grad, axis=0, keepdims=True)
    x_ref[...] = x_in[...].astype(F32)
    rows, cols = step_masks(*read_cuts(ids_ref, canvases))
    results = []
    for tile in range(TILES):
        field = first_grad[:, LANES * tile : LANES * (tile + 1)]
        other = x_ref[:, lane(tile)]
        others = {0: other, 1: shift_rows(other * rows[1], -1), -1: shift_rows(other * rows[-1], 1)}
        moved = [shift_cols(field, cols, col) for col in (-1, 0, 1)]
        result = field
        for row in (-1, 0, 1):
            line = None
            for col in (-1, 0, 1):
                tap = (1 - row) * 3 + 1 - col
                wide_tap = jnp.broadcast_to(cpe_ref[tap : tap + 1, lane(tile)], (PLACES, LANES))
                term = wide_tap * moved[col + 1]
                line = term if line is None else line + term
                product = others[row] * moved[col + 1]
                cpe_sum_ref[tap, :, lane(tile)] += jnp.sum(product.reshape(PLACES // 8, 8, LANES), axis=0)
            line = shift_rows(line, row)
            result = result + (line * rows[row] if row else line)
        results.append(result)
    result = jnp.concatenate(results, axis=1)
    x_ref[...] = result
    out0_ref[...] = x_ref[:, aligned(me, LANES)].astype(BF16)
    for move in (1, 2, 3):
        gone_ref[step, move - 1] = x_ref[:, aligned(lax.bitwise_xor(me, move), LANES)].astype(BF16)
    for move in (2, 3, 1):
        piece_copy(step, move).start()

    @pl.when(step == steps - 1)
    def _():
        sum_ref[3:12, :] = jnp.sum(cpe_sum_ref[...], axis=1)
        for move in range(4):
            mine_ref[move] = sum_ref[:, aligned(lax.bitwise_xor(me, move), LANES)]
        for move in (1, 2, 3):
            first_copy(move).start()
        run(canvases)
        total = mine_ref[0]
        for move in (1, 2, 3):
            first_copy(move).wait()
            total += first_got_ref[move - 1]
        total_ref[...] = total
        for hop in range(1, count):
            second_copy(hop).start()
        run(canvases + 1)
        for item in fc_sums:
            item.finish()
        fc1_own_ref[...] = fc_whole_ref[0, :D, :]
        fc2_own_ref[...] = fc_whole_ref[1, :D, :]
        for hop in range(1, count):
            second_copy(hop).wait()
            total += second_got_ref[hop - 1]
        last_own_ref[...] = total
        for piece, item in zip(pieces, sums):
            item.rest.finish()
            targets[piece[0]][piece[1] : piece[1] + piece[2], :] = item.whole[: piece[2], :]

        def settle(index, carry):
            for move in (1, 2, 3):
                piece_copy(index, move).wait()
            return carry

        lax.fori_loop(0, steps, settle, 0)


def tail(ids, x, three, first, second_grad, params_small, qkv, fc_mid, qkv_grad, proj_grad, small):
    rows = first.shape[0]
    canvases = rows // PLACES
    count = lax.axis_size("dp")
    segments = [small, proj_grad, qkv_grad]
    pieces = plan_pieces([item.shape[1:] for item in segments], count)
    slots = high_slots(count)
    wide = rows_spec(D)
    piece = rows_spec(LANES)
    hbm = pl.BlockSpec(memory_space=pl.ANY)
    half = fc_mid.shape[1]
    group = count // 2
    total_slots = 2 * slots + len(pieces) * (slots + 4)
    last = (LAST_ROWS, LANES)
    return pl.pallas_call(
        lambda *refs: tail_kernel(count, pieces, canvases, *refs),
        grid=(canvases,),
        in_specs=[pl.BlockSpec(memory_space=pltpu.SMEM), wide] + [
            pl.BlockSpec((TILES, PLACES, 3 * LANES), lambda i: (0, i, 0)), wide, wide,
            once(params_small.shape), once(qkv.shape), once(fc_mid.shape),
        ] + [once(item.shape) for item in segments],
        out_specs=[piece, hbm, hbm, hbm, once((D, D)), once((D, D))]
        + [once(item.shape[1:]) for item in segments] + [once(last)],
        out_shape=[like((rows, LANES), BF16)] * 4 + [like((D, D), BF16)] * 2
        + [like(item.shape[1:], BF16) for item in segments] + [like(last, F32)],
        scratch_shapes=[
            pltpu.VMEM((PLACES, D), F32), pltpu.VMEM((canvases, 3, PLACES, LANES), BF16),
            pltpu.VMEM((9, 8, D), F32), pltpu.VMEM((LAST_ROWS, D), F32),
            pltpu.VMEM((2, group - 1, half // group, D), BF16), pltpu.VMEM((2, 2 * half, D), BF16),
            pltpu.VMEM((2, half, D), BF16),
            pltpu.VMEM((4,) + last, F32), pltpu.VMEM((3,) + last, F32), pltpu.VMEM(last, F32),
            pltpu.VMEM((count - 1,) + last, F32),
            pltpu.SemaphoreType.DMA((canvases, 3)), pltpu.SemaphoreType.DMA((canvases, 3)),
            pltpu.SemaphoreType.DMA((total_slots,)), pltpu.SemaphoreType.DMA((total_slots,)),
            pltpu.SemaphoreType.DMA((2 + count,)), pltpu.SemaphoreType.DMA((2 + count,)),
        ] + [pltpu.VMEM((SMALL_SIZE, D), F32)]
        + [pltpu.VMEM(item.shape, BF16) for item in [fc_mid] + segments]
        + sum_scratch(pieces, count),
        compiler_params=params(collective_id=3, has_side_effects=True),
        cost_estimate=pl.CostEstimate(
            flops=rows * D * D * 12, bytes_accessed=canvases * 3 * 10**6, transcendentals=0
        ),
        name="tail",
    )(ids, x, three, first, second_grad, params_small, qkv, fc_mid, *segments)


def finish_kernel(
    me_ref, p0_ref, p1_ref, p2_ref, p3_ref, q0_ref, q1_ref, q2_ref, q3_ref, fc1_ref, fc2_ref, small_ref, proj_ref, qkv_ref, last_ref,
    grad_ref, block_out_ref, cpe_ref, vectors_ref, qkv_out_ref, qv_ref, crpe_ref, proj_out_ref, fc1_out_ref,
    bias_ref, fc2_out_ref,
):
    pairs = ((p0_ref, q0_ref), (p1_ref, q1_ref), (p2_ref, q2_ref), (p3_ref, q3_ref))
    for item, (piece_ref, out_piece_ref) in enumerate(pairs):

        @pl.when(pl.program_id(0) == item)
        def _():
            grad_ref[...] = piece_ref[...].astype(F32)
            block_out_ref[...] = out_piece_ref[...].astype(F32)

    @pl.when(pl.program_id(0) == 0)
    def _():
        cpe_ref[...] = last_ref[3:12, :]
        small = small_ref[...].astype(F32)
        vectors_ref[...] = jnp.concatenate(
            [last_ref[0:3, :], small[51:55, :], jnp.zeros((1, LANES), F32)], axis=0
        )
        qkv_out_ref[...] = qkv_ref[...].astype(F32)
        qv_ref[...] = small[49:51, :]
        crpe_ref[...] = small[:49, :]
        proj_out_ref[...] = proj_ref[...].astype(F32)
        fc1_out_ref[...] = fc1_ref[...].astype(F32)
        bias_ref[...] = small[64:68, :]
        fc2_out_ref[...] = fc2_ref[...].astype(F32)


def finish(me, pieces, out_pieces, fc1, fc2, small, proj, qkv, last):
    rows = pieces[0].shape[0]
    shapes = [
        (9, LANES), (8, LANES), qkv.shape, (2, LANES), (49, LANES), proj.shape, fc1.shape,
        (4, LANES), fc2.shape,
    ]
    return pl.pallas_call(
        finish_kernel,
        grid_spec=pltpu.PrefetchScalarGridSpec(
            num_scalar_prefetch=1,
            grid=(4,),
            in_specs=[once((rows, LANES))] * 8
            + [once(item.shape) for item in (fc1, fc2, small, proj, qkv, last)],
            out_specs=[
                pl.BlockSpec((rows, LANES), lambda i, me: (lax.bitwise_xor(me[0], i), 0)),
            ] * 2 + [once(shape) for shape in shapes],
        ),
        out_shape=[like((4 * rows, LANES), F32)] * 2 + [like(shape, F32) for shape in shapes],
        compiler_params=params(),
        name="finish",
    )(me, *pieces, *out_pieces, fc1, fc2, small, proj, qkv, last)


def body(
    block_in, crop_ids, cotangent, cpe_kernel, cpe_bias, norm1_gain, norm1_shift, qkv_weight,
    qv_bias, crpe_kernel, proj_weight, proj_bias, norm2_gain, norm2_shift, fc1_weight, fc1_bias,
    fc2_weight, fc2_bias,
):
    head = lax.axis_index("head")
    me = head.reshape(1).astype(jnp.int32)
    rows = block_in.shape[0] // 4
    ids = crop_ids.reshape(crop_ids.shape[0], PLACES)

    def swap(values, move):
        return lax.ppermute(values, "head", [(item, item ^ move) for item in range(4)])

    packed = jnp.concatenate([
        cpe_kernel, crpe_kernel, cpe_bias[None], norm1_gain[None], norm1_shift[None], qv_bias,
        proj_bias[None], norm2_gain[None], norm2_shift[None], fc2_bias[None],
        fc1_bias.reshape(4, LANES), jnp.zeros((1, LANES), BF16),
    ]).astype(F32)
    own_weights = jnp.concatenate([fc1_weight, fc2_weight, proj_weight])
    extra = padded_rows(own_weights.shape[0], lax.axis_size("dp")) - own_weights.shape[0]
    if extra:
        own_weights = jnp.pad(own_weights, ((0, extra), (0, 0)))
    first, hidden, query, key, value, x, qkv, small, far_weights = head_part(
        ids, packed, qkv_weight.reshape(D, 3 * LANES), block_in, own_weights
    )
    cotangent, query = lax.optimization_barrier((cotangent, query))
    cot_pieces = [
        lax.dynamic_slice_in_dim(cotangent, lax.bitwise_xor(head, move) * rows, rows, 0)
        for move in range(4)
    ]
    cot_parts = [cot_pieces[0]] + [swap(cot_pieces[move], move) for move in (1, 2, 3)]

    soft, context, conv, attended = front(ids, query, key, value, small)
    results = middle(attended, first, cot_parts, small, own_weights, far_weights)
    second_grad, att_grad, fc_mid, proj_grad, middle_sum, bias_grad = results[4:]
    out_parts = [results[0]] + [swap(results[move], move) for move in (1, 2, 3)]
    three, qkv_grad, small_grad = back(
        ids, att_grad, query, value, soft, context, conv, hidden, small, middle_sum, bias_grad
    )
    three, out_parts = lax.optimization_barrier((three, out_parts))
    results = tail(
        ids, x, three, first, second_grad, small, qkv, fc_mid, qkv_grad, proj_grad, small_grad
    )
    (input_grad, block_out, cpe_g, vectors, qkv_g, qv_g, crpe_g, proj_g, fc1_g, bias_g, fc2_g) = finish(
        me, results[:4], out_parts, *results[4:]
    )
    return (
        block_out, input_grad, cpe_g, vectors[0], vectors[1], vectors[2],
        qkv_g.reshape(D, 3, LANES), qv_g, crpe_g, proj_g, vectors[3], vectors[4], vectors[5],
        fc1_g, bias_g.reshape(D), fc2_g, vectors[6],
    )


def solution(mesh):
    return jax.shard_map(
        body,
        mesh=mesh,
        in_specs=(
            P("dp", "head"), P("dp", None, None), P("dp", "head"), P(None, "head"), P("head"),
            P("head"), P("head"), P(None, None, "head"), P(None, "head"), P(None, "head"),
            P("head", None), P("head"), P("head"), P("head"), P(None, "head"), P("head"),
            P("head", None), P("head"),
        ),
        out_specs=(
            P("dp", "head"), P("dp", "head"), P(None, "head"), P("head"), P("head"), P("head"),
            P(None, None, "head"), P(None, "head"), P(None, "head"), P("head", None), P("head"),
            P("head"), P("head"), P(None, "head"), P("head"), P("head", None), P("head"),
        ),
        check_vma=False,
    )
```
